32 devices in a mesh: seq: 8 (over z, x), mlp: 4 (over y, core).
Axes of the slice: x: 2, y: 2, z: 4, core: 2. Of those that a mesh axis runs over, the one named last changes fastest.
Arguments:
- tokens: bfloat16 [12, 2048, 1024], P(None, 'seq'), may hold values from -6 to 6
- lengths: int32 [12, 8], replicated, may hold values from 1 to 2048, as said below
- counts: int32 [12], replicated, may hold values from 1 to 8
- norm_gain: float32 [1024], replicated, may hold values from 0.5 to 1.5
- norm_bias: float32 [1024], replicated, may hold values from -4 to 4
- head_weight: bfloat16 [3, 1024, 1024], P(None, None, 'mlp'), may hold values from -0.1875 to 0.1875
- merge_weight: bfloat16 [1024, 1024], P('mlp'), may hold values from -1.5 to 1.5
- up_weight: bfloat16 [1024, 4096], P(None, 'mlp'), may hold values from -0.1875 to 0.1875
- up_bias: float32 [4096], P('mlp'), may hold values from -6 to 6
- down_weight: bfloat16 [4096, 1024], P('mlp'), may hold values from -0.09375 to 0.09375
- down_bias: float32 [1024], replicated, may hold values from -6 to 6
- cotangent: bfloat16 [12, 2048, 1024], P(None, 'seq', 'mlp'), may hold values from -6 to 6
Outputs:
- result: bfloat16 [12, 2048, 1024], P(None, 'seq', 'mlp')
- tokens_grad: bfloat16 [12, 2048, 1024], P(None, 'seq')
- gain_grad: float32 [1024], P('seq')
- shift_grad: float32 [1024], P('seq')
- head_grad: float32 [3, 1024, 1024], P(None, 'seq', 'mlp')
- merge_grad: float32 [1024, 1024], P('mlp', 'seq')
- up_grad: float32 [1024, 4096], P('seq', 'mlp')
- up_bias_grad: float32 [4096], P(('mlp', 'seq'))
- down_grad: float32 [4096, 1024], P('mlp', 'seq')
- down_bias_grad: float32 [1024], P('seq')
The draws below stay inside these ranges and needn't reach their ends.
Inputs may be any that keep to these rules, and one draw needn't show every extreme that they name: In row p the first counts[p] entries are the lengths of the proteins packed from position 0; they sum to at most 2048, and positions after them are padding. Later entries are to be ignored. In every draw one pack holds a single protein of 2048 residues.
All inputs are finite; a program needn't handle non-finite values.
Results may differ from the reference program's by a relative error of at most 0.011.
Values may be sent and summed in bfloat16 or wider, within the bound.
A program may use at most 320 MiB of HBM per device.

```python
import math
import jax
import jax.numpy as jnp
from jax import lax

D = 1024
H = 16
HD = 64
ROT = 32
FF = 4096
PACKS = 12
SLOTS = 8
PACK_LEN = 2048
HH = 1024


def pack_plan(key):
    keys = jax.random.split(key, 5)
    rows = jnp.arange(PACKS)
    full = jax.random.randint(keys[0], (), 0, PACKS)
    counts = jax.random.randint(keys[1], (PACKS,), 2, SLOTS + 1)
    counts = jnp.where(rows == (full + 1) % PACKS, SLOTS, counts)
    counts = jnp.where(rows == full, 1, counts)
    raw = jax.random.randint(keys[2], (PACKS, SLOTS), 1, 64)
    used = jnp.arange(SLOTS)[None, :] < counts[:, None]
    total = jnp.sum(jnp.where(used, raw, 0), axis=1)
    padding = jax.random.randint(keys[3], (PACKS,), 0, PACK_LEN // 8 + 1)
    room = PACK_LEN - SLOTS - padding
    sizes = jnp.maximum(raw * room[:, None] // total[:, None], 1)
    junk = jax.random.randint(keys[4], (PACKS, SLOTS), 1, PACK_LEN)
    sizes = jnp.where(used, sizes, junk)
    first = (rows[:, None] == full) & (jnp.arange(SLOTS)[None, :] == 0)
    sizes = jnp.where(first, PACK_LEN, sizes)
    return (sizes.astype(jnp.int32), counts.astype(jnp.int32))


def draw_lengths(key, part):
    return pack_plan(key)[0]


def draw_counts(key, part):
    return pack_plan(key)[1]


def raised(values, rng, source, target, blocks, factor):
    def block_of(dim):
        return (jnp.arange(values.shape[dim]) // (values.shape[dim] // blocks)).reshape((-1,) + (1,) * (values.ndim - 1 - dim))

    first = jax.random.permutation(rng, blocks)[block_of(target)]
    other_side = (block_of(target) + blocks // 2) % blocks
    return jnp.where((block_of(source) == first) | (block_of(source) == other_side), factor * values, values)


def levels(stream_key, dims, cuts, smallest, top_value):
    factor_of = 1.0
    for dim, blocks in cuts:
        steps = jax.random.uniform(jax.random.fold_in(jax.random.fold_in(stream_key, 6), dim), (blocks,), jnp.float32, smallest / len(cuts), top_value / len(cuts))
        factor_of = factor_of * jnp.repeat(jnp.exp(steps), dims[dim] // blocks).reshape((-1,) + (1,) * (len(dims) - 1 - dim))
    return factor_of


def noise(rng, dims, spread, bound, cuts=(), kind=jnp.bfloat16):
    level = levels(rng, dims, cuts, -0.22, 0.18) if cuts else 1.0
    values = jax.random.normal(rng, dims, jnp.float32) * spread * level
    return jnp.minimum(jnp.maximum(values, -bound), bound).astype(kind)


def gaussian_with(key, dims, width, most, cuts, heavy, kind=jnp.bfloat16):
    entries = width * jax.random.normal(key, dims, jnp.float32)
    if cuts:
        entries = entries * levels(key, dims, cuts, -0.22, 0.18)
    return jnp.clip(raised(entries, jax.random.fold_in(key, 3), *heavy), -most, most).astype(kind)


def setup_inputs(seed: int = 0) -> dict:
    splits = jax.random.split(jax.random.key(seed), 13)
    return {
        "tokens": gaussian_with(splits[0], (PACKS, PACK_LEN, D), 1.0, 6.0, ((1, 8),), (1, 2, 8, 2.0)),
        "lengths": draw_lengths(jax.random.fold_in(splits[12], 71), 0),
        "counts": draw_counts(jax.random.fold_in(splits[12], 71), 0),
        "norm_gain": jnp.clip(1.0 + 0.1 * jax.random.normal(splits[3], (D,), jnp.float32), 0.5, 1.5),
        "norm_bias": noise(splits[4], (D,), 0.3, 4.0, (), jnp.float32),
        "head_weight": noise(splits[5], (3, D, HH), D ** -0.5, 0.1875, ((2, 4),)),
        "merge_weight": noise(splits[6], (HH, D), (max(HH // 64, 1)) ** -0.5, 1.5, ((0, 4),)),
        "up_weight": noise(splits[7], (D, FF), D ** -0.5, 0.1875, ((1, 4),)),
        "up_bias": noise(splits[8], (FF,), 0.5, 6.0, ((0, 4),), jnp.float32),
        "down_weight": noise(splits[9], (FF, D), FF ** -0.5, 0.09375, ((0, 4),)),
        "down_bias": noise(splits[10], (D,), 0.5, 6.0, (), jnp.float32),
        "cotangent": gaussian_with(splits[11], (PACKS, PACK_LEN, D), 1.0, 6.0, ((1, 8), (2, 4)), (1, 2, 8, 2.0)),
    }


@jax.custom_vjp
def low(v):
    return lax.optimization_barrier(v.astype(jnp.bfloat16)).astype(jnp.float32)

@jax.custom_vjp
def low_back(v):
    return v

def low_keep(v):
    return (low(v), None)

def low_pass(kept, grad):
    return (grad,)

def back_keep(v):
    return (v, None)

def back_low(kept, grad):
    return (low(grad),)
low.defvjp(low_keep, low_pass)
low_back.defvjp(back_keep, back_low)
EPS = 1e-05
NEG = -1e+30

def normalize(inputs, gain, shift):
    mean = lax.optimization_barrier(jnp.mean(inputs, axis=-1, keepdims=True))
    cent = inputs - mean
    var = lax.optimization_barrier(jnp.mean(cent * cent, axis=-1, keepdims=True))
    return cent * lax.rsqrt(var + EPS) * gain + shift

def rotate(values, place, rot):
    half = rot // 2
    freq = 10000.0 ** (-(2.0 * jnp.arange(half, dtype=jnp.float32)) / rot)
    angle = place.astype(jnp.float32)[..., None, None] * freq
    cosine = jnp.cos(angle)
    sine = jnp.sin(angle)
    pairs = values[..., :rot].reshape(values.shape[:-1] + (half, 2))
    first = pairs[..., 0]
    second = pairs[..., 1]
    turned = jnp.stack([first * cosine - second * sine, second * cosine + first * sine], axis=-1)
    return jnp.concatenate([turned.reshape(values.shape[:-1] + (rot,)), values[..., rot:]], axis=-1)

def layout(lengths, counts, pack_len):
    slots = lengths.shape[-1]
    slot_ids = jnp.arange(slots, dtype=jnp.int32)
    used = slot_ids[None, :] < counts[:, None]
    sizes = jnp.where(used, lengths, 0).astype(jnp.int32)
    ends = jnp.cumsum(sizes, axis=-1).astype(jnp.int32)
    starts = (ends - sizes).astype(jnp.int32)
    filled = ends[:, -1:]
    place = jnp.arange(pack_len, dtype=jnp.int32)[None, :]
    ended = lax.optimization_barrier(jnp.sum(((place[:, :, None] >= ends[:, None, :]) & used[:, None, :]).astype(jnp.int32), axis=-1)).astype(jnp.int32)
    begin = lax.optimization_barrier(jnp.sum(jnp.where(slot_ids[None, None, :] == ended[:, :, None], starts[:, None, :], 0), axis=-1)).astype(jnp.int32)
    inside = place < filled
    segment = jnp.where(inside, ended, counts[:, None] + place).astype(jnp.int32)
    position = jnp.where(inside, place - begin, place - filled).astype(jnp.int32)
    return (segment, position)

def product(left, right, form):
    return jnp.einsum(form, left, right, precision=lax.Precision.HIGHEST)

def pack_forward(params, tokens_pack, segment, position):
    gain, shift, head_w, merge_w, up_w, up_b, down_w, down_b = params
    length = tokens_pack.shape[0]
    scale = 1.0 / math.sqrt(HD)
    normed_low = low(normalize(tokens_pack, gain, shift))
    projected = product(normed_low, head_w, 'td,jde->jte')

    def heads_of(values):
        return values.reshape(length, H, HD)
    query = low(rotate(heads_of(low_back(projected[0])), position, ROT))
    keys = low(rotate(heads_of(low_back(projected[1])), position, ROT))
    values = low(heads_of(low_back(projected[2])))
    rows = jnp.arange(length, dtype=jnp.int32)
    block = math.gcd(length, 512)

    @jax.checkpoint
    def attend_block(start):
        query_part = lax.dynamic_slice_in_dim(query, start, block, 0)
        seg_part = lax.dynamic_slice_in_dim(segment, start, block, 0)
        index_part = start + jnp.arange(block, dtype=jnp.int32)
        scores = low_back(product(query_part, keys, 'qhd,khd->hqk') * scale)
        allowed = (seg_part[:, None] == segment[None, :]) & (rows[None, :] <= index_part[:, None])
        scores = jnp.where(allowed[None], scores, NEG)
        top = lax.optimization_barrier(jnp.max(scores, axis=-1, keepdims=True))
        expo = jnp.exp(scores - top)
        probs = expo / lax.optimization_barrier(jnp.sum(expo, axis=-1, keepdims=True))
        return product(low(probs), values, 'hqk,khd->qhd')
    starts = jnp.arange(length // block, dtype=jnp.int32) * block
    attended = lax.map(attend_block, starts).reshape(length, H * HD)
    attended = low(low_back(attended))
    hidden = low_back(product(normed_low, up_w, 'td,df->tf') + up_b)
    active = low(jax.nn.gelu(hidden, approximate=True))
    return tokens_pack + product(attended, merge_w, 'th,hd->td') + product(active, down_w, 'tf,fd->td') + down_b

def reference(tokens, lengths, counts, norm_gain, norm_bias, head_weight, merge_weight, up_weight, up_bias, down_weight, down_bias, cotangent):
    segment, position = layout(lengths, counts, PACK_LEN)
    params = (norm_gain.astype(jnp.float32), norm_bias.astype(jnp.float32), head_weight.astype(jnp.float32), merge_weight.astype(jnp.float32), up_weight.astype(jnp.float32), up_bias.astype(jnp.float32), down_weight.astype(jnp.float32), down_bias.astype(jnp.float32))
    inputs = tokens.astype(jnp.float32)

    def forward(weights, layer_in):

        def step(carry, slices):
            pack_in, seg, pos = slices
            return (carry, jax.checkpoint(pack_forward)(weights, pack_in, seg, pos))
        _, outs = lax.scan(step, jnp.zeros((), jnp.float32), (layer_in, segment, position))
        return outs
    result, back = jax.vjp(forward, params, inputs)
    grads, input_grad = back(cotangent.astype(jnp.float32))
    return (result.astype(jnp.bfloat16), input_grad.astype(jnp.bfloat16), grads[0], grads[1], grads[2], grads[3], grads[4], grads[5], grads[6], grads[7])
```

```python
import functools
import math

import jax
import jax.numpy as jnp
from jax import lax
from jax.experimental import pallas as pl
from jax.experimental.pallas import tpu as pltpu
from jax.sharding import PartitionSpec as P

HD = 64
ROT = 32
EPS = 1e-05
NEG = -1e30
BF16 = jnp.bfloat16
F32 = jnp.float32
VMEM_LIMIT = 56 * 1024 * 1024


def dot(a, b, dims=((1,), (0,))):
    return lax.dot_general(a, b, (dims, ((), ())), preferred_element_type=F32)


def layout(lengths, counts, pack_len):
    slots = lengths.shape[-1]
    slot_ids = jnp.arange(slots, dtype=jnp.int32)
    used = slot_ids[None, :] < counts[:, None]
    sizes = jnp.where(used, lengths, 0)
    ends = jnp.cumsum(sizes, axis=-1)
    starts = ends - sizes
    filled = ends[:, -1:]
    place = jnp.arange(pack_len, dtype=jnp.int32)[None, :]
    begin = jnp.max(
        jnp.where(used[:, None, :] & (place[:, :, None] >= starts[:, None, :]), starts[:, None, :], 0),
        axis=-1,
    )
    inside = place < filled
    first = jnp.where(inside, begin, place)
    position = jnp.where(inside, place - begin, place - filled)
    cost = jnp.sum(sizes * sizes, axis=-1)
    return first, position, cost


def turn(values, cosine, sine, heads):
    out = []
    parity = lax.broadcasted_iota(jnp.int32, cosine.shape, 0) % 2
    for h in range(heads):
        part = values[h * HD : h * HD + ROT]
        ahead = jnp.concatenate([part[1:], part[:1]], axis=0)
        behind = jnp.concatenate([part[-1:], part[:-1]], axis=0)
        swapped = jnp.where(parity == 0, -ahead, behind)
        out.append(part * cosine + swapped * sine)
        out.append(values[h * HD + ROT : (h + 1) * HD])
    return jnp.concatenate(out, axis=0)


def head_kernel(n, heads, me_ref, pack_ref, x_ref, gain_ref, bias_ref, w_ref, cos_ref, sin_ref, *refs):
    normed_ref, outs, scr = refs[0], refs[1 : 1 + n], refs[1 + n]
    g = pl.program_id(1)
    me = me_ref[0]
    width = heads * HD
    x = x_ref[0].astype(F32)
    cent = x - jnp.mean(x, axis=-1, keepdims=True)
    var = jnp.mean(cent * cent, axis=-1, keepdims=True)
    normed = (cent * lax.rsqrt(var + EPS) * gain_ref[...] + bias_ref[...]).astype(BF16)
    normed_ref[0] = normed
    for j in range(3):
        part = dot(w_ref[j * width : (j + 1) * width, :], normed, ((1,), (1,)))
        if j < 2:
            part = turn(part, cos_ref[0], sin_ref[0], heads)
        if j == 0:
            part = part * (1.0 / math.sqrt(HD))
        part = part.astype(BF16)
        for h in range(heads):
            scr[h, j] = part[h * HD : (h + 1) * HD]
    for k in range(n):
        d = lax.bitwise_xor(jnp.int32(k), me)

        @pl.when(d // heads == g)
        def _():
            outs[k][0] = scr[d % heads]


def grad_kernel(n, heads, me_ref, pack_ref, c_ref, w_ref, *refs):
    outs, scr = refs[:n], refs[n]
    g = pl.program_id(1)
    me = me_ref[0]
    part = dot(w_ref[...], c_ref[0], ((1,), (1,))).astype(BF16)
    for h in range(heads):
        scr[h] = part[h * HD : (h + 1) * HD]
    for k in range(n):
        d = lax.bitwise_xor(jnp.int32(k), me)

        @pl.when(d // heads == g)
        def _():
            outs[k][0] = scr[d % heads]


def attend_kernel(n, block, me_ref, pack_ref, low_ref, first_ref, *refs):
    qkv, grads, outs = refs[:n], refs[n : 2 * n], refs[2 * n : 3 * n]
    qt, kt, vt, gt, qn, kn, vn, gn, dk, dv, res = refs[3 * n :]
    s_id = pl.program_id(0)
    me = me_ref[0]
    for k in range(n):
        d = lax.bitwise_xor(jnp.int32(k), me)
        for j, (t_ref, n_ref) in enumerate(((qt, qn), (kt, kn), (vt, vn), (gt, gn))):
            part = qkv[k][0, j] if j < 3 else grads[k][0]
            t_ref[d] = part
            n_ref[d] = part.T
    dk[...] = jnp.zeros_like(dk)
    dv[...] = jnp.zeros_like(dv)
    rows = lax.broadcasted_iota(jnp.int32, (block, block), 0)
    cols = lax.broadcasted_iota(jnp.int32, (block, block), 1)
    ahead = rows - cols

    def outer(i, carry):
        q_t, g_t, q_n, g_n = qt[i], gt[i], qn[i], gn[i]
        first = first_ref[0, pl.ds(i, 1), :]
        j0 = low_ref[s_id, i]

        def scores(j):
            s = dot(kn[j], q_t)
            allowed = (rows >= first - j * block) & (ahead <= (i - j) * block)
            return jnp.where(allowed, s, NEG)

        def forward(j, state):
            top, total, acc = state
            s = scores(j)
            new_top = jnp.maximum(top, jnp.max(s, axis=0, keepdims=True))
            p = jnp.exp(s - new_top)
            fade = jnp.exp(top - new_top)
            total = total * fade + jnp.sum(p, axis=0, keepdims=True)
            acc = acc * fade + dot(vt[j], p.astype(BF16))
            return new_top, total, acc

        top, total, acc = lax.fori_loop(
            j0,
            i + 1,
            forward,
            (
                jnp.full((1, block), NEG, F32),
                jnp.zeros((1, block), F32),
                jnp.zeros((HD, block), F32),
            ),
        )
        acc = acc / total
        logsum = top + jnp.log(total)
        inner = jnp.sum(acc * g_t.astype(F32), axis=0, keepdims=True)
        res[i, 0] = acc.astype(BF16)

        def backward(j, dq):
            p = jnp.exp(scores(j) - logsum)
            dp = dot(vn[j], g_t)
            ds = (p * (dp - inner)).astype(BF16)
            dk[j] += dot(ds, q_n)
            dv[j] += dot(p.astype(BF16), g_n)
            return dq + dot(kt[j], ds)

        dq = lax.fori_loop(j0, i + 1, backward, jnp.zeros((HD, block), F32))
        res[i, 1] = (dq * (1.0 / math.sqrt(HD))).astype(BF16)
        return carry

    lax.fori_loop(0, n, outer, 0)
    for i in range(n):
        res[i, 2] = dk[i].T.astype(BF16)
        res[i, 3] = dv[i].T.astype(BF16)
    for k in range(n):
        d = lax.bitwise_xor(jnp.int32(k), me)
        outs[k][0] = res[d]


def close_kernel(n, heads, slices, me_ref, pack_ref, *refs):
    recv = refs[:n]
    normed_ref, c_ref, w_ref, merge_ref, cos_ref, sin_ref, branch_ref, low_ref = refs[n : n + 8]
    out_branch, out_low, out_weight, scr, acc = refs[n + 8 :]
    s_id, g = pl.program_id(0), pl.program_id(1)
    groups = pl.num_programs(1)
    me = me_ref[0]
    width = heads * HD
    shard = normed_ref.shape[1]

    @pl.when((s_id == 0) & (g == 0))
    def _():
        acc[...] = jnp.zeros_like(acc)

    for k in range(n):
        d = lax.bitwise_xor(jnp.int32(k), me)

        @pl.when(d // heads == g)
        def _():
            for j in range(4):
                scr[j, d % heads] = recv[k][0, j]

    @pl.when(pack_ref[g, s_id] < pack_ref[groups, 0])
    def _():
        attended = scr[0].reshape(width, shard)
        parts = []
        for j in (1, 2):
            part = scr[j].reshape(width, shard).astype(F32)
            parts.append(turn(part, cos_ref[0], -sin_ref[0], heads).astype(BF16))
        parts.append(scr[3].reshape(width, shard))
        grads = jnp.concatenate(parts, axis=0)
        acc[: 3 * width] += dot(grads, normed_ref[0])
        acc[3 * width :] += dot(attended, c_ref[0])
        low = dot(grads.T, w_ref[...]) + low_ref[0].astype(F32)
        out_low[0] = low.astype(BF16)
        branch = dot(attended.T, merge_ref[...]) + branch_ref[0].astype(F32)
        cols = branch.shape[1] // slices
        for m in range(slices):
            out_branch[m, 0] = branch[:, m * cols : (m + 1) * cols].astype(BF16)

    @pl.when((s_id == pl.num_programs(0) - 1) & (g == groups - 1))
    def _():
        out_weight[...] = acc[...].astype(BF16)


def params():
    return pltpu.CompilerParams(vmem_limit_bytes=VMEM_LIMIT)


def swap(parts):
    out = [parts[0]]
    n = len(parts)
    for k in range(1, n):
        out.append(lax.ppermute(parts[k], "seq", [(i, i ^ k) for i in range(n)]))
    return out


def on_device(
    tokens,
    lengths,
    counts,
    norm_gain,
    norm_bias,
    head_weight,
    merge_weight,
    up_weight,
    up_bias,
    down_weight,
    down_bias,
    cotangent,
):
    packs, shard, width = tokens.shape
    n = lax.axis_size("seq")
    slices = lax.axis_size("mlp")
    pack_len = shard * n
    rank = lax.axis_index("seq")
    column = lax.axis_index("mlp")
    heads = merge_weight.shape[0] // HD
    joined = heads * HD
    groups = n // heads
    slots = -(-packs // groups)
    spare = 1 if groups * slots > packs else 0
    rows = packs * shard

    cot = lax.all_gather(cotangent, "mlp", axis=2, tiled=True)

    first, position, cost = layout(lengths, counts, pack_len)
    ids = jnp.arange(packs, dtype=jnp.int32)
    before = (cost[None, :] > cost[:, None]) | (
        (cost[None, :] == cost[:, None]) & (ids[None, :] < ids[:, None])
    )
    order = jnp.sum(before.astype(jnp.int32), axis=1)
    slot_of = order // groups
    group_of = jnp.where(slot_of % 2 == 0, order % groups, groups - 1 - order % groups)
    hit = (group_of[None, None, :] == jnp.arange(groups)[:, None, None]) & (
        slot_of[None, None, :] == jnp.arange(slots)[None, :, None]
    )
    pack_at = jnp.where(
        jnp.any(hit, axis=-1), jnp.sum(jnp.where(hit, ids, 0), axis=-1), packs
    ).astype(jnp.int32)
    pack_table = jnp.concatenate([pack_at, jnp.full((1, slots), packs, jnp.int32)], axis=0)
    me = rank.astype(jnp.int32).reshape(1)

    half = ROT // 2
    freq = 10000.0 ** (-(2.0 * jnp.arange(half, dtype=F32)) / ROT)
    own_position = lax.dynamic_slice_in_dim(position, rank * shard, shard, 1)
    angle = own_position.astype(F32)[:, None, :] * jnp.repeat(freq, 2)[None, :, None]
    cosine, sine = jnp.cos(angle), jnp.sin(angle)

    w_t = jnp.transpose(head_weight, (0, 2, 1)).reshape(3 * joined, width)

    def pack_in(s, g, me_ref, pack_ref):
        return (jnp.minimum(pack_ref[g, s], packs - 1), 0, 0)

    def pack_out(s, g, me_ref, pack_ref):
        return (pack_ref[g, s], 0, 0)

    def whole2(s, g, me_ref, pack_ref):
        return (0, 0)

    row_spec = pl.BlockSpec((1, shard, width), pack_in)
    table_spec = pl.BlockSpec((1, ROT, shard), pack_in)
    outs = pl.pallas_call(
        functools.partial(head_kernel, n, heads),
        grid_spec=pltpu.PrefetchScalarGridSpec(
            num_scalar_prefetch=2,
            grid=(slots, groups),
            in_specs=[
                row_spec,
                pl.BlockSpec((1, width), whole2),
                pl.BlockSpec((1, width), whole2),
                pl.BlockSpec((3 * joined, width), whole2),
                table_spec,
                table_spec,
            ],
            out_specs=[pl.BlockSpec((1, shard, width), pack_out)]
            + [pl.BlockSpec((1, 3, HD, shard), lambda s, g, a, b: (s, 0, 0, 0))] * n,
            scratch_shapes=[pltpu.VMEM((heads, 3, HD, shard), BF16)],
        ),
        out_shape=[jax.ShapeDtypeStruct((packs + spare, shard, width), BF16)]
        + [jax.ShapeDtypeStruct((slots, 3, HD, shard), BF16)] * n,
        compiler_params=params(),
        cost_estimate=pl.CostEstimate(
            flops=2 * rows * width * 3 * joined,
            bytes_accessed=rows * width * 4 + rows * joined * 6,
            transcendentals=0,
        ),
        name="heads",
    )(
        me,
        pack_table,
        tokens,
        norm_gain.reshape(1, width),
        norm_bias.reshape(1, width),
        w_t,
        cosine,
        sine,
    )
    normed_low = outs[0][:packs]
    qkv = swap(outs[1:])

    sends = pl.pallas_call(
        functools.partial(grad_kernel, n, heads),
        grid_spec=pltpu.PrefetchScalarGridSpec(
            num_scalar_prefetch=2,
            grid=(slots, groups),
            in_specs=[row_spec, pl.BlockSpec((joined, width), whole2)],
            out_specs=[pl.BlockSpec((1, HD, shard), lambda s, g, a, b: (s, 0, 0))] * n,
            scratch_shapes=[pltpu.VMEM((heads, HD, shard), BF16)],
        ),
        out_shape=[jax.ShapeDtypeStruct((slots, HD, shard), BF16)] * n,
        compiler_params=params(),
        cost_estimate=pl.CostEstimate(
            flops=2 * rows * width * joined,
            bytes_accessed=rows * width * 2 + rows * joined * 2,
            transcendentals=0,
        ),
        name="out_grads",
    )(me, pack_table, cot, merge_weight)
    grads = swap(sends)

    hidden = (
        jnp.einsum("psd,df->psf", normed_low, up_weight, preferred_element_type=F32) + up_bias
    )
    active_low = jax.nn.gelu(hidden, approximate=True).astype(BF16)
    active_grad = jnp.einsum("psd,fd->psf", cot, down_weight, preferred_element_type=F32)
    _, gelu_back = jax.vjp(lambda values: jax.nn.gelu(values, approximate=True), hidden)
    hidden_grad = gelu_back(active_grad)[0].astype(BF16)
    up_bias_grad = jnp.sum(hidden_grad.astype(F32), axis=(0, 1))
    down_bias_grad = jnp.sum(cot.astype(F32), axis=(0, 1))
    branch_ff = jnp.einsum(
        "psf,fd->psd", active_low, down_weight, preferred_element_type=F32
    ).astype(BF16)
    low_ff = jnp.einsum(
        "psf,df->psd", hidden_grad, up_weight, preferred_element_type=F32
    ).astype(BF16)
    up_grad = jnp.einsum(
        "psd,psf->df", normed_low, hidden_grad, preferred_element_type=F32
    ).astype(BF16)
    down_grad = jnp.einsum("psd,psf->df", cot, active_low, preferred_element_type=F32).astype(BF16)
    up_grad = lax.psum_scatter(up_grad, "seq", scatter_dimension=0, tiled=True)
    down_grad = lax.psum_scatter(down_grad, "seq", scatter_dimension=0, tiled=True)

    my_packs = lax.dynamic_slice_in_dim(pack_at, rank // heads, 1, 0)[0]
    safe = jnp.minimum(my_packs, packs - 1)
    lows = first.reshape(packs, n, shard)[:, :, 0] // shard
    lows = jnp.where((my_packs < packs)[:, None], lows[safe], jnp.arange(n)[None, :]).astype(
        jnp.int32
    )
    chunk_spec = pl.BlockSpec((1, 3, HD, shard), lambda s, a, b, c: (s, 0, 0, 0))
    grad_spec = pl.BlockSpec((1, HD, shard), lambda s, a, b, c: (s, 0, 0))
    backs = pl.pallas_call(
        functools.partial(attend_kernel, n, shard),
        grid_spec=pltpu.PrefetchScalarGridSpec(
            num_scalar_prefetch=3,
            grid=(slots,),
            in_specs=[pl.BlockSpec((1, n, shard), lambda s, a, b, c: (b[s], 0, 0))]
            + [chunk_spec] * n
            + [grad_spec] * n,
            out_specs=[pl.BlockSpec((1, 4, HD, shard), lambda s, a, b, c: (s, 0, 0, 0))] * n,
            scratch_shapes=[pltpu.VMEM((n, HD, shard), BF16)] * 4
            + [pltpu.VMEM((n, shard, HD), BF16)] * 4
            + [pltpu.VMEM((n, shard, HD), F32)] * 2
            + [pltpu.VMEM((n, 4, HD, shard), BF16)],
        ),
        out_shape=[jax.ShapeDtypeStruct((slots, 4, HD, shard), BF16)] * n,
        compiler_params=params(),
        cost_estimate=pl.CostEstimate(
            flops=slots * pack_len * pack_len * HD * 14,
            bytes_accessed=slots * pack_len * HD * 16,
            transcendentals=slots * pack_len * pack_len,
        ),
        name="attend",
    )(me, safe, lows, first.reshape(packs, n, shard), *qkv, *grads)
    backs = swap(backs)

    branch, low, weight = pl.pallas_call(
        functools.partial(close_kernel, n, heads, slices),
        grid_spec=pltpu.PrefetchScalarGridSpec(
            num_scalar_prefetch=2,
            grid=(slots, groups),
            in_specs=[pl.BlockSpec((1, 4, HD, shard), lambda s, g, a, b: (s, 0, 0, 0))] * n
            + [
                row_spec,
                row_spec,
                pl.BlockSpec((3 * joined, width), whole2),
                pl.BlockSpec((joined, width), whole2),
                table_spec,
                table_spec,
                row_spec,
                row_spec,
            ],
            out_specs=[
                pl.BlockSpec(
                    (slices, 1, shard, width // slices), lambda s, g, a, b: (0, b[g, s], 0, 0)
                ),
                pl.BlockSpec((1, shard, width), pack_out),
                pl.BlockSpec((4 * joined, width), whole2),
            ],
            scratch_shapes=[
                pltpu.VMEM((4, heads, HD, shard), BF16),
                pltpu.VMEM((4 * joined, width), F32),
            ],
        ),
        out_shape=[
            jax.ShapeDtypeStruct((slices, packs + spare, shard, width // slices), BF16),
            jax.ShapeDtypeStruct((packs + spare, shard, width), BF16),
            jax.ShapeDtypeStruct((4 * joined, width), BF16),
        ],
        compiler_params=params(),
        cost_estimate=pl.CostEstimate(
            flops=16 * rows * width * joined,
            bytes_accessed=rows * width * 12 + rows * joined * 8,
            transcendentals=0,
        ),
        name="close",
    )(
        me,
        pack_table,
        *backs,
        normed_low,
        cot,
        w_t,
        merge_weight,
        cosine,
        sine,
        branch_ff,
        low_ff,
    )
    branch = branch[:, :packs]
    low = low[:packs]
    summed = lax.psum_scatter(branch, "mlp", scatter_dimension=0, tiled=False)
    cols = width // slices
    result = (
        lax.dynamic_slice_in_dim(tokens, column * cols, cols, 2).astype(F32)
        + summed.astype(F32)
        + lax.dynamic_slice_in_dim(down_bias, column * cols, cols, 0)
    ).astype(BF16)

    share = rows // slices
    low_sum = lax.psum_scatter(
        low.reshape(rows, width), "mlp", scatter_dimension=0, tiled=True
    ).astype(F32)
    row_in = lax.dynamic_slice_in_dim(
        tokens.reshape(rows, width), column * share, share, 0
    ).astype(F32)
    row_cot = lax.dynamic_slice_in_dim(
        cot.reshape(rows, width), column * share, share, 0
    ).astype(F32)
    cent = row_in - jnp.mean(row_in, axis=-1, keepdims=True)
    inverse = lax.rsqrt(jnp.mean(cent * cent, axis=-1, keepdims=True) + EPS)
    xhat = cent * inverse
    g = low_sum * norm_gain
    row_grad = (
        row_cot
        + (
            g
            - jnp.mean(g, axis=-1, keepdims=True)
            - xhat * jnp.mean(g * xhat, axis=-1, keepdims=True)
        )
        * inverse
    ).astype(BF16)
    tokens_grad = lax.all_gather(row_grad, "mlp", axis=0, tiled=True).reshape(packs, shard, width)
    gain_grad = lax.psum(jnp.sum(low_sum * xhat, axis=0), "mlp")
    shift_grad = lax.psum(jnp.sum(low_sum, axis=0), "mlp")

    weight = lax.psum_scatter(weight, "seq", scatter_dimension=1, tiled=True).astype(F32)
    part = width // n
    head_grad = jnp.transpose(weight[: 3 * joined].reshape(3, joined, part), (0, 2, 1))
    merge_grad = weight[3 * joined :]
    gain_grad, shift_grad, up_bias_grad, down_bias_grad = (
        lax.psum_scatter(gain_grad, "seq", scatter_dimension=0, tiled=True),
        lax.psum_scatter(shift_grad, "seq", scatter_dimension=0, tiled=True),
        lax.psum_scatter(up_bias_grad, "seq", scatter_dimension=0, tiled=True),
        lax.psum_scatter(down_bias_grad, "seq", scatter_dimension=0, tiled=True),
    )
    return (
        result,
        tokens_grad,
        gain_grad,
        shift_grad,
        head_grad,
        merge_grad,
        up_grad.astype(F32),
        up_bias_grad,
        down_grad.astype(F32).T,
        down_bias_grad,
    )


def solution(mesh):
    in_specs = (
        P(None, "seq", None),
        P(),
        P(),
        P(),
        P(),
        P(None, None, "mlp"),
        P("mlp", None),
        P(None, "mlp"),
        P("mlp"),
        P("mlp", None),
        P(),
        P(None, "seq", "mlp"),
    )
    out_specs = (
        P(None, "seq", "mlp"),
        P(None, "seq", None),
        P("seq"),
        P("seq"),
        P(None, "seq", "mlp"),
        P("mlp", "seq"),
        P("seq", "mlp"),
        P(("mlp", "seq")),
        P("mlp", "seq"),
        P("seq"),
    )
    return jax.shard_map(
        on_device, mesh=mesh, in_specs=in_specs, out_specs=out_specs, check_vma=False
    )
```

```python
import functools
import math

import jax
import jax.numpy as jnp
from jax import lax
from jax.experimental import pallas as pl
from jax.experimental.pallas import tpu as pltpu
from jax.sharding import PartitionSpec as P

HD = 64
ROT = 32
EPS = 1e-05
NEG = -1e30
BF16 = jnp.bfloat16
F32 = jnp.float32
VMEM_LIMIT = 56 * 1024 * 1024


def dot(a, b, dims=((1,), (0,))):
    return lax.dot_general(a, b, (dims, ((), ())), preferred_element_type=F32)


def layout(lengths, counts, pack_len):
    slots = lengths.shape[-1]
    slot_ids = jnp.arange(slots, dtype=jnp.int32)
    used = slot_ids[None, :] < counts[:, None]
    sizes = jnp.where(used, lengths, 0)
    ends = jnp.cumsum(sizes, axis=-1)
    starts = ends - sizes
    filled = ends[:, -1:]
    place = jnp.arange(pack_len, dtype=jnp.int32)[None, :]
    begin = jnp.max(
        jnp.where(used[:, None, :] & (place[:, :, None] >= starts[:, None, :]), starts[:, None, :], 0),
        axis=-1,
    )
    inside = place < filled
    first = jnp.where(inside, begin, place)
    position = jnp.where(inside, place - begin, place - filled)
    cost = jnp.sum(sizes * sizes, axis=-1)
    return first, position, cost


def turn(values, cosine, sine, heads):
    out = []
    parity = lax.broadcasted_iota(jnp.int32, cosine.shape, 0) % 2
    for h in range(heads):
        part = values[h * HD : h * HD + ROT]
        ahead = jnp.concatenate([part[1:], part[:1]], axis=0)
        behind = jnp.concatenate([part[-1:], part[:-1]], axis=0)
        swapped = jnp.where(parity == 0, -ahead, behind)
        out.append(part * cosine + swapped * sine)
        out.append(values[h * HD + ROT : (h + 1) * HD])
    return jnp.concatenate(out, axis=0)


def head_kernel(n, heads, me_ref, pack_ref, x_ref, gain_ref, bias_ref, w_ref, cos_ref, sin_ref, *refs):
    normed_ref, outs, scr = refs[0], refs[1 : 1 + n], refs[1 + n]
    g = pl.program_id(1)
    me = me_ref[0]
    width = heads * HD
    x = x_ref[0].astype(F32)
    cent = x - jnp.mean(x, axis=-1, keepdims=True)
    var = jnp.mean(cent * cent, axis=-1, keepdims=True)
    normed = (cent * lax.rsqrt(var + EPS) * gain_ref[...] + bias_ref[...]).astype(BF16)
    normed_ref[0] = normed
    for j in range(3):
        part = dot(w_ref[j * width : (j + 1) * width, :], normed, ((1,), (1,)))
        if j < 2:
            part = turn(part, cos_ref[0], sin_ref[0], heads)
        if j == 0:
            part = part * (1.0 / math.sqrt(HD))
        part = part.astype(BF16)
        for h in range(heads):
            scr[h, j] = part[h * HD : (h + 1) * HD]
    for k in range(n):
        d = lax.bitwise_xor(jnp.int32(k), me)

        @pl.when(d // heads == g)
        def _():
            outs[k][0] = scr[d % heads]


def grad_kernel(n, heads, me_ref, pack_ref, c_ref, w_ref, *refs):
    outs, scr = refs[:n], refs[n]
    g = pl.program_id(1)
    me = me_ref[0]
    part = dot(w_ref[...], c_ref[0], ((1,), (1,))).astype(BF16)
    for h in range(heads):
        scr[h] = part[h * HD : (h + 1) * HD]
    for k in range(n):
        d = lax.bitwise_xor(jnp.int32(k), me)

        @pl.when(d // heads == g)
        def _():
            outs[k][0] = scr[d % heads]


def load_parts(n, me, pairs):
    for k in range(n):
        d = lax.bitwise_xor(jnp.int32(k), me)
        for part, t_ref, n_ref in pairs(k):
            if t_ref is not None:
                t_ref[d] = part
            if n_ref is not None:
                n_ref[d] = part.T


def score_of(block, first, i, kn, q_t):
    rows = lax.broadcasted_iota(jnp.int32, (block, block), 0)
    cols = lax.broadcasted_iota(jnp.int32, (block, block), 1)
    ahead = rows - cols

    def scores(j, at):
        s = dot(kn[at], q_t)
        allowed = (rows >= first - j * block) & (ahead <= (i - j) * block)
        return jnp.where(allowed, s, NEG)

    return scores


def attend_kernel(n, block, me_ref, pack_ref, low_ref, first_ref, *refs):
    qkv, outs, keep_ref, logsum_ref = refs[:n], refs[n : 2 * n], refs[2 * n], refs[2 * n + 1]
    qt, vt, kn = refs[2 * n + 2 :]
    s_id = pl.program_id(0)
    me = me_ref[0]
    load_parts(
        n,
        me,
        lambda k: (
            (qkv[k][0, 0], qt, None),
            (qkv[k][0, 1], None, kn),
            (qkv[k][0, 2], vt, None),
        ),
    )

    def outer(i, carry):
        scores = score_of(block, first_ref[0, pl.ds(i, 1), :], i, kn, qt[i])
        j0 = low_ref[s_id, i]

        def forward(t, state):
            top, total, acc = state
            j = j0 + 2 * t
            at = jnp.minimum(j + 1, n - 1)
            s0, s1 = scores(j, j), scores(j + 1, at)
            peak = jnp.max(jnp.maximum(s0, s1), axis=0, keepdims=True)
            new_top = jnp.maximum(top, peak)
            p0, p1 = jnp.exp(s0 - new_top), jnp.exp(s1 - new_top)
            fade = jnp.exp(top - new_top)
            total = total * fade + jnp.sum(p0 + p1, axis=0, keepdims=True)
            acc = acc * fade + dot(vt[j], p0.astype(BF16)) + dot(vt[at], p1.astype(BF16))
            return new_top, total, acc

        top, total, acc = lax.fori_loop(
            0,
            (i - j0) // 2 + 1,
            forward,
            (
                jnp.full((1, block), NEG, F32),
                jnp.zeros((1, block), F32),
                jnp.zeros((HD, block), F32),
            ),
        )
        keep_ref[0, i] = (acc / total).astype(BF16)
        logsum_ref[0, pl.ds(i, 1), :] = top + jnp.log(total)
        return carry

    lax.fori_loop(0, n, outer, 0)
    for k in range(n):
        outs[k][0] = keep_ref[0, lax.bitwise_xor(jnp.int32(k), me)]


def attend_back_kernel(n, block, me_ref, pack_ref, low_ref, first_ref, *refs):
    keep_ref, logsum_ref = refs[:2]
    qkv, grads, outs = refs[2 : n + 2], refs[n + 2 : 2 * n + 2], refs[2 * n + 2 : 3 * n + 2]
    qt, kt, gt, qn, kn, vn, gn, dk, dv, res = refs[3 * n + 2 :]
    s_id = pl.program_id(0)
    me = me_ref[0]
    load_parts(
        n,
        me,
        lambda k: (
            (qkv[k][0, 0], qt, qn),
            (qkv[k][0, 1], kt, kn),
            (qkv[k][0, 2], None, vn),
            (grads[k][0], gt, gn),
        ),
    )
    dk[...] = jnp.zeros_like(dk)
    dv[...] = jnp.zeros_like(dv)

    def outer(i, carry):
        q_t, g_t, q_n, g_n = qt[i], gt[i], qn[i], gn[i]
        scores = score_of(block, first_ref[0, pl.ds(i, 1), :], i, kn, q_t)
        j0 = low_ref[s_id, i]
        inner = jnp.sum(keep_ref[0, i].astype(F32) * g_t.astype(F32), axis=0, keepdims=True)
        logsum = logsum_ref[0, pl.ds(i, 1), :]

        def one(j, at):
            p = jnp.exp(scores(j, at) - logsum)
            ds = (p * (dot(vn[at], g_t) - inner)).astype(BF16)
            return ds, dot(ds, q_n), dot(p.astype(BF16), g_n), dot(kt[at], ds)

        def backward(t, dq):
            j = j0 + 2 * t
            at = jnp.minimum(j + 1, n - 1)
            _, dk0, dv0, dq0 = one(j, j)
            _, dk1, dv1, dq1 = one(j + 1, at)
            dk[j] += dk0
            dv[j] += dv0
            dk[at] += dk1
            dv[at] += dv1
            return dq + dq0 + dq1

        dq = lax.fori_loop(0, (i - j0) // 2 + 1, backward, jnp.zeros((HD, block), F32))
        res[i, 0] = (dq * (1.0 / math.sqrt(HD))).astype(BF16)
        return carry

    lax.fori_loop(0, n, outer, 0)
    for i in range(n):
        res[i, 1] = dk[i].T.astype(BF16)
        res[i, 2] = dv[i].T.astype(BF16)
    for k in range(n):
        outs[k][0] = res[lax.bitwise_xor(jnp.int32(k), me)]


def merge_kernel(n, heads, slices, me_ref, pack_ref, *refs):
    recv = refs[:n]
    c_ref, merge_ref, branch_ref, out_branch, out_weight, scr, acc = refs[n:]
    s_id, g = pl.program_id(0), pl.program_id(1)
    groups = pl.num_programs(1)
    me = me_ref[0]
    width = heads * HD

    @pl.when((s_id == 0) & (g == 0))
    def _():
        acc[...] = jnp.zeros_like(acc)

    for k in range(n):
        d = lax.bitwise_xor(jnp.int32(k), me)

        @pl.when(d // heads == g)
        def _():
            scr[d % heads] = recv[k][0]

    @pl.when(pack_ref[g, s_id] < pack_ref[groups, 0])
    def _():
        attended = scr[...].reshape(width, c_ref.shape[1])
        acc[...] += dot(attended, c_ref[0])
        branch = dot(attended.T, merge_ref[...]) + branch_ref[0].astype(F32)
        cols = branch.shape[1] // slices
        for m in range(slices):
            out_branch[m, 0] = branch[:, m * cols : (m + 1) * cols].astype(BF16)

    @pl.when((s_id == pl.num_programs(0) - 1) & (g == groups - 1))
    def _():
        out_weight[...] = acc[...].astype(BF16)


def close_kernel(n, heads, me_ref, pack_ref, *refs):
    recv = refs[:n]
    normed_ref, w_ref, cos_ref, sin_ref, low_ref, out_low, out_weight, scr, acc = refs[n:]
    s_id, g = pl.program_id(0), pl.program_id(1)
    groups = pl.num_programs(1)
    me = me_ref[0]
    width = heads * HD
    shard = normed_ref.shape[1]

    @pl.when((s_id == 0) & (g == 0))
    def _():
        acc[...] = jnp.zeros_like(acc)

    for k in range(n):
        d = lax.bitwise_xor(jnp.int32(k), me)

        @pl.when(d // heads == g)
        def _():
            for j in range(3):
                scr[j, d % heads] = recv[k][0, j]

    @pl.when(pack_ref[g, s_id] < pack_ref[groups, 0])
    def _():
        parts = []
        for j in (0, 1):
            part = scr[j].reshape(width, shard).astype(F32)
            parts.append(turn(part, cos_ref[0], -sin_ref[0], heads).astype(BF16))
        parts.append(scr[2].reshape(width, shard))
        grads = jnp.concatenate(parts, axis=0)
        acc[...] += dot(grads, normed_ref[0])
        low = dot(grads.T, w_ref[...]) + low_ref[0].astype(F32)
        out_low[0] = low.astype(BF16)

    @pl.when((s_id == pl.num_programs(0) - 1) & (g == groups - 1))
    def _():
        out_weight[...] = acc[...].astype(BF16)


def params():
    return pltpu.CompilerParams(vmem_limit_bytes=VMEM_LIMIT)


def swap(parts):
    out = [parts[0]]
    n = len(parts)
    for k in range(1, n):
        out.append(lax.ppermute(parts[k], "seq", [(i, i ^ k) for i in range(n)]))
    return out


def span(masks):
    out = [0]
    for m in masks:
        out += [v ^ m for v in out]
    return out


def cube_sum(chunks, axis, masks, kind):
    n = len(chunks)
    chunks = dict(enumerate(chunks))
    for step, m in enumerate(masks):
        kept = span(masks[step + 1 :])
        sent = jnp.stack([chunks[k ^ m] for k in kept]).astype(kind)
        got = lax.ppermute(sent, axis, [(i, i ^ m) for i in range(n)])
        chunks = {
            k: chunks[k].astype(F32) + got[at].astype(F32) for at, k in enumerate(kept)
        }
    return chunks[0]


def masks_of(n):
    return [1, 2, 6] if n == 8 else [1 << b for b in range(n.bit_length() - 1)]


def turned(masks, by):
    by = by % len(masks)
    return masks[by:] + masks[:by]


def cut(array, axis, n, me):
    size = array.shape[axis] // n
    return [
        lax.dynamic_slice_in_dim(array, lax.bitwise_xor(jnp.int32(k), me) * size, size, axis)
        for k in range(n)
    ]


def on_device(
    tokens,
    lengths,
    counts,
    norm_gain,
    norm_bias,
    head_weight,
    merge_weight,
    up_weight,
    up_bias,
    down_weight,
    down_bias,
    cotangent,
):
    packs, shard, width = tokens.shape
    n = lax.axis_size("seq")
    slices = lax.axis_size("mlp")
    pack_len = shard * n
    rank = lax.axis_index("seq")
    column = lax.axis_index("mlp")
    heads = merge_weight.shape[0] // HD
    joined = heads * HD
    groups = n // heads
    slots = -(-packs // groups)
    spare = 1 if groups * slots > packs else 0
    rows = packs * shard

    cot = lax.all_gather(cotangent, "mlp", axis=2, tiled=True)

    first, position, cost = layout(lengths, counts, pack_len)
    ids = jnp.arange(packs, dtype=jnp.int32)
    before = (cost[None, :] > cost[:, None]) | (
        (cost[None, :] == cost[:, None]) & (ids[None, :] < ids[:, None])
    )
    order = jnp.sum(before.astype(jnp.int32), axis=1)
    slot_of = order // groups
    group_of = jnp.where(slot_of % 2 == 0, order % groups, groups - 1 - order % groups)
    hit = (group_of[None, None, :] == jnp.arange(groups)[:, None, None]) & (
        slot_of[None, None, :] == jnp.arange(slots)[None, :, None]
    )
    pack_at = jnp.where(
        jnp.any(hit, axis=-1), jnp.sum(jnp.where(hit, ids, 0), axis=-1), packs
    ).astype(jnp.int32)
    pack_table = jnp.concatenate([pack_at, jnp.full((1, slots), packs, jnp.int32)], axis=0)
    me = rank.astype(jnp.int32).reshape(1)

    half = ROT // 2
    freq = 10000.0 ** (-(2.0 * jnp.arange(half, dtype=F32)) / ROT)
    own_position = lax.dynamic_slice_in_dim(position, rank * shard, shard, 1)
    angle = own_position.astype(F32)[:, None, :] * jnp.repeat(freq, 2)[None, :, None]
    cosine, sine = jnp.cos(angle), jnp.sin(angle)

    w_t = jnp.transpose(head_weight, (0, 2, 1)).reshape(3 * joined, width)

    def pack_in(s, g, me_ref, pack_ref):
        return (jnp.minimum(pack_ref[g, s], packs - 1), 0, 0)

    def pack_out(s, g, me_ref, pack_ref):
        return (pack_ref[g, s], 0, 0)

    def whole2(s, g, me_ref, pack_ref):
        return (0, 0)

    row_spec = pl.BlockSpec((1, shard, width), pack_in)
    table_spec = pl.BlockSpec((1, ROT, shard), pack_in)
    outs = pl.pallas_call(
        functools.partial(head_kernel, n, heads),
        grid_spec=pltpu.PrefetchScalarGridSpec(
            num_scalar_prefetch=2,
            grid=(slots, groups),
            in_specs=[
                row_spec,
                pl.BlockSpec((1, width), whole2),
                pl.BlockSpec((1, width), whole2),
                pl.BlockSpec((3 * joined, width), whole2),
                table_spec,
                table_spec,
            ],
            out_specs=[pl.BlockSpec((1, shard, width), pack_out)]
            + [pl.BlockSpec((1, 3, HD, shard), lambda s, g, a, b: (s, 0, 0, 0))] * n,
            scratch_shapes=[pltpu.VMEM((heads, 3, HD, shard), BF16)],
        ),
        out_shape=[jax.ShapeDtypeStruct((packs + spare, shard, width), BF16)]
        + [jax.ShapeDtypeStruct((slots, 3, HD, shard), BF16)] * n,
        compiler_params=params(),
        cost_estimate=pl.CostEstimate(
            flops=2 * rows * width * 3 * joined,
            bytes_accessed=rows * width * 4 + rows * joined * 6,
            transcendentals=0,
        ),
        name="heads",
    )(
        me,
        pack_table,
        tokens,
        norm_gain.reshape(1, width),
        norm_bias.reshape(1, width),
        w_t,
        cosine,
        sine,
    )
    normed_low = outs[0][:packs]
    qkv = swap(outs[1:])

    sends = pl.pallas_call(
        functools.partial(grad_kernel, n, heads),
        grid_spec=pltpu.PrefetchScalarGridSpec(
            num_scalar_prefetch=2,
            grid=(slots, groups),
            in_specs=[row_spec, pl.BlockSpec((joined, width), whole2)],
            out_specs=[pl.BlockSpec((1, HD, shard), lambda s, g, a, b: (s, 0, 0))] * n,
            scratch_shapes=[pltpu.VMEM((heads, HD, shard), BF16)],
        ),
        out_shape=[jax.ShapeDtypeStruct((slots, HD, shard), BF16)] * n,
        compiler_params=params(),
        cost_estimate=pl.CostEstimate(
            flops=2 * rows * width * joined,
            bytes_accessed=rows * width * 2 + rows * joined * 2,
            transcendentals=0,
        ),
        name="out_grads",
    )(me, pack_table, cot, merge_weight)
    grads = swap(sends)

    hidden = (
        jnp.einsum("psd,df->psf", normed_low, up_weight, preferred_element_type=F32) + up_bias
    )
    active_low = jax.nn.gelu(hidden, approximate=True).astype(BF16)
    active_grad = jnp.einsum("psd,fd->psf", cot, down_weight, preferred_element_type=F32)
    _, gelu_back = jax.vjp(lambda values: jax.nn.gelu(values, approximate=True), hidden)
    hidden_grad = gelu_back(active_grad)[0].astype(BF16)
    up_bias_grad = jnp.sum(hidden_grad.astype(F32), axis=(0, 1))
    down_bias_grad = jnp.sum(cot.astype(F32), axis=(0, 1))
    branch_ff = jnp.einsum(
        "psf,fd->psd", active_low, down_weight, preferred_element_type=F32
    ).astype(BF16)
    low_ff = jnp.einsum(
        "psf,df->psd", hidden_grad, up_weight, preferred_element_type=F32
    ).astype(BF16)
    up_grad = jnp.einsum(
        "psd,psf->df", normed_low, hidden_grad, preferred_element_type=F32
    ).astype(BF16)
    down_grad = jnp.einsum("psd,psf->df", cot, active_low, preferred_element_type=F32).astype(BF16)
    seq_masks = masks_of(n)
    up_cut, down_cut = cut(up_grad, 0, n, rank), cut(down_grad, 0, n, rank)
    both = [jnp.concatenate(pair, axis=1) for pair in zip(up_cut, down_cut)]
    third = both[0].shape[1] // 384 * 128
    edges = [0, third, 2 * third, both[0].shape[1]]
    both = jnp.concatenate(
        [
            cube_sum([v[:, lo:hi] for v in both], "seq", turned(seq_masks, r), BF16)
            for r, (lo, hi) in enumerate(zip(edges, edges[1:]))
        ],
        axis=1,
    )
    hidden_here = up_weight.shape[1]
    up_grad, down_grad = both[:, :hidden_here], both[:, hidden_here:].T
    biases = cube_sum(
        [
            jnp.concatenate(pair)
            for pair in zip(cut(up_bias_grad, 0, n, rank), cut(down_bias_grad, 0, n, rank))
        ],
        "seq",
        seq_masks,
        F32,
    )
    up_bias_grad = biases[: hidden_here // n]
    down_bias_grad = biases[hidden_here // n :]

    my_packs = lax.dynamic_slice_in_dim(pack_at, rank // heads, 1, 0)[0]
    safe = jnp.minimum(my_packs, packs - 1)
    lows = first.reshape(packs, n, shard)[:, :, 0] // shard
    lows = jnp.where((my_packs < packs)[:, None], lows[safe], jnp.arange(n)[None, :]).astype(
        jnp.int32
    )
    chunk_spec = pl.BlockSpec((1, 3, HD, shard), lambda s, a, b, c: (s, 0, 0, 0))
    grad_spec = pl.BlockSpec((1, HD, shard), lambda s, a, b, c: (s, 0, 0))
    first_spec = pl.BlockSpec((1, n, shard), lambda s, a, b, c: (b[s], 0, 0))
    row_chunk = pl.BlockSpec((1, n, shard), lambda s, a, b, c: (s, 0, 0))
    keep_spec = pl.BlockSpec((1, n, HD, shard), lambda s, a, b, c: (s, 0, 0, 0))
    first = first.reshape(packs, n, shard)
    wide = [pltpu.VMEM((n, HD, shard), BF16)]
    tall = [pltpu.VMEM((n, shard, HD), BF16)]
    outs = pl.pallas_call(
        functools.partial(attend_kernel, n, shard),
        grid_spec=pltpu.PrefetchScalarGridSpec(
            num_scalar_prefetch=3,
            grid=(slots,),
            in_specs=[first_spec] + [chunk_spec] * n,
            out_specs=[grad_spec] * n + [keep_spec, row_chunk],
            scratch_shapes=wide * 2 + tall,
        ),
        out_shape=[jax.ShapeDtypeStruct((slots, HD, shard), BF16)] * n
        + [
            jax.ShapeDtypeStruct((slots, n, HD, shard), BF16),
            jax.ShapeDtypeStruct((slots, n, shard), F32),
        ],
        compiler_params=params(),
        cost_estimate=pl.CostEstimate(
            flops=slots * pack_len * pack_len * HD * 8,
            bytes_accessed=slots * pack_len * HD * 10,
            transcendentals=slots * pack_len * pack_len // 4,
        ),
        name="attend",
    )(me, safe, lows, first, *qkv)
    kept, logsum = outs[n], outs[n + 1]
    attended = swap(outs[:n])
    backs = pl.pallas_call(
        functools.partial(attend_back_kernel, n, shard),
        grid_spec=pltpu.PrefetchScalarGridSpec(
            num_scalar_prefetch=3,
            grid=(slots,),
            in_specs=[first_spec, keep_spec, row_chunk] + [chunk_spec] * n + [grad_spec] * n,
            out_specs=[chunk_spec] * n,
            scratch_shapes=wide * 3
            + tall * 4
            + [pltpu.VMEM((n, shard, HD), F32)] * 2
            + [pltpu.VMEM((n, 3, HD, shard), BF16)],
        ),
        out_shape=[jax.ShapeDtypeStruct((slots, 3, HD, shard), BF16)] * n,
        compiler_params=params(),
        cost_estimate=pl.CostEstimate(
            flops=slots * pack_len * pack_len * HD * 16,
            bytes_accessed=slots * pack_len * HD * 16,
            transcendentals=slots * pack_len * pack_len // 4,
        ),
        name="attend_back",
    )(me, safe, lows, first, kept, logsum, *qkv, *grads)
    backs = swap(backs)

    branch, merge_part = pl.pallas_call(
        functools.partial(merge_kernel, n, heads, slices),
        grid_spec=pltpu.PrefetchScalarGridSpec(
            num_scalar_prefetch=2,
            grid=(slots, groups),
            in_specs=[pl.BlockSpec((1, HD, shard), lambda s, g, a, b: (s, 0, 0))] * n
            + [row_spec, pl.BlockSpec((joined, width), whole2), row_spec],
            out_specs=[
                pl.BlockSpec(
                    (slices, 1, shard, width // slices), lambda s, g, a, b: (0, b[g, s], 0, 0)
                ),
                pl.BlockSpec((joined, width), whole2),
            ],
            scratch_shapes=[
                pltpu.VMEM((heads, HD, shard), BF16),
                pltpu.VMEM((joined, width), F32),
            ],
        ),
        out_shape=[
            jax.ShapeDtypeStruct((slices, packs + spare, shard, width // slices), BF16),
            jax.ShapeDtypeStruct((joined, width), BF16),
        ],
        compiler_params=params(),
        cost_estimate=pl.CostEstimate(
            flops=4 * rows * width * joined,
            bytes_accessed=rows * width * 6 + rows * joined * 2,
            transcendentals=0,
        ),
        name="merge",
    )(me, pack_table, *attended, cot, merge_weight, branch_ff)
    low, head_part = pl.pallas_call(
        functools.partial(close_kernel, n, heads),
        grid_spec=pltpu.PrefetchScalarGridSpec(
            num_scalar_prefetch=2,
            grid=(slots, groups),
            in_specs=[pl.BlockSpec((1, 3, HD, shard), lambda s, g, a, b: (s, 0, 0, 0))] * n
            + [
                row_spec,
                pl.BlockSpec((3 * joined, width), whole2),
                table_spec,
                table_spec,
                row_spec,
            ],
            out_specs=[
                pl.BlockSpec((1, shard, width), pack_out),
                pl.BlockSpec((3 * joined, width), whole2),
            ],
            scratch_shapes=[
                pltpu.VMEM((3, heads, HD, shard), BF16),
                pltpu.VMEM((3 * joined, width), F32),
            ],
        ),
        out_shape=[
            jax.ShapeDtypeStruct((packs + spare, shard, width), BF16),
            jax.ShapeDtypeStruct((3 * joined, width), BF16),
        ],
        compiler_params=params(),
        cost_estimate=pl.CostEstimate(
            flops=12 * rows * width * joined,
            bytes_accessed=rows * width * 6 + rows * joined * 6,
            transcendentals=0,
        ),
        name="close",
    )(me, pack_table, *backs, normed_low, w_t, cosine, sine, low_ff)
    branch = branch[:, :packs]
    low = low[:packs]
    summed = lax.psum_scatter(branch, "mlp", scatter_dimension=0, tiled=False)
    cols = width // slices
    result = (
        lax.dynamic_slice_in_dim(tokens, column * cols, cols, 2).astype(F32)
        + summed.astype(F32)
        + lax.dynamic_slice_in_dim(down_bias, column * cols, cols, 0)
    ).astype(BF16)

    share = rows // slices
    low_sum = cube_sum(
        cut(low.reshape(rows, width), 0, slices, column), "mlp", masks_of(slices), BF16
    )
    row_in = lax.dynamic_slice_in_dim(
        tokens.reshape(rows, width), column * share, share, 0
    ).astype(F32)
    row_cot = lax.dynamic_slice_in_dim(
        cot.reshape(rows, width), column * share, share, 0
    ).astype(F32)
    cent = row_in - jnp.mean(row_in, axis=-1, keepdims=True)
    inverse = lax.rsqrt(jnp.mean(cent * cent, axis=-1, keepdims=True) + EPS)
    xhat = cent * inverse
    g = low_sum * norm_gain
    row_grad = (
        row_cot
        + (
            g
            - jnp.mean(g, axis=-1, keepdims=True)
            - xhat * jnp.mean(g * xhat, axis=-1, keepdims=True)
        )
        * inverse
    ).astype(BF16)
    tokens_grad = lax.all_gather(row_grad, "mlp", axis=0, tiled=True).reshape(packs, shard, width)
    vectors = jnp.stack([jnp.sum(low_sum * xhat, axis=0), jnp.sum(low_sum, axis=0)])
    vectors = cube_sum(cut(vectors, 1, n, rank), "seq", seq_masks, F32)
    for m in masks_of(slices):
        vectors = vectors + lax.ppermute(vectors, "mlp", [(i, i ^ m) for i in range(slices)])
    gain_grad, shift_grad = vectors[0], vectors[1]

    merge_grad = cube_sum(cut(merge_part, 1, n, rank), "seq", seq_masks, BF16)
    head_grad = jnp.stack(
        [
            cube_sum(
                cut(head_part[j * joined : (j + 1) * joined], 1, n, rank),
                "seq",
                turned(seq_masks, j),
                BF16,
            ).T
            for j in range(3)
        ]
    )
    return (
        result,
        tokens_grad,
        gain_grad,
        shift_grad,
        head_grad,
        merge_grad,
        up_grad,
        up_bias_grad,
        down_grad,
        down_bias_grad,
    )


def solution(mesh):
    in_specs = (
        P(None, "seq", None),
        P(),
        P(),
        P(),
        P(),
        P(None, None, "mlp"),
        P("mlp", None),
        P(None, "mlp"),
        P("mlp"),
        P("mlp", None),
        P(),
        P(None, "seq", "mlp"),
    )
    out_specs = (
        P(None, "seq", "mlp"),
        P(None, "seq", None),
        P("seq"),
        P("seq"),
        P(None, "seq", "mlp"),
        P("mlp", "seq"),
        P("seq", "mlp"),
        P(("mlp", "seq")),
        P("mlp", "seq"),
        P("seq"),
    )
    return jax.shard_map(
        on_device, mesh=mesh, in_specs=in_specs, out_specs=out_specs, check_vma=False
    )
```

```python
import functools
import math

import jax
import jax.numpy as jnp
from jax import lax
from jax.experimental import pallas as pl
from jax.experimental.pallas import tpu as pltpu
from jax.sharding import PartitionSpec as P

HD = 64
ROT = 32
EPS = 1e-05
NEG = -1e30
BF16 = jnp.bfloat16
F32 = jnp.float32
VMEM_LIMIT = 56 * 1024 * 1024
COST = pl.CostEstimate(flops=1 << 20, bytes_accessed=1 << 20, transcendentals=0)


def dot(a, b, dims=((1,), (0,))):
    return lax.dot_general(a, b, (dims, ((), ())), preferred_element_type=F32)


def layout(lengths, counts, pack_len):
    slots = lengths.shape[-1]
    slot_ids = jnp.arange(slots, dtype=jnp.int32)
    used = slot_ids[None, :] < counts[:, None]
    sizes = jnp.where(used, lengths, 0)
    ends = jnp.cumsum(sizes, axis=-1)
    starts = ends - sizes
    filled = ends[:, -1:]
    place = jnp.arange(pack_len, dtype=jnp.int32)[None, :]
    begin = jnp.max(
        jnp.where(used[:, None, :] & (place[:, :, None] >= starts[:, None, :]), starts[:, None, :], 0),
        axis=-1,
    )
    inside = place < filled
    first = jnp.where(inside, begin, place)
    position = jnp.where(inside, place - begin, place - filled)
    cost = jnp.sum(sizes * sizes, axis=-1)
    return first, position, cost


def turn(values, cosine, sine, heads):
    out = []
    parity = lax.broadcasted_iota(jnp.int32, cosine.shape, 0) % 2
    for h in range(heads):
        part = values[h * HD : h * HD + ROT]
        ahead = jnp.concatenate([part[1:], part[:1]], axis=0)
        behind = jnp.concatenate([part[-1:], part[:-1]], axis=0)
        swapped = jnp.where(parity == 0, -ahead, behind)
        out.append(part * cosine + swapped * sine)
        out.append(values[h * HD + ROT : (h + 1) * HD])
    return jnp.concatenate(out, axis=0)


def head_kernel(n, heads, per, me_ref, pack_ref, x_ref, gain_ref, bias_ref, w_ref, cos_ref, sin_ref, *refs):
    normed_ref, copy_ref, outs, scr = refs[0], refs[1], refs[2:-1], refs[-1]
    s_id, g = pl.program_id(0), pl.program_id(1)
    me = me_ref[0]
    width = heads * HD
    copy_ref[0] = x_ref[0]
    x = x_ref[0].astype(F32)
    cent = x - jnp.mean(x, axis=-1, keepdims=True)
    var = jnp.mean(cent * cent, axis=-1, keepdims=True)
    normed = (cent * lax.rsqrt(var + EPS) * gain_ref[...] + bias_ref[...]).astype(BF16)
    normed_ref[0] = normed
    for j in range(3):
        part = dot(w_ref[j * width : (j + 1) * width, :], normed, ((1,), (1,)))
        if j < 2:
            part = turn(part, cos_ref[0], sin_ref[0], heads)
        if j == 0:
            part = part * (1.0 / math.sqrt(HD))
        part = part.astype(BF16)
        for h in range(heads):
            scr[h, j] = part[h * HD : (h + 1) * HD]
    for at, out in enumerate(outs):
        d = lax.bitwise_xor(jnp.int32(at % n), me)

        @pl.when((d // heads == g) & (s_id // per == at // n))
        def _():
            out[0] = scr[d % heads]


def grad_kernel(n, heads, me_ref, c_ref, w_ref, *refs):
    outs, scr = refs[:n], refs[n]
    g = pl.program_id(1)
    me = me_ref[0]
    part = dot(w_ref[...], c_ref[0], ((1,), (1,))).astype(BF16)
    for h in range(heads):
        scr[h] = part[h * HD : (h + 1) * HD]
    for k in range(n):
        d = lax.bitwise_xor(jnp.int32(k), me)

        @pl.when(d // heads == g)
        def _():
            outs[k][0] = scr[d % heads]


def load_parts(n, me, pairs):
    for k in range(n):
        d = lax.bitwise_xor(jnp.int32(k), me)
        for part, t_ref, n_ref in pairs(k):
            if t_ref is not None:
                t_ref[d] = part
            if n_ref is not None:
                n_ref[d] = part.T


def score_of(block, first, i, kn, q_t):
    rows = lax.broadcasted_iota(jnp.int32, (block, block), 0)
    cols = lax.broadcasted_iota(jnp.int32, (block, block), 1)
    ahead = rows - cols

    def scores(j, at):
        s = dot(kn[at], q_t)
        allowed = (rows >= first - j * block) & (ahead <= (i - j) * block)
        return jnp.where(allowed, s, NEG)

    return scores


def attend_kernel(n, block, skip, me_ref, pack_ref, low_ref, first_ref, *refs):
    qkv, outs, keep_ref, logsum_ref = refs[:n], refs[n : 2 * n], refs[2 * n], refs[2 * n + 1]
    qt, vt, kn = refs[2 * n + 2 :]
    s_id = pl.program_id(0) + skip
    me = me_ref[0]
    load_parts(
        n,
        me,
        lambda k: (
            (qkv[k][0, 0, 0], qt, None),
            (qkv[k][0, 0, 1], None, kn),
            (qkv[k][0, 0, 2], vt, None),
        ),
    )

    def outer(i, carry):
        scores = score_of(block, first_ref[0, pl.ds(i, 1), :], i, kn, qt[i])
        j0 = low_ref[s_id, i]

        def forward(t, state):
            top, total, acc = state
            j = j0 + 2 * t
            at = jnp.minimum(j + 1, n - 1)
            s0, s1 = scores(j, j), scores(j + 1, at)
            peak = jnp.max(jnp.maximum(s0, s1), axis=0, keepdims=True)
            new_top = jnp.maximum(top, peak)
            p0, p1 = jnp.exp(s0 - new_top), jnp.exp(s1 - new_top)
            fade = jnp.exp(top - new_top)
            total = total * fade + jnp.sum(p0 + p1, axis=0, keepdims=True)
            acc = acc * fade + dot(vt[j], p0.astype(BF16)) + dot(vt[at], p1.astype(BF16))
            return new_top, total, acc

        top, total, acc = lax.fori_loop(
            0,
            (i - j0) // 2 + 1,
            forward,
            (
                jnp.full((1, block), NEG, F32),
                jnp.zeros((1, block), F32),
                jnp.zeros((HD, block), F32),
            ),
        )
        keep_ref[0, i] = (acc / total).astype(BF16)
        logsum_ref[0, pl.ds(i, 1), :] = top + jnp.log(total)
        return carry

    lax.fori_loop(0, n, outer, 0)
    for k in range(n):
        outs[k][0] = keep_ref[0, lax.bitwise_xor(jnp.int32(k), me)]


def attend_back_kernel(n, block, skip, me_ref, pack_ref, low_ref, first_ref, *refs):
    keep_ref, logsum_ref = refs[:2]
    qkv, grads, outs = refs[2 : n + 2], refs[n + 2 : 2 * n + 2], refs[2 * n + 2 : 3 * n + 2]
    qt, kt, gt, qn, kn, vn, gn, dk, dv, res = refs[3 * n + 2 :]
    s_id = pl.program_id(0) + skip
    me = me_ref[0]
    load_parts(
        n,
        me,
        lambda k: (
            (qkv[k][0, 0, 0], qt, qn),
            (qkv[k][0, 0, 1], kt, kn),
            (qkv[k][0, 0, 2], None, vn),
            (grads[k][0, 0], gt, gn),
        ),
    )
    dk[...] = jnp.zeros_like(dk)
    dv[...] = jnp.zeros_like(dv)

    def outer(i, carry):
        q_t, g_t, q_n, g_n = qt[i], gt[i], qn[i], gn[i]
        scores = score_of(block, first_ref[0, pl.ds(i, 1), :], i, kn, q_t)
        j0 = low_ref[s_id, i]
        inner = jnp.sum(keep_ref[0, i].astype(F32) * g_t.astype(F32), axis=0, keepdims=True)
        logsum = logsum_ref[0, pl.ds(i, 1), :]

        def one(j, at):
            p = jnp.exp(scores(j, at) - logsum)
            ds = (p * (dot(vn[at], g_t) - inner)).astype(BF16)
            return ds, dot(ds, q_n), dot(p.astype(BF16), g_n), dot(kt[at], ds)

        def backward(t, dq):
            j = j0 + 2 * t
            at = jnp.minimum(j + 1, n - 1)
            _, dk0, dv0, dq0 = one(j, j)
            _, dk1, dv1, dq1 = one(j + 1, at)
            dk[j] += dk0
            dv[j] += dv0
            dk[at] += dk1
            dv[at] += dv1
            return dq + dq0 + dq1

        dq = lax.fori_loop(0, (i - j0) // 2 + 1, backward, jnp.zeros((HD, block), F32))
        res[i, 0] = (dq * (1.0 / math.sqrt(HD))).astype(BF16)
        return carry

    lax.fori_loop(0, n, outer, 0)
    for i in range(n):
        res[i, 1] = dk[i].T.astype(BF16)
        res[i, 2] = dv[i].T.astype(BF16)
    for k in range(n):
        outs[k][0] = res[lax.bitwise_xor(jnp.int32(k), me)]


def merge_kernel(n, heads, slices, me_ref, *refs):
    recv = refs[:n]
    c_ref, merge_ref, branch_ref, out_branch, out_weight, scr, acc = refs[n:]
    s_id, g = pl.program_id(0), pl.program_id(1)
    groups = pl.num_programs(1)
    me = me_ref[0]
    width = heads * HD

    @pl.when((s_id == 0) & (g == 0))
    def _():
        acc[...] = jnp.zeros_like(acc)

    for k in range(n):
        d = lax.bitwise_xor(jnp.int32(k), me)

        @pl.when(d // heads == g)
        def _():
            scr[d % heads] = recv[k][0, 0, 0]

    attended = scr[...].reshape(width, c_ref.shape[1])
    acc[...] += dot(attended, c_ref[0])
    branch = dot(attended.T, merge_ref[...]) + branch_ref[0].astype(F32)
    cols = branch.shape[1] // slices
    for m in range(slices):
        out_branch[m, 0] = branch[:, m * cols : (m + 1) * cols].astype(BF16)

    @pl.when((s_id == pl.num_programs(0) - 1) & (g == groups - 1))
    def _():
        out_weight[...] = acc[...].astype(BF16)


def close_kernel(n, heads, me_ref, *refs):
    recv = refs[:n]
    normed_ref, w_ref, cos_ref, sin_ref, low_ref, out_low, out_weight, scr, acc = refs[n:]
    s_id, g = pl.program_id(0), pl.program_id(1)
    groups = pl.num_programs(1)
    me = me_ref[0]
    width = heads * HD
    shard = normed_ref.shape[1]

    @pl.when((s_id == 0) & (g == 0))
    def _():
        acc[...] = jnp.zeros_like(acc)

    for k in range(n):
        d = lax.bitwise_xor(jnp.int32(k), me)

        @pl.when(d // heads == g)
        def _():
            for j in range(3):
                scr[j, d % heads] = recv[k][0, 0, j]

    parts = []
    for j in (0, 1):
        part = scr[j].reshape(width, shard).astype(F32)
        parts.append(turn(part, cos_ref[0], -sin_ref[0], heads).astype(BF16))
    parts.append(scr[2].reshape(width, shard))
    grads = jnp.concatenate(parts, axis=0)
    acc[...] += dot(grads, normed_ref[0])
    low = dot(grads.T, w_ref[...]) + low_ref[0].astype(F32)
    out_low[0] = low.astype(BF16)

    @pl.when((s_id == pl.num_programs(0) - 1) & (g == groups - 1))
    def _():
        out_weight[...] = acc[...]


def place_kernel(block, share, shard, slices, chunks, per_piece, pack_ref, *refs):
    pieces, out, buf, sems, out_sems = refs[:-4], refs[-4], refs[-3], refs[-2], refs[-1]
    me = pack_ref[chunks * slices * share // shard]
    loads, stores = [], []
    arrays = max(ref for ref, _ in per_piece) + 1
    for c in range(chunks):
        for k in range(slices):
            ref, where = per_piece[k]
            for t in range(share // block):
                at = len(loads)
                row = (c * slices + lax.bitwise_xor(jnp.int32(k), me)) * share + t * block
                start = pl.multiple_of(lax.rem(row, shard), block)
                loads.append(
                    pltpu.make_async_copy(
                        pieces[c * arrays + ref].at[where, pl.ds(t * block, block)],
                        buf.at[at],
                        sems.at[at],
                    )
                )
                stores.append(
                    pltpu.make_async_copy(
                        buf.at[at],
                        out.at[pack_ref[row // shard], pl.ds(start, block)],
                        out_sems.at[at],
                    )
                )
    for copy in loads:
        copy.start()
    for load, store in zip(loads, stores):
        load.wait()
        store.start()
    for copy in stores:
        copy.wait()


def small_kernel(n, slices, x_ref, out_ref, first, second, sems, sems2):
    rank, column = lax.axis_index("seq"), lax.axis_index("mlp")
    barrier = pltpu.get_barrier_semaphore()
    peers = [{"seq": lax.bitwise_xor(rank, k)} for k in range(1, n)]
    rows = [{"mlp": lax.bitwise_xor(column, k)} for k in range(1, slices)]
    for peer in peers + rows:
        pl.semaphore_signal(barrier, inc=1, device_id=peer, device_id_type=pl.DeviceIdType.MESH)
    pl.semaphore_wait(barrier, len(peers) + len(rows))

    def exchange(source, target, sems, peers):
        copies = [
            pltpu.make_async_remote_copy(
                src_ref=source(k),
                dst_ref=target.at[k],
                send_sem=sems.at[0, k],
                recv_sem=sems.at[1, k],
                device_id=peer,
                device_id_type=pl.DeviceIdType.MESH,
            )
            for k, peer in enumerate(peers)
        ]
        for copy in copies:
            copy.start()
        for copy in copies:
            copy.wait()

    exchange(lambda k: x_ref.at[lax.bitwise_xor(rank, k + 1)], first, sems, peers)
    total = x_ref[rank]
    for k in range(n - 1):
        total = total + first[k]
    second[slices - 1] = total
    second[slices] = total
    exchange(lambda k: second.at[slices], second, sems2, rows)
    parts = [
        second[jnp.where(column == c, slices - 1, lax.bitwise_xor(column, c) - 1)]
        for c in range(slices)
    ]
    out_ref[...] = functools.reduce(jnp.add, parts)


def small_sum(vectors, n, slices):
    count, width = vectors.shape
    x = jnp.transpose(vectors.reshape(count, n, width // n), (1, 0, 2))
    return pl.pallas_call(
        functools.partial(small_kernel, n, slices),
        out_shape=jax.ShapeDtypeStruct((count, width // n), F32),
        in_specs=[pl.BlockSpec(memory_space=pltpu.VMEM)],
        out_specs=pl.BlockSpec(memory_space=pltpu.VMEM),
        scratch_shapes=[
            pltpu.VMEM((n - 1, count, width // n), F32),
            pltpu.VMEM((slices + 1, count, width // n), F32),
            pltpu.SemaphoreType.DMA((2, n - 1)),
            pltpu.SemaphoreType.DMA((2, slices - 1)),
        ],
        compiler_params=pltpu.CompilerParams(collective_id=0, has_side_effects=True),
        cost_estimate=COST,
        name="small_sum",
    )(x)


def params():
    return pltpu.CompilerParams(vmem_limit_bytes=VMEM_LIMIT)


def tie(*values):
    return lax.optimization_barrier(values)


def send_x(parts):
    n = len(parts)
    sent = jnp.stack([parts[k] for k in range(1, n, 2)])
    return lax.ppermute(sent, "seq", [(i, i ^ 1) for i in range(n)])


def send_z(parts, got, steps=None):
    n = len(parts)
    return [
        lax.ppermute(
            jnp.stack([parts[k], got[k // 2]]), "seq", [(i, i ^ k) for i in range(n)]
        )
        for k in (range(2, n, 2) if steps is None else steps)
    ]


def received(parts, got, gots):
    out = [(parts[0][None], 0), (got, 0)]
    for array in gots:
        out += [(array, 0), (array, 1)]
    return out


def span(masks):
    out = [0]
    for m in masks:
        out += [v ^ m for v in out]
    return out


def cube_send(chunks, axis, n, masks):
    kept = span(masks[1:])
    sent = jnp.stack([chunks[k ^ masks[0]] for k in kept])
    return lax.ppermute(sent, axis, [(i, i ^ masks[0]) for i in range(n)])


def cube_add(chunks, got, masks, kind):
    return {
        k: (chunks[k].astype(F32) + got[at].astype(F32)).astype(kind)
        for at, k in enumerate(span(masks[1:]))
    }


def cube_sum(chunks, axis, masks, kind):
    n = len(chunks)
    chunks = {k: v.astype(kind) for k, v in enumerate(chunks)}
    for step in range(len(masks)):
        got = cube_send(chunks, axis, n, masks[step:])
        chunks = cube_add(chunks, got, masks[step:], F32 if step == len(masks) - 1 else kind)
    return chunks[0]


def gather_step(arrays, axis, n, m):
    sent = jnp.concatenate(arrays, axis=0) if len(arrays) > 1 else arrays[0]
    return arrays + [lax.ppermute(sent, axis, [(i, i ^ m) for i in range(n)])]


def masks_of(n):
    return [1 << b for b in range(n.bit_length() - 1)]


def turned(masks, by):
    by = by % len(masks)
    return masks[by:] + masks[:by]


def cut(array, axis, n, me):
    size = array.shape[axis] // n
    return [
        lax.dynamic_slice_in_dim(array, lax.bitwise_xor(jnp.int32(k), me) * size, size, axis)
        for k in range(n)
    ]


def on_device(
    tokens,
    lengths,
    counts,
    norm_gain,
    norm_bias,
    head_weight,
    merge_weight,
    up_weight,
    up_bias,
    down_weight,
    down_bias,
    cotangent,
):
    packs, shard, width = tokens.shape
    n = lax.axis_size("seq")
    slices = lax.axis_size("mlp")
    pack_len = shard * n
    rank = lax.axis_index("seq")
    column = lax.axis_index("mlp")
    heads = merge_weight.shape[0] // HD
    joined = heads * HD
    groups = n // heads
    slots = -(-packs // groups)
    dealt = groups * slots
    spare = 1 if dealt > packs else 0
    rows = dealt * shard
    chunks = 2 if slots % 2 == 0 else 1
    per = slots // chunks
    seq_masks, mlp_masks = masks_of(n), masks_of(slices)

    first, position, cost = layout(lengths, counts, pack_len)
    ids = jnp.arange(packs, dtype=jnp.int32)
    before = (cost[None, :] > cost[:, None]) | (
        (cost[None, :] == cost[:, None]) & (ids[None, :] < ids[:, None])
    )
    order = jnp.sum(before.astype(jnp.int32), axis=1)
    slot_of = order // groups
    group_of = jnp.where(slot_of % 2 == 0, order % groups, groups - 1 - order % groups)
    at = slot_of * groups + group_of
    hit = at[None, :] == jnp.arange(dealt, dtype=jnp.int32)[:, None]
    pack_at = jnp.where(
        jnp.any(hit, axis=-1), jnp.sum(jnp.where(hit, ids, 0), axis=-1), packs
    ).astype(jnp.int32)
    safe = jnp.minimum(pack_at, packs - 1)
    me = rank.astype(jnp.int32).reshape(1)

    own_cot = jnp.take(cotangent, safe, axis=0, mode="clip")
    if spare:
        own_cot = jnp.where((pack_at < packs)[:, None, None], own_cot, 0)
    cot = lax.all_gather(own_cot, "mlp", axis=2, tiled=True)

    half = ROT // 2
    freq = 10000.0 ** (-(2.0 * jnp.arange(half, dtype=F32)) / ROT)
    own_position = jnp.take(
        lax.dynamic_slice_in_dim(position, rank * shard, shard, 1), safe, axis=0, mode="clip"
    )
    angle = own_position.astype(F32)[:, None, :] * jnp.repeat(freq, 2)[None, :, None]
    cosine, sine = jnp.cos(angle), jnp.sin(angle)

    w_t = jnp.transpose(head_weight, (0, 2, 1)).reshape(3 * joined, width)

    def whole2(s, g, *_):
        return (0, 0)

    def rows_at(skip):
        return pl.BlockSpec((1, shard, width), lambda s, g, *_: ((s + skip) * groups + g, 0, 0))

    def table_at(skip):
        return pl.BlockSpec((1, ROT, shard), lambda s, g, *_: ((s + skip) * groups + g, 0, 0))

    parts = [jax.ShapeDtypeStruct((per, 3, HD, shard), BF16)] * n

    def chunk_at(c):
        return pl.BlockSpec(
            (1, 3, HD, shard), lambda s, g, *_: (jnp.clip(s - c * per, 0, per - 1), 0, 0, 0)
        )

    outs = pl.pallas_call(
        functools.partial(head_kernel, n, heads, per),
        grid_spec=pltpu.PrefetchScalarGridSpec(
            num_scalar_prefetch=2,
            grid=(slots, groups),
            in_specs=[
                pl.BlockSpec((1, shard, width), lambda s, g, a, b: (b[s * groups + g], 0, 0)),
                pl.BlockSpec((1, width), whole2),
                pl.BlockSpec((1, width), whole2),
                pl.BlockSpec((3 * joined, width), whole2),
                table_at(0),
                table_at(0),
            ],
            out_specs=[rows_at(0)] * 2 + [chunk_at(c) for c in range(chunks) for _ in range(n)],
            scratch_shapes=[pltpu.VMEM((heads, 3, HD, shard), BF16)],
        ),
        out_shape=[jax.ShapeDtypeStruct((dealt, shard, width), BF16)] * 2 + parts * chunks,
        compiler_params=params(),
        cost_estimate=COST,
        name="heads",
    )(
        me,
        safe,
        tokens,
        norm_gain.reshape(1, width),
        norm_bias.reshape(1, width),
        w_t,
        cosine,
        sine,
    )
    normed_low, tokens_dealt = outs[0], outs[1]
    qkv = [list(outs[2 + c * n : 2 + (c + 1) * n]) for c in range(chunks)]

    def out_grads(cot, merge_weight):
        return pl.pallas_call(
            functools.partial(grad_kernel, n, heads),
            grid_spec=pltpu.PrefetchScalarGridSpec(
                num_scalar_prefetch=1,
                grid=(slots, groups),
                in_specs=[rows_at(0), pl.BlockSpec((joined, width), whole2)],
                out_specs=[pl.BlockSpec((1, HD, shard), lambda s, g, *_: (s, 0, 0))] * n,
                scratch_shapes=[pltpu.VMEM((heads, HD, shard), BF16)],
            ),
            out_shape=[jax.ShapeDtypeStruct((slots, HD, shard), BF16)] * n,
            compiler_params=params(),
            cost_estimate=COST,
            name="out_grads",
        )(me, cot, merge_weight)

    mine = rank // heads + groups * jnp.arange(slots, dtype=jnp.int32)
    my_packs = jnp.take(safe, mine, mode="clip")
    first = first.reshape(packs, n, shard)
    lows = (jnp.take(first[:, :, 0], my_packs, axis=0, mode="clip") // shard).astype(jnp.int32)
    wide = [pltpu.VMEM((n, HD, shard), BF16)]
    tall = [pltpu.VMEM((n, shard, HD), BF16)]

    def first_at(skip):
        return pl.BlockSpec((1, n, shard), lambda s, a, b, c: (b[s + skip], 0, 0))

    def qkv_at(lead):
        return pl.BlockSpec((1, 1, 3, HD, shard), lambda s, *_: (lead, s, 0, 0, 0))

    def grad_at(lead, skip):
        return pl.BlockSpec((1, 1, HD, shard), lambda s, *_: (lead, s + skip, 0, 0))

    def attend(c, sources):
        return pl.pallas_call(
            functools.partial(attend_kernel, n, shard, c * per),
            grid_spec=pltpu.PrefetchScalarGridSpec(
                num_scalar_prefetch=3,
                grid=(per,),
                in_specs=[first_at(c * per)] + [qkv_at(lead) for _, lead in sources],
                out_specs=[pl.BlockSpec((1, HD, shard), lambda s, *_: (s, 0, 0))] * n
                + [
                    pl.BlockSpec((1, n, HD, shard), lambda s, *_: (s, 0, 0, 0)),
                    pl.BlockSpec((1, n, shard), lambda s, *_: (s, 0, 0)),
                ],
                scratch_shapes=wide * 2 + tall,
            ),
            out_shape=[jax.ShapeDtypeStruct((per, HD, shard), BF16)] * n
            + [
                jax.ShapeDtypeStruct((per, n, HD, shard), BF16),
                jax.ShapeDtypeStruct((per, n, shard), F32),
            ],
            compiler_params=params(),
            cost_estimate=COST,
            name="attend",
        )(me, my_packs, lows, first, *[array for array, _ in sources])

    def attend_back(c, kept, logsum, sources, grads):
        return pl.pallas_call(
            functools.partial(attend_back_kernel, n, shard, c * per),
            grid_spec=pltpu.PrefetchScalarGridSpec(
                num_scalar_prefetch=3,
                grid=(per,),
                in_specs=[
                    first_at(c * per),
                    pl.BlockSpec((1, n, HD, shard), lambda s, *_: (s, 0, 0, 0)),
                    pl.BlockSpec((1, n, shard), lambda s, *_: (s, 0, 0)),
                ]
                + [qkv_at(lead) for _, lead in sources]
                + [grad_at(lead, c * per) for _, lead in grads],
                out_specs=[pl.BlockSpec((1, 3, HD, shard), lambda s, *_: (s, 0, 0, 0))] * n,
                scratch_shapes=wide * 3
                + tall * 4
                + [pltpu.VMEM((n, shard, HD), F32)] * 2
                + [pltpu.VMEM((n, 3, HD, shard), BF16)],
            ),
            out_shape=parts,
            compiler_params=params(),
            cost_estimate=COST,
            name="attend_back",
        )(
            me,
            my_packs,
            lows,
            first,
            kept,
            logsum,
            *[array for array, _ in sources],
            *[array for array, _ in grads],
        )

    def merge(sources, branch_ff):
        return pl.pallas_call(
            functools.partial(merge_kernel, n, heads, slices),
            grid_spec=pltpu.PrefetchScalarGridSpec(
                num_scalar_prefetch=1,
                grid=(slots, groups),
                in_specs=[
                    pl.BlockSpec(
                        (1, 1, 1, HD, shard),
                        lambda s, g, *_, lead=lead: (lead, s // per, s % per, 0, 0),
                    )
                    for _, lead in sources
                ]
                + [rows_at(0), pl.BlockSpec((joined, width), whole2), rows_at(0)],
                out_specs=[
                    pl.BlockSpec(
                        (slices, 1, shard, width // slices),
                        lambda s, g, *_: (0, s * groups + g, 0, 0),
                    ),
                    pl.BlockSpec((joined, width), whole2),
                ],
                scratch_shapes=[
                    pltpu.VMEM((heads, HD, shard), BF16),
                    pltpu.VMEM((joined, width), F32),
                ],
            ),
            out_shape=[
                jax.ShapeDtypeStruct((slices, dealt, shard, width // slices), BF16),
                jax.ShapeDtypeStruct((joined, width), BF16),
            ],
            compiler_params=params(),
            cost_estimate=COST,
            name="merge",
        )(me, *[array for array, _ in sources], cot, merge_weight, branch_ff)

    def close(c, sources):
        skip = c * per
        return pl.pallas_call(
            functools.partial(close_kernel, n, heads),
            grid_spec=pltpu.PrefetchScalarGridSpec(
                num_scalar_prefetch=1,
                grid=(per, groups),
                in_specs=[
                    pl.BlockSpec(
                        (1, 1, 3, HD, shard), lambda s, g, *_, lead=lead: (lead, s, 0, 0, 0)
                    )
                    for _, lead in sources
                ]
                + [
                    rows_at(skip),
                    pl.BlockSpec((3 * joined, width), whole2),
                    table_at(skip),
                    table_at(skip),
                    rows_at(skip),
                ],
                out_specs=[rows_at(0), pl.BlockSpec((3 * joined, width), whole2)],
                scratch_shapes=[
                    pltpu.VMEM((3, heads, HD, shard), BF16),
                    pltpu.VMEM((3 * joined, width), F32),
                ],
            ),
            out_shape=[
                jax.ShapeDtypeStruct((per * groups, shard, width), BF16),
                jax.ShapeDtypeStruct((3 * joined, width), F32),
            ],
            compiler_params=params(),
            cost_estimate=COST,
            name="close",
        )(me, *[array for array, _ in sources], normed_low, w_t, cosine, sine, low_ff)

    got_x = [None] * chunks
    got_z = [None] * chunks
    got_x[0] = send_x(qkv[0])
    hidden = (
        jnp.einsum("psd,df->psf", normed_low, up_weight, preferred_element_type=F32) + up_bias
    )
    active_low = jax.nn.gelu(hidden, approximate=True).astype(BF16)
    branch_ff = jnp.einsum(
        "psf,fd->psd", active_low, down_weight, preferred_element_type=F32
    ).astype(BF16)
    got_x[0], branch_ff, qkv, out_weight, back_weight = tie(
        got_x[0], branch_ff, qkv, merge_weight, down_weight
    )

    got_z[0] = send_z(qkv[0], got_x[0])
    if chunks > 1:
        got_x[1] = send_x(qkv[1])
    sends = out_grads(cot, out_weight)
    active_grad = jnp.einsum("psd,fd->psf", cot, back_weight, preferred_element_type=F32)
    _, gelu_back = jax.vjp(lambda values: jax.nn.gelu(values, approximate=True), hidden)
    hidden_grad = gelu_back(active_grad)[0].astype(BF16)
    got_x, got_z, qkv, sends, hidden_grad = tie(got_x, got_z, qkv, sends, hidden_grad)

    got_dx = send_x(sends)
    sources = [received(qkv[0], got_x[0], got_z[0])]
    if chunks > 1:
        got_z[1] = send_z(qkv[1], got_x[1])
        sources.append(received(qkv[1], got_x[1], got_z[1]))
    ahead = [attend(0, sources[0])]
    up_grad = jnp.einsum(
        "psd,psf->df", normed_low, hidden_grad, preferred_element_type=F32
    ).astype(BF16)
    down_grad = jnp.einsum("psd,psf->df", cot, active_low, preferred_element_type=F32).astype(BF16)
    biases = jnp.sum(hidden_grad.astype(F32), axis=(0, 1)), jnp.sum(cot.astype(F32), axis=(0, 1))
    got_dx, sources_arrays, ahead, sends, hidden_grad, up_grad, down_grad, biases = tie(
        got_dx,
        [[a for a, _ in v] for v in sources],
        ahead,
        sends,
        hidden_grad,
        up_grad,
        down_grad,
        biases,
    )
    def with_row(*parts):
        weight = jnp.concatenate(parts[:2], axis=1)
        row = jnp.concatenate(parts[2:])
        row = jnp.pad(row, (0, weight.shape[1] - row.shape[0])).reshape(1, -1)
        row = jnp.broadcast_to(row, (16, weight.shape[1])).astype(BF16)
        return jnp.concatenate([weight, row], axis=0)

    terms = dict(
        enumerate(
            with_row(*parts)
            for parts in zip(*[cut(v, 0, n, rank) for v in (up_grad, down_grad, *biases)])
        )
    )
    terms_got = cube_send(terms, "seq", n, seq_masks)
    sources = [
        [(a, lead) for a, (_, lead) in zip(arrays, v)] for arrays, v in zip(sources_arrays, sources)
    ]

    got_dz = send_z(sends, got_dx)
    if chunks > 1:
        ahead.append(attend(1, sources[1]))
    low_ff = jnp.einsum(
        "psf,df->psd", hidden_grad, up_weight, preferred_element_type=F32
    ).astype(BF16)
    got_dz, ahead, low_ff = tie(got_dz, ahead, low_ff)
    grads = received(sends, got_dx, got_dz)

    attended = [jnp.stack([outs[k] for outs in ahead]) for k in range(n)]
    got_ax = send_x(attended)
    backs = [attend_back(0, ahead[0][n], ahead[0][n + 1], sources[0], grads)]
    got_ax, terms_got, backs, attended, ahead = tie(got_ax, terms_got, backs, attended, ahead)

    terms = cube_add(terms, terms_got, seq_masks, BF16)
    terms_got = cube_send(terms, "seq", n, seq_masks[1:])
    got_az = send_z(attended, got_ax)
    back_x = [send_x(backs[0])]
    if chunks > 1:
        backs.append(attend_back(1, ahead[1][n], ahead[1][n + 1], sources[1], grads))
    got_az, terms_got, back_x, backs = tie(got_az, terms_got, back_x, backs)

    back_z = [send_z(backs[0], back_x[0])]
    if chunks > 1:
        back_x.append(send_x(backs[1]))
    for step in range(1, len(seq_masks)):
        last_step = step == len(seq_masks) - 1
        terms = cube_add(terms, terms_got, seq_masks[step:], F32 if last_step else BF16)
        if not last_step:
            terms_got = cube_send(terms, "seq", n, seq_masks[step + 1 :])
    terms = terms[0]
    branch, merge_part = merge(received(attended, got_ax, got_az), branch_ff)
    summed = lax.psum_scatter(branch, "mlp", scatter_dimension=0, tiled=False)
    back_x, back_z, backs, merge_part, terms = tie(back_x, back_z, backs, merge_part, terms)

    share = per * groups * shard // slices

    def share_sum(low):
        return cube_sum(
            cut(low.reshape(share * slices, width), 0, slices, column), "mlp", mlp_masks, BF16
        )

    def finish(c, low_sum):
        start = (c * slices + column) * share
        row_in = lax.dynamic_slice_in_dim(
            tokens_dealt.reshape(rows, width), start, share, 0
        ).astype(F32)
        row_cot = lax.dynamic_slice_in_dim(cot.reshape(rows, width), start, share, 0).astype(F32)
        cent = row_in - jnp.mean(row_in, axis=-1, keepdims=True)
        inverse = lax.rsqrt(jnp.mean(cent * cent, axis=-1, keepdims=True) + EPS)
        xhat = cent * inverse
        g = low_sum * norm_gain
        row_grad = (
            row_cot
            + (
                g
                - jnp.mean(g, axis=-1, keepdims=True)
                - xhat * jnp.mean(g * xhat, axis=-1, keepdims=True)
            )
            * inverse
        ).astype(BF16)
        return row_grad, jnp.stack([jnp.sum(low_sum * xhat, axis=0), jnp.sum(low_sum, axis=0)])

    low, head_part = close(0, received(backs[0], back_x[0], back_z[0]))
    head_parts = [head_part]
    if chunks > 1:
        second = send_z(backs[1], back_x[1], [n // 2])
        second, low, head_parts, backs, back_x = tie(second, low, head_parts, backs, back_x)
        others = send_z(backs[1], back_x[1], [k for k in range(2, n, 2) if k != n // 2])
        others.insert(n // 4 - 1, second[0])
        back_z.append(others)
    row_grad, vectors = finish(0, share_sum(low))
    back_z, row_grad, vectors = tie(back_z, row_grad, vectors)

    cols = width // slices
    pieces = gather_step([row_grad[None]], "mlp", slices, mlp_masks[-1])
    result = (
        lax.dynamic_slice_in_dim(tokens, column * cols, cols, 2).astype(F32)
        + jnp.take(summed, at, axis=0, mode="clip").astype(F32)
        + lax.dynamic_slice_in_dim(down_bias, column * cols, cols, 0)
    ).astype(BF16)
    if chunks > 1:
        low, head_part = close(1, received(backs[1], back_x[1], back_z[1]))
        head_parts.append(head_part)
        pieces, low, head_parts, result = tie(pieces, low, head_parts, result)
    weights = functools.reduce(jnp.add, head_parts)
    weights = jnp.concatenate([weights.astype(BF16), merge_part], axis=0)
    weights = dict(enumerate(cut(weights, 1, n, rank)))
    weights_got = cube_send(weights, "seq", n, seq_masks)
    if chunks > 1:
        low_sum = share_sum(low)
        for m in reversed(mlp_masks[:-1]):
            pieces = gather_step(pieces, "mlp", slices, m)
        row_grad, more = finish(1, low_sum)
        vectors = vectors + more
        row_grad, pieces, weights_got, vectors = tie(row_grad, pieces, weights_got, vectors)
        last = gather_step([row_grad[None]], "mlp", slices, mlp_masks[-1])
    else:
        last, pieces = pieces, []
    vectors = small_sum(vectors, n, slices)
    weights = cube_add(weights, weights_got, seq_masks, BF16)
    weights_got = cube_send(weights, "seq", n, seq_masks[1:])
    last, vectors, weights_got = tie(last, vectors, weights_got)
    for m in reversed(mlp_masks[:-1]):
        last = gather_step(last, "mlp", slices, m)
    pieces += last
    where = [(0, 0)]
    lookup = [0]
    for i, m in enumerate(reversed(mlp_masks)):
        where += [(i + 1, j) for j in range(len(lookup))]
        lookup += [k ^ m for k in lookup]
    per_piece = [where[lookup.index(k)] for k in range(slices)]
    block = math.gcd(share, shard)
    tokens_grad = pl.pallas_call(
        functools.partial(
            place_kernel, block, share, shard, slices, chunks, per_piece
        ),
        grid_spec=pltpu.PrefetchScalarGridSpec(
            num_scalar_prefetch=1,
            grid=(1,),
            in_specs=[pl.BlockSpec(memory_space=pl.ANY)] * len(pieces),
            out_specs=pl.BlockSpec(memory_space=pl.ANY),
            scratch_shapes=[
                pltpu.VMEM((rows // block, block, width), BF16),
                pltpu.SemaphoreType.DMA((rows // block,)),
                pltpu.SemaphoreType.DMA((rows // block,)),
            ],
        ),
        out_shape=jax.ShapeDtypeStruct((packs + spare, shard, width), BF16),
        compiler_params=params(),
        name="place",
    )(jnp.concatenate([pack_at, column.astype(jnp.int32).reshape(1)]), *pieces)[:packs]

    for step in range(1, len(seq_masks)):
        weights = cube_add(
            weights, weights_got, seq_masks[step:], F32 if step == len(seq_masks) - 1 else BF16
        )
        if step < len(seq_masks) - 1:
            weights_got = cube_send(weights, "seq", n, seq_masks[step + 1 :])
    weights = weights[0]
    head_grad = jnp.transpose(
        weights[: 3 * joined].reshape(3, joined, width // n), (0, 2, 1)
    )
    merge_grad = weights[3 * joined :]
    part, hidden_here = width // n, up_weight.shape[1]
    up_grad, down_grad = terms[:part, :hidden_here], terms[:part, hidden_here:].T
    up_bias_grad = terms[part, : hidden_here // n]
    down_bias_grad = terms[part, hidden_here // n : hidden_here // n + part]
    return (
        result,
        tokens_grad,
        vectors[0],
        vectors[1],
        head_grad,
        merge_grad,
        up_grad,
        up_bias_grad,
        down_grad,
        down_bias_grad,
    )


def solution(mesh):
    in_specs = (
        P(None, "seq", None),
        P(),
        P(),
        P(),
        P(),
        P(None, None, "mlp"),
        P("mlp", None),
        P(None, "mlp"),
        P("mlp"),
        P("mlp", None),
        P(),
        P(None, "seq", "mlp"),
    )
    out_specs = (
        P(None, "seq", "mlp"),
        P(None, "seq", None),
        P("seq"),
        P("seq"),
        P(None, "seq", "mlp"),
        P("mlp", "seq"),
        P("seq", "mlp"),
        P(("mlp", "seq")),
        P("mlp", "seq"),
        P("seq"),
    )
    return jax.shard_map(
        on_device, mesh=mesh, in_specs=in_specs, out_specs=out_specs, check_vma=False
    )
```

```python
import functools
import math

import jax
import jax.numpy as jnp
from jax import lax
from jax.experimental import pallas as pl
from jax.experimental.pallas import tpu as pltpu
from jax.sharding import PartitionSpec as P

HD = 64
ROT = 32
EPS = 1e-05
NEG = -1e30
BF16 = jnp.bfloat16
F32 = jnp.float32
VMEM_LIMIT = 56 * 1024 * 1024
COST = pl.CostEstimate(flops=1 << 20, bytes_accessed=1 << 20, transcendentals=0)


def dot(a, b, dims=((1,), (0,))):
    return lax.dot_general(a, b, (dims, ((), ())), preferred_element_type=F32)


def layout(lengths, counts, pack_len):
    slots = lengths.shape[-1]
    slot_ids = jnp.arange(slots, dtype=jnp.int32)
    used = slot_ids[None, :] < counts[:, None]
    sizes = jnp.where(used, lengths, 0)
    ends = jnp.cumsum(sizes, axis=-1)
    starts = ends - sizes
    filled = ends[:, -1:]
    place = jnp.arange(pack_len, dtype=jnp.int32)[None, :]
    begin = jnp.max(
        jnp.where(used[:, None, :] & (place[:, :, None] >= starts[:, None, :]), starts[:, None, :], 0),
        axis=-1,
    )
    inside = place < filled
    first = jnp.where(inside, begin, place)
    position = jnp.where(inside, place - begin, place - filled)
    cost = jnp.sum(sizes * sizes, axis=-1)
    return first, position, cost


def turn(values, cosine, sine, heads):
    out = []
    parity = lax.broadcasted_iota(jnp.int32, cosine.shape, 0) % 2
    for h in range(heads):
        part = values[h * HD : h * HD + ROT]
        ahead = jnp.concatenate([part[1:], part[:1]], axis=0)
        behind = jnp.concatenate([part[-1:], part[:-1]], axis=0)
        swapped = jnp.where(parity == 0, -ahead, behind)
        out.append(part * cosine + swapped * sine)
        out.append(values[h * HD + ROT : (h + 1) * HD])
    return jnp.concatenate(out, axis=0)


def head_kernel(n, heads, per, me_ref, pack_ref, x_ref, gain_ref, bias_ref, w_ref, cos_ref, sin_ref, *refs):
    normed_ref, copy_ref, outs, scr = refs[0], refs[1], refs[2:-1], refs[-1]
    s_id, g = pl.program_id(0), pl.program_id(1)
    me = me_ref[0]
    width = heads * HD
    copy_ref[0] = x_ref[0]
    x = x_ref[0].astype(F32)
    cent = x - jnp.mean(x, axis=-1, keepdims=True)
    var = jnp.mean(cent * cent, axis=-1, keepdims=True)
    normed = (cent * lax.rsqrt(var + EPS) * gain_ref[...] + bias_ref[...]).astype(BF16)
    normed_ref[0] = normed
    for j in range(3):
        part = dot(w_ref[j * width : (j + 1) * width, :], normed, ((1,), (1,)))
        if j < 2:
            part = turn(part, cos_ref[0], sin_ref[0], heads)
        if j == 0:
            part = part * (1.0 / math.sqrt(HD))
        part = part.astype(BF16)
        for h in range(heads):
            scr[h, j] = part[h * HD : (h + 1) * HD]
    for at, out in enumerate(outs):
        d = lax.bitwise_xor(jnp.int32(at % n), me)

        @pl.when((d // heads == g) & (s_id // per == at // n))
        def _():
            out[0] = scr[d % heads]


def grad_kernel(n, heads, me_ref, c_ref, w_ref, *refs):
    outs, scr = refs[:n], refs[n]
    g = pl.program_id(1)
    me = me_ref[0]
    part = dot(w_ref[...], c_ref[0], ((1,), (1,))).astype(BF16)
    for h in range(heads):
        scr[h] = part[h * HD : (h + 1) * HD]
    for k in range(n):
        d = lax.bitwise_xor(jnp.int32(k), me)

        @pl.when(d // heads == g)
        def _():
            outs[k][0] = scr[d % heads]


def load_parts(n, me, pairs):
    for k in range(n):
        d = lax.bitwise_xor(jnp.int32(k), me)
        for part, t_ref, n_ref in pairs(k):
            if t_ref is not None:
                t_ref[d] = part
            if n_ref is not None:
                n_ref[d] = part.T


def score_of(block, first, i, kn, q_t):
    rows = lax.broadcasted_iota(jnp.int32, (block, block), 0)
    cols = lax.broadcasted_iota(jnp.int32, (block, block), 1)
    ahead = rows - cols

    def scores(j, at):
        s = dot(kn[at], q_t)
        allowed = (rows >= first - j * block) & (ahead <= (i - j) * block)
        return jnp.where(allowed, s, NEG)

    return scores


def attend_kernel(n, block, skip, me_ref, pack_ref, low_ref, first_ref, *refs):
    qkv, outs, keep_ref, logsum_ref = refs[:n], refs[n : 2 * n], refs[2 * n], refs[2 * n + 1]
    qt, vt, kn = refs[2 * n + 2 :]
    s_id = pl.program_id(0) + skip
    me = me_ref[0]
    load_parts(
        n,
        me,
        lambda k: (
            (qkv[k][0, 0, 0], qt, None),
            (qkv[k][0, 0, 1], None, kn),
            (qkv[k][0, 0, 2], vt, None),
        ),
    )

    def outer(i, carry):
        scores = score_of(block, first_ref[0, pl.ds(i, 1), :], i, kn, qt[i])
        j0 = low_ref[s_id, i]

        def forward(t, state):
            top, total, acc = state
            j = j0 + 2 * t
            at = jnp.minimum(j + 1, n - 1)
            s0, s1 = scores(j, j), scores(j + 1, at)
            peak = jnp.max(jnp.maximum(s0, s1), axis=0, keepdims=True)
            new_top = jnp.maximum(top, peak)
            p0, p1 = jnp.exp(s0 - new_top), jnp.exp(s1 - new_top)
            fade = jnp.exp(top - new_top)
            total = total * fade + jnp.sum(p0 + p1, axis=0, keepdims=True)
            acc = acc * fade + dot(vt[j], p0.astype(BF16)) + dot(vt[at], p1.astype(BF16))
            return new_top, total, acc

        top, total, acc = lax.fori_loop(
            0,
            (i - j0) // 2 + 1,
            forward,
            (
                jnp.full((1, block), NEG, F32),
                jnp.zeros((1, block), F32),
                jnp.zeros((HD, block), F32),
            ),
        )
        keep_ref[0, i] = (acc / total).astype(BF16)
        logsum_ref[0, pl.ds(i, 1), :] = top + jnp.log(total)
        return carry

    lax.fori_loop(0, n, outer, 0)
    for k in range(n):
        outs[k][0] = keep_ref[0, lax.bitwise_xor(jnp.int32(k), me)]


def attend_back_kernel(n, block, skip, me_ref, pack_ref, low_ref, first_ref, *refs):
    keep_ref, logsum_ref = refs[:2]
    qkv, grads, outs = refs[2 : n + 2], refs[n + 2 : 2 * n + 2], refs[2 * n + 2 : 3 * n + 2]
    qt, kt, gt, qn, kn, vn, gn, dk, dv, res = refs[3 * n + 2 :]
    s_id = pl.program_id(0) + skip
    me = me_ref[0]
    load_parts(
        n,
        me,
        lambda k: (
            (qkv[k][0, 0, 0], qt, qn),
            (qkv[k][0, 0, 1], kt, kn),
            (qkv[k][0, 0, 2], None, vn),
            (grads[k][0, 0], gt, gn),
        ),
    )
    dk[...] = jnp.zeros_like(dk)
    dv[...] = jnp.zeros_like(dv)

    def outer(i, carry):
        q_t, g_t, q_n, g_n = qt[i], gt[i], qn[i], gn[i]
        scores = score_of(block, first_ref[0, pl.ds(i, 1), :], i, kn, q_t)
        j0 = low_ref[s_id, i]
        inner = jnp.sum(keep_ref[0, i].astype(F32) * g_t.astype(F32), axis=0, keepdims=True)
        logsum = logsum_ref[0, pl.ds(i, 1), :]

        def one(j, at):
            p = jnp.exp(scores(j, at) - logsum)
            ds = (p * (dot(vn[at], g_t) - inner)).astype(BF16)
            return ds, dot(ds, q_n), dot(p.astype(BF16), g_n), dot(kt[at], ds)

        def backward(t, dq):
            j = j0 + 2 * t
            at = jnp.minimum(j + 1, n - 1)
            _, dk0, dv0, dq0 = one(j, j)
            _, dk1, dv1, dq1 = one(j + 1, at)
            dk[j] += dk0
            dv[j] += dv0
            dk[at] += dk1
            dv[at] += dv1
            return dq + dq0 + dq1

        dq = lax.fori_loop(0, (i - j0) // 2 + 1, backward, jnp.zeros((HD, block), F32))
        res[i, 0] = (dq * (1.0 / math.sqrt(HD))).astype(BF16)
        return carry

    lax.fori_loop(0, n, outer, 0)
    for i in range(n):
        res[i, 1] = dk[i].T.astype(BF16)
        res[i, 2] = dv[i].T.astype(BF16)
    for k in range(n):
        outs[k][0] = res[lax.bitwise_xor(jnp.int32(k), me)]


def merge_kernel(n, heads, slices, me_ref, *refs):
    recv = refs[:n]
    c_ref, merge_ref, branch_ref, out_branch, out_weight, scr, acc = refs[n:]
    s_id, g = pl.program_id(0), pl.program_id(1)
    groups = pl.num_programs(1)
    me = me_ref[0]
    width = heads * HD

    @pl.when((s_id == 0) & (g == 0))
    def _():
        acc[...] = jnp.zeros_like(acc)

    for k in range(n):
        d = lax.bitwise_xor(jnp.int32(k), me)

        @pl.when(d // heads == g)
        def _():
            scr[d % heads] = recv[k][0, 0, 0]

    attended = scr[...].reshape(width, c_ref.shape[1])
    acc[...] += dot(attended, c_ref[0])
    branch = dot(attended.T, merge_ref[...]) + branch_ref[0].astype(F32)
    cols = branch.shape[1] // slices
    for m in range(slices):
        out_branch[m, 0] = branch[:, m * cols : (m + 1) * cols].astype(BF16)

    @pl.when((s_id == pl.num_programs(0) - 1) & (g == groups - 1))
    def _():
        out_weight[...] = acc[...].astype(BF16)


def close_kernel(n, heads, me_ref, *refs):
    recv = refs[:n]
    normed_ref, w_ref, cos_ref, sin_ref, low_ref, out_low, out_weight, scr, acc = refs[n:]
    s_id, g = pl.program_id(0), pl.program_id(1)
    groups = pl.num_programs(1)
    me = me_ref[0]
    width = heads * HD
    shard = normed_ref.shape[1]

    @pl.when((s_id == 0) & (g == 0))
    def _():
        acc[...] = jnp.zeros_like(acc)

    for k in range(n):
        d = lax.bitwise_xor(jnp.int32(k), me)

        @pl.when(d // heads == g)
        def _():
            for j in range(3):
                scr[j, d % heads] = recv[k][0, 0, j]

    parts = []
    for j in (0, 1):
        part = scr[j].reshape(width, shard).astype(F32)
        parts.append(turn(part, cos_ref[0], -sin_ref[0], heads).astype(BF16))
    parts.append(scr[2].reshape(width, shard))
    grads = jnp.concatenate(parts, axis=0)
    acc[...] += dot(grads, normed_ref[0])
    low = dot(grads.T, w_ref[...]) + low_ref[0].astype(F32)
    out_low[0] = low.astype(BF16)

    @pl.when((s_id == pl.num_programs(0) - 1) & (g == groups - 1))
    def _():
        out_weight[...] = acc[...]


def place_kernel(block, share, shard, slices, chunks, per_piece, pack_ref, *refs):
    pieces, out, buf, sems, out_sems = refs[:-4], refs[-4], refs[-3], refs[-2], refs[-1]
    me = pack_ref[chunks * slices * share // shard]
    loads, stores = [], []
    arrays = max(ref for ref, _ in per_piece) + 1
    for c in range(chunks):
        for k in range(slices):
            ref, where = per_piece[k]
            for t in range(share // block):
                at = len(loads)
                row = (c * slices + lax.bitwise_xor(jnp.int32(k), me)) * share + t * block
                start = pl.multiple_of(lax.rem(row, shard), block)
                loads.append(
                    pltpu.make_async_copy(
                        pieces[c * arrays + ref].at[where, pl.ds(t * block, block)],
                        buf.at[at],
                        sems.at[at],
                    )
                )
                stores.append(
                    pltpu.make_async_copy(
                        buf.at[at],
                        out.at[pack_ref[row // shard], pl.ds(start, block)],
                        out_sems.at[at],
                    )
                )
    for copy in loads:
        copy.start()
    for load, store in zip(loads, stores):
        load.wait()
        store.start()
    for copy in stores:
        copy.wait()


def small_kernel(n, slices, x_ref, out_ref, first, second, sems, sems2):
    rank, column = lax.axis_index("seq"), lax.axis_index("mlp")
    barrier = pltpu.get_barrier_semaphore()
    peers = [{"seq": lax.bitwise_xor(rank, k)} for k in range(1, n)]
    rows = [{"mlp": lax.bitwise_xor(column, k)} for k in range(1, slices)]
    for peer in peers + rows:
        pl.semaphore_signal(barrier, inc=1, device_id=peer, device_id_type=pl.DeviceIdType.MESH)
    pl.semaphore_wait(barrier, len(peers) + len(rows))

    def exchange(source, target, sems, peers):
        copies = [
            pltpu.make_async_remote_copy(
                src_ref=source(k),
                dst_ref=target.at[k],
                send_sem=sems.at[0, k],
                recv_sem=sems.at[1, k],
                device_id=peer,
                device_id_type=pl.DeviceIdType.MESH,
            )
            for k, peer in enumerate(peers)
        ]
        for copy in copies:
            copy.start()
        for copy in copies:
            copy.wait()

    exchange(lambda k: x_ref.at[lax.bitwise_xor(rank, k + 1)], first, sems, peers)
    total = x_ref[rank]
    for k in range(n - 1):
        total = total + first[k]
    second[slices - 1] = total
    second[slices] = total
    exchange(lambda k: second.at[slices], second, sems2, rows)
    parts = [
        second[jnp.where(column == c, slices - 1, lax.bitwise_xor(column, c) - 1)]
        for c in range(slices)
    ]
    out_ref[...] = functools.reduce(jnp.add, parts)


def small_sum(vectors, n, slices):
    count, width = vectors.shape
    x = jnp.transpose(vectors.reshape(count, n, width // n), (1, 0, 2))
    return pl.pallas_call(
        functools.partial(small_kernel, n, slices),
        out_shape=jax.ShapeDtypeStruct((count, width // n), F32),
        in_specs=[pl.BlockSpec(memory_space=pltpu.VMEM)],
        out_specs=pl.BlockSpec(memory_space=pltpu.VMEM),
        scratch_shapes=[
            pltpu.VMEM((n - 1, count, width // n), F32),
            pltpu.VMEM((slices + 1, count, width // n), F32),
            pltpu.SemaphoreType.DMA((2, n - 1)),
            pltpu.SemaphoreType.DMA((2, slices - 1)),
        ],
        compiler_params=pltpu.CompilerParams(collective_id=0, has_side_effects=True),
        cost_estimate=COST,
        name="small_sum",
    )(x)


def params():
    return pltpu.CompilerParams(vmem_limit_bytes=VMEM_LIMIT)


def tie(*values):
    return lax.optimization_barrier(values)


def send_x(parts):
    n = len(parts)
    sent = jnp.stack([parts[k] for k in range(1, n, 2)])
    return lax.ppermute(sent, "seq", [(i, i ^ 1) for i in range(n)])


def send_z(parts, got, steps=None):
    n = len(parts)
    return [
        lax.ppermute(
            jnp.stack([parts[k], got[k // 2]]), "seq", [(i, i ^ k) for i in range(n)]
        )
        for k in (range(2, n, 2) if steps is None else steps)
    ]


def received(parts, got, gots):
    out = [(parts[0][None], 0), (got, 0)]
    for array in gots:
        out += [(array, 0), (array, 1)]
    return out


def span(masks):
    out = [0]
    for m in masks:
        out += [v ^ m for v in out]
    return out


def cube_send(chunks, axis, n, masks):
    kept = span(masks[1:])
    sent = jnp.stack([chunks[k ^ masks[0]] for k in kept])
    return lax.ppermute(sent, axis, [(i, i ^ masks[0]) for i in range(n)])


def cube_add(chunks, got, masks, kind):
    return {
        k: (chunks[k].astype(F32) + got[at].astype(F32)).astype(kind)
        for at, k in enumerate(span(masks[1:]))
    }


def cube_sum(chunks, axis, masks, kind):
    n = len(chunks)
    chunks = {k: v.astype(kind) for k, v in enumerate(chunks)}
    for step in range(len(masks)):
        got = cube_send(chunks, axis, n, masks[step:])
        chunks = cube_add(chunks, got, masks[step:], F32 if step == len(masks) - 1 else kind)
    return chunks[0]


def gather_step(arrays, axis, n, m):
    sent = jnp.concatenate(arrays, axis=0) if len(arrays) > 1 else arrays[0]
    return arrays + [lax.ppermute(sent, axis, [(i, i ^ m) for i in range(n)])]


def masks_of(n):
    return [1 << b for b in range(n.bit_length() - 1)]


def turned(masks, by):
    by = by % len(masks)
    return masks[by:] + masks[:by]


def cut(array, axis, n, me):
    size = array.shape[axis] // n
    return [
        lax.dynamic_slice_in_dim(array, lax.bitwise_xor(jnp.int32(k), me) * size, size, axis)
        for k in range(n)
    ]


def on_device(
    tokens,
    lengths,
    counts,
    norm_gain,
    norm_bias,
    head_weight,
    merge_weight,
    up_weight,
    up_bias,
    down_weight,
    down_bias,
    cotangent,
):
    packs, shard, width = tokens.shape
    n = lax.axis_size("seq")
    slices = lax.axis_size("mlp")
    pack_len = shard * n
    rank = lax.axis_index("seq")
    column = lax.axis_index("mlp")
    heads = merge_weight.shape[0] // HD
    joined = heads * HD
    groups = n // heads
    slots = -(-packs // groups)
    dealt = groups * slots
    spare = 1 if dealt > packs else 0
    rows = dealt * shard
    chunks = 2 if slots % 2 == 0 else 1
    per = slots // chunks
    seq_masks, mlp_masks = masks_of(n), masks_of(slices)

    first, position, cost = layout(lengths, counts, pack_len)
    ids = jnp.arange(packs, dtype=jnp.int32)
    before = (cost[None, :] > cost[:, None]) | (
        (cost[None, :] == cost[:, None]) & (ids[None, :] < ids[:, None])
    )
    order = jnp.sum(before.astype(jnp.int32), axis=1)
    slot_of = order // groups
    group_of = jnp.where(slot_of % 2 == 0, order % groups, groups - 1 - order % groups)
    at = slot_of * groups + group_of
    hit = at[None, :] == jnp.arange(dealt, dtype=jnp.int32)[:, None]
    pack_at = jnp.where(
        jnp.any(hit, axis=-1), jnp.sum(jnp.where(hit, ids, 0), axis=-1), packs
    ).astype(jnp.int32)
    safe = jnp.minimum(pack_at, packs - 1)
    me = rank.astype(jnp.int32).reshape(1)

    own_cot = jnp.take(cotangent, safe, axis=0, mode="clip")
    if spare:
        own_cot = jnp.where((pack_at < packs)[:, None, None], own_cot, 0)
    cot = lax.all_gather(own_cot, "mlp", axis=2, tiled=True)

    half = ROT // 2
    freq = 10000.0 ** (-(2.0 * jnp.arange(half, dtype=F32)) / ROT)
    own_position = jnp.take(
        lax.dynamic_slice_in_dim(position, rank * shard, shard, 1), safe, axis=0, mode="clip"
    )
    angle = own_position.astype(F32)[:, None, :] * jnp.repeat(freq, 2)[None, :, None]
    cosine, sine = jnp.cos(angle), jnp.sin(angle)

    w_t = jnp.transpose(head_weight, (0, 2, 1)).reshape(3 * joined, width)

    def whole2(s, g, *_):
        return (0, 0)

    def rows_at(skip):
        return pl.BlockSpec((1, shard, width), lambda s, g, *_: ((s + skip) * groups + g, 0, 0))

    def table_at(skip):
        return pl.BlockSpec((1, ROT, shard), lambda s, g, *_: ((s + skip) * groups + g, 0, 0))

    parts = [jax.ShapeDtypeStruct((per, 3, HD, shard), BF16)] * n

    def chunk_at(c):
        return pl.BlockSpec(
            (1, 3, HD, shard), lambda s, g, *_: (jnp.clip(s - c * per, 0, per - 1), 0, 0, 0)
        )

    outs = pl.pallas_call(
        functools.partial(head_kernel, n, heads, per),
        grid_spec=pltpu.PrefetchScalarGridSpec(
            num_scalar_prefetch=2,
            grid=(slots, groups),
            in_specs=[
                pl.BlockSpec((1, shard, width), lambda s, g, a, b: (b[s * groups + g], 0, 0)),
                pl.BlockSpec((1, width), whole2),
                pl.BlockSpec((1, width), whole2),
                pl.BlockSpec((3 * joined, width), whole2),
                table_at(0),
                table_at(0),
            ],
            out_specs=[rows_at(0)] * 2 + [chunk_at(c) for c in range(chunks) for _ in range(n)],
            scratch_shapes=[pltpu.VMEM((heads, 3, HD, shard), BF16)],
        ),
        out_shape=[jax.ShapeDtypeStruct((dealt, shard, width), BF16)] * 2 + parts * chunks,
        compiler_params=params(),
        cost_estimate=COST,
        name="heads",
    )(
        me,
        safe,
        tokens,
        norm_gain.reshape(1, width),
        norm_bias.reshape(1, width),
        w_t,
        cosine,
        sine,
    )
    normed_low, tokens_dealt = outs[0], outs[1]
    qkv = [list(outs[2 + c * n : 2 + (c + 1) * n]) for c in range(chunks)]

    def out_grads(cot, merge_weight):
        return pl.pallas_call(
            functools.partial(grad_kernel, n, heads),
            grid_spec=pltpu.PrefetchScalarGridSpec(
                num_scalar_prefetch=1,
                grid=(slots, groups),
                in_specs=[rows_at(0), pl.BlockSpec((joined, width), whole2)],
                out_specs=[pl.BlockSpec((1, HD, shard), lambda s, g, *_: (s, 0, 0))] * n,
                scratch_shapes=[pltpu.VMEM((heads, HD, shard), BF16)],
            ),
            out_shape=[jax.ShapeDtypeStruct((slots, HD, shard), BF16)] * n,
            compiler_params=params(),
            cost_estimate=COST,
            name="out_grads",
        )(me, cot, merge_weight)

    mine = rank // heads + groups * jnp.arange(slots, dtype=jnp.int32)
    my_packs = jnp.take(safe, mine, mode="clip")
    first = first.reshape(packs, n, shard)
    lows = (jnp.take(first[:, :, 0], my_packs, axis=0, mode="clip") // shard).astype(jnp.int32)
    wide = [pltpu.VMEM((n, HD, shard), BF16)]
    tall = [pltpu.VMEM((n, shard, HD), BF16)]

    def first_at(skip):
        return pl.BlockSpec((1, n, shard), lambda s, a, b, c: (b[s + skip], 0, 0))

    def qkv_at(lead):
        return pl.BlockSpec((1, 1, 3, HD, shard), lambda s, *_: (lead, s, 0, 0, 0))

    def grad_at(lead, skip):
        return pl.BlockSpec((1, 1, HD, shard), lambda s, *_: (lead, s + skip, 0, 0))

    def attend(c, sources):
        return pl.pallas_call(
            functools.partial(attend_kernel, n, shard, c * per),
            grid_spec=pltpu.PrefetchScalarGridSpec(
                num_scalar_prefetch=3,
                grid=(per,),
                in_specs=[first_at(c * per)] + [qkv_at(lead) for _, lead in sources],
                out_specs=[pl.BlockSpec((1, HD, shard), lambda s, *_: (s, 0, 0))] * n
                + [
                    pl.BlockSpec((1, n, HD, shard), lambda s, *_: (s, 0, 0, 0)),
                    pl.BlockSpec((1, n, shard), lambda s, *_: (s, 0, 0)),
                ],
                scratch_shapes=wide * 2 + tall,
            ),
            out_shape=[jax.ShapeDtypeStruct((per, HD, shard), BF16)] * n
            + [
                jax.ShapeDtypeStruct((per, n, HD, shard), BF16),
                jax.ShapeDtypeStruct((per, n, shard), F32),
            ],
            compiler_params=params(),
            cost_estimate=COST,
            name="attend",
        )(me, my_packs, lows, first, *[array for array, _ in sources])

    def attend_back(c, kept, logsum, sources, grads):
        return pl.pallas_call(
            functools.partial(attend_back_kernel, n, shard, c * per),
            grid_spec=pltpu.PrefetchScalarGridSpec(
                num_scalar_prefetch=3,
                grid=(per,),
                in_specs=[
                    first_at(c * per),
                    pl.BlockSpec((1, n, HD, shard), lambda s, *_: (s, 0, 0, 0)),
                    pl.BlockSpec((1, n, shard), lambda s, *_: (s, 0, 0)),
                ]
                + [qkv_at(lead) for _, lead in sources]
                + [grad_at(lead, c * per) for _, lead in grads],
                out_specs=[pl.BlockSpec((1, 3, HD, shard), lambda s, *_: (s, 0, 0, 0))] * n,
                scratch_shapes=wide * 3
                + tall * 4
                + [pltpu.VMEM((n, shard, HD), F32)] * 2
                + [pltpu.VMEM((n, 3, HD, shard), BF16)],
            ),
            out_shape=parts,
            compiler_params=params(),
            cost_estimate=COST,
            name="attend_back",
        )(
            me,
            my_packs,
            lows,
            first,
            kept,
            logsum,
            *[array for array, _ in sources],
            *[array for array, _ in grads],
        )

    def merge(sources, branch_ff):
        return pl.pallas_call(
            functools.partial(merge_kernel, n, heads, slices),
            grid_spec=pltpu.PrefetchScalarGridSpec(
                num_scalar_prefetch=1,
                grid=(slots, groups),
                in_specs=[
                    pl.BlockSpec(
                        (1, 1, 1, HD, shard),
                        lambda s, g, *_, lead=lead: (lead, s // per, s % per, 0, 0),
                    )
                    for _, lead in sources
                ]
                + [rows_at(0), pl.BlockSpec((joined, width), whole2), rows_at(0)],
                out_specs=[
                    pl.BlockSpec(
                        (slices, 1, shard, width // slices),
                        lambda s, g, *_: (0, s * groups + g, 0, 0),
                    ),
                    pl.BlockSpec((joined, width), whole2),
                ],
                scratch_shapes=[
                    pltpu.VMEM((heads, HD, shard), BF16),
                    pltpu.VMEM((joined, width), F32),
                ],
            ),
            out_shape=[
                jax.ShapeDtypeStruct((slices, dealt, shard, width // slices), BF16),
                jax.ShapeDtypeStruct((joined, width), BF16),
            ],
            compiler_params=params(),
            cost_estimate=COST,
            name="merge",
        )(me, *[array for array, _ in sources], cot, merge_weight, branch_ff)

    def close(c, sources):
        skip = c * per
        return pl.pallas_call(
            functools.partial(close_kernel, n, heads),
            grid_spec=pltpu.PrefetchScalarGridSpec(
                num_scalar_prefetch=1,
                grid=(per, groups),
                in_specs=[
                    pl.BlockSpec(
                        (1, 1, 3, HD, shard), lambda s, g, *_, lead=lead: (lead, s, 0, 0, 0)
                    )
                    for _, lead in sources
                ]
                + [
                    rows_at(skip),
                    pl.BlockSpec((3 * joined, width), whole2),
                    table_at(skip),
                    table_at(skip),
                    rows_at(skip),
                ],
                out_specs=[rows_at(0), pl.BlockSpec((3 * joined, width), whole2)],
                scratch_shapes=[
                    pltpu.VMEM((3, heads, HD, shard), BF16),
                    pltpu.VMEM((3 * joined, width), F32),
                ],
            ),
            out_shape=[
                jax.ShapeDtypeStruct((per * groups, shard, width), BF16),
                jax.ShapeDtypeStruct((3 * joined, width), F32),
            ],
            compiler_params=params(),
            cost_estimate=COST,
            name="close",
        )(me, *[array for array, _ in sources], normed_low, w_t, cosine, sine, low_ff)

    got_x = [None] * chunks
    got_z = [None] * chunks
    got_x[0] = send_x(qkv[0])
    hidden = (
        jnp.einsum("psd,df->psf", normed_low, up_weight, preferred_element_type=F32) + up_bias
    )
    active_low = jax.nn.gelu(hidden, approximate=True).astype(BF16)
    branch_ff = jnp.einsum(
        "psf,fd->psd", active_low, down_weight, preferred_element_type=F32
    ).astype(BF16)
    got_x[0], branch_ff, qkv, out_weight, back_weight = tie(
        got_x[0], branch_ff, qkv, merge_weight, down_weight
    )

    got_z[0] = send_z(qkv[0], got_x[0])
    if chunks > 1:
        got_x[1] = send_x(qkv[1])
    sends = out_grads(cot, out_weight)
    active_grad = jnp.einsum("psd,fd->psf", cot, back_weight, preferred_element_type=F32)
    _, gelu_back = jax.vjp(lambda values: jax.nn.gelu(values, approximate=True), hidden)
    hidden_grad = gelu_back(active_grad)[0].astype(BF16)
    got_x, got_z, qkv, sends, hidden_grad = tie(got_x, got_z, qkv, sends, hidden_grad)

    got_dx = send_x(sends)
    sources = [received(qkv[0], got_x[0], got_z[0])]
    if chunks > 1:
        got_z[1] = send_z(qkv[1], got_x[1])
        sources.append(received(qkv[1], got_x[1], got_z[1]))
    ahead = [attend(0, sources[0])]
    up_grad = jnp.einsum(
        "psd,psf->df", normed_low, hidden_grad, preferred_element_type=F32
    ).astype(BF16)
    down_grad = jnp.einsum("psd,psf->df", cot, active_low, preferred_element_type=F32).astype(BF16)
    biases = jnp.sum(hidden_grad.astype(F32), axis=(0, 1)), jnp.sum(cot.astype(F32), axis=(0, 1))
    got_dx, sources_arrays, ahead, sends, hidden_grad, up_grad, down_grad, biases = tie(
        got_dx,
        [[a for a, _ in v] for v in sources],
        ahead,
        sends,
        hidden_grad,
        up_grad,
        down_grad,
        biases,
    )
    def with_row(*parts):
        weight = jnp.concatenate(parts[:2], axis=1)
        row = jnp.concatenate(parts[2:])
        row = jnp.pad(row, (0, weight.shape[1] - row.shape[0])).reshape(1, -1)
        row = jnp.broadcast_to(row, (16, weight.shape[1])).astype(BF16)
        return jnp.concatenate([weight, row], axis=0)

    terms = dict(
        enumerate(
            with_row(*parts)
            for parts in zip(*[cut(v, 0, n, rank) for v in (up_grad, down_grad, *biases)])
        )
    )
    terms_got = cube_send(terms, "seq", n, seq_masks)
    sources = [
        [(a, lead) for a, (_, lead) in zip(arrays, v)] for arrays, v in zip(sources_arrays, sources)
    ]

    got_dz = send_z(sends, got_dx)
    if chunks > 1:
        ahead.append(attend(1, sources[1]))
    low_ff = jnp.einsum(
        "psf,df->psd", hidden_grad, up_weight, preferred_element_type=F32
    ).astype(BF16)
    got_dz, ahead, low_ff = tie(got_dz, ahead, low_ff)
    grads = received(sends, got_dx, got_dz)

    attended = [jnp.stack([outs[k] for outs in ahead]) for k in range(n)]
    got_ax = send_x(attended)
    backs = [attend_back(0, ahead[0][n], ahead[0][n + 1], sources[0], grads)]
    got_ax, terms_got, backs, attended, ahead = tie(got_ax, terms_got, backs, attended, ahead)

    terms = cube_add(terms, terms_got, seq_masks, BF16)
    terms_got = cube_send(terms, "seq", n, seq_masks[1:])
    got_az = send_z(attended, got_ax)
    back_x = [send_x(backs[0])]
    if chunks > 1:
        backs.append(attend_back(1, ahead[1][n], ahead[1][n + 1], sources[1], grads))
    got_az, terms_got, back_x, backs = tie(got_az, terms_got, back_x, backs)

    back_z = [send_z(backs[0], back_x[0])]
    if chunks > 1:
        back_x.append(send_x(backs[1]))
    for step in range(1, len(seq_masks)):
        last_step = step == len(seq_masks) - 1
        terms = cube_add(terms, terms_got, seq_masks[step:], F32 if last_step else BF16)
        if not last_step:
            terms_got = cube_send(terms, "seq", n, seq_masks[step + 1 :])
    terms = terms[0]
    branch, merge_part = merge(received(attended, got_ax, got_az), branch_ff)
    summed = lax.psum_scatter(branch, "mlp", scatter_dimension=0, tiled=False)
    back_x, back_z, backs, merge_part, terms = tie(back_x, back_z, backs, merge_part, terms)

    share = per * groups * shard // slices

    def share_sum(low):
        return cube_sum(
            cut(low.reshape(share * slices, width), 0, slices, column), "mlp", mlp_masks, BF16
        )

    def finish(c, low_sum):
        start = (c * slices + column) * share
        row_in = lax.dynamic_slice_in_dim(
            tokens_dealt.reshape(rows, width), start, share, 0
        ).astype(F32)
        row_cot = lax.dynamic_slice_in_dim(cot.reshape(rows, width), start, share, 0).astype(F32)
        cent = row_in - jnp.mean(row_in, axis=-1, keepdims=True)
        inverse = lax.rsqrt(jnp.mean(cent * cent, axis=-1, keepdims=True) + EPS)
        xhat = cent * inverse
        g = low_sum * norm_gain
        row_grad = (
            row_cot
            + (
                g
                - jnp.mean(g, axis=-1, keepdims=True)
                - xhat * jnp.mean(g * xhat, axis=-1, keepdims=True)
            )
            * inverse
        ).astype(BF16)
        return row_grad, jnp.stack([jnp.sum(low_sum * xhat, axis=0), jnp.sum(low_sum, axis=0)])

    low, head_part = close(0, received(backs[0], back_x[0], back_z[0]))
    head_parts = [head_part]
    if chunks > 1:
        second = send_z(backs[1], back_x[1], [n // 2])
        second, low, head_parts, backs, back_x = tie(second, low, head_parts, backs, back_x)
        others = send_z(backs[1], back_x[1], [k for k in range(2, n, 2) if k != n // 2])
        others.insert(n // 4 - 1, second[0])
        back_z.append(others)
    row_grad, vectors = finish(0, share_sum(low))
    back_z, row_grad, vectors = tie(back_z, row_grad, vectors)

    cols = width // slices
    pieces = gather_step([row_grad[None]], "mlp", slices, mlp_masks[-1])
    result = (
        lax.dynamic_slice_in_dim(tokens, column * cols, cols, 2).astype(F32)
        + jnp.take(summed, at, axis=0, mode="clip").astype(F32)
        + lax.dynamic_slice_in_dim(down_bias, column * cols, cols, 0)
    ).astype(BF16)
    if chunks > 1:
        low, head_part = close(1, received(backs[1], back_x[1], back_z[1]))
        head_parts.append(head_part)
        pieces, low, head_parts, result = tie(pieces, low, head_parts, result)
    weights = functools.reduce(jnp.add, head_parts)
    weights = jnp.concatenate([weights.astype(BF16), merge_part], axis=0)
    weights = dict(enumerate(cut(weights, 1, n, rank)))
    weights_got = cube_send(weights, "seq", n, seq_masks)
    if chunks > 1:
        low_sum = share_sum(low)
        for m in reversed(mlp_masks[:-1]):
            pieces = gather_step(pieces, "mlp", slices, m)
        row_grad, more = finish(1, low_sum)
        vectors = vectors + more
        row_grad, pieces, weights_got, vectors = tie(row_grad, pieces, weights_got, vectors)
        last = gather_step([row_grad[None]], "mlp", slices, mlp_masks[-1])
    else:
        last, pieces = pieces, []
    vectors = small_sum(vectors, n, slices)
    weights = cube_add(weights, weights_got, seq_masks, BF16)
    weights_got = cube_send(weights, "seq", n, seq_masks[1:])
    last, vectors, weights_got = tie(last, vectors, weights_got)
    for m in reversed(mlp_masks[:-1]):
        last = gather_step(last, "mlp", slices, m)
    pieces += last
    where = [(0, 0)]
    lookup = [0]
    for i, m in enumerate(reversed(mlp_masks)):
        where += [(i + 1, j) for j in range(len(lookup))]
        lookup += [k ^ m for k in lookup]
    per_piece = [where[lookup.index(k)] for k in range(slices)]
    block = math.gcd(share, shard)
    tokens_grad = pl.pallas_call(
        functools.partial(
            place_kernel, block, share, shard, slices, chunks, per_piece
        ),
        grid_spec=pltpu.PrefetchScalarGridSpec(
            num_scalar_prefetch=1,
            grid=(1,),
            in_specs=[pl.BlockSpec(memory_space=pl.ANY)] * len(pieces),
            out_specs=pl.BlockSpec(memory_space=pl.ANY),
            scratch_shapes=[
                pltpu.VMEM((rows // block, block, width), BF16),
                pltpu.SemaphoreType.DMA((rows // block,)),
                pltpu.SemaphoreType.DMA((rows // block,)),
            ],
        ),
        out_shape=jax.ShapeDtypeStruct((packs + spare, shard, width), BF16),
        compiler_params=params(),
        name="place",
    )(jnp.concatenate([pack_at, column.astype(jnp.int32).reshape(1)]), *pieces)[:packs]

    for step in range(1, len(seq_masks)):
        weights = cube_add(
            weights, weights_got, seq_masks[step:], F32 if step == len(seq_masks) - 1 else BF16
        )
        if step < len(seq_masks) - 1:
            weights_got = cube_send(weights, "seq", n, seq_masks[step + 1 :])
    weights = weights[0]
    head_grad = jnp.transpose(
        weights[: 3 * joined].reshape(3, joined, width // n), (0, 2, 1)
    )
    merge_grad = weights[3 * joined :]
    part, hidden_here = width // n, up_weight.shape[1]
    up_grad, down_grad = terms[:part, :hidden_here], terms[:part, hidden_here:].T
    up_bias_grad = terms[part, : hidden_here // n]
    down_bias_grad = terms[part, hidden_here // n : hidden_here // n + part]
    return (
        result,
        tokens_grad,
        vectors[0],
        vectors[1],
        head_grad,
        merge_grad,
        up_grad,
        up_bias_grad,
        down_grad,
        down_bias_grad,
    )


def qkv_kernel(heads, me_ref, x_ref, w_ref, cos_ref, sin_ref, normed_ref, out_ref):
    width = heads * HD
    normed = x_ref[0]
    normed_ref[...] = normed
    for j in range(3):
        part = dot(w_ref[j * width : (j + 1) * width, :], normed, ((1,), (1,)))
        if j < 2:
            part = turn(part, cos_ref[...], sin_ref[...], heads)
        if j == 0:
            part = part * (1.0 / math.sqrt(HD))
        part = part.astype(BF16)
        for h in range(heads):
            out_ref[h, j] = part[h * HD : (h + 1) * HD]


def allowed_of(block, first, i):
    rows = lax.broadcasted_iota(jnp.int32, (block, block), 0)
    cols = lax.broadcasted_iota(jnp.int32, (block, block), 1)
    ahead = rows - cols
    return lambda j: (rows >= first - j * block) & (ahead <= (i - j) * block)


def unit_kernel(n, block, me_ref, low_ref, first_ref, qkv_ref, out_ref, keep_ref, logsum_ref, qt, vt, kn):
    me = me_ref[0]
    pair = range(qkv_ref.shape[0])
    for u in pair:
        for i in range(n):
            at = slice(i * block, (i + 1) * block)
            qt[u, i] = qkv_ref[u, 0, :, at]
            kn[u, i] = qkv_ref[u, 1, :, at].T
            vt[u, i] = qkv_ref[u, 2, :, at]

    def outer(i, carry):
        allowed = allowed_of(block, first_ref[pl.ds(i, 1), :], i)
        j0 = low_ref[i]

        def forward(t, states):
            j = j0 + 2 * t
            at = jnp.minimum(j + 1, n - 1)
            mask0, mask1 = allowed(j), allowed(j + 1)
            out = []
            for u, (top, total, acc) in zip(pair, states):
                q_t = qt[u, i]
                s0 = jnp.where(mask0, dot(kn[u, j], q_t), NEG)
                s1 = jnp.where(mask1, dot(kn[u, at], q_t), NEG)
                peak = jnp.max(jnp.maximum(s0, s1), axis=0, keepdims=True)
                new_top = jnp.maximum(top, peak)
                p0, p1 = jnp.exp(s0 - new_top), jnp.exp(s1 - new_top)
                fade = jnp.exp(top - new_top)
                total = total * fade + jnp.sum(p0 + p1, axis=0, keepdims=True)
                acc = acc * fade + dot(vt[u, j], p0.astype(BF16)) + dot(vt[u, at], p1.astype(BF16))
                out.append((new_top, total, acc))
            return tuple(out)

        states = lax.fori_loop(
            0,
            (i - j0) // 2 + 1,
            forward,
            tuple(
                (
                    jnp.full((1, block), NEG, F32),
                    jnp.zeros((1, block), F32),
                    jnp.zeros((HD, block), F32),
                )
                for _ in pair
            ),
        )
        for u, (top, total, acc) in zip(pair, states):
            keep_ref[u, i] = (acc / total).astype(BF16)
            logsum_ref[u, pl.ds(i, 1), :] = top + jnp.log(total)
        return carry

    lax.fori_loop(0, n, outer, 0)
    for k in range(n):
        for u in pair:
            out_ref[k, u] = keep_ref[u, lax.bitwise_xor(jnp.int32(k), me)]


def unit_back_kernel(
    n, block, me_ref, low_ref, first_ref, keep_ref, logsum_ref, qkv_ref, grad_ref, out_ref,
    qt, kt, gt, qn, kn, vn, gn, dk, dv, dqs
):
    me = me_ref[0]
    pair = range(qkv_ref.shape[0])
    for u in pair:
        for i in range(n):
            at = slice(i * block, (i + 1) * block)
            for j, (t_ref, n_ref) in enumerate(((qt, qn), (kt, kn), (None, vn))):
                part = qkv_ref[u, j, :, at]
                if t_ref is not None:
                    t_ref[u, i] = part
                n_ref[u, i] = part.T
        for k in range(n):
            d = lax.bitwise_xor(jnp.int32(k), me)
            part = grad_ref[k, u]
            gt[u, d] = part
            gn[u, d] = part.T
    dk[...] = jnp.zeros_like(dk)
    dv[...] = jnp.zeros_like(dv)

    def outer(i, carry):
        allowed = allowed_of(block, first_ref[pl.ds(i, 1), :], i)
        j0 = low_ref[i]
        inner = [
            jnp.sum(keep_ref[u, i].astype(F32) * gt[u, i].astype(F32), axis=0, keepdims=True)
            for u in pair
        ]
        logsum = [logsum_ref[u, pl.ds(i, 1), :] for u in pair]

        def one(u, mask, at):
            s = jnp.where(mask, dot(kn[u, at], qt[u, i]), NEG)
            p = jnp.exp(s - logsum[u])
            ds = (p * (dot(vn[u, at], gt[u, i]) - inner[u])).astype(BF16)
            return dot(ds, qn[u, i]), dot(p.astype(BF16), gn[u, i]), dot(kt[u, at], ds)

        def backward(t, dqs):
            j = j0 + 2 * t
            at = jnp.minimum(j + 1, n - 1)
            mask0, mask1 = allowed(j), allowed(j + 1)
            out = []
            for u, dq in zip(pair, dqs):
                dk0, dv0, dq0 = one(u, mask0, j)
                dk1, dv1, dq1 = one(u, mask1, at)
                dk[u, j] += dk0
                dv[u, j] += dv0
                dk[u, at] += dk1
                dv[u, at] += dv1
                out.append(dq + dq0 + dq1)
            return tuple(out)

        dq = lax.fori_loop(
            0, (i - j0) // 2 + 1, backward, tuple(jnp.zeros((HD, block), F32) for _ in pair)
        )
        for u in pair:
            dqs[u, i] = (dq[u] * (1.0 / math.sqrt(HD))).astype(BF16)
        return carry

    lax.fori_loop(0, n, outer, 0)
    for u in pair:
        for i in range(n):
            at = slice(i * block, (i + 1) * block)
            out_ref[u, 0, :, at] = dqs[u, i]
            out_ref[u, 1, :, at] = dk[u, i].T.astype(BF16)
            out_ref[u, 2, :, at] = dv[u, i].T.astype(BF16)


def rows_kernel(heads, slices, me_ref, grad_ref, normed_ref, w_ref, cos_ref, sin_ref, low_ref, weight_ref):
    width = heads * HD
    column = me_ref[1]

    @pl.when(pl.program_id(0) == 0)
    def _():
        weight_ref[...] = jnp.zeros_like(weight_ref)

    parts = []
    for j in range(3):
        part = jnp.concatenate([grad_ref[h, j] for h in range(heads)], axis=0)
        if j < 2:
            part = turn(part.astype(F32), cos_ref[...], -sin_ref[...], heads).astype(BF16)
        parts.append(part)
    grads = jnp.concatenate(parts, axis=0)
    weight_ref[...] += dot(grads, normed_ref[...])
    low = dot(grads.T, w_ref[...]).astype(BF16)
    part = low.shape[0] // slices
    for m in range(slices):
        low_ref[lax.bitwise_xor(jnp.int32(m), column), 0] = low[m * part : (m + 1) * part]


def norm_kernel(x_ref, gain_ref, bias_ref, normed_ref):
    x = x_ref[0].astype(F32)
    cent = x - jnp.mean(x, axis=-1, keepdims=True)
    var = jnp.mean(cent * cent, axis=-1, keepdims=True)
    normed_ref[0] = (cent * lax.rsqrt(var + EPS) * gain_ref[...] + bias_ref[...]).astype(BF16)


def finish_kernel(terms, which_ref, *refs):
    lows = refs[:terms]
    low_ref, x_ref, c_ref, gain_ref, out_ref, sums_ref = refs[terms:]

    @pl.when(pl.program_id(0) == 0)
    def _():
        sums_ref[...] = jnp.zeros_like(sums_ref)

    low = low_ref[0].astype(F32)
    for ref in lows:
        low = low + ref[0].astype(F32)
    x = x_ref[0].astype(F32)
    cent = x - jnp.mean(x, axis=-1, keepdims=True)
    inverse = lax.rsqrt(jnp.mean(cent * cent, axis=-1, keepdims=True) + EPS)
    xhat = cent * inverse
    g = low * gain_ref[...]
    inner = jnp.mean(g * xhat, axis=-1, keepdims=True)
    back = (g - jnp.mean(g, axis=-1, keepdims=True) - xhat * inner) * inverse
    out_ref[0] = (c_ref[0].astype(F32) + back).astype(BF16)
    sums_ref[0:1] += jnp.sum(low * xhat, axis=0, keepdims=True)
    sums_ref[1:2] += jnp.sum(low, axis=0, keepdims=True)


def join_kernel(slices, attended_ref, c_ref, merge_ref, branch_ref, out_branch, out_weight):
    @pl.when(pl.program_id(0) == 0)
    def _():
        out_weight[...] = jnp.zeros_like(out_weight)

    attended = attended_ref[0]
    out_weight[...] += dot(attended, c_ref[0])
    branch = dot(attended.T, merge_ref[...]) + branch_ref[0].astype(F32)
    cols = branch.shape[1] // slices
    for m in range(slices):
        out_branch[m, 0] = branch[:, m * cols : (m + 1) * cols].astype(BF16)


def settle_kernel(counts, slices, sub, per_piece, table_ref, *refs):
    pieces, out, buf, sems, out_sems = refs[:-4], refs[-4], refs[-3], refs[-2], refs[-1]
    column = table_ref[sum(counts)]
    loads, stores = [], []
    arrays = max(ref for ref, _ in per_piece) + 1
    first = 0
    for c, count in enumerate(counts):
        for k in range(slices):
            ref, where = per_piece[k]
            start = pl.multiple_of(lax.bitwise_xor(jnp.int32(k), column) * sub, sub)
            for t in range(count):
                at = len(loads)
                loads.append(
                    pltpu.make_async_copy(
                        pieces[c * arrays + ref].at[where, t], buf.at[at], sems.at[at]
                    )
                )
                stores.append(
                    pltpu.make_async_copy(
                        buf.at[at],
                        out.at[table_ref[first + t], pl.ds(start, sub)],
                        out_sems.at[at],
                    )
                )
        first += count
    for copy in loads:
        copy.start()
    for load, store in zip(loads, stores):
        load.wait()
        store.start()
    for copy in stores:
        copy.wait()


def exchange_x(array):
    n = array.shape[0]
    return lax.ppermute(array[1::2], "seq", [(i, i ^ 1) for i in range(n)])


def exchange_z(array, got):
    n = array.shape[0]
    return [
        lax.ppermute(jnp.stack([array[k], got[k // 2]]), "seq", [(i, i ^ k) for i in range(n)])
        for k in range(2, n, 2)
    ]


def exchanged(array, got, gots):
    return jnp.concatenate([array[:1], got[:1], *gots], axis=0)


def take(array, index):
    return jnp.take(array, index, axis=0, mode="clip")


def on_device_pairs(
    tokens,
    lengths,
    counts,
    norm_gain,
    norm_bias,
    head_weight,
    merge_weight,
    up_weight,
    up_bias,
    down_weight,
    down_bias,
    cotangent,
):
    packs, shard, width = tokens.shape
    n = lax.axis_size("seq")
    slices = lax.axis_size("mlp")
    pack_len = shard * n
    rank = lax.axis_index("seq").astype(jnp.int32)
    column = lax.axis_index("mlp").astype(jnp.int32)
    heads = merge_weight.shape[0] // HD
    joined = heads * HD
    half = heads // 2
    cols = width // slices
    sub = shard // slices
    seq_masks, mlp_masks = masks_of(n), masks_of(slices)
    pairs = n // 2

    cot = lax.all_gather(cotangent, "mlp", axis=2, tiled=True)

    first, position, cost = layout(lengths, counts, pack_len)
    ids = jnp.arange(packs, dtype=jnp.int32)
    before = (cost[None, :] > cost[:, None]) | (
        (cost[None, :] == cost[:, None]) & (ids[None, :] < ids[:, None])
    )
    order = jnp.sum(before.astype(jnp.int32), axis=1)
    by_order = jnp.sum(
        jnp.where(order[None, :] == ids[:, None], ids[None, :], 0), axis=-1
    ).astype(jnp.int32)
    devices = jnp.arange(n, dtype=jnp.int32)
    shared_of = by_order[:pairs]
    own_of = by_order[pairs + 2 * (pairs - 1 - devices // 2) + devices % 2]
    late = order - pairs
    pair_of = jnp.where(late < 0, order, pairs - 1 - late // 2)
    device_of = 2 * pair_of + jnp.where(late < 0, 0, late % 2)
    dest = jnp.bitwise_xor(rank, devices)
    own_dest, shared_dest = own_of[dest], shared_of[dest // 2]
    me = jnp.stack([rank, column])

    token_cols = lax.dynamic_slice_in_dim(tokens, column * cols, cols, 2)
    head_ids = jnp.arange(heads, dtype=jnp.int32)
    half_ids = jnp.arange(half, dtype=jnp.int32)
    units_out = jnp.concatenate(
        [
            own_dest[:, None] * heads + head_ids[None, :],
            shared_dest[:, None] * heads + (dest % 2)[:, None] * half + half_ids[None, :],
        ],
        axis=1,
    ).reshape(-1)
    is_shared = (order < pairs)[:, None]
    holder = device_of[:, None] + jnp.where(is_shared, head_ids[None, :] // half, 0)
    units_in = (
        jnp.bitwise_xor(holder, rank) * (heads + half)
        + jnp.where(is_shared, heads + head_ids[None, :] % half, head_ids[None, :])
    ).reshape(-1)

    def tables(pack):
        freq = 10000.0 ** (-(2.0 * jnp.arange(ROT // 2, dtype=F32)) / ROT)
        angle = take(position, pack).astype(F32)[None, :] * jnp.repeat(freq, 2)[:, None]
        return jnp.cos(angle), jnp.sin(angle)

    w_heads = jnp.transpose(head_weight, (0, 2, 1)).reshape(3, heads, HD, width)
    w_own = w_heads.reshape(3 * joined, width)
    part_at = (rank % 2) * half
    w_shared = lax.dynamic_slice_in_dim(w_heads, part_at, half, 1).reshape(3 * half * HD, width)
    packs_here = (own_of[rank], shared_of[rank // 2])
    turns = [tables(p) for p in packs_here]
    firsts = [take(first, p).reshape(n, shard) for p in packs_here]
    lows = [(f[:, 0] // shard).astype(jnp.int32) for f in firsts]
    gain, bias = norm_gain.reshape(1, width), norm_bias.reshape(1, width)

    def whole2(s, *_):
        return (0, 0)

    def lane_at(s, *_):
        return (0, s)

    def project(rows, weight, cosine, sine):
        h = weight.shape[0] // (3 * HD)
        return pl.pallas_call(
            functools.partial(qkv_kernel, h),
            grid_spec=pltpu.PrefetchScalarGridSpec(
                num_scalar_prefetch=1,
                grid=(n,),
                in_specs=[
                    pl.BlockSpec(
                        (1, shard, width), lambda s, me: (lax.bitwise_xor(s, me[0]), 0, 0)
                    ),
                    pl.BlockSpec(weight.shape, whole2),
                    pl.BlockSpec((ROT, shard), lane_at),
                    pl.BlockSpec((ROT, shard), lane_at),
                ],
                out_specs=[
                    pl.BlockSpec((shard, width), lambda s, *_: (s, 0)),
                    pl.BlockSpec((h, 3, HD, shard), lambda s, *_: (0, 0, 0, s)),
                ],
            ),
            out_shape=[
                jax.ShapeDtypeStruct((pack_len, width), BF16),
                jax.ShapeDtypeStruct((h, 3, HD, pack_len), BF16),
            ],
            compiler_params=params(),
            cost_estimate=COST,
            name="project",
        )(me, rows, weight, cosine, sine)

    wide = [pltpu.VMEM((2, n, HD, shard), BF16)]
    tall = [pltpu.VMEM((2, n, shard, HD), BF16)]
    keep_spec = pl.BlockSpec((2, n, HD, shard), lambda u, *_: (u, 0, 0, 0))
    log_spec = pl.BlockSpec((2, n, shard), lambda u, *_: (u, 0, 0))
    unit_spec = pl.BlockSpec((2, 3, HD, pack_len), lambda u, *_: (u, 0, 0, 0))

    def attend(c, qkv):
        h = qkv.shape[0]
        return pl.pallas_call(
            functools.partial(unit_kernel, n, shard),
            grid_spec=pltpu.PrefetchScalarGridSpec(
                num_scalar_prefetch=2,
                grid=(h // 2,),
                in_specs=[pl.BlockSpec((n, shard), whole2), unit_spec],
                out_specs=[
                    pl.BlockSpec((n, 2, HD, shard), lambda u, *_: (0, u, 0, 0)),
                    keep_spec,
                    log_spec,
                ],
                scratch_shapes=wide * 2 + tall,
            ),
            out_shape=[
                jax.ShapeDtypeStruct((n, h, HD, shard), BF16),
                jax.ShapeDtypeStruct((h, n, HD, shard), BF16),
                jax.ShapeDtypeStruct((h, n, shard), F32),
            ],
            compiler_params=params(),
            cost_estimate=COST,
            name="attend",
        )(me, lows[c], firsts[c], qkv)

    def attend_back(c, kept, logsum, qkv, grads):
        h = qkv.shape[0]
        skip = c * heads // 2
        return pl.pallas_call(
            functools.partial(unit_back_kernel, n, shard),
            grid_spec=pltpu.PrefetchScalarGridSpec(
                num_scalar_prefetch=2,
                grid=(h // 2,),
                in_specs=[
                    pl.BlockSpec((n, shard), whole2),
                    keep_spec,
                    log_spec,
                    unit_spec,
                    pl.BlockSpec((n, 2, HD, shard), lambda u, *_: (0, u + skip, 0, 0)),
                ],
                out_specs=unit_spec,
                scratch_shapes=wide * 3
                + tall * 4
                + [pltpu.VMEM((2, n, shard, HD), F32)] * 2
                + [pltpu.VMEM((2, n, HD, shard), BF16)],
            ),
            out_shape=jax.ShapeDtypeStruct((h, 3, HD, pack_len), BF16),
            compiler_params=params(),
            cost_estimate=COST,
            name="attend_back",
        )(me, lows[c], firsts[c], kept, logsum, qkv, grads)

    def rows_back(grads, normed, weight, cosine, sine):
        h = grads.shape[0]
        return pl.pallas_call(
            functools.partial(rows_kernel, h, slices),
            grid_spec=pltpu.PrefetchScalarGridSpec(
                num_scalar_prefetch=1,
                grid=(n,),
                in_specs=[
                    pl.BlockSpec((h, 3, HD, shard), lambda s, *_: (0, 0, 0, s)),
                    pl.BlockSpec((shard, width), lambda s, *_: (s, 0)),
                    pl.BlockSpec(weight.shape, whole2),
                    pl.BlockSpec((ROT, shard), lane_at),
                    pl.BlockSpec((ROT, shard), lane_at),
                ],
                out_specs=[
                    pl.BlockSpec(
                        (slices, 1, sub, width),
                        lambda s, me: (0, lax.bitwise_xor(s, me[0]), 0, 0),
                    ),
                    pl.BlockSpec(weight.shape, whole2),
                ],
            ),
            out_shape=[
                jax.ShapeDtypeStruct((slices, n, sub, width), BF16),
                jax.ShapeDtypeStruct(weight.shape, F32),
            ],
            compiler_params=params(),
            cost_estimate=COST,
            name="rows_back",
        )(me, grads, normed, weight, cosine, sine)

    pack_spec = pl.BlockSpec((1, shard, width), lambda p: (p, 0, 0))
    normed_low = pl.pallas_call(
        norm_kernel,
        grid=(packs,),
        in_specs=[pack_spec, pl.BlockSpec((1, width), whole2), pl.BlockSpec((1, width), whole2)],
        out_specs=pack_spec,
        out_shape=jax.ShapeDtypeStruct((packs, shard, width), BF16),
        compiler_params=params(),
        cost_estimate=COST,
        name="norm",
    )(tokens, gain, bias)
    normed_cols = lax.dynamic_slice_in_dim(normed_low, column * cols, cols, 2)
    send_own = take(normed_cols, own_dest)
    send_shared = take(normed_cols, shared_dest)
    own_x = exchange_x(send_own)

    hidden = (
        jnp.einsum("psd,df->psf", normed_low, up_weight, preferred_element_type=F32) + up_bias
    )
    own_x, hidden, send_own, send_shared = tie(own_x, hidden, send_own, send_shared)

    own_z = exchange_z(send_own, own_x)
    shared_x = exchange_x(send_shared)
    active_low = jax.nn.gelu(hidden, approximate=True).astype(BF16)
    branch_ff = jnp.einsum(
        "psf,fd->psd", active_low, down_weight, preferred_element_type=F32
    ).astype(BF16)
    own_z, shared_x, branch_ff, send_own, own_x, merge_here, down_here = tie(
        own_z, shared_x, branch_ff, send_own, own_x, merge_weight, down_weight
    )
    rows_own = lax.all_gather(exchanged(send_own, own_x, own_z), "mlp", axis=2, tiled=True)

    shared_z = exchange_z(send_shared, shared_x)
    out_grad = jnp.einsum("hd,psd->phs", merge_here, cot, preferred_element_type=F32).astype(BF16)
    send_grad = take(out_grad.reshape(packs * heads, HD, shard), units_out).reshape(
        n, heads + half, HD, shard
    )
    active_grad = jnp.einsum("psd,fd->psf", cot, down_here, preferred_element_type=F32)
    _, gelu_back = jax.vjp(lambda values: jax.nn.gelu(values, approximate=True), hidden)
    hidden_grad = gelu_back(active_grad)[0].astype(BF16)
    shared_z, send_grad, hidden_grad, send_shared, shared_x = tie(
        shared_z, send_grad, hidden_grad, send_shared, shared_x
    )
    rows_shared = lax.all_gather(
        exchanged(send_shared, shared_x, shared_z), "mlp", axis=2, tiled=True
    )

    grad_x = exchange_x(send_grad)
    low_ff = jnp.einsum(
        "psf,df->psd", hidden_grad, up_weight, preferred_element_type=F32
    ).astype(BF16)
    up_grad = jnp.einsum(
        "psd,psf->df", normed_low, hidden_grad, preferred_element_type=F32
    ).astype(BF16)
    grad_x, send_grad, low_ff, up_grad, rows_own, hidden_grad = tie(
        grad_x, send_grad, low_ff, up_grad, rows_own, hidden_grad
    )

    grad_z = exchange_z(send_grad, grad_x)
    normed_own, qkv_own = project(rows_own, w_own, *turns[0])
    down_grad = jnp.einsum("psd,psf->df", cot, active_low, preferred_element_type=F32).astype(BF16)
    biases = jnp.sum(hidden_grad.astype(F32), axis=(0, 1)), jnp.sum(cot.astype(F32), axis=(0, 1))
    out_own, kept_own, log_own = attend(0, qkv_own)
    grad_z, out_own, kept_own, log_own, down_grad, biases, rows_shared, low_ff = tie(
        grad_z, out_own, kept_own, log_own, down_grad, biases, rows_shared, low_ff
    )
    grads = exchanged(send_grad, grad_x, grad_z)
    low_ff = lax.psum_scatter(
        jnp.transpose(low_ff.reshape(packs, slices, sub, width), (1, 0, 2, 3)).reshape(
            slices * packs * sub, width
        ),
        "mlp",
        scatter_dimension=0,
        tiled=True,
    ).reshape(packs, sub, width)

    def with_row(*parts):
        weight = jnp.concatenate(parts[:2], axis=1)
        row = jnp.concatenate(parts[2:])
        row = jnp.pad(row, (0, weight.shape[1] - row.shape[0])).reshape(1, -1)
        row = jnp.broadcast_to(row, (16, weight.shape[1])).astype(BF16)
        return jnp.concatenate([weight, row], axis=0)

    terms = dict(
        enumerate(
            with_row(*parts)
            for parts in zip(*[cut(v, 0, n, rank) for v in (up_grad, down_grad, *biases)])
        )
    )
    terms_got = cube_send(terms, "seq", n, seq_masks)
    normed_shared, qkv_shared = project(rows_shared, w_shared, *turns[1])
    out_shared, kept_shared, log_shared = attend(1, qkv_shared)
    out_shared, kept_shared, log_shared, grads = tie(out_shared, kept_shared, log_shared, grads)

    send_out = jnp.concatenate([out_own, out_shared], axis=1)
    out_x = exchange_x(send_out)
    back_own = attend_back(0, kept_own, log_own, qkv_own, grads)
    out_x, back_own, terms_got, send_out = tie(out_x, back_own, terms_got, send_out)

    terms = cube_add(terms, terms_got, seq_masks, BF16)
    terms_got = cube_send(terms, "seq", n, seq_masks[1:])
    out_z = exchange_z(send_out, out_x)
    low_own, head_own = rows_back(back_own, normed_own, w_own, *turns[0])
    back_shared = attend_back(1, kept_shared, log_shared, qkv_shared, grads)
    out_z, terms_got, low_own, back_shared, send_out, out_x = tie(
        out_z, terms_got, low_own, back_shared, send_out, out_x
    )

    low_own = cube_sum([low_own[k] for k in range(slices)], "mlp", mlp_masks, BF16).astype(BF16)
    for step in range(1, len(seq_masks)):
        last_step = step == len(seq_masks) - 1
        terms = cube_add(terms, terms_got, seq_masks[step:], F32 if last_step else BF16)
        if not last_step:
            terms_got = cube_send(terms, "seq", n, seq_masks[step + 1 :])
    terms = terms[0]
    low_shared, head_shared = rows_back(back_shared, normed_shared, w_shared, *turns[1])
    attended = take(
        exchanged(send_out, out_x, out_z).reshape(n * (heads + half), HD, shard), units_in
    ).reshape(packs, joined, shard)
    branch, merge_part = pl.pallas_call(
        functools.partial(join_kernel, slices),
        grid=(packs,),
        in_specs=[
            pl.BlockSpec((1, joined, shard), lambda p: (p, 0, 0)),
            pl.BlockSpec((1, shard, width), lambda p: (p, 0, 0)),
            pl.BlockSpec((joined, width), whole2),
            pl.BlockSpec((1, shard, width), lambda p: (p, 0, 0)),
        ],
        out_specs=[
            pl.BlockSpec((slices, 1, shard, cols), lambda p: (0, p, 0, 0)),
            pl.BlockSpec((joined, width), whole2),
        ],
        out_shape=[
            jax.ShapeDtypeStruct((slices, packs, shard, cols), BF16),
            jax.ShapeDtypeStruct((joined, width), F32),
        ],
        compiler_params=params(),
        cost_estimate=COST,
        name="join",
    )(attended, cot, merge_weight, branch_ff)
    low_shared, low_own, branch, terms, low_ff, head_shared = tie(
        low_shared, low_own, branch, terms, low_ff, head_shared
    )

    low_own_x = exchange_x(low_own)
    low_shared = cube_sum(
        [low_shared[k] for k in range(slices)], "mlp", mlp_masks, BF16
    ).astype(BF16)
    head_all = head_own.reshape(3, heads, HD, width)
    there = lax.dynamic_slice_in_dim(head_all, part_at, half, 1)
    head_all = lax.dynamic_update_slice_in_dim(
        head_all, there + head_shared.reshape(3, half, HD, width), part_at, 1
    ).reshape(3 * joined, width)
    weights = jnp.concatenate([head_all, merge_part], axis=0).astype(BF16)
    weights = dict(enumerate(cut(weights, 1, n, rank)))
    low_own_x, low_shared, low_own, weights, branch = tie(
        low_own_x, low_shared, low_own, weights, branch
    )
    summed = lax.psum_scatter(branch, "mlp", scatter_dimension=0, tiled=False)

    low_own_z = exchange_z(low_own, low_own_x)
    low_shared_x = exchange_x(low_shared)
    low_own_z, low_shared_x, low_shared = tie(low_own_z, low_shared_x, low_shared)

    def finish(lows, index, which):
        count = which.shape[0]
        row_spec = pl.BlockSpec((1, sub, width), lambda t, at: (at[count + t], at[0], 0))

        def part(i):
            return pl.BlockSpec(
                (1, sub, width), lambda t, at: (at[(2 + i) * count + t], 0, 0)
            )

        table = [jnp.full((count,), column), which, *index]
        return pl.pallas_call(
            functools.partial(finish_kernel, len(lows)),
            grid_spec=pltpu.PrefetchScalarGridSpec(
                num_scalar_prefetch=1,
                grid=(count,),
                in_specs=[part(i) for i in range(len(lows))]
                + [
                    pl.BlockSpec((1, sub, width), lambda t, at: (at[count + t], 0, 0)),
                    row_spec,
                    row_spec,
                    pl.BlockSpec((1, width), whole2),
                ],
                out_specs=[
                    pl.BlockSpec((1, sub, width), lambda t, *_: (t, 0, 0)),
                    pl.BlockSpec((2, width), whole2),
                ],
            ),
            out_shape=[
                jax.ShapeDtypeStruct((count, sub, width), BF16),
                jax.ShapeDtypeStruct((2, width), F32),
            ],
            compiler_params=params(),
            cost_estimate=COST,
            name="finish",
        )(jnp.concatenate(table), *lows, low_ff, tokens, cot, gain)

    low_shared_z = exchange_z(low_shared, low_shared_x)
    row_own, sums_own = finish(
        [exchanged(low_own, low_own_x, low_own_z)], [devices], own_dest
    )
    pieces = gather_step([row_own[None]], "mlp", slices, mlp_masks[-1])
    weights_got = cube_send(weights, "seq", n, seq_masks)
    low_shared_z, pieces, weights, weights_got = tie(low_shared_z, pieces, weights, weights_got)

    weights = cube_add(weights, weights_got, seq_masks, BF16)
    weights_got = cube_send(weights, "seq", n, seq_masks[1:])
    for m in reversed(mlp_masks[:-1]):
        pieces = gather_step(pieces, "mlp", slices, m)
    both = exchanged(low_shared, low_shared_x, low_shared_z)
    even = jnp.bitwise_xor(2 * jnp.arange(pairs, dtype=jnp.int32), rank)
    row_shared, sums = finish([both, both], [even, jnp.bitwise_xor(even, 1)], shared_of)
    last = gather_step([row_shared[None]], "mlp", slices, mlp_masks[-1])
    vectors = small_sum(sums_own + sums, n, slices)
    result = (
        token_cols.astype(F32)
        + summed.astype(F32)
        + lax.dynamic_slice_in_dim(down_bias, column * cols, cols, 0)
    ).astype(BF16)
    last, pieces, vectors, weights_got, result = tie(last, pieces, vectors, weights_got, result)

    for m in reversed(mlp_masks[:-1]):
        last = gather_step(last, "mlp", slices, m)
    pieces += last
    for step in range(1, len(seq_masks)):
        weights = cube_add(
            weights, weights_got, seq_masks[step:], F32 if step == len(seq_masks) - 1 else BF16
        )
        if step < len(seq_masks) - 1:
            weights_got = cube_send(weights, "seq", n, seq_masks[step + 1 :])
    weights = weights[0]
    where = [(0, 0)]
    lookup = [0]
    for i, m in enumerate(reversed(mlp_masks)):
        where += [(i + 1, j) for j in range(len(lookup))]
        lookup += [k ^ m for k in lookup]
    per_piece = [where[lookup.index(k)] for k in range(slices)]
    tokens_grad = pl.pallas_call(
        functools.partial(settle_kernel, (n, pairs), slices, sub, per_piece),
        grid_spec=pltpu.PrefetchScalarGridSpec(
            num_scalar_prefetch=1,
            grid=(1,),
            in_specs=[pl.BlockSpec(memory_space=pl.ANY)] * len(pieces),
            out_specs=pl.BlockSpec(memory_space=pl.ANY),
            scratch_shapes=[
                pltpu.VMEM((packs * slices, sub, width), BF16),
                pltpu.SemaphoreType.DMA((packs * slices,)),
                pltpu.SemaphoreType.DMA((packs * slices,)),
            ],
        ),
        out_shape=jax.ShapeDtypeStruct((packs, shard, width), BF16),
        compiler_params=params(),
        name="settle",
    )(jnp.concatenate([own_dest, shared_of, column.reshape(1)]), *pieces)

    part, hidden_here = width // n, up_weight.shape[1]
    return (
        result,
        tokens_grad,
        vectors[0],
        vectors[1],
        jnp.transpose(weights[: 3 * joined].reshape(3, joined, part), (0, 2, 1)),
        weights[3 * joined :],
        terms[:part, :hidden_here],
        terms[part, : hidden_here // n],
        terms[:part, hidden_here:].T,
        terms[part, hidden_here // n : hidden_here // n + part],
    )


def solution(mesh):
    in_specs = (
        P(None, "seq", None),
        P(),
        P(),
        P(),
        P(),
        P(None, None, "mlp"),
        P("mlp", None),
        P(None, "mlp"),
        P("mlp"),
        P("mlp", None),
        P(),
        P(None, "seq", "mlp"),
    )
    out_specs = (
        P(None, "seq", "mlp"),
        P(None, "seq", None),
        P("seq"),
        P("seq"),
        P(None, "seq", "mlp"),
        P("mlp", "seq"),
        P("seq", "mlp"),
        P(("mlp", "seq")),
        P("mlp", "seq"),
        P("seq"),
    )
    n, slices = mesh.shape["seq"], mesh.shape["mlp"]

    def plan(*args):
        packs, pack_len, _ = args[0].shape
        heads = args[6].shape[0] // HD // slices
        pairs = (
            2 * packs == 3 * n
            and n >= 4
            and heads % 4 == 0
            and (pack_len // n) % 128 == 0
            and (pack_len // n) % (16 * slices) == 0
        )
        return jax.shard_map(
            on_device_pairs if pairs else on_device,
            mesh=mesh,
            in_specs=in_specs,
            out_specs=out_specs,
            check_vma=False,
        )(*args)

    return plan
```

```python
import functools
import math

import jax
import jax.numpy as jnp
from jax import lax
from jax.experimental import pallas as pl
from jax.experimental.pallas import tpu as pltpu
from jax.sharding import PartitionSpec as P

HD = 64
ROT = 32
EPS = 1e-05
NEG = -1e30
BF16 = jnp.bfloat16
F32 = jnp.float32
VMEM_LIMIT = 56 * 1024 * 1024
COST = pl.CostEstimate(flops=1 << 20, bytes_accessed=1 << 20, transcendentals=0)


def dot(a, b, dims=((1,), (0,))):
    return lax.dot_general(a, b, (dims, ((), ())), preferred_element_type=F32)


def layout(lengths, counts, pack_len):
    slots = lengths.shape[-1]
    slot_ids = jnp.arange(slots, dtype=jnp.int32)
    used = slot_ids[None, :] < counts[:, None]
    sizes = jnp.where(used, lengths, 0)
    ends = jnp.cumsum(sizes, axis=-1)
    starts = ends - sizes
    filled = ends[:, -1:]
    place = jnp.arange(pack_len, dtype=jnp.int32)[None, :]
    begin = jnp.max(
        jnp.where(used[:, None, :] & (place[:, :, None] >= starts[:, None, :]), starts[:, None, :], 0),
        axis=-1,
    )
    inside = place < filled
    first = jnp.where(inside, begin, place)
    position = jnp.where(inside, place - begin, place - filled)
    cost = jnp.sum(sizes * sizes, axis=-1)
    return first, position, cost


def turn(values, cosine, sine, heads):
    out = []
    parity = lax.broadcasted_iota(jnp.int32, cosine.shape, 0) % 2
    for h in range(heads):
        part = values[h * HD : h * HD + ROT]
        ahead = jnp.concatenate([part[1:], part[:1]], axis=0)
        behind = jnp.concatenate([part[-1:], part[:-1]], axis=0)
        swapped = jnp.where(parity == 0, -ahead, behind)
        out.append(part * cosine + swapped * sine)
        out.append(values[h * HD + ROT : (h + 1) * HD])
    return jnp.concatenate(out, axis=0)


def head_kernel(n, heads, per, me_ref, pack_ref, x_ref, gain_ref, bias_ref, w_ref, cos_ref, sin_ref, *refs):
    normed_ref, copy_ref, outs, scr = refs[0], refs[1], refs[2:-1], refs[-1]
    s_id, g = pl.program_id(0), pl.program_id(1)
    me = me_ref[0]
    width = heads * HD
    copy_ref[0] = x_ref[0]
    x = x_ref[0].astype(F32)
    cent = x - jnp.mean(x, axis=-1, keepdims=True)
    var = jnp.mean(cent * cent, axis=-1, keepdims=True)
    normed = (cent * lax.rsqrt(var + EPS) * gain_ref[...] + bias_ref[...]).astype(BF16)
    normed_ref[0] = normed
    for j in range(3):
        part = dot(w_ref[j * width : (j + 1) * width, :], normed, ((1,), (1,)))
        if j < 2:
            part = turn(part, cos_ref[0], sin_ref[0], heads)
        if j == 0:
            part = part * (1.0 / math.sqrt(HD))
        part = part.astype(BF16)
        for h in range(heads):
            scr[h, j] = part[h * HD : (h + 1) * HD]
    for at, out in enumerate(outs):
        d = lax.bitwise_xor(jnp.int32(at % n), me)

        @pl.when((d // heads == g) & (s_id // per == at // n))
        def _():
            out[0] = scr[d % heads]


def grad_kernel(n, heads, me_ref, c_ref, w_ref, *refs):
    outs, scr = refs[:n], refs[n]
    g = pl.program_id(1)
    me = me_ref[0]
    part = dot(w_ref[...], c_ref[0], ((1,), (1,))).astype(BF16)
    for h in range(heads):
        scr[h] = part[h * HD : (h + 1) * HD]
    for k in range(n):
        d = lax.bitwise_xor(jnp.int32(k), me)

        @pl.when(d // heads == g)
        def _():
            outs[k][0] = scr[d % heads]


def load_parts(n, me, pairs):
    for k in range(n):
        d = lax.bitwise_xor(jnp.int32(k), me)
        for part, t_ref, n_ref in pairs(k):
            if t_ref is not None:
                t_ref[d] = part
            if n_ref is not None:
                n_ref[d] = part.T


def score_of(block, first, i, kn, q_t):
    rows = lax.broadcasted_iota(jnp.int32, (block, block), 0)
    cols = lax.broadcasted_iota(jnp.int32, (block, block), 1)
    ahead = rows - cols

    def scores(j, at):
        s = dot(kn[at], q_t)
        allowed = (rows >= first - j * block) & (ahead <= (i - j) * block)
        return jnp.where(allowed, s, NEG)

    return scores


def attend_kernel(n, block, skip, me_ref, pack_ref, low_ref, first_ref, *refs):
    qkv, outs, keep_ref, logsum_ref = refs[:n], refs[n : 2 * n], refs[2 * n], refs[2 * n + 1]
    qt, vt, kn = refs[2 * n + 2 :]
    s_id = pl.program_id(0) + skip
    me = me_ref[0]
    load_parts(
        n,
        me,
        lambda k: (
            (qkv[k][0, 0, 0], qt, None),
            (qkv[k][0, 0, 1], None, kn),
            (qkv[k][0, 0, 2], vt, None),
        ),
    )

    def outer(i, carry):
        scores = score_of(block, first_ref[0, pl.ds(i, 1), :], i, kn, qt[i])
        j0 = low_ref[s_id, i]

        def forward(t, state):
            top, total, acc = state
            j = j0 + 2 * t
            at = jnp.minimum(j + 1, n - 1)
            s0, s1 = scores(j, j), scores(j + 1, at)
            peak = jnp.max(jnp.maximum(s0, s1), axis=0, keepdims=True)
            new_top = jnp.maximum(top, peak)
            p0, p1 = jnp.exp(s0 - new_top), jnp.exp(s1 - new_top)
            fade = jnp.exp(top - new_top)
            total = total * fade + jnp.sum(p0 + p1, axis=0, keepdims=True)
            acc = acc * fade + dot(vt[j], p0.astype(BF16)) + dot(vt[at], p1.astype(BF16))
            return new_top, total, acc

        top, total, acc = lax.fori_loop(
            0,
            (i - j0) // 2 + 1,
            forward,
            (
                jnp.full((1, block), NEG, F32),
                jnp.zeros((1, block), F32),
                jnp.zeros((HD, block), F32),
            ),
        )
        keep_ref[0, i] = (acc / total).astype(BF16)
        logsum_ref[0, pl.ds(i, 1), :] = top + jnp.log(total)
        return carry

    lax.fori_loop(0, n, outer, 0)
    for k in range(n):
        outs[k][0] = keep_ref[0, lax.bitwise_xor(jnp.int32(k), me)]


def attend_back_kernel(n, block, skip, me_ref, pack_ref, low_ref, first_ref, *refs):
    keep_ref, logsum_ref = refs[:2]
    qkv, grads, outs = refs[2 : n + 2], refs[n + 2 : 2 * n + 2], refs[2 * n + 2 : 3 * n + 2]
    qt, kt, gt, qn, kn, vn, gn, dk, dv, res = refs[3 * n + 2 :]
    s_id = pl.program_id(0) + skip
    me = me_ref[0]
    load_parts(
        n,
        me,
        lambda k: (
            (qkv[k][0, 0, 0], qt, qn),
            (qkv[k][0, 0, 1], kt, kn),
            (qkv[k][0, 0, 2], None, vn),
            (grads[k][0, 0], gt, gn),
        ),
    )
    dk[...] = jnp.zeros_like(dk)
    dv[...] = jnp.zeros_like(dv)

    def outer(i, carry):
        q_t, g_t, q_n, g_n = qt[i], gt[i], qn[i], gn[i]
        scores = score_of(block, first_ref[0, pl.ds(i, 1), :], i, kn, q_t)
        j0 = low_ref[s_id, i]
        inner = jnp.sum(keep_ref[0, i].astype(F32) * g_t.astype(F32), axis=0, keepdims=True)
        logsum = logsum_ref[0, pl.ds(i, 1), :]

        def one(j, at):
            p = jnp.exp(scores(j, at) - logsum)
            ds = (p * (dot(vn[at], g_t) - inner)).astype(BF16)
            return ds, dot(ds, q_n), dot(p.astype(BF16), g_n), dot(kt[at], ds)

        def backward(t, dq):
            j = j0 + 2 * t
            at = jnp.minimum(j + 1, n - 1)
            _, dk0, dv0, dq0 = one(j, j)
            _, dk1, dv1, dq1 = one(j + 1, at)
            dk[j] += dk0
            dv[j] += dv0
            dk[at] += dk1
            dv[at] += dv1
            return dq + dq0 + dq1

        dq = lax.fori_loop(0, (i - j0) // 2 + 1, backward, jnp.zeros((HD, block), F32))
        res[i, 0] = (dq * (1.0 / math.sqrt(HD))).astype(BF16)
        return carry

    lax.fori_loop(0, n, outer, 0)
    for i in range(n):
        res[i, 1] = dk[i].T.astype(BF16)
        res[i, 2] = dv[i].T.astype(BF16)
    for k in range(n):
        outs[k][0] = res[lax.bitwise_xor(jnp.int32(k), me)]


def merge_kernel(n, heads, slices, me_ref, *refs):
    recv = refs[:n]
    c_ref, merge_ref, branch_ref, out_branch, out_weight, scr, acc = refs[n:]
    s_id, g = pl.program_id(0), pl.program_id(1)
    groups = pl.num_programs(1)
    me = me_ref[0]
    width = heads * HD

    @pl.when((s_id == 0) & (g == 0))
    def _():
        acc[...] = jnp.zeros_like(acc)

    for k in range(n):
        d = lax.bitwise_xor(jnp.int32(k), me)

        @pl.when(d // heads == g)
        def _():
            scr[d % heads] = recv[k][0, 0, 0]

    attended = scr[...].reshape(width, c_ref.shape[1])
    acc[...] += dot(attended, c_ref[0])
    branch = dot(attended.T, merge_ref[...]) + branch_ref[0].astype(F32)
    cols = branch.shape[1] // slices
    for m in range(slices):
        out_branch[m, 0] = branch[:, m * cols : (m + 1) * cols].astype(BF16)

    @pl.when((s_id == pl.num_programs(0) - 1) & (g == groups - 1))
    def _():
        out_weight[...] = acc[...].astype(BF16)


def close_kernel(n, heads, me_ref, *refs):
    recv = refs[:n]
    normed_ref, w_ref, cos_ref, sin_ref, low_ref, out_low, out_weight, scr, acc = refs[n:]
    s_id, g = pl.program_id(0), pl.program_id(1)
    groups = pl.num_programs(1)
    me = me_ref[0]
    width = heads * HD
    shard = normed_ref.shape[1]

    @pl.when((s_id == 0) & (g == 0))
    def _():
        acc[...] = jnp.zeros_like(acc)

    for k in range(n):
        d = lax.bitwise_xor(jnp.int32(k), me)

        @pl.when(d // heads == g)
        def _():
            for j in range(3):
                scr[j, d % heads] = recv[k][0, 0, j]

    parts = []
    for j in (0, 1):
        part = scr[j].reshape(width, shard).astype(F32)
        parts.append(turn(part, cos_ref[0], -sin_ref[0], heads).astype(BF16))
    parts.append(scr[2].reshape(width, shard))
    grads = jnp.concatenate(parts, axis=0)
    acc[...] += dot(grads, normed_ref[0])
    low = dot(grads.T, w_ref[...]) + low_ref[0].astype(F32)
    out_low[0] = low.astype(BF16)

    @pl.when((s_id == pl.num_programs(0) - 1) & (g == groups - 1))
    def _():
        out_weight[...] = acc[...]


def place_kernel(block, share, shard, slices, chunks, per_piece, pack_ref, *refs):
    pieces, out, buf, sems, out_sems = refs[:-4], refs[-4], refs[-3], refs[-2], refs[-1]
    me = pack_ref[chunks * slices * share // shard]
    loads, stores = [], []
    arrays = max(ref for ref, _ in per_piece) + 1
    for c in range(chunks):
        for k in range(slices):
            ref, where = per_piece[k]
            for t in range(share // block):
                at = len(loads)
                row = (c * slices + lax.bitwise_xor(jnp.int32(k), me)) * share + t * block
                start = pl.multiple_of(lax.rem(row, shard), block)
                loads.append(
                    pltpu.make_async_copy(
                        pieces[c * arrays + ref].at[where, pl.ds(t * block, block)],
                        buf.at[at],
                        sems.at[at],
                    )
                )
                stores.append(
                    pltpu.make_async_copy(
                        buf.at[at],
                        out.at[pack_ref[row // shard], pl.ds(start, block)],
                        out_sems.at[at],
                    )
                )
    for copy in loads:
        copy.start()
    for load, store in zip(loads, stores):
        load.wait()
        store.start()
    for copy in stores:
        copy.wait()


def small_kernel(n, slices, x_ref, out_ref, first, second, sems, sems2):
    rank, column = lax.axis_index("seq"), lax.axis_index("mlp")
    barrier = pltpu.get_barrier_semaphore()
    peers = [{"seq": lax.bitwise_xor(rank, k)} for k in range(1, n)]
    rows = [{"mlp": lax.bitwise_xor(column, k)} for k in range(1, slices)]
    for peer in peers + rows:
        pl.semaphore_signal(barrier, inc=1, device_id=peer, device_id_type=pl.DeviceIdType.MESH)
    pl.semaphore_wait(barrier, len(peers) + len(rows))

    def exchange(source, target, sems, peers):
        copies = [
            pltpu.make_async_remote_copy(
                src_ref=source(k),
                dst_ref=target.at[k],
                send_sem=sems.at[0, k],
                recv_sem=sems.at[1, k],
                device_id=peer,
                device_id_type=pl.DeviceIdType.MESH,
            )
            for k, peer in enumerate(peers)
        ]
        for copy in copies:
            copy.start()
        for copy in copies:
            copy.wait()

    exchange(lambda k: x_ref.at[lax.bitwise_xor(rank, k + 1)], first, sems, peers)
    total = x_ref[rank]
    for k in range(n - 1):
        total = total + first[k]
    second[slices - 1] = total
    second[slices] = total
    exchange(lambda k: second.at[slices], second, sems2, rows)
    parts = [
        second[jnp.where(column == c, slices - 1, lax.bitwise_xor(column, c) - 1)]
        for c in range(slices)
    ]
    out_ref[...] = functools.reduce(jnp.add, parts)


def small_sum(vectors, n, slices):
    count, width = vectors.shape
    x = jnp.transpose(vectors.reshape(count, n, width // n), (1, 0, 2))
    return pl.pallas_call(
        functools.partial(small_kernel, n, slices),
        out_shape=jax.ShapeDtypeStruct((count, width // n), F32),
        in_specs=[pl.BlockSpec(memory_space=pltpu.VMEM)],
        out_specs=pl.BlockSpec(memory_space=pltpu.VMEM),
        scratch_shapes=[
            pltpu.VMEM((n - 1, count, width // n), F32),
            pltpu.VMEM((slices + 1, count, width // n), F32),
            pltpu.SemaphoreType.DMA((2, n - 1)),
            pltpu.SemaphoreType.DMA((2, slices - 1)),
        ],
        compiler_params=pltpu.CompilerParams(collective_id=0, has_side_effects=True),
        cost_estimate=COST,
        name="small_sum",
    )(x)


def params():
    return pltpu.CompilerParams(vmem_limit_bytes=VMEM_LIMIT)


def tie(*values):
    return lax.optimization_barrier(values)


def send_x(parts):
    n = len(parts)
    sent = jnp.stack([parts[k] for k in range(1, n, 2)])
    return lax.ppermute(sent, "seq", [(i, i ^ 1) for i in range(n)])


def send_z(parts, got, steps=None):
    n = len(parts)
    return [
        lax.ppermute(
            jnp.stack([parts[k], got[k // 2]]), "seq", [(i, i ^ k) for i in range(n)]
        )
        for k in (range(2, n, 2) if steps is None else steps)
    ]


def received(parts, got, gots):
    out = [(parts[0][None], 0), (got, 0)]
    for array in gots:
        out += [(array, 0), (array, 1)]
    return out


def span(masks):
    out = [0]
    for m in masks:
        out += [v ^ m for v in out]
    return out


def cube_send(chunks, axis, n, masks):
    kept = span(masks[1:])
    sent = jnp.stack([chunks[k ^ masks[0]] for k in kept])
    return lax.ppermute(sent, axis, [(i, i ^ masks[0]) for i in range(n)])


def cube_add(chunks, got, masks, kind):
    return {
        k: (chunks[k].astype(F32) + got[at].astype(F32)).astype(kind)
        for at, k in enumerate(span(masks[1:]))
    }


def cube_sum(chunks, axis, masks, kind):
    n = len(chunks)
    chunks = {k: v.astype(kind) for k, v in enumerate(chunks)}
    for step in range(len(masks)):
        got = cube_send(chunks, axis, n, masks[step:])
        chunks = cube_add(chunks, got, masks[step:], F32 if step == len(masks) - 1 else kind)
    return chunks[0]


def gather_step(arrays, axis, n, m):
    sent = jnp.concatenate(arrays, axis=0) if len(arrays) > 1 else arrays[0]
    return arrays + [lax.ppermute(sent, axis, [(i, i ^ m) for i in range(n)])]


def masks_of(n):
    return [1 << b for b in range(n.bit_length() - 1)]


def turned(masks, by):
    by = by % len(masks)
    return masks[by:] + masks[:by]


def cut(array, axis, n, me):
    size = array.shape[axis] // n
    return [
        lax.dynamic_slice_in_dim(array, lax.bitwise_xor(jnp.int32(k), me) * size, size, axis)
        for k in range(n)
    ]


def on_device(
    tokens,
    lengths,
    counts,
    norm_gain,
    norm_bias,
    head_weight,
    merge_weight,
    up_weight,
    up_bias,
    down_weight,
    down_bias,
    cotangent,
):
    packs, shard, width = tokens.shape
    n = lax.axis_size("seq")
    slices = lax.axis_size("mlp")
    pack_len = shard * n
    rank = lax.axis_index("seq")
    column = lax.axis_index("mlp")
    heads = merge_weight.shape[0] // HD
    joined = heads * HD
    groups = n // heads
    slots = -(-packs // groups)
    dealt = groups * slots
    spare = 1 if dealt > packs else 0
    rows = dealt * shard
    chunks = 2 if slots % 2 == 0 else 1
    per = slots // chunks
    seq_masks, mlp_masks = masks_of(n), masks_of(slices)

    first, position, cost = layout(lengths, counts, pack_len)
    ids = jnp.arange(packs, dtype=jnp.int32)
    before = (cost[None, :] > cost[:, None]) | (
        (cost[None, :] == cost[:, None]) & (ids[None, :] < ids[:, None])
    )
    order = jnp.sum(before.astype(jnp.int32), axis=1)
    slot_of = order // groups
    group_of = jnp.where(slot_of % 2 == 0, order % groups, groups - 1 - order % groups)
    at = slot_of * groups + group_of
    hit = at[None, :] == jnp.arange(dealt, dtype=jnp.int32)[:, None]
    pack_at = jnp.where(
        jnp.any(hit, axis=-1), jnp.sum(jnp.where(hit, ids, 0), axis=-1), packs
    ).astype(jnp.int32)
    safe = jnp.minimum(pack_at, packs - 1)
    me = rank.astype(jnp.int32).reshape(1)

    own_cot = jnp.take(cotangent, safe, axis=0, mode="clip")
    if spare:
        own_cot = jnp.where((pack_at < packs)[:, None, None], own_cot, 0)
    cot = lax.all_gather(own_cot, "mlp", axis=2, tiled=True)

    half = ROT // 2
    freq = 10000.0 ** (-(2.0 * jnp.arange(half, dtype=F32)) / ROT)
    own_position = jnp.take(
        lax.dynamic_slice_in_dim(position, rank * shard, shard, 1), safe, axis=0, mode="clip"
    )
    angle = own_position.astype(F32)[:, None, :] * jnp.repeat(freq, 2)[None, :, None]
    cosine, sine = jnp.cos(angle), jnp.sin(angle)

    w_t = jnp.transpose(head_weight, (0, 2, 1)).reshape(3 * joined, width)

    def whole2(s, g, *_):
        return (0, 0)

    def rows_at(skip):
        return pl.BlockSpec((1, shard, width), lambda s, g, *_: ((s + skip) * groups + g, 0, 0))

    def table_at(skip):
        return pl.BlockSpec((1, ROT, shard), lambda s, g, *_: ((s + skip) * groups + g, 0, 0))

    parts = [jax.ShapeDtypeStruct((per, 3, HD, shard), BF16)] * n

    def chunk_at(c):
        return pl.BlockSpec(
            (1, 3, HD, shard), lambda s, g, *_: (jnp.clip(s - c * per, 0, per - 1), 0, 0, 0)
        )

    outs = pl.pallas_call(
        functools.partial(head_kernel, n, heads, per),
        grid_spec=pltpu.PrefetchScalarGridSpec(
            num_scalar_prefetch=2,
            grid=(slots, groups),
            in_specs=[
                pl.BlockSpec((1, shard, width), lambda s, g, a, b: (b[s * groups + g], 0, 0)),
                pl.BlockSpec((1, width), whole2),
                pl.BlockSpec((1, width), whole2),
                pl.BlockSpec((3 * joined, width), whole2),
                table_at(0),
                table_at(0),
            ],
            out_specs=[rows_at(0)] * 2 + [chunk_at(c) for c in range(chunks) for _ in range(n)],
            scratch_shapes=[pltpu.VMEM((heads, 3, HD, shard), BF16)],
        ),
        out_shape=[jax.ShapeDtypeStruct((dealt, shard, width), BF16)] * 2 + parts * chunks,
        compiler_params=params(),
        cost_estimate=COST,
        name="heads",
    )(
        me,
        safe,
        tokens,
        norm_gain.reshape(1, width),
        norm_bias.reshape(1, width),
        w_t,
        cosine,
        sine,
    )
    normed_low, tokens_dealt = outs[0], outs[1]
    qkv = [list(outs[2 + c * n : 2 + (c + 1) * n]) for c in range(chunks)]

    def out_grads(cot, merge_weight):
        return pl.pallas_call(
            functools.partial(grad_kernel, n, heads),
            grid_spec=pltpu.PrefetchScalarGridSpec(
                num_scalar_prefetch=1,
                grid=(slots, groups),
                in_specs=[rows_at(0), pl.BlockSpec((joined, width), whole2)],
                out_specs=[pl.BlockSpec((1, HD, shard), lambda s, g, *_: (s, 0, 0))] * n,
                scratch_shapes=[pltpu.VMEM((heads, HD, shard), BF16)],
            ),
            out_shape=[jax.ShapeDtypeStruct((slots, HD, shard), BF16)] * n,
            compiler_params=params(),
            cost_estimate=COST,
            name="out_grads",
        )(me, cot, merge_weight)

    mine = rank // heads + groups * jnp.arange(slots, dtype=jnp.int32)
    my_packs = jnp.take(safe, mine, mode="clip")
    first = first.reshape(packs, n, shard)
    lows = (jnp.take(first[:, :, 0], my_packs, axis=0, mode="clip") // shard).astype(jnp.int32)
    wide = [pltpu.VMEM((n, HD, shard), BF16)]
    tall = [pltpu.VMEM((n, shard, HD), BF16)]

    def first_at(skip):
        return pl.BlockSpec((1, n, shard), lambda s, a, b, c: (b[s + skip], 0, 0))

    def qkv_at(lead):
        return pl.BlockSpec((1, 1, 3, HD, shard), lambda s, *_: (lead, s, 0, 0, 0))

    def grad_at(lead, skip):
        return pl.BlockSpec((1, 1, HD, shard), lambda s, *_: (lead, s + skip, 0, 0))

    def attend(c, sources):
        return pl.pallas_call(
            functools.partial(attend_kernel, n, shard, c * per),
            grid_spec=pltpu.PrefetchScalarGridSpec(
                num_scalar_prefetch=3,
                grid=(per,),
                in_specs=[first_at(c * per)] + [qkv_at(lead) for _, lead in sources],
                out_specs=[pl.BlockSpec((1, HD, shard), lambda s, *_: (s, 0, 0))] * n
                + [
                    pl.BlockSpec((1, n, HD, shard), lambda s, *_: (s, 0, 0, 0)),
                    pl.BlockSpec((1, n, shard), lambda s, *_: (s, 0, 0)),
                ],
                scratch_shapes=wide * 2 + tall,
            ),
            out_shape=[jax.ShapeDtypeStruct((per, HD, shard), BF16)] * n
            + [
                jax.ShapeDtypeStruct((per, n, HD, shard), BF16),
                jax.ShapeDtypeStruct((per, n, shard), F32),
            ],
            compiler_params=params(),
            cost_estimate=COST,
            name="attend",
        )(me, my_packs, lows, first, *[array for array, _ in sources])

    def attend_back(c, kept, logsum, sources, grads):
        return pl.pallas_call(
            functools.partial(attend_back_kernel, n, shard, c * per),
            grid_spec=pltpu.PrefetchScalarGridSpec(
                num_scalar_prefetch=3,
                grid=(per,),
                in_specs=[
                    first_at(c * per),
                    pl.BlockSpec((1, n, HD, shard), lambda s, *_: (s, 0, 0, 0)),
                    pl.BlockSpec((1, n, shard), lambda s, *_: (s, 0, 0)),
                ]
                + [qkv_at(lead) for _, lead in sources]
                + [grad_at(lead, c * per) for _, lead in grads],
                out_specs=[pl.BlockSpec((1, 3, HD, shard), lambda s, *_: (s, 0, 0, 0))] * n,
                scratch_shapes=wide * 3
                + tall * 4
                + [pltpu.VMEM((n, shard, HD), F32)] * 2
                + [pltpu.VMEM((n, 3, HD, shard), BF16)],
            ),
            out_shape=parts,
            compiler_params=params(),
            cost_estimate=COST,
            name="attend_back",
        )(
            me,
            my_packs,
            lows,
            first,
            kept,
            logsum,
            *[array for array, _ in sources],
            *[array for array, _ in grads],
        )

    def merge(sources, branch_ff):
        return pl.pallas_call(
            functools.partial(merge_kernel, n, heads, slices),
            grid_spec=pltpu.PrefetchScalarGridSpec(
                num_scalar_prefetch=1,
                grid=(slots, groups),
                in_specs=[
                    pl.BlockSpec(
                        (1, 1, 1, HD, shard),
                        lambda s, g, *_, lead=lead: (lead, s // per, s % per, 0, 0),
                    )
                    for _, lead in sources
                ]
                + [rows_at(0), pl.BlockSpec((joined, width), whole2), rows_at(0)],
                out_specs=[
                    pl.BlockSpec(
                        (slices, 1, shard, width // slices),
                        lambda s, g, *_: (0, s * groups + g, 0, 0),
                    ),
                    pl.BlockSpec((joined, width), whole2),
                ],
                scratch_shapes=[
                    pltpu.VMEM((heads, HD, shard), BF16),
                    pltpu.VMEM((joined, width), F32),
                ],
            ),
            out_shape=[
                jax.ShapeDtypeStruct((slices, dealt, shard, width // slices), BF16),
                jax.ShapeDtypeStruct((joined, width), BF16),
            ],
            compiler_params=params(),
            cost_estimate=COST,
            name="merge",
        )(me, *[array for array, _ in sources], cot, merge_weight, branch_ff)

    def close(c, sources):
        skip = c * per
        return pl.pallas_call(
            functools.partial(close_kernel, n, heads),
            grid_spec=pltpu.PrefetchScalarGridSpec(
                num_scalar_prefetch=1,
                grid=(per, groups),
                in_specs=[
                    pl.BlockSpec(
                        (1, 1, 3, HD, shard), lambda s, g, *_, lead=lead: (lead, s, 0, 0, 0)
                    )
                    for _, lead in sources
                ]
                + [
                    rows_at(skip),
                    pl.BlockSpec((3 * joined, width), whole2),
                    table_at(skip),
                    table_at(skip),
                    rows_at(skip),
                ],
                out_specs=[rows_at(0), pl.BlockSpec((3 * joined, width), whole2)],
                scratch_shapes=[
                    pltpu.VMEM((3, heads, HD, shard), BF16),
                    pltpu.VMEM((3 * joined, width), F32),
                ],
            ),
            out_shape=[
                jax.ShapeDtypeStruct((per * groups, shard, width), BF16),
                jax.ShapeDtypeStruct((3 * joined, width), F32),
            ],
            compiler_params=params(),
            cost_estimate=COST,
            name="close",
        )(me, *[array for array, _ in sources], normed_low, w_t, cosine, sine, low_ff)

    got_x = [None] * chunks
    got_z = [None] * chunks
    got_x[0] = send_x(qkv[0])
    hidden = (
        jnp.einsum("psd,df->psf", normed_low, up_weight, preferred_element_type=F32) + up_bias
    )
    active_low = jax.nn.gelu(hidden, approximate=True).astype(BF16)
    branch_ff = jnp.einsum(
        "psf,fd->psd", active_low, down_weight, preferred_element_type=F32
    ).astype(BF16)
    got_x[0], branch_ff, qkv, out_weight, back_weight = tie(
        got_x[0], branch_ff, qkv, merge_weight, down_weight
    )

    got_z[0] = send_z(qkv[0], got_x[0])
    if chunks > 1:
        got_x[1] = send_x(qkv[1])
    sends = out_grads(cot, out_weight)
    active_grad = jnp.einsum("psd,fd->psf", cot, back_weight, preferred_element_type=F32)
    _, gelu_back = jax.vjp(lambda values: jax.nn.gelu(values, approximate=True), hidden)
    hidden_grad = gelu_back(active_grad)[0].astype(BF16)
    got_x, got_z, qkv, sends, hidden_grad = tie(got_x, got_z, qkv, sends, hidden_grad)

    got_dx = send_x(sends)
    sources = [received(qkv[0], got_x[0], got_z[0])]
    if chunks > 1:
        got_z[1] = send_z(qkv[1], got_x[1])
        sources.append(received(qkv[1], got_x[1], got_z[1]))
    ahead = [attend(0, sources[0])]
    up_grad = jnp.einsum(
        "psd,psf->df", normed_low, hidden_grad, preferred_element_type=F32
    ).astype(BF16)
    down_grad = jnp.einsum("psd,psf->df", cot, active_low, preferred_element_type=F32).astype(BF16)
    biases = jnp.sum(hidden_grad.astype(F32), axis=(0, 1)), jnp.sum(cot.astype(F32), axis=(0, 1))
    got_dx, sources_arrays, ahead, sends, hidden_grad, up_grad, down_grad, biases = tie(
        got_dx,
        [[a for a, _ in v] for v in sources],
        ahead,
        sends,
        hidden_grad,
        up_grad,
        down_grad,
        biases,
    )
    def with_row(*parts):
        weight = jnp.concatenate(parts[:2], axis=1)
        row = jnp.concatenate(parts[2:])
        row = jnp.pad(row, (0, weight.shape[1] - row.shape[0])).reshape(1, -1)
        row = jnp.broadcast_to(row, (16, weight.shape[1])).astype(BF16)
        return jnp.concatenate([weight, row], axis=0)

    terms = dict(
        enumerate(
            with_row(*parts)
            for parts in zip(*[cut(v, 0, n, rank) for v in (up_grad, down_grad, *biases)])
        )
    )
    terms_got = cube_send(terms, "seq", n, seq_masks)
    sources = [
        [(a, lead) for a, (_, lead) in zip(arrays, v)] for arrays, v in zip(sources_arrays, sources)
    ]

    got_dz = send_z(sends, got_dx)
    if chunks > 1:
        ahead.append(attend(1, sources[1]))
    low_ff = jnp.einsum(
        "psf,df->psd", hidden_grad, up_weight, preferred_element_type=F32
    ).astype(BF16)
    got_dz, ahead, low_ff = tie(got_dz, ahead, low_ff)
    grads = received(sends, got_dx, got_dz)

    attended = [jnp.stack([outs[k] for outs in ahead]) for k in range(n)]
    got_ax = send_x(attended)
    backs = [attend_back(0, ahead[0][n], ahead[0][n + 1], sources[0], grads)]
    got_ax, terms_got, backs, attended, ahead = tie(got_ax, terms_got, backs, attended, ahead)

    terms = cube_add(terms, terms_got, seq_masks, BF16)
    terms_got = cube_send(terms, "seq", n, seq_masks[1:])
    got_az = send_z(attended, got_ax)
    back_x = [send_x(backs[0])]
    if chunks > 1:
        backs.append(attend_back(1, ahead[1][n], ahead[1][n + 1], sources[1], grads))
    got_az, terms_got, back_x, backs = tie(got_az, terms_got, back_x, backs)

    back_z = [send_z(backs[0], back_x[0])]
    if chunks > 1:
        back_x.append(send_x(backs[1]))
    for step in range(1, len(seq_masks)):
        last_step = step == len(seq_masks) - 1
        terms = cube_add(terms, terms_got, seq_masks[step:], F32 if last_step else BF16)
        if not last_step:
            terms_got = cube_send(terms, "seq", n, seq_masks[step + 1 :])
    terms = terms[0]
    branch, merge_part = merge(received(attended, got_ax, got_az), branch_ff)
    summed = lax.psum_scatter(branch, "mlp", scatter_dimension=0, tiled=False)
    back_x, back_z, backs, merge_part, terms = tie(back_x, back_z, backs, merge_part, terms)

    share = per * groups * shard // slices

    def share_sum(low):
        return cube_sum(
            cut(low.reshape(share * slices, width), 0, slices, column), "mlp", mlp_masks, BF16
        )

    def finish(c, low_sum):
        start = (c * slices + column) * share
        row_in = lax.dynamic_slice_in_dim(
            tokens_dealt.reshape(rows, width), start, share, 0
        ).astype(F32)
        row_cot = lax.dynamic_slice_in_dim(cot.reshape(rows, width), start, share, 0).astype(F32)
        cent = row_in - jnp.mean(row_in, axis=-1, keepdims=True)
        inverse = lax.rsqrt(jnp.mean(cent * cent, axis=-1, keepdims=True) + EPS)
        xhat = cent * inverse
        g = low_sum * norm_gain
        row_grad = (
            row_cot
            + (
                g
                - jnp.mean(g, axis=-1, keepdims=True)
                - xhat * jnp.mean(g * xhat, axis=-1, keepdims=True)
            )
            * inverse
        ).astype(BF16)
        return row_grad, jnp.stack([jnp.sum(low_sum * xhat, axis=0), jnp.sum(low_sum, axis=0)])

    low, head_part = close(0, received(backs[0], back_x[0], back_z[0]))
    head_parts = [head_part]
    if chunks > 1:
        second = send_z(backs[1], back_x[1], [n // 2])
        second, low, head_parts, backs, back_x = tie(second, low, head_parts, backs, back_x)
        others = send_z(backs[1], back_x[1], [k for k in range(2, n, 2) if k != n // 2])
        others.insert(n // 4 - 1, second[0])
        back_z.append(others)
    row_grad, vectors = finish(0, share_sum(low))
    back_z, row_grad, vectors = tie(back_z, row_grad, vectors)

    cols = width // slices
    pieces = gather_step([row_grad[None]], "mlp", slices, mlp_masks[-1])
    result = (
        lax.dynamic_slice_in_dim(tokens, column * cols, cols, 2).astype(F32)
        + jnp.take(summed, at, axis=0, mode="clip").astype(F32)
        + lax.dynamic_slice_in_dim(down_bias, column * cols, cols, 0)
    ).astype(BF16)
    if chunks > 1:
        low, head_part = close(1, received(backs[1], back_x[1], back_z[1]))
        head_parts.append(head_part)
        pieces, low, head_parts, result = tie(pieces, low, head_parts, result)
    weights = functools.reduce(jnp.add, head_parts)
    weights = jnp.concatenate([weights.astype(BF16), merge_part], axis=0)
    weights = dict(enumerate(cut(weights, 1, n, rank)))
    weights_got = cube_send(weights, "seq", n, seq_masks)
    if chunks > 1:
        low_sum = share_sum(low)
        for m in reversed(mlp_masks[:-1]):
            pieces = gather_step(pieces, "mlp", slices, m)
        row_grad, more = finish(1, low_sum)
        vectors = vectors + more
        row_grad, pieces, weights_got, vectors = tie(row_grad, pieces, weights_got, vectors)
        last = gather_step([row_grad[None]], "mlp", slices, mlp_masks[-1])
    else:
        last, pieces = pieces, []
    vectors = small_sum(vectors, n, slices)
    weights = cube_add(weights, weights_got, seq_masks, BF16)
    weights_got = cube_send(weights, "seq", n, seq_masks[1:])
    last, vectors, weights_got = tie(last, vectors, weights_got)
    for m in reversed(mlp_masks[:-1]):
        last = gather_step(last, "mlp", slices, m)
    pieces += last
    where = [(0, 0)]
    lookup = [0]
    for i, m in enumerate(reversed(mlp_masks)):
        where += [(i + 1, j) for j in range(len(lookup))]
        lookup += [k ^ m for k in lookup]
    per_piece = [where[lookup.index(k)] for k in range(slices)]
    block = math.gcd(share, shard)
    tokens_grad = pl.pallas_call(
        functools.partial(
            place_kernel, block, share, shard, slices, chunks, per_piece
        ),
        grid_spec=pltpu.PrefetchScalarGridSpec(
            num_scalar_prefetch=1,
            grid=(1,),
            in_specs=[pl.BlockSpec(memory_space=pl.ANY)] * len(pieces),
            out_specs=pl.BlockSpec(memory_space=pl.ANY),
            scratch_shapes=[
                pltpu.VMEM((rows // block, block, width), BF16),
                pltpu.SemaphoreType.DMA((rows // block,)),
                pltpu.SemaphoreType.DMA((rows // block,)),
            ],
        ),
        out_shape=jax.ShapeDtypeStruct((packs + spare, shard, width), BF16),
        compiler_params=params(),
        name="place",
    )(jnp.concatenate([pack_at, column.astype(jnp.int32).reshape(1)]), *pieces)[:packs]

    for step in range(1, len(seq_masks)):
        weights = cube_add(
            weights, weights_got, seq_masks[step:], F32 if step == len(seq_masks) - 1 else BF16
        )
        if step < len(seq_masks) - 1:
            weights_got = cube_send(weights, "seq", n, seq_masks[step + 1 :])
    weights = weights[0]
    head_grad = jnp.transpose(
        weights[: 3 * joined].reshape(3, joined, width // n), (0, 2, 1)
    )
    merge_grad = weights[3 * joined :]
    part, hidden_here = width // n, up_weight.shape[1]
    up_grad, down_grad = terms[:part, :hidden_here], terms[:part, hidden_here:].T
    up_bias_grad = terms[part, : hidden_here // n]
    down_bias_grad = terms[part, hidden_here // n : hidden_here // n + part]
    return (
        result,
        tokens_grad,
        vectors[0],
        vectors[1],
        head_grad,
        merge_grad,
        up_grad,
        up_bias_grad,
        down_grad,
        down_bias_grad,
    )


def qkv_kernel(heads, me_ref, x_ref, w_ref, cos_ref, sin_ref, normed_ref, out_ref):
    width = heads * HD
    normed = x_ref[0]
    normed_ref[...] = normed
    for j in range(3):
        part = dot(w_ref[j * width : (j + 1) * width, :], normed, ((1,), (1,)))
        if j < 2:
            part = turn(part, cos_ref[...], sin_ref[...], heads)
        if j == 0:
            part = part * (1.0 / math.sqrt(HD))
        part = part.astype(BF16)
        for h in range(heads):
            out_ref[h, j] = part[h * HD : (h + 1) * HD]


def allowed_of(block, first, i):
    rows = lax.broadcasted_iota(jnp.int32, (block, block), 0)
    cols = lax.broadcasted_iota(jnp.int32, (block, block), 1)
    ahead = rows - cols
    return lambda j: (rows >= first - j * block) & (ahead <= (i - j) * block)


def unit_kernel(n, block, me_ref, low_ref, first_ref, qkv_ref, out_ref, keep_ref, logsum_ref, qt, vt, kn):
    me = me_ref[0]
    pair = range(qkv_ref.shape[0])
    for u in pair:
        for i in range(n):
            at = slice(i * block, (i + 1) * block)
            qt[u, i] = qkv_ref[u, 0, :, at]
            kn[u, i] = qkv_ref[u, 1, :, at].T
            vt[u, i] = qkv_ref[u, 2, :, at]

    def outer(i, carry):
        allowed = allowed_of(block, first_ref[pl.ds(i, 1), :], i)
        j0 = low_ref[i]

        def forward(t, states):
            j = j0 + 2 * t
            at = jnp.minimum(j + 1, n - 1)
            mask0, mask1 = allowed(j), allowed(j + 1)
            out = []
            for u, (top, total, acc) in zip(pair, states):
                q_t = qt[u, i]
                s0 = jnp.where(mask0, dot(kn[u, j], q_t), NEG)
                s1 = jnp.where(mask1, dot(kn[u, at], q_t), NEG)
                peak = jnp.max(jnp.maximum(s0, s1), axis=0, keepdims=True)
                new_top = jnp.maximum(top, peak)
                p0, p1 = jnp.exp(s0 - new_top), jnp.exp(s1 - new_top)
                fade = jnp.exp(top - new_top)
                total = total * fade + jnp.sum(p0 + p1, axis=0, keepdims=True)
                acc = acc * fade + dot(vt[u, j], p0.astype(BF16)) + dot(vt[u, at], p1.astype(BF16))
                out.append((new_top, total, acc))
            return tuple(out)

        states = lax.fori_loop(
            0,
            (i - j0) // 2 + 1,
            forward,
            tuple(
                (
                    jnp.full((1, block), NEG, F32),
                    jnp.zeros((1, block), F32),
                    jnp.zeros((HD, block), F32),
                )
                for _ in pair
            ),
        )
        for u, (top, total, acc) in zip(pair, states):
            keep_ref[u, i] = (acc / total).astype(BF16)
            logsum_ref[u, pl.ds(i, 1), :] = top + jnp.log(total)
        return carry

    lax.fori_loop(0, n, outer, 0)
    for k in range(n):
        for u in pair:
            out_ref[k, u] = keep_ref[u, lax.bitwise_xor(jnp.int32(k), me)]


def unit_back_kernel(
    n, block, me_ref, low_ref, first_ref, keep_ref, logsum_ref, qkv_ref, grad_ref, out_ref,
    qt, kt, gt, qn, kn, vn, gn, dk, dv, dqs
):
    me = me_ref[0]
    pair = range(qkv_ref.shape[0])
    for u in pair:
        for i in range(n):
            at = slice(i * block, (i + 1) * block)
            for j, (t_ref, n_ref) in enumerate(((qt, qn), (kt, kn), (None, vn))):
                part = qkv_ref[u, j, :, at]
                if t_ref is not None:
                    t_ref[u, i] = part
                n_ref[u, i] = part.T
        for k in range(n):
            d = lax.bitwise_xor(jnp.int32(k), me)
            part = grad_ref[k, u]
            gt[u, d] = part
            gn[u, d] = part.T
    dk[...] = jnp.zeros_like(dk)
    dv[...] = jnp.zeros_like(dv)

    def outer(i, carry):
        allowed = allowed_of(block, first_ref[pl.ds(i, 1), :], i)
        j0 = low_ref[i]
        inner = [
            jnp.sum(keep_ref[u, i].astype(F32) * gt[u, i].astype(F32), axis=0, keepdims=True)
            for u in pair
        ]
        logsum = [logsum_ref[u, pl.ds(i, 1), :] for u in pair]

        def one(u, mask, at):
            s = jnp.where(mask, dot(kn[u, at], qt[u, i]), NEG)
            p = jnp.exp(s - logsum[u])
            ds = (p * (dot(vn[u, at], gt[u, i]) - inner[u])).astype(BF16)
            return dot(ds, qn[u, i]), dot(p.astype(BF16), gn[u, i]), dot(kt[u, at], ds)

        def backward(t, dqs):
            j = j0 + 2 * t
            at = jnp.minimum(j + 1, n - 1)
            mask0, mask1 = allowed(j), allowed(j + 1)
            out = []
            for u, dq in zip(pair, dqs):
                dk0, dv0, dq0 = one(u, mask0, j)
                dk1, dv1, dq1 = one(u, mask1, at)
                dk[u, j] += dk0
                dv[u, j] += dv0
                dk[u, at] += dk1
                dv[u, at] += dv1
                out.append(dq + dq0 + dq1)
            return tuple(out)

        dq = lax.fori_loop(
            0, (i - j0) // 2 + 1, backward, tuple(jnp.zeros((HD, block), F32) for _ in pair)
        )
        for u in pair:
            dqs[u, i] = (dq[u] * (1.0 / math.sqrt(HD))).astype(BF16)
        return carry

    lax.fori_loop(0, n, outer, 0)
    for u in pair:
        for i in range(n):
            at = slice(i * block, (i + 1) * block)
            out_ref[u, 0, :, at] = dqs[u, i]
            out_ref[u, 1, :, at] = dk[u, i].T.astype(BF16)
            out_ref[u, 2, :, at] = dv[u, i].T.astype(BF16)


def rows_kernel(heads, slices, me_ref, grad_ref, normed_ref, w_ref, cos_ref, sin_ref, low_ref, weight_ref):
    width = heads * HD
    column = me_ref[1]

    @pl.when(pl.program_id(0) == 0)
    def _():
        weight_ref[...] = jnp.zeros_like(weight_ref)

    parts = []
    for j in range(3):
        part = jnp.concatenate([grad_ref[h, j] for h in range(heads)], axis=0)
        if j < 2:
            part = turn(part.astype(F32), cos_ref[...], -sin_ref[...], heads).astype(BF16)
        parts.append(part)
    grads = jnp.concatenate(parts, axis=0)
    weight_ref[...] += dot(grads, normed_ref[...])
    low = dot(grads.T, w_ref[...]).astype(BF16)
    part = low.shape[0] // slices
    for m in range(slices):
        low_ref[lax.bitwise_xor(jnp.int32(m), column), 0] = low[m * part : (m + 1) * part]


def norm_kernel(x_ref, gain_ref, bias_ref, normed_ref):
    x = x_ref[0].astype(F32)
    cent = x - jnp.mean(x, axis=-1, keepdims=True)
    var = jnp.mean(cent * cent, axis=-1, keepdims=True)
    normed_ref[0] = (cent * lax.rsqrt(var + EPS) * gain_ref[...] + bias_ref[...]).astype(BF16)


def finish_kernel(terms, which_ref, *refs):
    lows = refs[:terms]
    low_ref, x_ref, c_ref, gain_ref, out_ref, sums_ref = refs[terms:]

    @pl.when(pl.program_id(0) == 0)
    def _():
        sums_ref[...] = jnp.zeros_like(sums_ref)

    low = low_ref[0].astype(F32)
    for ref in lows:
        low = low + ref[0].astype(F32)
    x = x_ref[0].astype(F32)
    cent = x - jnp.mean(x, axis=-1, keepdims=True)
    inverse = lax.rsqrt(jnp.mean(cent * cent, axis=-1, keepdims=True) + EPS)
    xhat = cent * inverse
    g = low * gain_ref[...]
    inner = jnp.mean(g * xhat, axis=-1, keepdims=True)
    back = (g - jnp.mean(g, axis=-1, keepdims=True) - xhat * inner) * inverse
    out_ref[0] = (c_ref[0].astype(F32) + back).astype(BF16)
    sums_ref[0:1] += jnp.sum(low * xhat, axis=0, keepdims=True)
    sums_ref[1:2] += jnp.sum(low, axis=0, keepdims=True)


def join_kernel(slices, attended_ref, c_ref, merge_ref, branch_ref, out_branch, out_weight):
    @pl.when(pl.program_id(0) == 0)
    def _():
        out_weight[...] = jnp.zeros_like(out_weight)

    attended = attended_ref[0]
    out_weight[...] += dot(attended, c_ref[0])
    branch = dot(attended.T, merge_ref[...]) + branch_ref[0].astype(F32)
    cols = branch.shape[1] // slices
    for m in range(slices):
        out_branch[m, 0] = branch[:, m * cols : (m + 1) * cols].astype(BF16)


def settle_kernel(counts, slices, sub, per_piece, table_ref, *refs):
    pieces, out, buf, sems, out_sems = refs[:-4], refs[-4], refs[-3], refs[-2], refs[-1]
    column = table_ref[sum(counts)]
    loads, stores = [], []
    arrays = max(ref for ref, _ in per_piece) + 1
    first = 0
    for c, count in enumerate(counts):
        for k in range(slices):
            ref, where = per_piece[k]
            start = pl.multiple_of(lax.bitwise_xor(jnp.int32(k), column) * sub, sub)
            for t in range(count):
                at = len(loads)
                loads.append(
                    pltpu.make_async_copy(
                        pieces[c * arrays + ref].at[where, t], buf.at[at], sems.at[at]
                    )
                )
                stores.append(
                    pltpu.make_async_copy(
                        buf.at[at],
                        out.at[table_ref[first + t], pl.ds(start, sub)],
                        out_sems.at[at],
                    )
                )
        first += count
    for copy in loads:
        copy.start()
    for load, store in zip(loads, stores):
        load.wait()
        store.start()
    for copy in stores:
        copy.wait()


def exchange_x(array):
    n = array.shape[0]
    return lax.ppermute(array[1::2], "seq", [(i, i ^ 1) for i in range(n)])


def exchange_z(array, got, steps=None):
    n = array.shape[0]
    return [
        lax.ppermute(jnp.stack([array[k], got[k // 2]]), "seq", [(i, i ^ k) for i in range(n)])
        for k in (range(2, n, 2) if steps is None else steps)
    ]


def exchanged(array, got, gots):
    return jnp.concatenate([array[:1], got[:1], *gots], axis=0)


def take(array, index):
    return jnp.take(array, index, axis=0, mode="clip")


def on_device_pairs(
    tokens,
    lengths,
    counts,
    norm_gain,
    norm_bias,
    head_weight,
    merge_weight,
    up_weight,
    up_bias,
    down_weight,
    down_bias,
    cotangent,
):
    packs, shard, width = tokens.shape
    n = lax.axis_size("seq")
    slices = lax.axis_size("mlp")
    pack_len = shard * n
    rank = lax.axis_index("seq").astype(jnp.int32)
    column = lax.axis_index("mlp").astype(jnp.int32)
    heads = merge_weight.shape[0] // HD
    joined = heads * HD
    half = heads // 2
    cols = width // slices
    sub = shard // slices
    seq_masks, mlp_masks = masks_of(n), masks_of(slices)
    pairs = n // 2

    cot = lax.all_gather(cotangent, "mlp", axis=2, tiled=True)

    first, position, cost = layout(lengths, counts, pack_len)
    ids = jnp.arange(packs, dtype=jnp.int32)
    before = (cost[None, :] > cost[:, None]) | (
        (cost[None, :] == cost[:, None]) & (ids[None, :] < ids[:, None])
    )
    order = jnp.sum(before.astype(jnp.int32), axis=1)
    by_order = jnp.sum(
        jnp.where(order[None, :] == ids[:, None], ids[None, :], 0), axis=-1
    ).astype(jnp.int32)
    devices = jnp.arange(n, dtype=jnp.int32)
    shared_of = by_order[:pairs]
    own_of = by_order[pairs + 2 * (pairs - 1 - devices // 2) + devices % 2]
    late = order - pairs
    pair_of = jnp.where(late < 0, order, pairs - 1 - late // 2)
    device_of = 2 * pair_of + jnp.where(late < 0, 0, late % 2)
    dest = jnp.bitwise_xor(rank, devices)
    own_dest, shared_dest = own_of[dest], shared_of[dest // 2]
    me = jnp.stack([rank, column])

    token_cols = lax.dynamic_slice_in_dim(tokens, column * cols, cols, 2)
    head_ids = jnp.arange(heads, dtype=jnp.int32)
    half_ids = jnp.arange(half, dtype=jnp.int32)
    units_out = jnp.concatenate(
        [
            own_dest[:, None] * heads + head_ids[None, :],
            shared_dest[:, None] * heads + (dest % 2)[:, None] * half + half_ids[None, :],
        ],
        axis=1,
    ).reshape(-1)
    is_shared = (order < pairs)[:, None]
    holder = device_of[:, None] + jnp.where(is_shared, head_ids[None, :] // half, 0)
    units_in = (
        jnp.bitwise_xor(holder, rank) * (heads + half)
        + jnp.where(is_shared, heads + head_ids[None, :] % half, head_ids[None, :])
    ).reshape(-1)

    def tables(pack):
        freq = 10000.0 ** (-(2.0 * jnp.arange(ROT // 2, dtype=F32)) / ROT)
        angle = take(position, pack).astype(F32)[None, :] * jnp.repeat(freq, 2)[:, None]
        return jnp.cos(angle), jnp.sin(angle)

    w_heads = jnp.transpose(head_weight, (0, 2, 1)).reshape(3, heads, HD, width)
    w_own = w_heads.reshape(3 * joined, width)
    part_at = (rank % 2) * half
    w_shared = lax.dynamic_slice_in_dim(w_heads, part_at, half, 1).reshape(3 * half * HD, width)
    packs_here = (own_of[rank], shared_of[rank // 2])
    turns = [tables(p) for p in packs_here]
    firsts = [take(first, p).reshape(n, shard) for p in packs_here]
    lows = [(f[:, 0] // shard).astype(jnp.int32) for f in firsts]
    gain, bias = norm_gain.reshape(1, width), norm_bias.reshape(1, width)

    def whole2(s, *_):
        return (0, 0)

    def lane_at(s, *_):
        return (0, s)

    def project(rows, weight, cosine, sine):
        h = weight.shape[0] // (3 * HD)
        return pl.pallas_call(
            functools.partial(qkv_kernel, h),
            grid_spec=pltpu.PrefetchScalarGridSpec(
                num_scalar_prefetch=1,
                grid=(n,),
                in_specs=[
                    pl.BlockSpec(
                        (1, shard, width), lambda s, me: (lax.bitwise_xor(s, me[0]), 0, 0)
                    ),
                    pl.BlockSpec(weight.shape, whole2),
                    pl.BlockSpec((ROT, shard), lane_at),
                    pl.BlockSpec((ROT, shard), lane_at),
                ],
                out_specs=[
                    pl.BlockSpec((shard, width), lambda s, *_: (s, 0)),
                    pl.BlockSpec((h, 3, HD, shard), lambda s, *_: (0, 0, 0, s)),
                ],
            ),
            out_shape=[
                jax.ShapeDtypeStruct((pack_len, width), BF16),
                jax.ShapeDtypeStruct((h, 3, HD, pack_len), BF16),
            ],
            compiler_params=params(),
            cost_estimate=COST,
            name="project",
        )(me, rows, weight, cosine, sine)

    wide = [pltpu.VMEM((2, n, HD, shard), BF16)]
    tall = [pltpu.VMEM((2, n, shard, HD), BF16)]
    keep_spec = pl.BlockSpec((2, n, HD, shard), lambda u, *_: (u, 0, 0, 0))
    log_spec = pl.BlockSpec((2, n, shard), lambda u, *_: (u, 0, 0))
    unit_spec = pl.BlockSpec((2, 3, HD, pack_len), lambda u, *_: (u, 0, 0, 0))

    def attend(c, qkv):
        h = qkv.shape[0]
        return pl.pallas_call(
            functools.partial(unit_kernel, n, shard),
            grid_spec=pltpu.PrefetchScalarGridSpec(
                num_scalar_prefetch=2,
                grid=(h // 2,),
                in_specs=[pl.BlockSpec((n, shard), whole2), unit_spec],
                out_specs=[
                    pl.BlockSpec((n, 2, HD, shard), lambda u, *_: (0, u, 0, 0)),
                    keep_spec,
                    log_spec,
                ],
                scratch_shapes=wide * 2 + tall,
            ),
            out_shape=[
                jax.ShapeDtypeStruct((n, h, HD, shard), BF16),
                jax.ShapeDtypeStruct((h, n, HD, shard), BF16),
                jax.ShapeDtypeStruct((h, n, shard), F32),
            ],
            compiler_params=params(),
            cost_estimate=COST,
            name="attend",
        )(me, lows[c], firsts[c], qkv)

    def attend_back(c, kept, logsum, qkv, grads):
        h = qkv.shape[0]
        skip = c * heads // 2
        return pl.pallas_call(
            functools.partial(unit_back_kernel, n, shard),
            grid_spec=pltpu.PrefetchScalarGridSpec(
                num_scalar_prefetch=2,
                grid=(h // 2,),
                in_specs=[
                    pl.BlockSpec((n, shard), whole2),
                    keep_spec,
                    log_spec,
                    unit_spec,
                    pl.BlockSpec((n, 2, HD, shard), lambda u, *_: (0, u + skip, 0, 0)),
                ],
                out_specs=unit_spec,
                scratch_shapes=wide * 3
                + tall * 4
                + [pltpu.VMEM((2, n, shard, HD), F32)] * 2
                + [pltpu.VMEM((2, n, HD, shard), BF16)],
            ),
            out_shape=jax.ShapeDtypeStruct((h, 3, HD, pack_len), BF16),
            compiler_params=params(),
            cost_estimate=COST,
            name="attend_back",
        )(me, lows[c], firsts[c], kept, logsum, qkv, grads)

    def rows_back(grads, normed, weight, cosine, sine):
        h = grads.shape[0]
        return pl.pallas_call(
            functools.partial(rows_kernel, h, slices),
            grid_spec=pltpu.PrefetchScalarGridSpec(
                num_scalar_prefetch=1,
                grid=(n,),
                in_specs=[
                    pl.BlockSpec((h, 3, HD, shard), lambda s, *_: (0, 0, 0, s)),
                    pl.BlockSpec((shard, width), lambda s, *_: (s, 0)),
                    pl.BlockSpec(weight.shape, whole2),
                    pl.BlockSpec((ROT, shard), lane_at),
                    pl.BlockSpec((ROT, shard), lane_at),
                ],
                out_specs=[
                    pl.BlockSpec(
                        (slices, 1, sub, width),
                        lambda s, me: (0, lax.bitwise_xor(s, me[0]), 0, 0),
                    ),
                    pl.BlockSpec(weight.shape, whole2),
                ],
            ),
            out_shape=[
                jax.ShapeDtypeStruct((slices, n, sub, width), BF16),
                jax.ShapeDtypeStruct(weight.shape, F32),
            ],
            compiler_params=params(),
            cost_estimate=COST,
            name="rows_back",
        )(me, grads, normed, weight, cosine, sine)

    pack_spec = pl.BlockSpec((1, shard, width), lambda p: (p, 0, 0))
    normed_low = pl.pallas_call(
        norm_kernel,
        grid=(packs,),
        in_specs=[pack_spec, pl.BlockSpec((1, width), whole2), pl.BlockSpec((1, width), whole2)],
        out_specs=pack_spec,
        out_shape=jax.ShapeDtypeStruct((packs, shard, width), BF16),
        compiler_params=params(),
        cost_estimate=COST,
        name="norm",
    )(tokens, gain, bias)
    normed_cols = lax.dynamic_slice_in_dim(normed_low, column * cols, cols, 2)
    send_own = take(normed_cols, own_dest)
    send_shared = take(normed_cols, shared_dest)
    own_x = exchange_x(send_own)

    hidden = (
        jnp.einsum("psd,df->psf", normed_low, up_weight, preferred_element_type=F32) + up_bias
    )
    own_x, hidden, send_own, send_shared = tie(own_x, hidden, send_own, send_shared)

    own_z = exchange_z(send_own, own_x, [2])
    shared_x = exchange_x(send_shared)
    active_low = jax.nn.gelu(hidden, approximate=True).astype(BF16)
    branch_ff = jnp.einsum(
        "psf,fd->psd", active_low, down_weight, preferred_element_type=F32
    ).astype(BF16)
    own_z, shared_x, branch_ff, send_own, own_x, merge_here, down_here, turns, w_own, w_shared = tie(
        own_z,
        shared_x,
        branch_ff,
        send_own,
        own_x,
        merge_weight,
        down_weight,
        turns,
        w_own,
        w_shared,
    )

    own_z += exchange_z(send_own, own_x, range(4, n, 2))
    active_grad = jnp.einsum("psd,fd->psf", cot, down_here, preferred_element_type=F32)
    _, gelu_back = jax.vjp(lambda values: jax.nn.gelu(values, approximate=True), hidden)
    hidden_grad = gelu_back(active_grad)[0].astype(BF16)
    own_z, hidden_grad, send_shared, shared_x = tie(own_z, hidden_grad, send_shared, shared_x)
    rows_own = lax.all_gather(exchanged(send_own, own_x, own_z), "mlp", axis=2, tiled=True)

    shared_z = exchange_z(send_shared, shared_x)
    out_grad = jnp.einsum("hd,psd->phs", merge_here, cot, preferred_element_type=F32).astype(BF16)
    send_grad = take(out_grad.reshape(packs * heads, HD, shard), units_out).reshape(
        n, heads + half, HD, shard
    )
    up_grad = jnp.einsum(
        "psd,psf->df", normed_low, hidden_grad, preferred_element_type=F32
    ).astype(BF16)
    down_grad = jnp.einsum("psd,psf->df", cot, active_low, preferred_element_type=F32).astype(BF16)
    shared_z, send_grad, up_grad, down_grad, send_shared, shared_x, hidden_grad = tie(
        shared_z, send_grad, up_grad, down_grad, send_shared, shared_x, hidden_grad
    )
    rows_shared = lax.all_gather(
        exchanged(send_shared, shared_x, shared_z), "mlp", axis=2, tiled=True
    )

    grad_x = exchange_x(send_grad)
    low_ff = jnp.einsum(
        "psf,df->psd", hidden_grad, up_weight, preferred_element_type=F32
    ).astype(BF16)
    low_ff = jnp.transpose(low_ff.reshape(packs, slices, sub, width), (1, 0, 2, 3)).reshape(
        slices * packs * sub, width
    )
    biases = jnp.sum(hidden_grad.astype(F32), axis=(0, 1)), jnp.sum(cot.astype(F32), axis=(0, 1))
    grad_x, send_grad, low_ff, rows_own, biases = tie(grad_x, send_grad, low_ff, rows_own, biases)
    low_ff = lax.psum_scatter(low_ff, "mlp", scatter_dimension=0, tiled=True).reshape(
        packs, sub, width
    )

    grad_z = exchange_z(send_grad, grad_x)
    normed_own, qkv_own = project(rows_own, w_own, *turns[0])
    out_own, kept_own, log_own = attend(0, qkv_own)
    grad_z, out_own, kept_own, log_own, rows_shared = tie(
        grad_z, out_own, kept_own, log_own, rows_shared
    )
    grads = exchanged(send_grad, grad_x, grad_z)

    def with_row(*parts):
        weight = jnp.concatenate(parts[:2], axis=1)
        row = jnp.concatenate(parts[2:])
        row = jnp.pad(row, (0, weight.shape[1] - row.shape[0])).reshape(1, -1)
        row = jnp.broadcast_to(row, (16, weight.shape[1])).astype(BF16)
        return jnp.concatenate([weight, row], axis=0)

    terms = dict(
        enumerate(
            with_row(*parts)
            for parts in zip(*[cut(v, 0, n, rank) for v in (up_grad, down_grad, *biases)])
        )
    )
    terms_got = cube_send(terms, "seq", n, seq_masks)
    normed_shared, qkv_shared = project(rows_shared, w_shared, *turns[1])
    out_shared, kept_shared, log_shared = attend(1, qkv_shared)
    out_shared, kept_shared, log_shared, grads = tie(out_shared, kept_shared, log_shared, grads)

    send_out = jnp.concatenate([out_own, out_shared], axis=1)
    out_x = exchange_x(send_out)
    back_own = attend_back(0, kept_own, log_own, qkv_own, grads)
    out_x, back_own, terms_got, send_out = tie(out_x, back_own, terms_got, send_out)

    terms = cube_add(terms, terms_got, seq_masks, BF16)
    terms_got = cube_send(terms, "seq", n, seq_masks[1:])
    out_z = exchange_z(send_out, out_x)
    low_own, head_own = rows_back(back_own, normed_own, w_own, *turns[0])
    back_shared = attend_back(1, kept_shared, log_shared, qkv_shared, grads)
    out_z, terms_got, low_own, back_shared, send_out, out_x = tie(
        out_z, terms_got, low_own, back_shared, send_out, out_x
    )

    low_own = cube_sum([low_own[k] for k in range(slices)], "mlp", mlp_masks, BF16).astype(BF16)
    for step in range(1, len(seq_masks)):
        last_step = step == len(seq_masks) - 1
        terms = cube_add(terms, terms_got, seq_masks[step:], F32 if last_step else BF16)
        if not last_step:
            terms_got = cube_send(terms, "seq", n, seq_masks[step + 1 :])
    terms = terms[0]
    low_shared, head_shared = rows_back(back_shared, normed_shared, w_shared, *turns[1])
    attended = take(
        exchanged(send_out, out_x, out_z).reshape(n * (heads + half), HD, shard), units_in
    ).reshape(packs, joined, shard)
    branch, merge_part = pl.pallas_call(
        functools.partial(join_kernel, slices),
        grid=(packs,),
        in_specs=[
            pl.BlockSpec((1, joined, shard), lambda p: (p, 0, 0)),
            pl.BlockSpec((1, shard, width), lambda p: (p, 0, 0)),
            pl.BlockSpec((joined, width), whole2),
            pl.BlockSpec((1, shard, width), lambda p: (p, 0, 0)),
        ],
        out_specs=[
            pl.BlockSpec((slices, 1, shard, cols), lambda p: (0, p, 0, 0)),
            pl.BlockSpec((joined, width), whole2),
        ],
        out_shape=[
            jax.ShapeDtypeStruct((slices, packs, shard, cols), BF16),
            jax.ShapeDtypeStruct((joined, width), F32),
        ],
        compiler_params=params(),
        cost_estimate=COST,
        name="join",
    )(attended, cot, merge_weight, branch_ff)
    low_terms = {k: low_shared[k] for k in range(slices)}
    low_got = cube_send(low_terms, "mlp", slices, mlp_masks)
    low_terms, low_got, low_own, branch, terms, low_ff, head_shared = tie(
        low_terms, low_got, low_own, branch, terms, low_ff, head_shared
    )

    summed = lax.psum_scatter(branch, "mlp", scatter_dimension=0, tiled=False)

    low_own_x = exchange_x(low_own)
    for step in range(len(mlp_masks)):
        low_terms = cube_add(low_terms, low_got, mlp_masks[step:], BF16)
        if step < len(mlp_masks) - 1:
            low_got = cube_send(low_terms, "mlp", slices, mlp_masks[step + 1 :])
    low_shared = low_terms[0]
    head_all = head_own.reshape(3, heads, HD, width)
    there = lax.dynamic_slice_in_dim(head_all, part_at, half, 1)
    head_all = lax.dynamic_update_slice_in_dim(
        head_all, there + head_shared.reshape(3, half, HD, width), part_at, 1
    ).reshape(3 * joined, width)
    weights = jnp.concatenate([head_all, merge_part], axis=0).astype(BF16)
    weights = dict(enumerate(cut(weights, 1, n, rank)))
    low_own_z = exchange_z(low_own, low_own_x)
    weights_got = cube_send(weights, "seq", n, seq_masks)
    low_own_z, low_shared, low_own, low_own_x, weights, weights_got = tie(
        low_own_z, low_shared, low_own, low_own_x, weights, weights_got
    )

    low_shared_x = exchange_x(low_shared)
    weights = cube_add(weights, weights_got, seq_masks, BF16)
    weights_got = cube_send(weights, "seq", n, seq_masks[1:])

    def finish(lows, index, which):
        count = which.shape[0]
        row_spec = pl.BlockSpec((1, sub, width), lambda t, at: (at[count + t], at[0], 0))

        def part(i):
            return pl.BlockSpec(
                (1, sub, width), lambda t, at: (at[(2 + i) * count + t], 0, 0)
            )

        table = [jnp.full((count,), column), which, *index]
        return pl.pallas_call(
            functools.partial(finish_kernel, len(lows)),
            grid_spec=pltpu.PrefetchScalarGridSpec(
                num_scalar_prefetch=1,
                grid=(count,),
                in_specs=[part(i) for i in range(len(lows))]
                + [
                    pl.BlockSpec((1, sub, width), lambda t, at: (at[count + t], 0, 0)),
                    row_spec,
                    row_spec,
                    pl.BlockSpec((1, width), whole2),
                ],
                out_specs=[
                    pl.BlockSpec((1, sub, width), lambda t, *_: (t, 0, 0)),
                    pl.BlockSpec((2, width), whole2),
                ],
            ),
            out_shape=[
                jax.ShapeDtypeStruct((count, sub, width), BF16),
                jax.ShapeDtypeStruct((2, width), F32),
            ],
            compiler_params=params(),
            cost_estimate=COST,
            name="finish",
        )(jnp.concatenate(table), *lows, low_ff, tokens, cot, gain)

    row_own, sums_own = finish(
        [exchanged(low_own, low_own_x, low_own_z)], [devices], own_dest
    )
    low_shared_x, row_own, sums_own, low_shared, weights_got = tie(
        low_shared_x, row_own, sums_own, low_shared, weights_got
    )
    for step in range(1, len(seq_masks)):
        last_step = step == len(seq_masks) - 1
        weights = cube_add(weights, weights_got, seq_masks[step:], F32 if last_step else BF16)
        if not last_step:
            weights_got = cube_send(weights, "seq", n, seq_masks[step + 1 :])
    weights = weights[0]
    low_shared_z = exchange_z(low_shared, low_shared_x)
    pieces = gather_step([row_own[None]], "mlp", slices, mlp_masks[-1])
    low_shared_z, pieces, weights = tie(low_shared_z, pieces, weights)

    for m in reversed(mlp_masks[:-1]):
        pieces = gather_step(pieces, "mlp", slices, m)
    both = exchanged(low_shared, low_shared_x, low_shared_z)
    even = jnp.bitwise_xor(2 * jnp.arange(pairs, dtype=jnp.int32), rank)
    row_shared, sums = finish([both, both], [even, jnp.bitwise_xor(even, 1)], shared_of)
    last = gather_step([row_shared[None]], "mlp", slices, mlp_masks[-1])
    vectors = small_sum(sums_own + sums, n, slices)
    result = (
        token_cols.astype(F32)
        + summed.astype(F32)
        + lax.dynamic_slice_in_dim(down_bias, column * cols, cols, 0)
    ).astype(BF16)
    last, pieces, vectors, result = tie(last, pieces, vectors, result)

    for m in reversed(mlp_masks[:-1]):
        last = gather_step(last, "mlp", slices, m)
    pieces += last
    where = [(0, 0)]
    lookup = [0]
    for i, m in enumerate(reversed(mlp_masks)):
        where += [(i + 1, j) for j in range(len(lookup))]
        lookup += [k ^ m for k in lookup]
    per_piece = [where[lookup.index(k)] for k in range(slices)]
    tokens_grad = pl.pallas_call(
        functools.partial(settle_kernel, (n, pairs), slices, sub, per_piece),
        grid_spec=pltpu.PrefetchScalarGridSpec(
            num_scalar_prefetch=1,
            grid=(1,),
            in_specs=[pl.BlockSpec(memory_space=pl.ANY)] * len(pieces),
            out_specs=pl.BlockSpec(memory_space=pl.ANY),
            scratch_shapes=[
                pltpu.VMEM((packs * slices, sub, width), BF16),
                pltpu.SemaphoreType.DMA((packs * slices,)),
                pltpu.SemaphoreType.DMA((packs * slices,)),
            ],
        ),
        out_shape=jax.ShapeDtypeStruct((packs, shard, width), BF16),
        compiler_params=params(),
        name="settle",
    )(jnp.concatenate([own_dest, shared_of, column.reshape(1)]), *pieces)

    part, hidden_here = width // n, up_weight.shape[1]
    return (
        result,
        tokens_grad,
        vectors[0],
        vectors[1],
        jnp.transpose(weights[: 3 * joined].reshape(3, joined, part), (0, 2, 1)),
        weights[3 * joined :],
        terms[:part, :hidden_here],
        terms[part, : hidden_here // n],
        terms[:part, hidden_here:].T,
        terms[part, hidden_here // n : hidden_here // n + part],
    )


def solution(mesh):
    in_specs = (
        P(None, "seq", None),
        P(),
        P(),
        P(),
        P(),
        P(None, None, "mlp"),
        P("mlp", None),
        P(None, "mlp"),
        P("mlp"),
        P("mlp", None),
        P(),
        P(None, "seq", "mlp"),
    )
    out_specs = (
        P(None, "seq", "mlp"),
        P(None, "seq", None),
        P("seq"),
        P("seq"),
        P(None, "seq", "mlp"),
        P("mlp", "seq"),
        P("seq", "mlp"),
        P(("mlp", "seq")),
        P("mlp", "seq"),
        P("seq"),
    )
    n, slices = mesh.shape["seq"], mesh.shape["mlp"]

    def plan(*args):
        packs, pack_len, _ = args[0].shape
        heads = args[6].shape[0] // HD // slices
        pairs = (
            2 * packs == 3 * n
            and n >= 4
            and heads % 4 == 0
            and (pack_len // n) % 128 == 0
            and (pack_len // n) % (16 * slices) == 0
        )
        return jax.shard_map(
            on_device_pairs if pairs else on_device,
            mesh=mesh,
            in_specs=in_specs,
            out_specs=out_specs,
            check_vma=False,
        )(*args)

    return plan
```

```python
import functools
import math

import jax
import jax.numpy as jnp
from jax import lax
from jax.experimental import pallas as pl
from jax.experimental.pallas import tpu as pltpu
from jax.sharding import PartitionSpec as P

HD = 64
ROT = 32
EPS = 1e-05
NEG = -1e30
BF16 = jnp.bfloat16
F32 = jnp.float32
VMEM_LIMIT = 56 * 1024 * 1024
COST = pl.CostEstimate(flops=1 << 20, bytes_accessed=1 << 20, transcendentals=0)


def dot(a, b, dims=((1,), (0,))):
    return lax.dot_general(a, b, (dims, ((), ())), preferred_element_type=F32)


def layout(lengths, counts, pack_len):
    slots = lengths.shape[-1]
    slot_ids = jnp.arange(slots, dtype=jnp.int32)
    used = slot_ids[None, :] < counts[:, None]
    sizes = jnp.where(used, lengths, 0)
    ends = jnp.cumsum(sizes, axis=-1)
    starts = ends - sizes
    filled = ends[:, -1:]
    place = jnp.arange(pack_len, dtype=jnp.int32)[None, :]
    begin = jnp.max(
        jnp.where(used[:, None, :] & (place[:, :, None] >= starts[:, None, :]), starts[:, None, :], 0),
        axis=-1,
    )
    inside = place < filled
    first = jnp.where(inside, begin, place)
    position = jnp.where(inside, place - begin, place - filled)
    cost = jnp.sum(sizes * sizes, axis=-1)
    return first, position, cost


def turn(values, cosine, sine, heads):
    out = []
    parity = lax.broadcasted_iota(jnp.int32, cosine.shape, 0) % 2
    for h in range(heads):
        part = values[h * HD : h * HD + ROT]
        ahead = jnp.concatenate([part[1:], part[:1]], axis=0)
        behind = jnp.concatenate([part[-1:], part[:-1]], axis=0)
        swapped = jnp.where(parity == 0, -ahead, behind)
        out.append(part * cosine + swapped * sine)
        out.append(values[h * HD + ROT : (h + 1) * HD])
    return jnp.concatenate(out, axis=0)


def head_kernel(n, heads, per, me_ref, pack_ref, x_ref, gain_ref, bias_ref, w_ref, cos_ref, sin_ref, *refs):
    normed_ref, copy_ref, outs, scr = refs[0], refs[1], refs[2:-1], refs[-1]
    s_id, g = pl.program_id(0), pl.program_id(1)
    me = me_ref[0]
    width = heads * HD
    copy_ref[0] = x_ref[0]
    x = x_ref[0].astype(F32)
    cent = x - jnp.mean(x, axis=-1, keepdims=True)
    var = jnp.mean(cent * cent, axis=-1, keepdims=True)
    normed = (cent * lax.rsqrt(var + EPS) * gain_ref[...] + bias_ref[...]).astype(BF16)
    normed_ref[0] = normed
    for j in range(3):
        part = dot(w_ref[j * width : (j + 1) * width, :], normed, ((1,), (1,)))
        if j < 2:
            part = turn(part, cos_ref[0], sin_ref[0], heads)
        if j == 0:
            part = part * (1.0 / math.sqrt(HD))
        part = part.astype(BF16)
        for h in range(heads):
            scr[h, j] = part[h * HD : (h + 1) * HD]
    for at, out in enumerate(outs):
        d = lax.bitwise_xor(jnp.int32(at % n), me)

        @pl.when((d // heads == g) & (s_id // per == at // n))
        def _():
            out[0] = scr[d % heads]


def grad_kernel(n, heads, me_ref, c_ref, w_ref, *refs):
    outs, scr = refs[:n], refs[n]
    g = pl.program_id(1)
    me = me_ref[0]
    part = dot(w_ref[...], c_ref[0], ((1,), (1,))).astype(BF16)
    for h in range(heads):
        scr[h] = part[h * HD : (h + 1) * HD]
    for k in range(n):
        d = lax.bitwise_xor(jnp.int32(k), me)

        @pl.when(d // heads == g)
        def _():
            outs[k][0] = scr[d % heads]


def load_parts(n, me, pairs):
    for k in range(n):
        d = lax.bitwise_xor(jnp.int32(k), me)
        for part, t_ref, n_ref in pairs(k):
            if t_ref is not None:
                t_ref[d] = part
            if n_ref is not None:
                n_ref[d] = part.T


def score_of(block, first, i, kn, q_t):
    rows = lax.broadcasted_iota(jnp.int32, (block, block), 0)
    cols = lax.broadcasted_iota(jnp.int32, (block, block), 1)
    ahead = rows - cols

    def scores(j, at):
        s = dot(kn[at], q_t)
        allowed = (rows >= first - j * block) & (ahead <= (i - j) * block)
        return jnp.where(allowed, s, NEG)

    return scores


def attend_kernel(n, block, skip, me_ref, pack_ref, low_ref, first_ref, *refs):
    qkv, outs, keep_ref, logsum_ref = refs[:n], refs[n : 2 * n], refs[2 * n], refs[2 * n + 1]
    qt, vt, kn = refs[2 * n + 2 :]
    s_id = pl.program_id(0) + skip
    me = me_ref[0]
    load_parts(
        n,
        me,
        lambda k: (
            (qkv[k][0, 0, 0], qt, None),
            (qkv[k][0, 0, 1], None, kn),
            (qkv[k][0, 0, 2], vt, None),
        ),
    )

    def outer(i, carry):
        scores = score_of(block, first_ref[0, pl.ds(i, 1), :], i, kn, qt[i])
        j0 = low_ref[s_id, i]

        def forward(t, state):
            top, total, acc = state
            j = j0 + 2 * t
            at = jnp.minimum(j + 1, n - 1)
            s0, s1 = scores(j, j), scores(j + 1, at)
            peak = jnp.max(jnp.maximum(s0, s1), axis=0, keepdims=True)
            new_top = jnp.maximum(top, peak)
            p0, p1 = jnp.exp(s0 - new_top), jnp.exp(s1 - new_top)
            fade = jnp.exp(top - new_top)
            total = total * fade + jnp.sum(p0 + p1, axis=0, keepdims=True)
            acc = acc * fade + dot(vt[j], p0.astype(BF16)) + dot(vt[at], p1.astype(BF16))
            return new_top, total, acc

        top, total, acc = lax.fori_loop(
            0,
            (i - j0) // 2 + 1,
            forward,
            (
                jnp.full((1, block), NEG, F32),
                jnp.zeros((1, block), F32),
                jnp.zeros((HD, block), F32),
            ),
        )
        keep_ref[0, i] = (acc / total).astype(BF16)
        logsum_ref[0, pl.ds(i, 1), :] = top + jnp.log(total)
        return carry

    lax.fori_loop(0, n, outer, 0)
    for k in range(n):
        outs[k][0] = keep_ref[0, lax.bitwise_xor(jnp.int32(k), me)]


def attend_back_kernel(n, block, skip, me_ref, pack_ref, low_ref, first_ref, *refs):
    keep_ref, logsum_ref = refs[:2]
    qkv, grads, outs = refs[2 : n + 2], refs[n + 2 : 2 * n + 2], refs[2 * n + 2 : 3 * n + 2]
    qt, kt, gt, qn, kn, vn, gn, dk, dv, res = refs[3 * n + 2 :]
    s_id = pl.program_id(0) + skip
    me = me_ref[0]
    load_parts(
        n,
        me,
        lambda k: (
            (qkv[k][0, 0, 0], qt, qn),
            (qkv[k][0, 0, 1], kt, kn),
            (qkv[k][0, 0, 2], None, vn),
            (grads[k][0, 0], gt, gn),
        ),
    )
    dk[...] = jnp.zeros_like(dk)
    dv[...] = jnp.zeros_like(dv)

    def outer(i, carry):
        q_t, g_t, q_n, g_n = qt[i], gt[i], qn[i], gn[i]
        scores = score_of(block, first_ref[0, pl.ds(i, 1), :], i, kn, q_t)
        j0 = low_ref[s_id, i]
        inner = jnp.sum(keep_ref[0, i].astype(F32) * g_t.astype(F32), axis=0, keepdims=True)
        logsum = logsum_ref[0, pl.ds(i, 1), :]

        def one(j, at):
            p = jnp.exp(scores(j, at) - logsum)
            ds = (p * (dot(vn[at], g_t) - inner)).astype(BF16)
            return ds, dot(ds, q_n), dot(p.astype(BF16), g_n), dot(kt[at], ds)

        def backward(t, dq):
            j = j0 + 2 * t
            at = jnp.minimum(j + 1, n - 1)
            _, dk0, dv0, dq0 = one(j, j)
            _, dk1, dv1, dq1 = one(j + 1, at)
            dk[j] += dk0
            dv[j] += dv0
            dk[at] += dk1
            dv[at] += dv1
            return dq + dq0 + dq1

        dq = lax.fori_loop(0, (i - j0) // 2 + 1, backward, jnp.zeros((HD, block), F32))
        res[i, 0] = (dq * (1.0 / math.sqrt(HD))).astype(BF16)
        return carry

    lax.fori_loop(0, n, outer, 0)
    for i in range(n):
        res[i, 1] = dk[i].T.astype(BF16)
        res[i, 2] = dv[i].T.astype(BF16)
    for k in range(n):
        outs[k][0] = res[lax.bitwise_xor(jnp.int32(k), me)]


def merge_kernel(n, heads, slices, me_ref, *refs):
    recv = refs[:n]
    c_ref, merge_ref, branch_ref, out_branch, out_weight, scr, acc = refs[n:]
    s_id, g = pl.program_id(0), pl.program_id(1)
    groups = pl.num_programs(1)
    me = me_ref[0]
    width = heads * HD

    @pl.when((s_id == 0) & (g == 0))
    def _():
        acc[...] = jnp.zeros_like(acc)

    for k in range(n):
        d = lax.bitwise_xor(jnp.int32(k), me)

        @pl.when(d // heads == g)
        def _():
            scr[d % heads] = recv[k][0, 0, 0]

    attended = scr[...].reshape(width, c_ref.shape[1])
    acc[...] += dot(attended, c_ref[0])
    branch = dot(attended.T, merge_ref[...]) + branch_ref[0].astype(F32)
    cols = branch.shape[1] // slices
    for m in range(slices):
        out_branch[m, 0] = branch[:, m * cols : (m + 1) * cols].astype(BF16)

    @pl.when((s_id == pl.num_programs(0) - 1) & (g == groups - 1))
    def _():
        out_weight[...] = acc[...].astype(BF16)


def close_kernel(n, heads, me_ref, *refs):
    recv = refs[:n]
    normed_ref, w_ref, cos_ref, sin_ref, low_ref, out_low, out_weight, scr, acc = refs[n:]
    s_id, g = pl.program_id(0), pl.program_id(1)
    groups = pl.num_programs(1)
    me = me_ref[0]
    width = heads * HD
    shard = normed_ref.shape[1]

    @pl.when((s_id == 0) & (g == 0))
    def _():
        acc[...] = jnp.zeros_like(acc)

    for k in range(n):
        d = lax.bitwise_xor(jnp.int32(k), me)

        @pl.when(d // heads == g)
        def _():
            for j in range(3):
                scr[j, d % heads] = recv[k][0, 0, j]

    parts = []
    for j in (0, 1):
        part = scr[j].reshape(width, shard).astype(F32)
        parts.append(turn(part, cos_ref[0], -sin_ref[0], heads).astype(BF16))
    parts.append(scr[2].reshape(width, shard))
    grads = jnp.concatenate(parts, axis=0)
    acc[...] += dot(grads, normed_ref[0])
    low = dot(grads.T, w_ref[...]) + low_ref[0].astype(F32)
    out_low[0] = low.astype(BF16)

    @pl.when((s_id == pl.num_programs(0) - 1) & (g == groups - 1))
    def _():
        out_weight[...] = acc[...]


def place_kernel(block, share, shard, slices, chunks, per_piece, pack_ref, *refs):
    pieces, out, buf, sems, out_sems = refs[:-4], refs[-4], refs[-3], refs[-2], refs[-1]
    me = pack_ref[chunks * slices * share // shard]
    loads, stores = [], []
    arrays = max(ref for ref, _ in per_piece) + 1
    for c in range(chunks):
        for k in range(slices):
            ref, where = per_piece[k]
            for t in range(share // block):
                at = len(loads)
                row = (c * slices + lax.bitwise_xor(jnp.int32(k), me)) * share + t * block
                start = pl.multiple_of(lax.rem(row, shard), block)
                loads.append(
                    pltpu.make_async_copy(
                        pieces[c * arrays + ref].at[where, pl.ds(t * block, block)],
                        buf.at[at],
                        sems.at[at],
                    )
                )
                stores.append(
                    pltpu.make_async_copy(
                        buf.at[at],
                        out.at[pack_ref[row // shard], pl.ds(start, block)],
                        out_sems.at[at],
                    )
                )
    for copy in loads:
        copy.start()
    for load, store in zip(loads, stores):
        load.wait()
        store.start()
    for copy in stores:
        copy.wait()


def small_kernel(n, slices, x_ref, out_ref, first, second, sems, sems2):
    rank, column = lax.axis_index("seq"), lax.axis_index("mlp")
    barrier = pltpu.get_barrier_semaphore()
    peers = [{"seq": lax.bitwise_xor(rank, k)} for k in range(1, n)]
    rows = [{"mlp": lax.bitwise_xor(column, k)} for k in range(1, slices)]
    for peer in peers + rows:
        pl.semaphore_signal(barrier, inc=1, device_id=peer, device_id_type=pl.DeviceIdType.MESH)
    pl.semaphore_wait(barrier, len(peers) + len(rows))

    def exchange(source, target, sems, peers):
        copies = [
            pltpu.make_async_remote_copy(
                src_ref=source(k),
                dst_ref=target.at[k],
                send_sem=sems.at[0, k],
                recv_sem=sems.at[1, k],
                device_id=peer,
                device_id_type=pl.DeviceIdType.MESH,
            )
            for k, peer in enumerate(peers)
        ]
        for copy in copies:
            copy.start()
        for copy in copies:
            copy.wait()

    exchange(lambda k: x_ref.at[lax.bitwise_xor(rank, k + 1)], first, sems, peers)
    total = x_ref[rank]
    for k in range(n - 1):
        total = total + first[k]
    second[slices - 1] = total
    second[slices] = total
    exchange(lambda k: second.at[slices], second, sems2, rows)
    parts = [
        second[jnp.where(column == c, slices - 1, lax.bitwise_xor(column, c) - 1)]
        for c in range(slices)
    ]
    out_ref[...] = functools.reduce(jnp.add, parts)


def small_sum(vectors, n, slices):
    count, width = vectors.shape
    x = jnp.transpose(vectors.reshape(count, n, width // n), (1, 0, 2))
    return pl.pallas_call(
        functools.partial(small_kernel, n, slices),
        out_shape=jax.ShapeDtypeStruct((count, width // n), F32),
        in_specs=[pl.BlockSpec(memory_space=pltpu.VMEM)],
        out_specs=pl.BlockSpec(memory_space=pltpu.VMEM),
        scratch_shapes=[
            pltpu.VMEM((n - 1, count, width // n), F32),
            pltpu.VMEM((slices + 1, count, width // n), F32),
            pltpu.SemaphoreType.DMA((2, n - 1)),
            pltpu.SemaphoreType.DMA((2, slices - 1)),
        ],
        compiler_params=pltpu.CompilerParams(collective_id=0, has_side_effects=True),
        cost_estimate=COST,
        name="small_sum",
    )(x)


def params():
    return pltpu.CompilerParams(vmem_limit_bytes=VMEM_LIMIT)


def tie(*values):
    return lax.optimization_barrier(values)


def send_x(parts):
    n = len(parts)
    sent = jnp.stack([parts[k] for k in range(1, n, 2)])
    return lax.ppermute(sent, "seq", [(i, i ^ 1) for i in range(n)])


def send_z(parts, got, steps=None):
    n = len(parts)
    return [
        lax.ppermute(
            jnp.stack([parts[k], got[k // 2]]), "seq", [(i, i ^ k) for i in range(n)]
        )
        for k in (range(2, n, 2) if steps is None else steps)
    ]


def received(parts, got, gots):
    out = [(parts[0][None], 0), (got, 0)]
    for array in gots:
        out += [(array, 0), (array, 1)]
    return out


def span(masks):
    out = [0]
    for m in masks:
        out += [v ^ m for v in out]
    return out


def cube_send(chunks, axis, n, masks):
    kept = span(masks[1:])
    sent = jnp.stack([chunks[k ^ masks[0]] for k in kept])
    return lax.ppermute(sent, axis, [(i, i ^ masks[0]) for i in range(n)])


def cube_add(chunks, got, masks, kind):
    return {
        k: (chunks[k].astype(F32) + got[at].astype(F32)).astype(kind)
        for at, k in enumerate(span(masks[1:]))
    }


def cube_sum(chunks, axis, masks, kind):
    n = len(chunks)
    chunks = {k: v.astype(kind) for k, v in enumerate(chunks)}
    for step in range(len(masks)):
        got = cube_send(chunks, axis, n, masks[step:])
        chunks = cube_add(chunks, got, masks[step:], F32 if step == len(masks) - 1 else kind)
    return chunks[0]


def gather_step(arrays, axis, n, m):
    sent = jnp.concatenate(arrays, axis=0) if len(arrays) > 1 else arrays[0]
    return arrays + [lax.ppermute(sent, axis, [(i, i ^ m) for i in range(n)])]


def masks_of(n):
    return [1 << b for b in range(n.bit_length() - 1)]


def turned(masks, by):
    by = by % len(masks)
    return masks[by:] + masks[:by]


def cut(array, axis, n, me):
    size = array.shape[axis] // n
    return [
        lax.dynamic_slice_in_dim(array, lax.bitwise_xor(jnp.int32(k), me) * size, size, axis)
        for k in range(n)
    ]


def on_device(
    tokens,
    lengths,
    counts,
    norm_gain,
    norm_bias,
    head_weight,
    merge_weight,
    up_weight,
    up_bias,
    down_weight,
    down_bias,
    cotangent,
):
    packs, shard, width = tokens.shape
    n = lax.axis_size("seq")
    slices = lax.axis_size("mlp")
    pack_len = shard * n
    rank = lax.axis_index("seq")
    column = lax.axis_index("mlp")
    heads = merge_weight.shape[0] // HD
    joined = heads * HD
    groups = n // heads
    slots = -(-packs // groups)
    dealt = groups * slots
    spare = 1 if dealt > packs else 0
    rows = dealt * shard
    chunks = 2 if slots % 2 == 0 else 1
    per = slots // chunks
    seq_masks, mlp_masks = masks_of(n), masks_of(slices)

    first, position, cost = layout(lengths, counts, pack_len)
    ids = jnp.arange(packs, dtype=jnp.int32)
    before = (cost[None, :] > cost[:, None]) | (
        (cost[None, :] == cost[:, None]) & (ids[None, :] < ids[:, None])
    )
    order = jnp.sum(before.astype(jnp.int32), axis=1)
    slot_of = order // groups
    group_of = jnp.where(slot_of % 2 == 0, order % groups, groups - 1 - order % groups)
    at = slot_of * groups + group_of
    hit = at[None, :] == jnp.arange(dealt, dtype=jnp.int32)[:, None]
    pack_at = jnp.where(
        jnp.any(hit, axis=-1), jnp.sum(jnp.where(hit, ids, 0), axis=-1), packs
    ).astype(jnp.int32)
    safe = jnp.minimum(pack_at, packs - 1)
    me = rank.astype(jnp.int32).reshape(1)

    own_cot = jnp.take(cotangent, safe, axis=0, mode="clip")
    if spare:
        own_cot = jnp.where((pack_at < packs)[:, None, None], own_cot, 0)
    cot = lax.all_gather(own_cot, "mlp", axis=2, tiled=True)

    half = ROT // 2
    freq = 10000.0 ** (-(2.0 * jnp.arange(half, dtype=F32)) / ROT)
    own_position = jnp.take(
        lax.dynamic_slice_in_dim(position, rank * shard, shard, 1), safe, axis=0, mode="clip"
    )
    angle = own_position.astype(F32)[:, None, :] * jnp.repeat(freq, 2)[None, :, None]
    cosine, sine = jnp.cos(angle), jnp.sin(angle)

    w_t = jnp.transpose(head_weight, (0, 2, 1)).reshape(3 * joined, width)

    def whole2(s, g, *_):
        return (0, 0)

    def rows_at(skip):
        return pl.BlockSpec((1, shard, width), lambda s, g, *_: ((s + skip) * groups + g, 0, 0))

    def table_at(skip):
        return pl.BlockSpec((1, ROT, shard), lambda s, g, *_: ((s + skip) * groups + g, 0, 0))

    parts = [jax.ShapeDtypeStruct((per, 3, HD, shard), BF16)] * n

    def chunk_at(c):
        return pl.BlockSpec(
            (1, 3, HD, shard), lambda s, g, *_: (jnp.clip(s - c * per, 0, per - 1), 0, 0, 0)
        )

    outs = pl.pallas_call(
        functools.partial(head_kernel, n, heads, per),
        grid_spec=pltpu.PrefetchScalarGridSpec(
            num_scalar_prefetch=2,
            grid=(slots, groups),
            in_specs=[
                pl.BlockSpec((1, shard, width), lambda s, g, a, b: (b[s * groups + g], 0, 0)),
                pl.BlockSpec((1, width), whole2),
                pl.BlockSpec((1, width), whole2),
                pl.BlockSpec((3 * joined, width), whole2),
                table_at(0),
                table_at(0),
            ],
            out_specs=[rows_at(0)] * 2 + [chunk_at(c) for c in range(chunks) for _ in range(n)],
            scratch_shapes=[pltpu.VMEM((heads, 3, HD, shard), BF16)],
        ),
        out_shape=[jax.ShapeDtypeStruct((dealt, shard, width), BF16)] * 2 + parts * chunks,
        compiler_params=params(),
        cost_estimate=COST,
        name="heads",
    )(
        me,
        safe,
        tokens,
        norm_gain.reshape(1, width),
        norm_bias.reshape(1, width),
        w_t,
        cosine,
        sine,
    )
    normed_low, tokens_dealt = outs[0], outs[1]
    qkv = [list(outs[2 + c * n : 2 + (c + 1) * n]) for c in range(chunks)]

    def out_grads(cot, merge_weight):
        return pl.pallas_call(
            functools.partial(grad_kernel, n, heads),
            grid_spec=pltpu.PrefetchScalarGridSpec(
                num_scalar_prefetch=1,
                grid=(slots, groups),
                in_specs=[rows_at(0), pl.BlockSpec((joined, width), whole2)],
                out_specs=[pl.BlockSpec((1, HD, shard), lambda s, g, *_: (s, 0, 0))] * n,
                scratch_shapes=[pltpu.VMEM((heads, HD, shard), BF16)],
            ),
            out_shape=[jax.ShapeDtypeStruct((slots, HD, shard), BF16)] * n,
            compiler_params=params(),
            cost_estimate=COST,
            name="out_grads",
        )(me, cot, merge_weight)

    mine = rank // heads + groups * jnp.arange(slots, dtype=jnp.int32)
    my_packs = jnp.take(safe, mine, mode="clip")
    first = first.reshape(packs, n, shard)
    lows = (jnp.take(first[:, :, 0], my_packs, axis=0, mode="clip") // shard).astype(jnp.int32)
    wide = [pltpu.VMEM((n, HD, shard), BF16)]
    tall = [pltpu.VMEM((n, shard, HD), BF16)]

    def first_at(skip):
        return pl.BlockSpec((1, n, shard), lambda s, a, b, c: (b[s + skip], 0, 0))

    def qkv_at(lead):
        return pl.BlockSpec((1, 1, 3, HD, shard), lambda s, *_: (lead, s, 0, 0, 0))

    def grad_at(lead, skip):
        return pl.BlockSpec((1, 1, HD, shard), lambda s, *_: (lead, s + skip, 0, 0))

    def attend(c, sources):
        return pl.pallas_call(
            functools.partial(attend_kernel, n, shard, c * per),
            grid_spec=pltpu.PrefetchScalarGridSpec(
                num_scalar_prefetch=3,
                grid=(per,),
                in_specs=[first_at(c * per)] + [qkv_at(lead) for _, lead in sources],
                out_specs=[pl.BlockSpec((1, HD, shard), lambda s, *_: (s, 0, 0))] * n
                + [
                    pl.BlockSpec((1, n, HD, shard), lambda s, *_: (s, 0, 0, 0)),
                    pl.BlockSpec((1, n, shard), lambda s, *_: (s, 0, 0)),
                ],
                scratch_shapes=wide * 2 + tall,
            ),
            out_shape=[jax.ShapeDtypeStruct((per, HD, shard), BF16)] * n
            + [
                jax.ShapeDtypeStruct((per, n, HD, shard), BF16),
                jax.ShapeDtypeStruct((per, n, shard), F32),
            ],
            compiler_params=params(),
            cost_estimate=COST,
            name="attend",
        )(me, my_packs, lows, first, *[array for array, _ in sources])

    def attend_back(c, kept, logsum, sources, grads):
        return pl.pallas_call(
            functools.partial(attend_back_kernel, n, shard, c * per),
            grid_spec=pltpu.PrefetchScalarGridSpec(
                num_scalar_prefetch=3,
                grid=(per,),
                in_specs=[
                    first_at(c * per),
                    pl.BlockSpec((1, n, HD, shard), lambda s, *_: (s, 0, 0, 0)),
                    pl.BlockSpec((1, n, shard), lambda s, *_: (s, 0, 0)),
                ]
                + [qkv_at(lead) for _, lead in sources]
                + [grad_at(lead, c * per) for _, lead in grads],
                out_specs=[pl.BlockSpec((1, 3, HD, shard), lambda s, *_: (s, 0, 0, 0))] * n,
                scratch_shapes=wide * 3
                + tall * 4
                + [pltpu.VMEM((n, shard, HD), F32)] * 2
                + [pltpu.VMEM((n, 3, HD, shard), BF16)],
            ),
            out_shape=parts,
            compiler_params=params(),
            cost_estimate=COST,
            name="attend_back",
        )(
            me,
            my_packs,
            lows,
            first,
            kept,
            logsum,
            *[array for array, _ in sources],
            *[array for array, _ in grads],
        )

    def merge(sources, branch_ff):
        return pl.pallas_call(
            functools.partial(merge_kernel, n, heads, slices),
            grid_spec=pltpu.PrefetchScalarGridSpec(
                num_scalar_prefetch=1,
                grid=(slots, groups),
                in_specs=[
                    pl.BlockSpec(
                        (1, 1, 1, HD, shard),
                        lambda s, g, *_, lead=lead: (lead, s // per, s % per, 0, 0),
                    )
                    for _, lead in sources
                ]
                + [rows_at(0), pl.BlockSpec((joined, width), whole2), rows_at(0)],
                out_specs=[
                    pl.BlockSpec(
                        (slices, 1, shard, width // slices),
                        lambda s, g, *_: (0, s * groups + g, 0, 0),
                    ),
                    pl.BlockSpec((joined, width), whole2),
                ],
                scratch_shapes=[
                    pltpu.VMEM((heads, HD, shard), BF16),
                    pltpu.VMEM((joined, width), F32),
                ],
            ),
            out_shape=[
                jax.ShapeDtypeStruct((slices, dealt, shard, width // slices), BF16),
                jax.ShapeDtypeStruct((joined, width), BF16),
            ],
            compiler_params=params(),
            cost_estimate=COST,
            name="merge",
        )(me, *[array for array, _ in sources], cot, merge_weight, branch_ff)

    def close(c, sources):
        skip = c * per
        return pl.pallas_call(
            functools.partial(close_kernel, n, heads),
            grid_spec=pltpu.PrefetchScalarGridSpec(
                num_scalar_prefetch=1,
                grid=(per, groups),
                in_specs=[
                    pl.BlockSpec(
                        (1, 1, 3, HD, shard), lambda s, g, *_, lead=lead: (lead, s, 0, 0, 0)
                    )
                    for _, lead in sources
                ]
                + [
                    rows_at(skip),
                    pl.BlockSpec((3 * joined, width), whole2),
                    table_at(skip),
                    table_at(skip),
                    rows_at(skip),
                ],
                out_specs=[rows_at(0), pl.BlockSpec((3 * joined, width), whole2)],
                scratch_shapes=[
                    pltpu.VMEM((3, heads, HD, shard), BF16),
                    pltpu.VMEM((3 * joined, width), F32),
                ],
            ),
            out_shape=[
                jax.ShapeDtypeStruct((per * groups, shard, width), BF16),
                jax.ShapeDtypeStruct((3 * joined, width), F32),
            ],
            compiler_params=params(),
            cost_estimate=COST,
            name="close",
        )(me, *[array for array, _ in sources], normed_low, w_t, cosine, sine, low_ff)

    got_x = [None] * chunks
    got_z = [None] * chunks
    got_x[0] = send_x(qkv[0])
    hidden = (
        jnp.einsum("psd,df->psf", normed_low, up_weight, preferred_element_type=F32) + up_bias
    )
    active_low = jax.nn.gelu(hidden, approximate=True).astype(BF16)
    branch_ff = jnp.einsum(
        "psf,fd->psd", active_low, down_weight, preferred_element_type=F32
    ).astype(BF16)
    got_x[0], branch_ff, qkv, out_weight, back_weight = tie(
        got_x[0], branch_ff, qkv, merge_weight, down_weight
    )

    got_z[0] = send_z(qkv[0], got_x[0])
    if chunks > 1:
        got_x[1] = send_x(qkv[1])
    sends = out_grads(cot, out_weight)
    active_grad = jnp.einsum("psd,fd->psf", cot, back_weight, preferred_element_type=F32)
    _, gelu_back = jax.vjp(lambda values: jax.nn.gelu(values, approximate=True), hidden)
    hidden_grad = gelu_back(active_grad)[0].astype(BF16)
    got_x, got_z, qkv, sends, hidden_grad = tie(got_x, got_z, qkv, sends, hidden_grad)

    got_dx = send_x(sends)
    sources = [received(qkv[0], got_x[0], got_z[0])]
    if chunks > 1:
        got_z[1] = send_z(qkv[1], got_x[1])
        sources.append(received(qkv[1], got_x[1], got_z[1]))
    ahead = [attend(0, sources[0])]
    up_grad = jnp.einsum(
        "psd,psf->df", normed_low, hidden_grad, preferred_element_type=F32
    ).astype(BF16)
    down_grad = jnp.einsum("psd,psf->df", cot, active_low, preferred_element_type=F32).astype(BF16)
    biases = jnp.sum(hidden_grad.astype(F32), axis=(0, 1)), jnp.sum(cot.astype(F32), axis=(0, 1))
    got_dx, sources_arrays, ahead, sends, hidden_grad, up_grad, down_grad, biases = tie(
        got_dx,
        [[a for a, _ in v] for v in sources],
        ahead,
        sends,
        hidden_grad,
        up_grad,
        down_grad,
        biases,
    )
    def with_row(*parts):
        weight = jnp.concatenate(parts[:2], axis=1)
        row = jnp.concatenate(parts[2:])
        row = jnp.pad(row, (0, weight.shape[1] - row.shape[0])).reshape(1, -1)
        row = jnp.broadcast_to(row, (16, weight.shape[1])).astype(BF16)
        return jnp.concatenate([weight, row], axis=0)

    terms = dict(
        enumerate(
            with_row(*parts)
            for parts in zip(*[cut(v, 0, n, rank) for v in (up_grad, down_grad, *biases)])
        )
    )
    terms_got = cube_send(terms, "seq", n, seq_masks)
    sources = [
        [(a, lead) for a, (_, lead) in zip(arrays, v)] for arrays, v in zip(sources_arrays, sources)
    ]

    got_dz = send_z(sends, got_dx)
    if chunks > 1:
        ahead.append(attend(1, sources[1]))
    low_ff = jnp.einsum(
        "psf,df->psd", hidden_grad, up_weight, preferred_element_type=F32
    ).astype(BF16)
    got_dz, ahead, low_ff = tie(got_dz, ahead, low_ff)
    grads = received(sends, got_dx, got_dz)

    attended = [jnp.stack([outs[k] for outs in ahead]) for k in range(n)]
    got_ax = send_x(attended)
    backs = [attend_back(0, ahead[0][n], ahead[0][n + 1], sources[0], grads)]
    got_ax, terms_got, backs, attended, ahead = tie(got_ax, terms_got, backs, attended, ahead)

    terms = cube_add(terms, terms_got, seq_masks, BF16)
    terms_got = cube_send(terms, "seq", n, seq_masks[1:])
    got_az = send_z(attended, got_ax)
    back_x = [send_x(backs[0])]
    if chunks > 1:
        backs.append(attend_back(1, ahead[1][n], ahead[1][n + 1], sources[1], grads))
    got_az, terms_got, back_x, backs = tie(got_az, terms_got, back_x, backs)

    back_z = [send_z(backs[0], back_x[0])]
    if chunks > 1:
        back_x.append(send_x(backs[1]))
    for step in range(1, len(seq_masks)):
        last_step = step == len(seq_masks) - 1
        terms = cube_add(terms, terms_got, seq_masks[step:], F32 if last_step else BF16)
        if not last_step:
            terms_got = cube_send(terms, "seq", n, seq_masks[step + 1 :])
    terms = terms[0]
    branch, merge_part = merge(received(attended, got_ax, got_az), branch_ff)
    summed = lax.psum_scatter(branch, "mlp", scatter_dimension=0, tiled=False)
    back_x, back_z, backs, merge_part, terms = tie(back_x, back_z, backs, merge_part, terms)

    share = per * groups * shard // slices

    def share_sum(low):
        return cube_sum(
            cut(low.reshape(share * slices, width), 0, slices, column), "mlp", mlp_masks, BF16
        )

    def finish(c, low_sum):
        start = (c * slices + column) * share
        row_in = lax.dynamic_slice_in_dim(
            tokens_dealt.reshape(rows, width), start, share, 0
        ).astype(F32)
        row_cot = lax.dynamic_slice_in_dim(cot.reshape(rows, width), start, share, 0).astype(F32)
        cent = row_in - jnp.mean(row_in, axis=-1, keepdims=True)
        inverse = lax.rsqrt(jnp.mean(cent * cent, axis=-1, keepdims=True) + EPS)
        xhat = cent * inverse
        g = low_sum * norm_gain
        row_grad = (
            row_cot
            + (
                g
                - jnp.mean(g, axis=-1, keepdims=True)
                - xhat * jnp.mean(g * xhat, axis=-1, keepdims=True)
            )
            * inverse
        ).astype(BF16)
        return row_grad, jnp.stack([jnp.sum(low_sum * xhat, axis=0), jnp.sum(low_sum, axis=0)])

    low, head_part = close(0, received(backs[0], back_x[0], back_z[0]))
    head_parts = [head_part]
    if chunks > 1:
        second = send_z(backs[1], back_x[1], [n // 2])
        second, low, head_parts, backs, back_x = tie(second, low, head_parts, backs, back_x)
        others = send_z(backs[1], back_x[1], [k for k in range(2, n, 2) if k != n // 2])
        others.insert(n // 4 - 1, second[0])
        back_z.append(others)
    row_grad, vectors = finish(0, share_sum(low))
    back_z, row_grad, vectors = tie(back_z, row_grad, vectors)

    cols = width // slices
    pieces = gather_step([row_grad[None]], "mlp", slices, mlp_masks[-1])
    result = (
        lax.dynamic_slice_in_dim(tokens, column * cols, cols, 2).astype(F32)
        + jnp.take(summed, at, axis=0, mode="clip").astype(F32)
        + lax.dynamic_slice_in_dim(down_bias, column * cols, cols, 0)
    ).astype(BF16)
    if chunks > 1:
        low, head_part = close(1, received(backs[1], back_x[1], back_z[1]))
        head_parts.append(head_part)
        pieces, low, head_parts, result = tie(pieces, low, head_parts, result)
    weights = functools.reduce(jnp.add, head_parts)
    weights = jnp.concatenate([weights.astype(BF16), merge_part], axis=0)
    weights = dict(enumerate(cut(weights, 1, n, rank)))
    weights_got = cube_send(weights, "seq", n, seq_masks)
    if chunks > 1:
        low_sum = share_sum(low)
        for m in reversed(mlp_masks[:-1]):
            pieces = gather_step(pieces, "mlp", slices, m)
        row_grad, more = finish(1, low_sum)
        vectors = vectors + more
        row_grad, pieces, weights_got, vectors = tie(row_grad, pieces, weights_got, vectors)
        last = gather_step([row_grad[None]], "mlp", slices, mlp_masks[-1])
    else:
        last, pieces = pieces, []
    vectors = small_sum(vectors, n, slices)
    weights = cube_add(weights, weights_got, seq_masks, BF16)
    weights_got = cube_send(weights, "seq", n, seq_masks[1:])
    last, vectors, weights_got = tie(last, vectors, weights_got)
    for m in reversed(mlp_masks[:-1]):
        last = gather_step(last, "mlp", slices, m)
    pieces += last
    where = [(0, 0)]
    lookup = [0]
    for i, m in enumerate(reversed(mlp_masks)):
        where += [(i + 1, j) for j in range(len(lookup))]
        lookup += [k ^ m for k in lookup]
    per_piece = [where[lookup.index(k)] for k in range(slices)]
    block = math.gcd(share, shard)
    tokens_grad = pl.pallas_call(
        functools.partial(
            place_kernel, block, share, shard, slices, chunks, per_piece
        ),
        grid_spec=pltpu.PrefetchScalarGridSpec(
            num_scalar_prefetch=1,
            grid=(1,),
            in_specs=[pl.BlockSpec(memory_space=pl.ANY)] * len(pieces),
            out_specs=pl.BlockSpec(memory_space=pl.ANY),
            scratch_shapes=[
                pltpu.VMEM((rows // block, block, width), BF16),
                pltpu.SemaphoreType.DMA((rows // block,)),
                pltpu.SemaphoreType.DMA((rows // block,)),
            ],
        ),
        out_shape=jax.ShapeDtypeStruct((packs + spare, shard, width), BF16),
        compiler_params=params(),
        name="place",
    )(jnp.concatenate([pack_at, column.astype(jnp.int32).reshape(1)]), *pieces)[:packs]

    for step in range(1, len(seq_masks)):
        weights = cube_add(
            weights, weights_got, seq_masks[step:], F32 if step == len(seq_masks) - 1 else BF16
        )
        if step < len(seq_masks) - 1:
            weights_got = cube_send(weights, "seq", n, seq_masks[step + 1 :])
    weights = weights[0]
    head_grad = jnp.transpose(
        weights[: 3 * joined].reshape(3, joined, width // n), (0, 2, 1)
    )
    merge_grad = weights[3 * joined :]
    part, hidden_here = width // n, up_weight.shape[1]
    up_grad, down_grad = terms[:part, :hidden_here], terms[:part, hidden_here:].T
    up_bias_grad = terms[part, : hidden_here // n]
    down_bias_grad = terms[part, hidden_here // n : hidden_here // n + part]
    return (
        result,
        tokens_grad,
        vectors[0],
        vectors[1],
        head_grad,
        merge_grad,
        up_grad,
        up_bias_grad,
        down_grad,
        down_bias_grad,
    )


def qkv_kernel(heads, me_ref, x_ref, w_ref, cos_ref, sin_ref, normed_ref, out_ref):
    width = heads * HD
    normed = x_ref[0]
    normed_ref[...] = normed
    for j in range(3):
        part = dot(w_ref[j * width : (j + 1) * width, :], normed, ((1,), (1,)))
        if j < 2:
            part = turn(part, cos_ref[...], sin_ref[...], heads)
        if j == 0:
            part = part * (1.0 / math.sqrt(HD))
        part = part.astype(BF16)
        for h in range(heads):
            out_ref[h, j] = part[h * HD : (h + 1) * HD]


def allowed_of(block, first, i):
    rows = lax.broadcasted_iota(jnp.int32, (block, block), 0)
    cols = lax.broadcasted_iota(jnp.int32, (block, block), 1)
    ahead = rows - cols
    return lambda j: (rows >= first - j * block) & (ahead <= (i - j) * block)


def unit_kernel(n, block, me_ref, low_ref, first_ref, qkv_ref, out_ref, keep_ref, logsum_ref, qt, vt, kn):
    me = me_ref[0]
    pair = range(qkv_ref.shape[0])
    for u in pair:
        for i in range(n):
            at = slice(i * block, (i + 1) * block)
            qt[u, i] = qkv_ref[u, 0, :, at]
            kn[u, i] = qkv_ref[u, 1, :, at].T
            vt[u, i] = qkv_ref[u, 2, :, at]

    def outer(i, carry):
        allowed = allowed_of(block, first_ref[pl.ds(i, 1), :], i)
        j0 = low_ref[i]

        def forward(t, states):
            j = j0 + 2 * t
            at = jnp.minimum(j + 1, n - 1)
            mask0, mask1 = allowed(j), allowed(j + 1)
            out = []
            for u, (top, total, acc) in zip(pair, states):
                q_t = qt[u, i]
                s0 = jnp.where(mask0, dot(kn[u, j], q_t), NEG)
                s1 = jnp.where(mask1, dot(kn[u, at], q_t), NEG)
                peak = jnp.max(jnp.maximum(s0, s1), axis=0, keepdims=True)
                new_top = jnp.maximum(top, peak)
                p0, p1 = jnp.exp(s0 - new_top), jnp.exp(s1 - new_top)
                fade = jnp.exp(top - new_top)
                total = total * fade + jnp.sum(p0 + p1, axis=0, keepdims=True)
                acc = acc * fade + dot(vt[u, j], p0.astype(BF16)) + dot(vt[u, at], p1.astype(BF16))
                out.append((new_top, total, acc))
            return tuple(out)

        states = lax.fori_loop(
            0,
            (i - j0) // 2 + 1,
            forward,
            tuple(
                (
                    jnp.full((1, block), NEG, F32),
                    jnp.zeros((1, block), F32),
                    jnp.zeros((HD, block), F32),
                )
                for _ in pair
            ),
        )
        for u, (top, total, acc) in zip(pair, states):
            keep_ref[u, i] = (acc / total).astype(BF16)
            logsum_ref[u, pl.ds(i, 1), :] = top + jnp.log(total)
        return carry

    lax.fori_loop(0, n, outer, 0)
    for k in range(n):
        for u in pair:
            out_ref[k, u] = keep_ref[u, lax.bitwise_xor(jnp.int32(k), me)]


def unit_back_kernel(
    n, block, by, me_ref, low_ref, first_ref, keep_ref, logsum_ref, qkv_ref, grad_ref, out_ref,
    qt, kt, gt, qn, kn, vn, gn, dk, dv, dqs
):
    me = me_ref[0]
    pair = range(qkv_ref.shape[0])
    for u in pair:
        for i in range(n):
            at = slice(i * block, (i + 1) * block)
            for j, (t_ref, n_ref) in enumerate(((qt, qn), (kt, kn), (None, vn))):
                part = qkv_ref[u, j, :, at]
                if t_ref is not None:
                    t_ref[u, i] = part
                n_ref[u, i] = part.T
        for k in range(n):
            d = lax.bitwise_xor(jnp.int32(k), me)
            part = grad_ref[k, u]
            gt[u, d] = part
            gn[u, d] = part.T
    dk[...] = jnp.zeros_like(dk)
    dv[...] = jnp.zeros_like(dv)

    def outer(i, carry):
        allowed = allowed_of(block, first_ref[pl.ds(i, 1), :], i)
        j0 = low_ref[i]
        inner = [
            jnp.sum(keep_ref[u, i].astype(F32) * gt[u, i].astype(F32), axis=0, keepdims=True)
            for u in pair
        ]
        logsum = [logsum_ref[u, pl.ds(i, 1), :] for u in pair]

        def one(u, mask, at):
            s = jnp.where(mask, dot(kn[u, at], qt[u, i]), NEG)
            p = jnp.exp(s - logsum[u])
            ds = (p * (dot(vn[u, at], gt[u, i]) - inner[u])).astype(BF16)
            return dot(ds, qn[u, i]), dot(p.astype(BF16), gn[u, i]), dot(kt[u, at], ds)

        def backward(t, dqs):
            j = j0 + by * t
            spots = [jnp.minimum(j + b, n - 1) if b else j for b in range(by)]
            masks = [allowed(j + b) for b in range(by)]
            out = []
            for u, dq in zip(pair, dqs):
                terms = [one(u, mask, at) for mask, at in zip(masks, spots)]
                for (dk0, dv0, dq0), at in zip(terms, spots):
                    dk[u, at] += dk0
                    dv[u, at] += dv0
                    dq = dq + dq0
                out.append(dq)
            return tuple(out)

        dq = lax.fori_loop(
            0, (i - j0) // by + 1, backward, tuple(jnp.zeros((HD, block), F32) for _ in pair)
        )
        for u in pair:
            dqs[u, i] = (dq[u] * (1.0 / math.sqrt(HD))).astype(BF16)
        return carry

    lax.fori_loop(0, n, outer, 0)
    for u in pair:
        for i in range(n):
            at = slice(i * block, (i + 1) * block)
            out_ref[u, 0, :, at] = dqs[u, i]
            out_ref[u, 1, :, at] = dk[u, i].T.astype(BF16)
            out_ref[u, 2, :, at] = dv[u, i].T.astype(BF16)


def rows_kernel(heads, slices, me_ref, grad_ref, normed_ref, w_ref, cos_ref, sin_ref, *refs):
    low_ref, weight_ref = refs[-2:]
    width = heads * HD
    column = me_ref[1]

    @pl.when(pl.program_id(0) == 0)
    def _():
        if len(refs) > 2:
            weight_ref[...] = refs[0][...]
        else:
            weight_ref[...] = jnp.zeros_like(weight_ref)

    parts = []
    for j in range(3):
        part = jnp.concatenate([grad_ref[h, j] for h in range(heads)], axis=0)
        if j < 2:
            part = turn(part.astype(F32), cos_ref[...], -sin_ref[...], heads).astype(BF16)
        parts.append(part)
    grads = jnp.concatenate(parts, axis=0)
    if len(refs) > 2:
        whole = weight_ref.shape[0] // 3
        start = lax.rem(me_ref[0], 2) * width
        for j in range(3):
            rows = pl.ds(pl.multiple_of(j * whole + start, width), width)
            weight_ref[rows, :] += dot(parts[j], normed_ref[...])
    else:
        weight_ref[...] += dot(grads, normed_ref[...])
    low = dot(grads.T, w_ref[...]).astype(BF16)
    part = low.shape[0] // slices
    for m in range(slices):
        low_ref[lax.bitwise_xor(jnp.int32(m), column), 0] = low[m * part : (m + 1) * part]


def norm_kernel(x_ref, gain_ref, bias_ref, normed_ref):
    step = math.gcd(x_ref.shape[1], 32)
    for r in range(0, x_ref.shape[1], step):
        x = x_ref[0, r : r + step].astype(F32)
        cent = x - jnp.mean(x, axis=-1, keepdims=True)
        var = jnp.mean(cent * cent, axis=-1, keepdims=True)
        normed = cent * lax.rsqrt(var + EPS) * gain_ref[...] + bias_ref[...]
        normed_ref[0, r : r + step] = normed.astype(BF16)


def finish_kernel(terms, which_ref, *refs):
    lows = refs[:terms]
    low_ref, x_ref, c_ref, gain_ref, out_ref, sums_ref = refs[terms:]

    @pl.when(pl.program_id(0) == 0)
    def _():
        sums_ref[...] = jnp.zeros_like(sums_ref)

    low = low_ref[0].astype(F32)
    for ref in lows:
        low = low + ref[0].astype(F32)
    x = x_ref[0].astype(F32)
    cent = x - jnp.mean(x, axis=-1, keepdims=True)
    inverse = lax.rsqrt(jnp.mean(cent * cent, axis=-1, keepdims=True) + EPS)
    xhat = cent * inverse
    g = low * gain_ref[...]
    inner = jnp.mean(g * xhat, axis=-1, keepdims=True)
    back = (g - jnp.mean(g, axis=-1, keepdims=True) - xhat * inner) * inverse
    out_ref[0] = (c_ref[0].astype(F32) + back).astype(BF16)
    sums_ref[0:1] += jnp.sum(low * xhat, axis=0, keepdims=True)
    sums_ref[1:2] += jnp.sum(low, axis=0, keepdims=True)


def join_kernel(slices, attended_ref, c_ref, merge_ref, branch_ref, out_branch, out_weight):
    @pl.when(pl.program_id(0) == 0)
    def _():
        out_weight[...] = jnp.zeros_like(out_weight)

    attended = attended_ref[0]
    out_weight[...] += dot(attended, c_ref[0])
    branch = dot(attended.T, merge_ref[...]) + branch_ref[0].astype(F32)
    cols = branch.shape[1] // slices
    for m in range(slices):
        out_branch[m, 0] = branch[:, m * cols : (m + 1) * cols].astype(BF16)


def settle_kernel(counts, slices, sub, per_piece, table_ref, *refs):
    pieces, out, buf, sems, out_sems = refs[:-4], refs[-4], refs[-3], refs[-2], refs[-1]
    column = table_ref[sum(counts)]
    loads, stores = [], []
    arrays = max(ref for ref, _ in per_piece) + 1
    first = 0
    for c, count in enumerate(counts):
        for k in range(slices):
            ref, where = per_piece[k]
            start = pl.multiple_of(lax.bitwise_xor(jnp.int32(k), column) * sub, sub)
            for t in range(count):
                at = len(loads)
                loads.append(
                    pltpu.make_async_copy(
                        pieces[c * arrays + ref].at[where, t], buf.at[at], sems.at[at]
                    )
                )
                stores.append(
                    pltpu.make_async_copy(
                        buf.at[at],
                        out.at[table_ref[first + t], pl.ds(start, sub)],
                        out_sems.at[at],
                    )
                )
        first += count
    for copy in loads:
        copy.start()
    for load, store in zip(loads, stores):
        load.wait()
        store.start()
    for copy in stores:
        copy.wait()


def exchange_x(array):
    n = array.shape[0]
    return lax.ppermute(array[1::2], "seq", [(i, i ^ 1) for i in range(n)])


def exchange_z(array, got, steps=None):
    n = array.shape[0]
    return [
        lax.ppermute(jnp.stack([array[k], got[k // 2]]), "seq", [(i, i ^ k) for i in range(n)])
        for k in (range(2, n, 2) if steps is None else steps)
    ]


def exchanged(array, got, gots):
    return jnp.concatenate([array[:1], got[:1], *gots], axis=0)


def take(array, index):
    return jnp.take(array, index, axis=0, mode="clip")


def on_device_pairs(
    tokens,
    lengths,
    counts,
    norm_gain,
    norm_bias,
    head_weight,
    merge_weight,
    up_weight,
    up_bias,
    down_weight,
    down_bias,
    cotangent,
):
    packs, shard, width = tokens.shape
    n = lax.axis_size("seq")
    slices = lax.axis_size("mlp")
    pack_len = shard * n
    rank = lax.axis_index("seq").astype(jnp.int32)
    column = lax.axis_index("mlp").astype(jnp.int32)
    heads = merge_weight.shape[0] // HD
    joined = heads * HD
    half = heads // 2
    cols = width // slices
    sub = shard // slices
    seq_masks, mlp_masks = masks_of(n), masks_of(slices)
    pairs = n // 2

    cot = lax.all_gather(cotangent, "mlp", axis=2, tiled=True)

    first, position, cost = layout(lengths, counts, pack_len)
    ids = jnp.arange(packs, dtype=jnp.int32)
    before = (cost[None, :] > cost[:, None]) | (
        (cost[None, :] == cost[:, None]) & (ids[None, :] < ids[:, None])
    )
    order = jnp.sum(before.astype(jnp.int32), axis=1)
    by_order = jnp.sum(
        jnp.where(order[None, :] == ids[:, None], ids[None, :], 0), axis=-1
    ).astype(jnp.int32)
    devices = jnp.arange(n, dtype=jnp.int32)
    shared_of = by_order[:pairs]
    own_of = by_order[pairs + 2 * (pairs - 1 - devices // 2) + devices % 2]
    late = order - pairs
    pair_of = jnp.where(late < 0, order, pairs - 1 - late // 2)
    device_of = 2 * pair_of + jnp.where(late < 0, 0, late % 2)
    dest = jnp.bitwise_xor(rank, devices)
    own_dest, shared_dest = own_of[dest], shared_of[dest // 2]
    me = jnp.stack([rank, column])

    head_ids = jnp.arange(heads, dtype=jnp.int32)
    half_ids = jnp.arange(half, dtype=jnp.int32)
    units_out = jnp.concatenate(
        [
            own_dest[:, None] * heads + head_ids[None, :],
            shared_dest[:, None] * heads + (dest % 2)[:, None] * half + half_ids[None, :],
        ],
        axis=1,
    ).reshape(-1)
    is_shared = (order < pairs)[:, None]
    holder = device_of[:, None] + jnp.where(is_shared, head_ids[None, :] // half, 0)
    units_in = (
        jnp.bitwise_xor(holder, rank) * (heads + half)
        + jnp.where(is_shared, heads + head_ids[None, :] % half, head_ids[None, :])
    ).reshape(-1)

    def tables(pack):
        freq = 10000.0 ** (-(2.0 * jnp.arange(ROT // 2, dtype=F32)) / ROT)
        angle = take(position, pack).astype(F32)[None, :] * jnp.repeat(freq, 2)[:, None]
        return jnp.cos(angle), jnp.sin(angle)

    w_heads = jnp.transpose(head_weight, (0, 2, 1)).reshape(3, heads, HD, width)
    w_own = w_heads.reshape(3 * joined, width)
    part_at = (rank % 2) * half
    w_shared = lax.dynamic_slice_in_dim(w_heads, part_at, half, 1).reshape(3 * half * HD, width)
    packs_here = (own_of[rank], shared_of[rank // 2])
    turns = [tables(p) for p in packs_here]
    firsts = [take(first, p).reshape(n, shard) for p in packs_here]
    lows = [(f[:, 0] // shard).astype(jnp.int32) for f in firsts]
    gain, bias = norm_gain.reshape(1, width), norm_bias.reshape(1, width)

    def whole2(s, *_):
        return (0, 0)

    def lane_at(s, *_):
        return (0, s)

    def project(rows, weight, cosine, sine):
        h = weight.shape[0] // (3 * HD)
        return pl.pallas_call(
            functools.partial(qkv_kernel, h),
            grid_spec=pltpu.PrefetchScalarGridSpec(
                num_scalar_prefetch=1,
                grid=(n,),
                in_specs=[
                    pl.BlockSpec(
                        (1, shard, width), lambda s, me: (lax.bitwise_xor(s, me[0]), 0, 0)
                    ),
                    pl.BlockSpec(weight.shape, whole2),
                    pl.BlockSpec((ROT, shard), lane_at),
                    pl.BlockSpec((ROT, shard), lane_at),
                ],
                out_specs=[
                    pl.BlockSpec((shard, width), lambda s, *_: (s, 0)),
                    pl.BlockSpec((h, 3, HD, shard), lambda s, *_: (0, 0, 0, s)),
                ],
            ),
            out_shape=[
                jax.ShapeDtypeStruct((pack_len, width), BF16),
                jax.ShapeDtypeStruct((h, 3, HD, pack_len), BF16),
            ],
            compiler_params=params(),
            cost_estimate=COST,
            name="project",
        )(me, rows, weight, cosine, sine)

    def wide(h):
        return [pltpu.VMEM((h, n, HD, shard), BF16)]

    def tall(h, kind=BF16):
        return [pltpu.VMEM((h, n, shard, HD), kind)]

    def keep_spec(h):
        return pl.BlockSpec((h, n, HD, shard), lambda u, *_: (u, 0, 0, 0))

    def log_spec(h):
        return pl.BlockSpec((h, n, shard), lambda u, *_: (u, 0, 0))

    def unit_spec(h):
        return pl.BlockSpec((h, 3, HD, pack_len), lambda u, *_: (u, 0, 0, 0))

    def attend(c, qkv):
        h = qkv.shape[0]
        return pl.pallas_call(
            functools.partial(unit_kernel, n, shard),
            grid_spec=pltpu.PrefetchScalarGridSpec(
                num_scalar_prefetch=2,
                grid=(1,),
                in_specs=[pl.BlockSpec((n, shard), whole2), unit_spec(h)],
                out_specs=[
                    pl.BlockSpec((n, h, HD, shard), lambda u, *_: (0, u, 0, 0)),
                    keep_spec(h),
                    log_spec(h),
                ],
                scratch_shapes=wide(h) * 2 + tall(h),
            ),
            out_shape=[
                jax.ShapeDtypeStruct((n, h, HD, shard), BF16),
                jax.ShapeDtypeStruct((h, n, HD, shard), BF16),
                jax.ShapeDtypeStruct((h, n, shard), F32),
            ],
            compiler_params=params(),
            cost_estimate=COST,
            name="attend",
        )(me, lows[c], firsts[c], qkv)

    def attend_back(c, kept, logsum, qkv, grads):
        h = qkv.shape[0]
        step = h if c == 0 else 2
        skip = c * heads // step
        return pl.pallas_call(
            functools.partial(unit_back_kernel, n, shard, c + 1),
            grid_spec=pltpu.PrefetchScalarGridSpec(
                num_scalar_prefetch=2,
                grid=(h // step,),
                in_specs=[
                    pl.BlockSpec((n, shard), whole2),
                    keep_spec(step),
                    log_spec(step),
                    unit_spec(step),
                    pl.BlockSpec((n, step, HD, shard), lambda u, *_: (0, u + skip, 0, 0)),
                ],
                out_specs=unit_spec(step),
                scratch_shapes=wide(step) * 3 + tall(step) * 4 + tall(step, F32) * 2 + wide(step),
            ),
            out_shape=jax.ShapeDtypeStruct((h, 3, HD, pack_len), BF16),
            compiler_params=params(),
            cost_estimate=COST,
            name="attend_back",
        )(me, lows[c], firsts[c], kept, logsum, qkv, grads)

    def rows_back(grads, normed, weight, cosine, sine, *base):
        h = grads.shape[0]
        return pl.pallas_call(
            functools.partial(rows_kernel, h, slices),
            grid_spec=pltpu.PrefetchScalarGridSpec(
                num_scalar_prefetch=1,
                grid=(n,),
                in_specs=[
                    pl.BlockSpec((h, 3, HD, shard), lambda s, *_: (0, 0, 0, s)),
                    pl.BlockSpec((shard, width), lambda s, *_: (s, 0)),
                    pl.BlockSpec(weight.shape, whole2),
                    pl.BlockSpec((ROT, shard), lane_at),
                    pl.BlockSpec((ROT, shard), lane_at),
                ]
                + [pl.BlockSpec(v.shape, whole2) for v in base],
                out_specs=[
                    pl.BlockSpec(
                        (slices, 1, sub, width),
                        lambda s, me: (0, lax.bitwise_xor(s, me[0]), 0, 0),
                    ),
                    pl.BlockSpec((3 * joined, width), whole2),
                ],
            ),
            out_shape=[
                jax.ShapeDtypeStruct((slices, n, sub, width), BF16),
                jax.ShapeDtypeStruct((3 * joined, width), F32),
            ],
            compiler_params=params(),
            cost_estimate=COST,
            name="rows_back",
        )(me, grads, normed, weight, cosine, sine, *base)

    pack_spec = pl.BlockSpec((1, shard, width), lambda p: (p, 0, 0))
    normed_low = pl.pallas_call(
        norm_kernel,
        grid=(packs,),
        in_specs=[pack_spec, pl.BlockSpec((1, width), whole2), pl.BlockSpec((1, width), whole2)],
        out_specs=pack_spec,
        out_shape=jax.ShapeDtypeStruct((packs, shard, width), BF16),
        compiler_params=params(),
        cost_estimate=COST,
        name="norm",
    )(tokens, gain, bias)
    normed_cols = lax.dynamic_slice_in_dim(normed_low, column * cols, cols, 2)
    send_own = take(normed_cols, own_dest)
    send_shared = take(normed_cols, shared_dest)
    own_x = exchange_x(send_own)

    hidden = (
        jnp.einsum("psd,df->psf", normed_low, up_weight, preferred_element_type=F32) + up_bias
    )
    own_x, hidden, send_own, send_shared = tie(own_x, hidden, send_own, send_shared)

    own_z = exchange_z(send_own, own_x, [2])
    shared_x = exchange_x(send_shared)
    active_low = jax.nn.gelu(hidden, approximate=True).astype(BF16)
    branch_ff = jnp.einsum(
        "psf,fd->psd", active_low, down_weight, preferred_element_type=F32
    ).astype(BF16)
    own_z, shared_x, branch_ff, send_own, own_x, merge_here, down_here, turns, w_own, w_shared = tie(
        own_z,
        shared_x,
        branch_ff,
        send_own,
        own_x,
        merge_weight,
        down_weight,
        turns,
        w_own,
        w_shared,
    )

    own_z += exchange_z(send_own, own_x, range(4, n, 2))
    active_grad = jnp.einsum("psd,fd->psf", cot, down_here, preferred_element_type=F32)
    _, gelu_back = jax.vjp(lambda values: jax.nn.gelu(values, approximate=True), hidden)
    hidden_grad = gelu_back(active_grad)[0].astype(BF16)
    own_z, hidden_grad, send_shared, shared_x = tie(own_z, hidden_grad, send_shared, shared_x)
    rows_own = lax.all_gather(exchanged(send_own, own_x, own_z), "mlp", axis=2, tiled=True)

    shared_z = exchange_z(send_shared, shared_x)
    out_grad = jnp.einsum("hd,psd->phs", merge_here, cot, preferred_element_type=F32).astype(BF16)
    send_grad = take(out_grad.reshape(packs * heads, HD, shard), units_out).reshape(
        n, heads + half, HD, shard
    )
    up_grad = jnp.einsum(
        "psd,psf->df", normed_low, hidden_grad, preferred_element_type=F32
    ).astype(BF16)
    down_grad = jnp.einsum("psd,psf->df", cot, active_low, preferred_element_type=F32).astype(BF16)
    shared_z, send_grad, up_grad, down_grad, send_shared, shared_x, hidden_grad = tie(
        shared_z, send_grad, up_grad, down_grad, send_shared, shared_x, hidden_grad
    )
    rows_shared = lax.all_gather(
        exchanged(send_shared, shared_x, shared_z), "mlp", axis=2, tiled=True
    )

    grad_x = exchange_x(send_grad)
    low_ff = jnp.einsum(
        "psf,df->psd", hidden_grad, up_weight, preferred_element_type=F32
    ).astype(BF16)
    low_ff = jnp.transpose(low_ff.reshape(packs, slices, sub, width), (1, 0, 2, 3)).reshape(
        slices * packs * sub, width
    )
    biases = jnp.sum(hidden_grad.astype(F32), axis=(0, 1)), jnp.sum(cot.astype(F32), axis=(0, 1))
    grad_x, send_grad, low_ff, rows_own, biases = tie(grad_x, send_grad, low_ff, rows_own, biases)
    low_ff = lax.psum_scatter(low_ff, "mlp", scatter_dimension=0, tiled=True).reshape(
        packs, sub, width
    )

    grad_z = exchange_z(send_grad, grad_x)
    normed_own, qkv_own = project(rows_own, w_own, *turns[0])
    out_own, kept_own, log_own = attend(0, qkv_own)
    grad_z, out_own, kept_own, log_own, rows_shared = tie(
        grad_z, out_own, kept_own, log_own, rows_shared
    )
    grads = exchanged(send_grad, grad_x, grad_z)

    def with_row(*parts):
        weight = jnp.concatenate(parts[:2], axis=1)
        row = jnp.concatenate(parts[2:])
        row = jnp.pad(row, (0, weight.shape[1] - row.shape[0])).reshape(1, -1)
        row = jnp.broadcast_to(row, (16, weight.shape[1])).astype(BF16)
        return jnp.concatenate([weight, row], axis=0)

    terms = dict(
        enumerate(
            with_row(*parts)
            for parts in zip(*[cut(v, 0, n, rank) for v in (up_grad, down_grad, *biases)])
        )
    )
    terms_got = cube_send(terms, "seq", n, seq_masks)
    normed_shared, qkv_shared = project(rows_shared, w_shared, *turns[1])
    out_shared, kept_shared, log_shared = attend(1, qkv_shared)
    out_shared, kept_shared, log_shared, grads = tie(out_shared, kept_shared, log_shared, grads)

    send_out = jnp.concatenate([out_own, out_shared], axis=1)
    out_x = exchange_x(send_out)
    back_own = attend_back(0, kept_own, log_own, qkv_own, grads)
    out_x, back_own, terms_got, send_out = tie(out_x, back_own, terms_got, send_out)

    terms = cube_add(terms, terms_got, seq_masks, BF16)
    terms_got = cube_send(terms, "seq", n, seq_masks[1:])
    out_z = exchange_z(send_out, out_x)
    low_own, head_own = rows_back(back_own, normed_own, w_own, *turns[0])
    back_shared = attend_back(1, kept_shared, log_shared, qkv_shared, grads)
    out_z, terms_got, low_own, back_shared, send_out, out_x = tie(
        out_z, terms_got, low_own, back_shared, send_out, out_x
    )

    low_own = cube_sum([low_own[k] for k in range(slices)], "mlp", mlp_masks, BF16).astype(BF16)
    for step in range(1, len(seq_masks)):
        last_step = step == len(seq_masks) - 1
        terms = cube_add(terms, terms_got, seq_masks[step:], F32 if last_step else BF16)
        if not last_step:
            terms_got = cube_send(terms, "seq", n, seq_masks[step + 1 :])
    terms = terms[0]
    low_shared, head_all = rows_back(back_shared, normed_shared, w_shared, *turns[1], head_own)
    attended = take(
        exchanged(send_out, out_x, out_z).reshape(n * (heads + half), HD, shard), units_in
    ).reshape(packs, joined, shard)
    branch, merge_part = pl.pallas_call(
        functools.partial(join_kernel, slices),
        grid=(packs,),
        in_specs=[
            pl.BlockSpec((1, joined, shard), lambda p: (p, 0, 0)),
            pl.BlockSpec((1, shard, width), lambda p: (p, 0, 0)),
            pl.BlockSpec((joined, width), whole2),
            pl.BlockSpec((1, shard, width), lambda p: (p, 0, 0)),
        ],
        out_specs=[
            pl.BlockSpec((slices, 1, shard, cols), lambda p: (0, p, 0, 0)),
            pl.BlockSpec((joined, width), whole2),
        ],
        out_shape=[
            jax.ShapeDtypeStruct((slices, packs, shard, cols), BF16),
            jax.ShapeDtypeStruct((joined, width), F32),
        ],
        compiler_params=params(),
        cost_estimate=COST,
        name="join",
    )(attended, cot, merge_weight, branch_ff)
    low_terms = {k: low_shared[k] for k in range(slices)}
    low_got = cube_send(low_terms, "mlp", slices, mlp_masks)
    low_terms, low_got, low_own, branch, terms, low_ff, head_all = tie(
        low_terms, low_got, low_own, branch, terms, low_ff, head_all
    )

    summed = lax.psum_scatter(branch, "mlp", scatter_dimension=0, tiled=False)

    low_own_x = exchange_x(low_own)
    for step in range(len(mlp_masks)):
        low_terms = cube_add(low_terms, low_got, mlp_masks[step:], BF16)
        if step < len(mlp_masks) - 1:
            low_got = cube_send(low_terms, "mlp", slices, mlp_masks[step + 1 :])
    low_shared = low_terms[0]
    weights = {
        k: jnp.concatenate(pair, axis=0).astype(BF16)
        for k, pair in enumerate(zip(cut(head_all, 1, n, rank), cut(merge_part, 1, n, rank)))
    }
    low_own_z = exchange_z(low_own, low_own_x)
    weights_got = cube_send(weights, "seq", n, seq_masks)
    low_own_z, low_shared, low_own, low_own_x, weights, weights_got = tie(
        low_own_z, low_shared, low_own, low_own_x, weights, weights_got
    )

    low_shared_x = exchange_x(low_shared)
    weights = cube_add(weights, weights_got, seq_masks, BF16)
    weights_got = cube_send(weights, "seq", n, seq_masks[1:])

    def finish(lows, index, which):
        count = which.shape[0]
        row_spec = pl.BlockSpec((1, sub, width), lambda t, at: (at[count + t], at[0], 0))

        def part(i):
            return pl.BlockSpec(
                (1, sub, width), lambda t, at: (at[(2 + i) * count + t], 0, 0)
            )

        table = [jnp.full((count,), column), which, *index]
        return pl.pallas_call(
            functools.partial(finish_kernel, len(lows)),
            grid_spec=pltpu.PrefetchScalarGridSpec(
                num_scalar_prefetch=1,
                grid=(count,),
                in_specs=[part(i) for i in range(len(lows))]
                + [
                    pl.BlockSpec((1, sub, width), lambda t, at: (at[count + t], 0, 0)),
                    row_spec,
                    row_spec,
                    pl.BlockSpec((1, width), whole2),
                ],
                out_specs=[
                    pl.BlockSpec((1, sub, width), lambda t, *_: (t, 0, 0)),
                    pl.BlockSpec((2, width), whole2),
                ],
            ),
            out_shape=[
                jax.ShapeDtypeStruct((count, sub, width), BF16),
                jax.ShapeDtypeStruct((2, width), F32),
            ],
            compiler_params=params(),
            cost_estimate=COST,
            name="finish",
        )(jnp.concatenate(table), *lows, low_ff, tokens, cot, gain)

    row_own, sums_own = finish(
        [exchanged(low_own, low_own_x, low_own_z)], [devices], own_dest
    )
    low_shared_x, row_own, sums_own, low_shared, weights_got = tie(
        low_shared_x, row_own, sums_own, low_shared, weights_got
    )
    for step in range(1, len(seq_masks)):
        last_step = step == len(seq_masks) - 1
        weights = cube_add(weights, weights_got, seq_masks[step:], F32 if last_step else BF16)
        if not last_step:
            weights_got = cube_send(weights, "seq", n, seq_masks[step + 1 :])
    weights = weights[0]
    low_shared_z = exchange_z(low_shared, low_shared_x)
    pieces = gather_step([row_own[None]], "mlp", slices, mlp_masks[-1])
    result = (
        lax.dynamic_slice_in_dim(tokens, column * cols, cols, 2).astype(F32)
        + summed.astype(F32)
        + lax.dynamic_slice_in_dim(down_bias, column * cols, cols, 0)
    ).astype(BF16)
    low_shared_z, pieces, weights, result = tie(low_shared_z, pieces, weights, result)

    for m in reversed(mlp_masks[:-1]):
        pieces = gather_step(pieces, "mlp", slices, m)
    both = exchanged(low_shared, low_shared_x, low_shared_z)
    even = jnp.bitwise_xor(2 * jnp.arange(pairs, dtype=jnp.int32), rank)
    row_shared, sums = finish([both, both], [even, jnp.bitwise_xor(even, 1)], shared_of)
    last = gather_step([row_shared[None]], "mlp", slices, mlp_masks[-1])
    vectors = small_sum(sums_own + sums, n, slices)
    last, pieces, vectors = tie(last, pieces, vectors)

    for m in reversed(mlp_masks[:-1]):
        last = gather_step(last, "mlp", slices, m)
    pieces += last
    where = [(0, 0)]
    lookup = [0]
    for i, m in enumerate(reversed(mlp_masks)):
        where += [(i + 1, j) for j in range(len(lookup))]
        lookup += [k ^ m for k in lookup]
    per_piece = [where[lookup.index(k)] for k in range(slices)]
    tokens_grad = pl.pallas_call(
        functools.partial(settle_kernel, (n, pairs), slices, sub, per_piece),
        grid_spec=pltpu.PrefetchScalarGridSpec(
            num_scalar_prefetch=1,
            grid=(1,),
            in_specs=[pl.BlockSpec(memory_space=pl.ANY)] * len(pieces),
            out_specs=pl.BlockSpec(memory_space=pl.ANY),
            scratch_shapes=[
                pltpu.VMEM((packs * slices, sub, width), BF16),
                pltpu.SemaphoreType.DMA((packs * slices,)),
                pltpu.SemaphoreType.DMA((packs * slices,)),
            ],
        ),
        out_shape=jax.ShapeDtypeStruct((packs, shard, width), BF16),
        compiler_params=params(),
        name="settle",
    )(jnp.concatenate([own_dest, shared_of, column.reshape(1)]), *pieces)

    part, hidden_here = width // n, up_weight.shape[1]
    return (
        result,
        tokens_grad,
        vectors[0],
        vectors[1],
        jnp.transpose(weights[: 3 * joined].reshape(3, joined, part), (0, 2, 1)),
        weights[3 * joined :],
        terms[:part, :hidden_here],
        terms[part, : hidden_here // n],
        terms[:part, hidden_here:].T,
        terms[part, hidden_here // n : hidden_here // n + part],
    )


def solution(mesh):
    in_specs = (
        P(None, "seq", None),
        P(),
        P(),
        P(),
        P(),
        P(None, None, "mlp"),
        P("mlp", None),
        P(None, "mlp"),
        P("mlp"),
        P("mlp", None),
        P(),
        P(None, "seq", "mlp"),
    )
    out_specs = (
        P(None, "seq", "mlp"),
        P(None, "seq", None),
        P("seq"),
        P("seq"),
        P(None, "seq", "mlp"),
        P("mlp", "seq"),
        P("seq", "mlp"),
        P(("mlp", "seq")),
        P("mlp", "seq"),
        P("seq"),
    )
    n, slices = mesh.shape["seq"], mesh.shape["mlp"]

    def plan(*args):
        packs, pack_len, _ = args[0].shape
        heads = args[6].shape[0] // HD // slices
        pairs = (
            2 * packs == 3 * n
            and n >= 4
            and heads % 4 == 0
            and (pack_len // n) % 128 == 0
            and (pack_len // n) % (16 * slices) == 0
        )
        return jax.shard_map(
            on_device_pairs if pairs else on_device,
            mesh=mesh,
            in_specs=in_specs,
            out_specs=out_specs,
            check_vma=False,
        )(*args)

    return plan
```

```python
import functools
import math

import jax
import jax.numpy as jnp
from jax import lax
from jax.experimental import pallas as pl
from jax.experimental.pallas import tpu as pltpu
from jax.sharding import PartitionSpec as P

HD = 64
ROT = 32
EPS = 1e-05
NEG = -1e30
BF16 = jnp.bfloat16
F32 = jnp.float32
VMEM_LIMIT = 56 * 1024 * 1024
COST = pl.CostEstimate(flops=1 << 20, bytes_accessed=1 << 20, transcendentals=0)


def dot(a, b, dims=((1,), (0,))):
    return lax.dot_general(a, b, (dims, ((), ())), preferred_element_type=F32)


def layout(lengths, counts, pack_len):
    slots = lengths.shape[-1]
    slot_ids = jnp.arange(slots, dtype=jnp.int32)
    used = slot_ids[None, :] < counts[:, None]
    sizes = jnp.where(used, lengths, 0)
    ends = jnp.cumsum(sizes, axis=-1)
    starts = ends - sizes
    filled = ends[:, -1:]
    place = jnp.arange(pack_len, dtype=jnp.int32)[None, :]
    begin = jnp.max(
        jnp.where(used[:, None, :] & (place[:, :, None] >= starts[:, None, :]), starts[:, None, :], 0),
        axis=-1,
    )
    inside = place < filled
    first = jnp.where(inside, begin, place)
    position = jnp.where(inside, place - begin, place - filled)
    cost = jnp.sum(sizes * sizes, axis=-1)
    return first, position, cost


def turn(values, cosine, sine, heads):
    out = []
    parity = lax.broadcasted_iota(jnp.int32, cosine.shape, 0) % 2
    for h in range(heads):
        part = values[h * HD : h * HD + ROT]
        ahead = jnp.concatenate([part[1:], part[:1]], axis=0)
        behind = jnp.concatenate([part[-1:], part[:-1]], axis=0)
        swapped = jnp.where(parity == 0, -ahead, behind)
        out.append(part * cosine + swapped * sine)
        out.append(values[h * HD + ROT : (h + 1) * HD])
    return jnp.concatenate(out, axis=0)


def head_kernel(n, heads, per, me_ref, pack_ref, x_ref, gain_ref, bias_ref, w_ref, cos_ref, sin_ref, *refs):
    normed_ref, copy_ref, outs, scr = refs[0], refs[1], refs[2:-1], refs[-1]
    s_id, g = pl.program_id(0), pl.program_id(1)
    me = me_ref[0]
    width = heads * HD
    copy_ref[0] = x_ref[0]
    x = x_ref[0].astype(F32)
    cent = x - jnp.mean(x, axis=-1, keepdims=True)
    var = jnp.mean(cent * cent, axis=-1, keepdims=True)
    normed = (cent * lax.rsqrt(var + EPS) * gain_ref[...] + bias_ref[...]).astype(BF16)
    normed_ref[0] = normed
    for j in range(3):
        part = dot(w_ref[j * width : (j + 1) * width, :], normed, ((1,), (1,)))
        if j < 2:
            part = turn(part, cos_ref[0], sin_ref[0], heads)
        if j == 0:
            part = part * (1.0 / math.sqrt(HD))
        part = part.astype(BF16)
        for h in range(heads):
            scr[h, j] = part[h * HD : (h + 1) * HD]
    for at, out in enumerate(outs):
        d = lax.bitwise_xor(jnp.int32(at % n), me)

        @pl.when((d // heads == g) & (s_id // per == at // n))
        def _():
            out[0] = scr[d % heads]


def grad_kernel(n, heads, me_ref, c_ref, w_ref, *refs):
    outs, scr = refs[:n], refs[n]
    g = pl.program_id(1)
    me = me_ref[0]
    part = dot(w_ref[...], c_ref[0], ((1,), (1,))).astype(BF16)
    for h in range(heads):
        scr[h] = part[h * HD : (h + 1) * HD]
    for k in range(n):
        d = lax.bitwise_xor(jnp.int32(k), me)

        @pl.when(d // heads == g)
        def _():
            outs[k][0] = scr[d % heads]


def load_parts(n, me, pairs):
    for k in range(n):
        d = lax.bitwise_xor(jnp.int32(k), me)
        for part, t_ref, n_ref in pairs(k):
            if t_ref is not None:
                t_ref[d] = part
            if n_ref is not None:
                n_ref[d] = part.T


def score_of(block, first, i, kn, q_t):
    rows = lax.broadcasted_iota(jnp.int32, (block, block), 0)
    cols = lax.broadcasted_iota(jnp.int32, (block, block), 1)
    ahead = rows - cols

    def scores(j, at):
        s = dot(kn[at], q_t)
        allowed = (rows >= first - j * block) & (ahead <= (i - j) * block)
        return jnp.where(allowed, s, NEG)

    return scores


def attend_kernel(n, block, skip, me_ref, pack_ref, low_ref, first_ref, *refs):
    qkv, outs, keep_ref, logsum_ref = refs[:n], refs[n : 2 * n], refs[2 * n], refs[2 * n + 1]
    qt, vt, kn = refs[2 * n + 2 :]
    s_id = pl.program_id(0) + skip
    me = me_ref[0]
    load_parts(
        n,
        me,
        lambda k: (
            (qkv[k][0, 0, 0], qt, None),
            (qkv[k][0, 0, 1], None, kn),
            (qkv[k][0, 0, 2], vt, None),
        ),
    )

    def outer(i, carry):
        scores = score_of(block, first_ref[0, pl.ds(i, 1), :], i, kn, qt[i])
        j0 = low_ref[s_id, i]

        def forward(t, state):
            top, total, acc = state
            j = j0 + 2 * t
            at = jnp.minimum(j + 1, n - 1)
            s0, s1 = scores(j, j), scores(j + 1, at)
            peak = jnp.max(jnp.maximum(s0, s1), axis=0, keepdims=True)
            new_top = jnp.maximum(top, peak)
            p0, p1 = jnp.exp(s0 - new_top), jnp.exp(s1 - new_top)
            fade = jnp.exp(top - new_top)
            total = total * fade + jnp.sum(p0 + p1, axis=0, keepdims=True)
            acc = acc * fade + dot(vt[j], p0.astype(BF16)) + dot(vt[at], p1.astype(BF16))
            return new_top, total, acc

        top, total, acc = lax.fori_loop(
            0,
            (i - j0) // 2 + 1,
            forward,
            (
                jnp.full((1, block), NEG, F32),
                jnp.zeros((1, block), F32),
                jnp.zeros((HD, block), F32),
            ),
        )
        keep_ref[0, i] = (acc / total).astype(BF16)
        logsum_ref[0, pl.ds(i, 1), :] = top + jnp.log(total)
        return carry

    lax.fori_loop(0, n, outer, 0)
    for k in range(n):
        outs[k][0] = keep_ref[0, lax.bitwise_xor(jnp.int32(k), me)]


def attend_back_kernel(n, block, skip, me_ref, pack_ref, low_ref, first_ref, *refs):
    keep_ref, logsum_ref = refs[:2]
    qkv, grads, outs = refs[2 : n + 2], refs[n + 2 : 2 * n + 2], refs[2 * n + 2 : 3 * n + 2]
    qt, kt, gt, qn, kn, vn, gn, dk, dv, res = refs[3 * n + 2 :]
    s_id = pl.program_id(0) + skip
    me = me_ref[0]
    load_parts(
        n,
        me,
        lambda k: (
            (qkv[k][0, 0, 0], qt, qn),
            (qkv[k][0, 0, 1], kt, kn),
            (qkv[k][0, 0, 2], None, vn),
            (grads[k][0, 0], gt, gn),
        ),
    )
    dk[...] = jnp.zeros_like(dk)
    dv[...] = jnp.zeros_like(dv)

    def outer(i, carry):
        q_t, g_t, q_n, g_n = qt[i], gt[i], qn[i], gn[i]
        scores = score_of(block, first_ref[0, pl.ds(i, 1), :], i, kn, q_t)
        j0 = low_ref[s_id, i]
        inner = jnp.sum(keep_ref[0, i].astype(F32) * g_t.astype(F32), axis=0, keepdims=True)
        logsum = logsum_ref[0, pl.ds(i, 1), :]

        def one(j, at):
            p = jnp.exp(scores(j, at) - logsum)
            ds = (p * (dot(vn[at], g_t) - inner)).astype(BF16)
            return ds, dot(ds, q_n), dot(p.astype(BF16), g_n), dot(kt[at], ds)

        def backward(t, dq):
            j = j0 + 2 * t
            at = jnp.minimum(j + 1, n - 1)
            _, dk0, dv0, dq0 = one(j, j)
            _, dk1, dv1, dq1 = one(j + 1, at)
            dk[j] += dk0
            dv[j] += dv0
            dk[at] += dk1
            dv[at] += dv1
            return dq + dq0 + dq1

        dq = lax.fori_loop(0, (i - j0) // 2 + 1, backward, jnp.zeros((HD, block), F32))
        res[i, 0] = (dq * (1.0 / math.sqrt(HD))).astype(BF16)
        return carry

    lax.fori_loop(0, n, outer, 0)
    for i in range(n):
        res[i, 1] = dk[i].T.astype(BF16)
        res[i, 2] = dv[i].T.astype(BF16)
    for k in range(n):
        outs[k][0] = res[lax.bitwise_xor(jnp.int32(k), me)]


def merge_kernel(n, heads, slices, me_ref, *refs):
    recv = refs[:n]
    c_ref, merge_ref, branch_ref, out_branch, out_weight, scr, acc = refs[n:]
    s_id, g = pl.program_id(0), pl.program_id(1)
    groups = pl.num_programs(1)
    me = me_ref[0]
    width = heads * HD

    @pl.when((s_id == 0) & (g == 0))
    def _():
        acc[...] = jnp.zeros_like(acc)

    for k in range(n):
        d = lax.bitwise_xor(jnp.int32(k), me)

        @pl.when(d // heads == g)
        def _():
            scr[d % heads] = recv[k][0, 0, 0]

    attended = scr[...].reshape(width, c_ref.shape[1])
    acc[...] += dot(attended, c_ref[0])
    branch = dot(attended.T, merge_ref[...]) + branch_ref[0].astype(F32)
    cols = branch.shape[1] // slices
    for m in range(slices):
        out_branch[m, 0] = branch[:, m * cols : (m + 1) * cols].astype(BF16)

    @pl.when((s_id == pl.num_programs(0) - 1) & (g == groups - 1))
    def _():
        out_weight[...] = acc[...].astype(BF16)


def close_kernel(n, heads, me_ref, *refs):
    recv = refs[:n]
    normed_ref, w_ref, cos_ref, sin_ref, low_ref, out_low, out_weight, scr, acc = refs[n:]
    s_id, g = pl.program_id(0), pl.program_id(1)
    groups = pl.num_programs(1)
    me = me_ref[0]
    width = heads * HD
    shard = normed_ref.shape[1]

    @pl.when((s_id == 0) & (g == 0))
    def _():
        acc[...] = jnp.zeros_like(acc)

    for k in range(n):
        d = lax.bitwise_xor(jnp.int32(k), me)

        @pl.when(d // heads == g)
        def _():
            for j in range(3):
                scr[j, d % heads] = recv[k][0, 0, j]

    parts = []
    for j in (0, 1):
        part = scr[j].reshape(width, shard).astype(F32)
        parts.append(turn(part, cos_ref[0], -sin_ref[0], heads).astype(BF16))
    parts.append(scr[2].reshape(width, shard))
    grads = jnp.concatenate(parts, axis=0)
    acc[...] += dot(grads, normed_ref[0])
    low = dot(grads.T, w_ref[...]) + low_ref[0].astype(F32)
    out_low[0] = low.astype(BF16)

    @pl.when((s_id == pl.num_programs(0) - 1) & (g == groups - 1))
    def _():
        out_weight[...] = acc[...]


def place_kernel(block, share, shard, slices, chunks, per_piece, pack_ref, *refs):
    pieces, out, buf, sems, out_sems = refs[:-4], refs[-4], refs[-3], refs[-2], refs[-1]
    me = pack_ref[chunks * slices * share // shard]
    loads, stores = [], []
    arrays = max(ref for ref, _ in per_piece) + 1
    for c in range(chunks):
        for k in range(slices):
            ref, where = per_piece[k]
            for t in range(share // block):
                at = len(loads)
                row = (c * slices + lax.bitwise_xor(jnp.int32(k), me)) * share + t * block
                start = pl.multiple_of(lax.rem(row, shard), block)
                loads.append(
                    pltpu.make_async_copy(
                        pieces[c * arrays + ref].at[where, pl.ds(t * block, block)],
                        buf.at[at],
                        sems.at[at],
                    )
                )
                stores.append(
                    pltpu.make_async_copy(
                        buf.at[at],
                        out.at[pack_ref[row // shard], pl.ds(start, block)],
                        out_sems.at[at],
                    )
                )
    for copy in loads:
        copy.start()
    for load, store in zip(loads, stores):
        load.wait()
        store.start()
    for copy in stores:
        copy.wait()


def small_kernel(n, slices, x_ref, out_ref, first, second, sems, sems2):
    rank, column = lax.axis_index("seq"), lax.axis_index("mlp")
    barrier = pltpu.get_barrier_semaphore()
    peers = [{"seq": lax.bitwise_xor(rank, k)} for k in range(1, n)]
    rows = [{"mlp": lax.bitwise_xor(column, k)} for k in range(1, slices)]
    for peer in peers + rows:
        pl.semaphore_signal(barrier, inc=1, device_id=peer, device_id_type=pl.DeviceIdType.MESH)
    pl.semaphore_wait(barrier, len(peers) + len(rows))

    def exchange(source, target, sems, peers):
        copies = [
            pltpu.make_async_remote_copy(
                src_ref=source(k),
                dst_ref=target.at[k],
                send_sem=sems.at[0, k],
                recv_sem=sems.at[1, k],
                device_id=peer,
                device_id_type=pl.DeviceIdType.MESH,
            )
            for k, peer in enumerate(peers)
        ]
        for copy in copies:
            copy.start()
        for copy in copies:
            copy.wait()

    exchange(lambda k: x_ref.at[lax.bitwise_xor(rank, k + 1)], first, sems, peers)
    total = x_ref[rank]
    for k in range(n - 1):
        total = total + first[k]
    second[slices - 1] = total
    second[slices] = total
    exchange(lambda k: second.at[slices], second, sems2, rows)
    parts = [
        second[jnp.where(column == c, slices - 1, lax.bitwise_xor(column, c) - 1)]
        for c in range(slices)
    ]
    out_ref[...] = functools.reduce(jnp.add, parts)


def small_sum(vectors, n, slices):
    count, width = vectors.shape
    x = jnp.transpose(vectors.reshape(count, n, width // n), (1, 0, 2))
    return pl.pallas_call(
        functools.partial(small_kernel, n, slices),
        out_shape=jax.ShapeDtypeStruct((count, width // n), F32),
        in_specs=[pl.BlockSpec(memory_space=pltpu.VMEM)],
        out_specs=pl.BlockSpec(memory_space=pltpu.VMEM),
        scratch_shapes=[
            pltpu.VMEM((n - 1, count, width // n), F32),
            pltpu.VMEM((slices + 1, count, width // n), F32),
            pltpu.SemaphoreType.DMA((2, n - 1)),
            pltpu.SemaphoreType.DMA((2, slices - 1)),
        ],
        compiler_params=pltpu.CompilerParams(collective_id=0, has_side_effects=True),
        cost_estimate=COST,
        name="small_sum",
    )(x)


def params():
    return pltpu.CompilerParams(vmem_limit_bytes=VMEM_LIMIT)


def tie(*values):
    return lax.optimization_barrier(values)


def send_x(parts):
    n = len(parts)
    sent = jnp.stack([parts[k] for k in range(1, n, 2)])
    return lax.ppermute(sent, "seq", [(i, i ^ 1) for i in range(n)])


def send_z(parts, got, steps=None):
    n = len(parts)
    return [
        lax.ppermute(
            jnp.stack([parts[k], got[k // 2]]), "seq", [(i, i ^ k) for i in range(n)]
        )
        for k in (range(2, n, 2) if steps is None else steps)
    ]


def received(parts, got, gots):
    out = [(parts[0][None], 0), (got, 0)]
    for array in gots:
        out += [(array, 0), (array, 1)]
    return out


def span(masks):
    out = [0]
    for m in masks:
        out += [v ^ m for v in out]
    return out


def cube_send(chunks, axis, n, masks):
    kept = span(masks[1:])
    sent = jnp.stack([chunks[k ^ masks[0]] for k in kept])
    return lax.ppermute(sent, axis, [(i, i ^ masks[0]) for i in range(n)])


def cube_add(chunks, got, masks, kind):
    return {
        k: (chunks[k].astype(F32) + got[at].astype(F32)).astype(kind)
        for at, k in enumerate(span(masks[1:]))
    }


def cube_sum(chunks, axis, masks, kind):
    n = len(chunks)
    chunks = {k: v.astype(kind) for k, v in enumerate(chunks)}
    for step in range(len(masks)):
        got = cube_send(chunks, axis, n, masks[step:])
        chunks = cube_add(chunks, got, masks[step:], F32 if step == len(masks) - 1 else kind)
    return chunks[0]


def gather_step(arrays, axis, n, m):
    sent = jnp.concatenate(arrays, axis=0) if len(arrays) > 1 else arrays[0]
    return arrays + [lax.ppermute(sent, axis, [(i, i ^ m) for i in range(n)])]


def masks_of(n):
    return [1 << b for b in range(n.bit_length() - 1)]


def turned(masks, by):
    by = by % len(masks)
    return masks[by:] + masks[:by]


def cut(array, axis, n, me):
    size = array.shape[axis] // n
    return [
        lax.dynamic_slice_in_dim(array, lax.bitwise_xor(jnp.int32(k), me) * size, size, axis)
        for k in range(n)
    ]


def on_device(
    tokens,
    lengths,
    counts,
    norm_gain,
    norm_bias,
    head_weight,
    merge_weight,
    up_weight,
    up_bias,
    down_weight,
    down_bias,
    cotangent,
):
    packs, shard, width = tokens.shape
    n = lax.axis_size("seq")
    slices = lax.axis_size("mlp")
    pack_len = shard * n
    rank = lax.axis_index("seq")
    column = lax.axis_index("mlp")
    heads = merge_weight.shape[0] // HD
    joined = heads * HD
    groups = n // heads
    slots = -(-packs // groups)
    dealt = groups * slots
    spare = 1 if dealt > packs else 0
    rows = dealt * shard
    chunks = 2 if slots % 2 == 0 else 1
    per = slots // chunks
    seq_masks, mlp_masks = masks_of(n), masks_of(slices)

    first, position, cost = layout(lengths, counts, pack_len)
    ids = jnp.arange(packs, dtype=jnp.int32)
    before = (cost[None, :] > cost[:, None]) | (
        (cost[None, :] == cost[:, None]) & (ids[None, :] < ids[:, None])
    )
    order = jnp.sum(before.astype(jnp.int32), axis=1)
    slot_of = order // groups
    group_of = jnp.where(slot_of % 2 == 0, order % groups, groups - 1 - order % groups)
    at = slot_of * groups + group_of
    hit = at[None, :] == jnp.arange(dealt, dtype=jnp.int32)[:, None]
    pack_at = jnp.where(
        jnp.any(hit, axis=-1), jnp.sum(jnp.where(hit, ids, 0), axis=-1), packs
    ).astype(jnp.int32)
    safe = jnp.minimum(pack_at, packs - 1)
    me = rank.astype(jnp.int32).reshape(1)

    own_cot = jnp.take(cotangent, safe, axis=0, mode="clip")
    if spare:
        own_cot = jnp.where((pack_at < packs)[:, None, None], own_cot, 0)
    cot = lax.all_gather(own_cot, "mlp", axis=2, tiled=True)

    half = ROT // 2
    freq = 10000.0 ** (-(2.0 * jnp.arange(half, dtype=F32)) / ROT)
    own_position = jnp.take(
        lax.dynamic_slice_in_dim(position, rank * shard, shard, 1), safe, axis=0, mode="clip"
    )
    angle = own_position.astype(F32)[:, None, :] * jnp.repeat(freq, 2)[None, :, None]
    cosine, sine = jnp.cos(angle), jnp.sin(angle)

    w_t = jnp.transpose(head_weight, (0, 2, 1)).reshape(3 * joined, width)

    def whole2(s, g, *_):
        return (0, 0)

    def rows_at(skip):
        return pl.BlockSpec((1, shard, width), lambda s, g, *_: ((s + skip) * groups + g, 0, 0))

    def table_at(skip):
        return pl.BlockSpec((1, ROT, shard), lambda s, g, *_: ((s + skip) * groups + g, 0, 0))

    parts = [jax.ShapeDtypeStruct((per, 3, HD, shard), BF16)] * n

    def chunk_at(c):
        return pl.BlockSpec(
            (1, 3, HD, shard), lambda s, g, *_: (jnp.clip(s - c * per, 0, per - 1), 0, 0, 0)
        )

    outs = pl.pallas_call(
        functools.partial(head_kernel, n, heads, per),
        grid_spec=pltpu.PrefetchScalarGridSpec(
            num_scalar_prefetch=2,
            grid=(slots, groups),
            in_specs=[
                pl.BlockSpec((1, shard, width), lambda s, g, a, b: (b[s * groups + g], 0, 0)),
                pl.BlockSpec((1, width), whole2),
                pl.BlockSpec((1, width), whole2),
                pl.BlockSpec((3 * joined, width), whole2),
                table_at(0),
                table_at(0),
            ],
            out_specs=[rows_at(0)] * 2 + [chunk_at(c) for c in range(chunks) for _ in range(n)],
            scratch_shapes=[pltpu.VMEM((heads, 3, HD, shard), BF16)],
        ),
        out_shape=[jax.ShapeDtypeStruct((dealt, shard, width), BF16)] * 2 + parts * chunks,
        compiler_params=params(),
        cost_estimate=COST,
        name="heads",
    )(
        me,
        safe,
        tokens,
        norm_gain.reshape(1, width),
        norm_bias.reshape(1, width),
        w_t,
        cosine,
        sine,
    )
    normed_low, tokens_dealt = outs[0], outs[1]
    qkv = [list(outs[2 + c * n : 2 + (c + 1) * n]) for c in range(chunks)]

    def out_grads(cot, merge_weight):
        return pl.pallas_call(
            functools.partial(grad_kernel, n, heads),
            grid_spec=pltpu.PrefetchScalarGridSpec(
                num_scalar_prefetch=1,
                grid=(slots, groups),
                in_specs=[rows_at(0), pl.BlockSpec((joined, width), whole2)],
                out_specs=[pl.BlockSpec((1, HD, shard), lambda s, g, *_: (s, 0, 0))] * n,
                scratch_shapes=[pltpu.VMEM((heads, HD, shard), BF16)],
            ),
            out_shape=[jax.ShapeDtypeStruct((slots, HD, shard), BF16)] * n,
            compiler_params=params(),
            cost_estimate=COST,
            name="out_grads",
        )(me, cot, merge_weight)

    mine = rank // heads + groups * jnp.arange(slots, dtype=jnp.int32)
    my_packs = jnp.take(safe, mine, mode="clip")
    first = first.reshape(packs, n, shard)
    lows = (jnp.take(first[:, :, 0], my_packs, axis=0, mode="clip") // shard).astype(jnp.int32)
    wide = [pltpu.VMEM((n, HD, shard), BF16)]
    tall = [pltpu.VMEM((n, shard, HD), BF16)]

    def first_at(skip):
        return pl.BlockSpec((1, n, shard), lambda s, a, b, c: (b[s + skip], 0, 0))

    def qkv_at(lead):
        return pl.BlockSpec((1, 1, 3, HD, shard), lambda s, *_: (lead, s, 0, 0, 0))

    def grad_at(lead, skip):
        return pl.BlockSpec((1, 1, HD, shard), lambda s, *_: (lead, s + skip, 0, 0))

    def attend(c, sources):
        return pl.pallas_call(
            functools.partial(attend_kernel, n, shard, c * per),
            grid_spec=pltpu.PrefetchScalarGridSpec(
                num_scalar_prefetch=3,
                grid=(per,),
                in_specs=[first_at(c * per)] + [qkv_at(lead) for _, lead in sources],
                out_specs=[pl.BlockSpec((1, HD, shard), lambda s, *_: (s, 0, 0))] * n
                + [
                    pl.BlockSpec((1, n, HD, shard), lambda s, *_: (s, 0, 0, 0)),
                    pl.BlockSpec((1, n, shard), lambda s, *_: (s, 0, 0)),
                ],
                scratch_shapes=wide * 2 + tall,
            ),
            out_shape=[jax.ShapeDtypeStruct((per, HD, shard), BF16)] * n
            + [
                jax.ShapeDtypeStruct((per, n, HD, shard), BF16),
                jax.ShapeDtypeStruct((per, n, shard), F32),
            ],
            compiler_params=params(),
            cost_estimate=COST,
            name="attend",
        )(me, my_packs, lows, first, *[array for array, _ in sources])

    def attend_back(c, kept, logsum, sources, grads):
        return pl.pallas_call(
            functools.partial(attend_back_kernel, n, shard, c * per),
            grid_spec=pltpu.PrefetchScalarGridSpec(
                num_scalar_prefetch=3,
                grid=(per,),
                in_specs=[
                    first_at(c * per),
                    pl.BlockSpec((1, n, HD, shard), lambda s, *_: (s, 0, 0, 0)),
                    pl.BlockSpec((1, n, shard), lambda s, *_: (s, 0, 0)),
                ]
                + [qkv_at(lead) for _, lead in sources]
                + [grad_at(lead, c * per) for _, lead in grads],
                out_specs=[pl.BlockSpec((1, 3, HD, shard), lambda s, *_: (s, 0, 0, 0))] * n,
                scratch_shapes=wide * 3
                + tall * 4
                + [pltpu.VMEM((n, shard, HD), F32)] * 2
                + [pltpu.VMEM((n, 3, HD, shard), BF16)],
            ),
            out_shape=parts,
            compiler_params=params(),
            cost_estimate=COST,
            name="attend_back",
        )(
            me,
            my_packs,
            lows,
            first,
            kept,
            logsum,
            *[array for array, _ in sources],
            *[array for array, _ in grads],
        )

    def merge(sources, branch_ff):
        return pl.pallas_call(
            functools.partial(merge_kernel, n, heads, slices),
            grid_spec=pltpu.PrefetchScalarGridSpec(
                num_scalar_prefetch=1,
                grid=(slots, groups),
                in_specs=[
                    pl.BlockSpec(
                        (1, 1, 1, HD, shard),
                        lambda s, g, *_, lead=lead: (lead, s // per, s % per, 0, 0),
                    )
                    for _, lead in sources
                ]
                + [rows_at(0), pl.BlockSpec((joined, width), whole2), rows_at(0)],
                out_specs=[
                    pl.BlockSpec(
                        (slices, 1, shard, width // slices),
                        lambda s, g, *_: (0, s * groups + g, 0, 0),
                    ),
                    pl.BlockSpec((joined, width), whole2),
                ],
                scratch_shapes=[
                    pltpu.VMEM((heads, HD, shard), BF16),
                    pltpu.VMEM((joined, width), F32),
                ],
            ),
            out_shape=[
                jax.ShapeDtypeStruct((slices, dealt, shard, width // slices), BF16),
                jax.ShapeDtypeStruct((joined, width), BF16),
            ],
            compiler_params=params(),
            cost_estimate=COST,
            name="merge",
        )(me, *[array for array, _ in sources], cot, merge_weight, branch_ff)

    def close(c, sources):
        skip = c * per
        return pl.pallas_call(
            functools.partial(close_kernel, n, heads),
            grid_spec=pltpu.PrefetchScalarGridSpec(
                num_scalar_prefetch=1,
                grid=(per, groups),
                in_specs=[
                    pl.BlockSpec(
                        (1, 1, 3, HD, shard), lambda s, g, *_, lead=lead: (lead, s, 0, 0, 0)
                    )
                    for _, lead in sources
                ]
                + [
                    rows_at(skip),
                    pl.BlockSpec((3 * joined, width), whole2),
                    table_at(skip),
                    table_at(skip),
                    rows_at(skip),
                ],
                out_specs=[rows_at(0), pl.BlockSpec((3 * joined, width), whole2)],
                scratch_shapes=[
                    pltpu.VMEM((3, heads, HD, shard), BF16),
                    pltpu.VMEM((3 * joined, width), F32),
                ],
            ),
            out_shape=[
                jax.ShapeDtypeStruct((per * groups, shard, width), BF16),
                jax.ShapeDtypeStruct((3 * joined, width), F32),
            ],
            compiler_params=params(),
            cost_estimate=COST,
            name="close",
        )(me, *[array for array, _ in sources], normed_low, w_t, cosine, sine, low_ff)

    got_x = [None] * chunks
    got_z = [None] * chunks
    got_x[0] = send_x(qkv[0])
    hidden = (
        jnp.einsum("psd,df->psf", normed_low, up_weight, preferred_element_type=F32) + up_bias
    )
    active_low = jax.nn.gelu(hidden, approximate=True).astype(BF16)
    branch_ff = jnp.einsum(
        "psf,fd->psd", active_low, down_weight, preferred_element_type=F32
    ).astype(BF16)
    got_x[0], branch_ff, qkv, out_weight, back_weight = tie(
        got_x[0], branch_ff, qkv, merge_weight, down_weight
    )

    got_z[0] = send_z(qkv[0], got_x[0])
    if chunks > 1:
        got_x[1] = send_x(qkv[1])
    sends = out_grads(cot, out_weight)
    active_grad = jnp.einsum("psd,fd->psf", cot, back_weight, preferred_element_type=F32)
    _, gelu_back = jax.vjp(lambda values: jax.nn.gelu(values, approximate=True), hidden)
    hidden_grad = gelu_back(active_grad)[0].astype(BF16)
    got_x, got_z, qkv, sends, hidden_grad = tie(got_x, got_z, qkv, sends, hidden_grad)

    got_dx = send_x(sends)
    sources = [received(qkv[0], got_x[0], got_z[0])]
    if chunks > 1:
        got_z[1] = send_z(qkv[1], got_x[1])
        sources.append(received(qkv[1], got_x[1], got_z[1]))
    ahead = [attend(0, sources[0])]
    up_grad = jnp.einsum(
        "psd,psf->df", normed_low, hidden_grad, preferred_element_type=F32
    ).astype(BF16)
    down_grad = jnp.einsum("psd,psf->df", cot, active_low, preferred_element_type=F32).astype(BF16)
    biases = jnp.sum(hidden_grad.astype(F32), axis=(0, 1)), jnp.sum(cot.astype(F32), axis=(0, 1))
    got_dx, sources_arrays, ahead, sends, hidden_grad, up_grad, down_grad, biases = tie(
        got_dx,
        [[a for a, _ in v] for v in sources],
        ahead,
        sends,
        hidden_grad,
        up_grad,
        down_grad,
        biases,
    )
    def with_row(*parts):
        weight = jnp.concatenate(parts[:2], axis=1)
        row = jnp.concatenate(parts[2:])
        row = jnp.pad(row, (0, weight.shape[1] - row.shape[0])).reshape(1, -1)
        row = jnp.broadcast_to(row, (16, weight.shape[1])).astype(BF16)
        return jnp.concatenate([weight, row], axis=0)

    terms = dict(
        enumerate(
            with_row(*parts)
            for parts in zip(*[cut(v, 0, n, rank) for v in (up_grad, down_grad, *biases)])
        )
    )
    terms_got = cube_send(terms, "seq", n, seq_masks)
    sources = [
        [(a, lead) for a, (_, lead) in zip(arrays, v)] for arrays, v in zip(sources_arrays, sources)
    ]

    got_dz = send_z(sends, got_dx)
    if chunks > 1:
        ahead.append(attend(1, sources[1]))
    low_ff = jnp.einsum(
        "psf,df->psd", hidden_grad, up_weight, preferred_element_type=F32
    ).astype(BF16)
    got_dz, ahead, low_ff = tie(got_dz, ahead, low_ff)
    grads = received(sends, got_dx, got_dz)

    attended = [jnp.stack([outs[k] for outs in ahead]) for k in range(n)]
    got_ax = send_x(attended)
    backs = [attend_back(0, ahead[0][n], ahead[0][n + 1], sources[0], grads)]
    got_ax, terms_got, backs, attended, ahead = tie(got_ax, terms_got, backs, attended, ahead)

    terms = cube_add(terms, terms_got, seq_masks, BF16)
    terms_got = cube_send(terms, "seq", n, seq_masks[1:])
    got_az = send_z(attended, got_ax)
    back_x = [send_x(backs[0])]
    if chunks > 1:
        backs.append(attend_back(1, ahead[1][n], ahead[1][n + 1], sources[1], grads))
    got_az, terms_got, back_x, backs = tie(got_az, terms_got, back_x, backs)

    back_z = [send_z(backs[0], back_x[0])]
    if chunks > 1:
        back_x.append(send_x(backs[1]))
    for step in range(1, len(seq_masks)):
        last_step = step == len(seq_masks) - 1
        terms = cube_add(terms, terms_got, seq_masks[step:], F32 if last_step else BF16)
        if not last_step:
            terms_got = cube_send(terms, "seq", n, seq_masks[step + 1 :])
    terms = terms[0]
    branch, merge_part = merge(received(attended, got_ax, got_az), branch_ff)
    summed = lax.psum_scatter(branch, "mlp", scatter_dimension=0, tiled=False)
    back_x, back_z, backs, merge_part, terms = tie(back_x, back_z, backs, merge_part, terms)

    share = per * groups * shard // slices

    def share_sum(low):
        return cube_sum(
            cut(low.reshape(share * slices, width), 0, slices, column), "mlp", mlp_masks, BF16
        )

    def finish(c, low_sum):
        start = (c * slices + column) * share
        row_in = lax.dynamic_slice_in_dim(
            tokens_dealt.reshape(rows, width), start, share, 0
        ).astype(F32)
        row_cot = lax.dynamic_slice_in_dim(cot.reshape(rows, width), start, share, 0).astype(F32)
        cent = row_in - jnp.mean(row_in, axis=-1, keepdims=True)
        inverse = lax.rsqrt(jnp.mean(cent * cent, axis=-1, keepdims=True) + EPS)
        xhat = cent * inverse
        g = low_sum * norm_gain
        row_grad = (
            row_cot
            + (
                g
                - jnp.mean(g, axis=-1, keepdims=True)
                - xhat * jnp.mean(g * xhat, axis=-1, keepdims=True)
            )
            * inverse
        ).astype(BF16)
        return row_grad, jnp.stack([jnp.sum(low_sum * xhat, axis=0), jnp.sum(low_sum, axis=0)])

    low, head_part = close(0, received(backs[0], back_x[0], back_z[0]))
    head_parts = [head_part]
    if chunks > 1:
        second = send_z(backs[1], back_x[1], [n // 2])
        second, low, head_parts, backs, back_x = tie(second, low, head_parts, backs, back_x)
        others = send_z(backs[1], back_x[1], [k for k in range(2, n, 2) if k != n // 2])
        others.insert(n // 4 - 1, second[0])
        back_z.append(others)
    row_grad, vectors = finish(0, share_sum(low))
    back_z, row_grad, vectors = tie(back_z, row_grad, vectors)

    cols = width // slices
    pieces = gather_step([row_grad[None]], "mlp", slices, mlp_masks[-1])
    result = (
        lax.dynamic_slice_in_dim(tokens, column * cols, cols, 2).astype(F32)
        + jnp.take(summed, at, axis=0, mode="clip").astype(F32)
        + lax.dynamic_slice_in_dim(down_bias, column * cols, cols, 0)
    ).astype(BF16)
    if chunks > 1:
        low, head_part = close(1, received(backs[1], back_x[1], back_z[1]))
        head_parts.append(head_part)
        pieces, low, head_parts, result = tie(pieces, low, head_parts, result)
    weights = functools.reduce(jnp.add, head_parts)
    weights = jnp.concatenate([weights.astype(BF16), merge_part], axis=0)
    weights = dict(enumerate(cut(weights, 1, n, rank)))
    weights_got = cube_send(weights, "seq", n, seq_masks)
    if chunks > 1:
        low_sum = share_sum(low)
        for m in reversed(mlp_masks[:-1]):
            pieces = gather_step(pieces, "mlp", slices, m)
        row_grad, more = finish(1, low_sum)
        vectors = vectors + more
        row_grad, pieces, weights_got, vectors = tie(row_grad, pieces, weights_got, vectors)
        last = gather_step([row_grad[None]], "mlp", slices, mlp_masks[-1])
    else:
        last, pieces = pieces, []
    vectors = small_sum(vectors, n, slices)
    weights = cube_add(weights, weights_got, seq_masks, BF16)
    weights_got = cube_send(weights, "seq", n, seq_masks[1:])
    last, vectors, weights_got = tie(last, vectors, weights_got)
    for m in reversed(mlp_masks[:-1]):
        last = gather_step(last, "mlp", slices, m)
    pieces += last
    where = [(0, 0)]
    lookup = [0]
    for i, m in enumerate(reversed(mlp_masks)):
        where += [(i + 1, j) for j in range(len(lookup))]
        lookup += [k ^ m for k in lookup]
    per_piece = [where[lookup.index(k)] for k in range(slices)]
    block = math.gcd(share, shard)
    tokens_grad = pl.pallas_call(
        functools.partial(
            place_kernel, block, share, shard, slices, chunks, per_piece
        ),
        grid_spec=pltpu.PrefetchScalarGridSpec(
            num_scalar_prefetch=1,
            grid=(1,),
            in_specs=[pl.BlockSpec(memory_space=pl.ANY)] * len(pieces),
            out_specs=pl.BlockSpec(memory_space=pl.ANY),
            scratch_shapes=[
                pltpu.VMEM((rows // block, block, width), BF16),
                pltpu.SemaphoreType.DMA((rows // block,)),
                pltpu.SemaphoreType.DMA((rows // block,)),
            ],
        ),
        out_shape=jax.ShapeDtypeStruct((packs + spare, shard, width), BF16),
        compiler_params=params(),
        name="place",
    )(jnp.concatenate([pack_at, column.astype(jnp.int32).reshape(1)]), *pieces)[:packs]

    for step in range(1, len(seq_masks)):
        weights = cube_add(
            weights, weights_got, seq_masks[step:], F32 if step == len(seq_masks) - 1 else BF16
        )
        if step < len(seq_masks) - 1:
            weights_got = cube_send(weights, "seq", n, seq_masks[step + 1 :])
    weights = weights[0]
    head_grad = jnp.transpose(
        weights[: 3 * joined].reshape(3, joined, width // n), (0, 2, 1)
    )
    merge_grad = weights[3 * joined :]
    part, hidden_here = width // n, up_weight.shape[1]
    up_grad, down_grad = terms[:part, :hidden_here], terms[:part, hidden_here:].T
    up_bias_grad = terms[part, : hidden_here // n]
    down_bias_grad = terms[part, hidden_here // n : hidden_here // n + part]
    return (
        result,
        tokens_grad,
        vectors[0],
        vectors[1],
        head_grad,
        merge_grad,
        up_grad,
        up_bias_grad,
        down_grad,
        down_bias_grad,
    )


def qkv_kernel(heads, me_ref, x_ref, w_ref, cos_ref, sin_ref, normed_ref, out_ref):
    width = heads * HD
    normed = x_ref[0]
    normed_ref[...] = normed
    for j in range(3):
        part = dot(w_ref[j * width : (j + 1) * width, :], normed, ((1,), (1,)))
        if j < 2:
            part = turn(part, cos_ref[...], sin_ref[...], heads)
        if j == 0:
            part = part * (1.0 / math.sqrt(HD))
        part = part.astype(BF16)
        for h in range(heads):
            out_ref[h, j] = part[h * HD : (h + 1) * HD]


def allowed_of(block, first, i):
    rows = lax.broadcasted_iota(jnp.int32, (block, block), 0)
    cols = lax.broadcasted_iota(jnp.int32, (block, block), 1)
    ahead = rows - cols
    return lambda j: (rows >= first - j * block) & (ahead <= (i - j) * block)


def unit_kernel(n, block, me_ref, low_ref, first_ref, qkv_ref, out_ref, keep_ref, logsum_ref, qt, vt, kn):
    me = me_ref[0]
    pair = range(qkv_ref.shape[0])
    for u in pair:
        for i in range(n):
            at = slice(i * block, (i + 1) * block)
            qt[u, i] = qkv_ref[u, 0, :, at]
            kn[u, i] = qkv_ref[u, 1, :, at].T
            vt[u, i] = qkv_ref[u, 2, :, at]

    def outer(i, carry):
        allowed = allowed_of(block, first_ref[pl.ds(i, 1), :], i)
        j0 = low_ref[i]

        def forward(t, states):
            j = j0 + 2 * t
            at = jnp.minimum(j + 1, n - 1)
            mask0, mask1 = allowed(j), allowed(j + 1)
            out = []
            for u, (top, total, acc) in zip(pair, states):
                q_t = qt[u, i]
                s0 = jnp.where(mask0, dot(kn[u, j], q_t), NEG)
                s1 = jnp.where(mask1, dot(kn[u, at], q_t), NEG)
                peak = jnp.max(jnp.maximum(s0, s1), axis=0, keepdims=True)
                new_top = jnp.maximum(top, peak)
                p0, p1 = jnp.exp(s0 - new_top), jnp.exp(s1 - new_top)
                fade = jnp.exp(top - new_top)
                total = total * fade + jnp.sum(p0 + p1, axis=0, keepdims=True)
                acc = acc * fade + dot(vt[u, j], p0.astype(BF16)) + dot(vt[u, at], p1.astype(BF16))
                out.append((new_top, total, acc))
            return tuple(out)

        states = lax.fori_loop(
            0,
            (i - j0) // 2 + 1,
            forward,
            tuple(
                (
                    jnp.full((1, block), NEG, F32),
                    jnp.zeros((1, block), F32),
                    jnp.zeros((HD, block), F32),
                )
                for _ in pair
            ),
        )
        for u, (top, total, acc) in zip(pair, states):
            keep_ref[u, i] = (acc / total).astype(BF16)
            logsum_ref[u, pl.ds(i, 1), :] = top + jnp.log(total)
        return carry

    lax.fori_loop(0, n, outer, 0)
    for k in range(n):
        for u in pair:
            out_ref[k, u] = keep_ref[u, lax.bitwise_xor(jnp.int32(k), me)]


def unit_back_kernel(
    n, block, by, me_ref, low_ref, first_ref, keep_ref, logsum_ref, qkv_ref, grad_ref, out_ref,
    qt, kt, gt, qn, kn, vn, gn, dk, dv, dqs
):
    me = me_ref[0]
    pair = range(qkv_ref.shape[0])
    for u in pair:
        for i in range(n):
            at = slice(i * block, (i + 1) * block)
            for j, (t_ref, n_ref) in enumerate(((qt, qn), (kt, kn), (None, vn))):
                part = qkv_ref[u, j, :, at]
                if t_ref is not None:
                    t_ref[u, i] = part
                n_ref[u, i] = part.T
        for k in range(n):
            d = lax.bitwise_xor(jnp.int32(k), me)
            part = grad_ref[k, u]
            gt[u, d] = part
            gn[u, d] = part.T
    dk[...] = jnp.zeros_like(dk)
    dv[...] = jnp.zeros_like(dv)

    def outer(i, carry):
        allowed = allowed_of(block, first_ref[pl.ds(i, 1), :], i)
        j0 = low_ref[i]
        inner = [
            jnp.sum(keep_ref[u, i].astype(F32) * gt[u, i].astype(F32), axis=0, keepdims=True)
            for u in pair
        ]
        logsum = [logsum_ref[u, pl.ds(i, 1), :] for u in pair]

        def one(u, mask, at):
            s = jnp.where(mask, dot(kn[u, at], qt[u, i]), NEG)
            p = jnp.exp(s - logsum[u])
            ds = (p * (dot(vn[u, at], gt[u, i]) - inner[u])).astype(BF16)
            return dot(ds, qn[u, i]), dot(p.astype(BF16), gn[u, i]), dot(kt[u, at], ds)

        def backward(t, dqs):
            j = j0 + by * t
            spots = [jnp.minimum(j + b, n - 1) if b else j for b in range(by)]
            masks = [allowed(j + b) for b in range(by)]
            out = []
            for u, dq in zip(pair, dqs):
                terms = [one(u, mask, at) for mask, at in zip(masks, spots)]
                for (dk0, dv0, dq0), at in zip(terms, spots):
                    dk[u, at] += dk0
                    dv[u, at] += dv0
                    dq = dq + dq0
                out.append(dq)
            return tuple(out)

        dq = lax.fori_loop(
            0, (i - j0) // by + 1, backward, tuple(jnp.zeros((HD, block), F32) for _ in pair)
        )
        for u in pair:
            dqs[u, i] = (dq[u] * (1.0 / math.sqrt(HD))).astype(BF16)
        return carry

    lax.fori_loop(0, n, outer, 0)
    for u in pair:
        for i in range(n):
            at = slice(i * block, (i + 1) * block)
            out_ref[u, 0, :, at] = dqs[u, i]
            out_ref[u, 1, :, at] = dk[u, i].T.astype(BF16)
            out_ref[u, 2, :, at] = dv[u, i].T.astype(BF16)


def rows_kernel(heads, slices, me_ref, grad_ref, normed_ref, w_ref, cos_ref, sin_ref, *refs):
    kept_ref, sent_ref, weight_ref = refs[-3:]
    width = heads * HD
    column = me_ref[1]

    @pl.when(pl.program_id(0) == 0)
    def _():
        if len(refs) > 3:
            weight_ref[...] = refs[0][...]
        else:
            weight_ref[...] = jnp.zeros_like(weight_ref)

    parts = []
    for j in range(3):
        part = jnp.concatenate([grad_ref[h, j] for h in range(heads)], axis=0)
        if j < 2:
            part = turn(part.astype(F32), cos_ref[...], -sin_ref[...], heads).astype(BF16)
        parts.append(part)
    grads = jnp.concatenate(parts, axis=0)
    if len(refs) > 3:
        whole = weight_ref.shape[0] // 3
        start = lax.rem(me_ref[0], 2) * width
        for j in range(3):
            rows = pl.ds(pl.multiple_of(j * whole + start, width), width)
            weight_ref[rows, :] += dot(parts[j], normed_ref[...])
    else:
        weight_ref[...] += dot(grads, normed_ref[...])
    low = dot(grads.T, w_ref[...]).astype(BF16)
    part = low.shape[0] // slices
    for m in range(slices):
        at = lax.bitwise_xor(jnp.int32(m), column)
        for bit, ref in enumerate((kept_ref, sent_ref)):

            @pl.when(at % 2 == bit)
            def _():
                ref[at // 2, 0] = low[m * part : (m + 1) * part]


def norm_kernel(me_ref, x_ref, gain_ref, bias_ref, normed_ref, cols_ref):
    cols = cols_ref.shape[2]
    start = pl.multiple_of(me_ref[1] * cols, cols)
    step = math.gcd(x_ref.shape[1], 32)
    for r in range(0, x_ref.shape[1], step):
        x = x_ref[0, r : r + step].astype(F32)
        cent = x - jnp.mean(x, axis=-1, keepdims=True)
        var = jnp.mean(cent * cent, axis=-1, keepdims=True)
        normed = cent * lax.rsqrt(var + EPS) * gain_ref[...] + bias_ref[...]
        normed_ref[0, r : r + step] = normed.astype(BF16)
    cols_ref[0] = normed_ref[0, :, pl.ds(start, cols)]


def finish_kernel(terms, which_ref, *refs):
    lows = refs[:terms]
    low_ref, x_ref, c_ref, gain_ref, out_ref, sums_ref = refs[terms:]

    @pl.when(pl.program_id(0) == 0)
    def _():
        sums_ref[...] = jnp.zeros_like(sums_ref)

    low = low_ref[0].astype(F32)
    for ref in lows:
        low = low + ref[0].astype(F32)
    x = x_ref[0].astype(F32)
    cent = x - jnp.mean(x, axis=-1, keepdims=True)
    inverse = lax.rsqrt(jnp.mean(cent * cent, axis=-1, keepdims=True) + EPS)
    xhat = cent * inverse
    g = low * gain_ref[...]
    inner = jnp.mean(g * xhat, axis=-1, keepdims=True)
    back = (g - jnp.mean(g, axis=-1, keepdims=True) - xhat * inner) * inverse
    out_ref[0] = (c_ref[0].astype(F32) + back).astype(BF16)
    sums_ref[0:1] += jnp.sum(low * xhat, axis=0, keepdims=True)
    sums_ref[1:2] += jnp.sum(low, axis=0, keepdims=True)


def join_kernel(slices, attended_ref, c_ref, merge_ref, branch_ref, out_branch, out_weight):
    @pl.when(pl.program_id(0) == 0)
    def _():
        out_weight[...] = jnp.zeros_like(out_weight)

    attended = attended_ref[0]
    out_weight[...] += dot(attended, c_ref[0])
    branch = dot(attended.T, merge_ref[...]) + branch_ref[0].astype(F32)
    cols = branch.shape[1] // slices
    for m in range(slices):
        out_branch[m, 0] = branch[:, m * cols : (m + 1) * cols].astype(BF16)


def settle_kernel(counts, slices, sub, per_piece, table_ref, *refs):
    pieces, out, buf, sems, out_sems = refs[:-4], refs[-4], refs[-3], refs[-2], refs[-1]
    column = table_ref[sum(counts)]
    loads, stores = [], []
    arrays = max(ref for ref, _ in per_piece) + 1
    first = 0
    for c, count in enumerate(counts):
        for k in range(slices):
            ref, where = per_piece[k]
            start = pl.multiple_of(lax.bitwise_xor(jnp.int32(k), column) * sub, sub)
            for t in range(count):
                at = len(loads)
                loads.append(
                    pltpu.make_async_copy(
                        pieces[c * arrays + ref].at[where, t], buf.at[at], sems.at[at]
                    )
                )
                stores.append(
                    pltpu.make_async_copy(
                        buf.at[at],
                        out.at[table_ref[first + t], pl.ds(start, sub)],
                        out_sems.at[at],
                    )
                )
        first += count
    for copy in loads:
        copy.start()
    for load, store in zip(loads, stores):
        load.wait()
        store.start()
    for copy in stores:
        copy.wait()


def exchange_x(array):
    n = array.shape[0]
    return lax.ppermute(array[1::2], "seq", [(i, i ^ 1) for i in range(n)])


def exchange_z(array, got, steps=None):
    n = array.shape[0]
    return [
        lax.ppermute(jnp.stack([array[k], got[k // 2]]), "seq", [(i, i ^ k) for i in range(n)])
        for k in (range(2, n, 2) if steps is None else steps)
    ]


def exchanged(array, got, gots):
    return jnp.concatenate([array[:1], got[:1], *gots], axis=0)


def sum_on(terms, axis, n, masks):
    for step in range(len(masks)):
        terms = {k: v.astype(BF16) for k, v in terms.items()}
        got = cube_send(terms, axis, n, masks[step:])
        terms = cube_add(terms, got, masks[step:], F32)
    return terms[0].astype(BF16)


def take(array, index):
    return jnp.take(array, index, axis=0, mode="clip")


def on_device_pairs(
    tokens,
    lengths,
    counts,
    norm_gain,
    norm_bias,
    head_weight,
    merge_weight,
    up_weight,
    up_bias,
    down_weight,
    down_bias,
    cotangent,
):
    packs, shard, width = tokens.shape
    n = lax.axis_size("seq")
    slices = lax.axis_size("mlp")
    pack_len = shard * n
    rank = lax.axis_index("seq").astype(jnp.int32)
    column = lax.axis_index("mlp").astype(jnp.int32)
    heads = merge_weight.shape[0] // HD
    joined = heads * HD
    half = heads // 2
    cols = width // slices
    sub = shard // slices
    seq_masks, mlp_masks = masks_of(n), masks_of(slices)
    pairs = n // 2

    cot = lax.all_gather(cotangent, "mlp", axis=2, tiled=True)

    first, position, cost = layout(lengths, counts, pack_len)
    ids = jnp.arange(packs, dtype=jnp.int32)
    before = (cost[None, :] > cost[:, None]) | (
        (cost[None, :] == cost[:, None]) & (ids[None, :] < ids[:, None])
    )
    order = jnp.sum(before.astype(jnp.int32), axis=1)
    by_order = jnp.sum(
        jnp.where(order[None, :] == ids[:, None], ids[None, :], 0), axis=-1
    ).astype(jnp.int32)
    devices = jnp.arange(n, dtype=jnp.int32)
    shared_of = by_order[:pairs]
    own_of = by_order[pairs + 2 * (pairs - 1 - devices // 2) + devices % 2]
    late = order - pairs
    pair_of = jnp.where(late < 0, order, pairs - 1 - late // 2)
    device_of = 2 * pair_of + jnp.where(late < 0, 0, late % 2)
    dest = jnp.bitwise_xor(rank, devices)
    own_dest, shared_dest = own_of[dest], shared_of[dest // 2]
    me = jnp.stack([rank, column])

    head_ids = jnp.arange(heads, dtype=jnp.int32)
    half_ids = jnp.arange(half, dtype=jnp.int32)
    units_out = jnp.concatenate(
        [
            own_dest[:, None] * heads + head_ids[None, :],
            shared_dest[:, None] * heads + (dest % 2)[:, None] * half + half_ids[None, :],
        ],
        axis=1,
    ).reshape(-1)
    is_shared = (order < pairs)[:, None]
    holder = device_of[:, None] + jnp.where(is_shared, head_ids[None, :] // half, 0)
    units_in = (
        jnp.bitwise_xor(holder, rank) * (heads + half)
        + jnp.where(is_shared, heads + head_ids[None, :] % half, head_ids[None, :])
    ).reshape(-1)

    def tables(pack):
        freq = 10000.0 ** (-(2.0 * jnp.arange(ROT // 2, dtype=F32)) / ROT)
        angle = take(position, pack).astype(F32)[None, :] * jnp.repeat(freq, 2)[:, None]
        return jnp.cos(angle), jnp.sin(angle)

    w_heads = jnp.transpose(head_weight, (0, 2, 1)).reshape(3, heads, HD, width)
    w_own = w_heads.reshape(3 * joined, width)
    part_at = (rank % 2) * half
    w_shared = lax.dynamic_slice_in_dim(w_heads, part_at, half, 1).reshape(3 * half * HD, width)
    packs_here = (own_of[rank], shared_of[rank // 2])
    turns = [tables(p) for p in packs_here]
    firsts = [take(first, p).reshape(n, shard) for p in packs_here]
    lows = [(f[:, 0] // shard).astype(jnp.int32) for f in firsts]
    gain, bias = norm_gain.reshape(1, width), norm_bias.reshape(1, width)

    def whole2(s, *_):
        return (0, 0)

    def lane_at(s, *_):
        return (0, s)

    def project(rows, weight, cosine, sine):
        h = weight.shape[0] // (3 * HD)
        return pl.pallas_call(
            functools.partial(qkv_kernel, h),
            grid_spec=pltpu.PrefetchScalarGridSpec(
                num_scalar_prefetch=1,
                grid=(n,),
                in_specs=[
                    pl.BlockSpec(
                        (1, shard, width), lambda s, me: (lax.bitwise_xor(s, me[0]), 0, 0)
                    ),
                    pl.BlockSpec(weight.shape, whole2),
                    pl.BlockSpec((ROT, shard), lane_at),
                    pl.BlockSpec((ROT, shard), lane_at),
                ],
                out_specs=[
                    pl.BlockSpec((shard, width), lambda s, *_: (s, 0)),
                    pl.BlockSpec((h, 3, HD, shard), lambda s, *_: (0, 0, 0, s)),
                ],
            ),
            out_shape=[
                jax.ShapeDtypeStruct((pack_len, width), BF16),
                jax.ShapeDtypeStruct((h, 3, HD, pack_len), BF16),
            ],
            compiler_params=params(),
            cost_estimate=COST,
            name="project",
        )(me, rows, weight, cosine, sine)

    def wide(h):
        return [pltpu.VMEM((h, n, HD, shard), BF16)]

    def tall(h, kind=BF16):
        return [pltpu.VMEM((h, n, shard, HD), kind)]

    def keep_spec(h):
        return pl.BlockSpec((h, n, HD, shard), lambda u, *_: (u, 0, 0, 0))

    def log_spec(h):
        return pl.BlockSpec((h, n, shard), lambda u, *_: (u, 0, 0))

    def unit_spec(h):
        return pl.BlockSpec((h, 3, HD, pack_len), lambda u, *_: (u, 0, 0, 0))

    def attend(c, qkv):
        h = qkv.shape[0]
        return pl.pallas_call(
            functools.partial(unit_kernel, n, shard),
            grid_spec=pltpu.PrefetchScalarGridSpec(
                num_scalar_prefetch=2,
                grid=(1,),
                in_specs=[pl.BlockSpec((n, shard), whole2), unit_spec(h)],
                out_specs=[
                    pl.BlockSpec((n, h, HD, shard), lambda u, *_: (0, u, 0, 0)),
                    keep_spec(h),
                    log_spec(h),
                ],
                scratch_shapes=wide(h) * 2 + tall(h),
            ),
            out_shape=[
                jax.ShapeDtypeStruct((n, h, HD, shard), BF16),
                jax.ShapeDtypeStruct((h, n, HD, shard), BF16),
                jax.ShapeDtypeStruct((h, n, shard), F32),
            ],
            compiler_params=params(),
            cost_estimate=COST,
            name="attend",
        )(me, lows[c], firsts[c], qkv)

    def attend_back(c, kept, logsum, qkv, grads):
        h = qkv.shape[0]
        step = h if c == 0 else 2
        skip = c * heads // step
        return pl.pallas_call(
            functools.partial(unit_back_kernel, n, shard, c + 1),
            grid_spec=pltpu.PrefetchScalarGridSpec(
                num_scalar_prefetch=2,
                grid=(h // step,),
                in_specs=[
                    pl.BlockSpec((n, shard), whole2),
                    keep_spec(step),
                    log_spec(step),
                    unit_spec(step),
                    pl.BlockSpec((n, step, HD, shard), lambda u, *_: (0, u + skip, 0, 0)),
                ],
                out_specs=unit_spec(step),
                scratch_shapes=wide(step) * 3 + tall(step) * 4 + tall(step, F32) * 2 + wide(step),
            ),
            out_shape=jax.ShapeDtypeStruct((h, 3, HD, pack_len), BF16),
            compiler_params=params(),
            cost_estimate=COST,
            name="attend_back",
        )(me, lows[c], firsts[c], kept, logsum, qkv, grads)

    def rows_back(grads, normed, weight, cosine, sine, *base):
        h = grads.shape[0]
        return pl.pallas_call(
            functools.partial(rows_kernel, h, slices),
            grid_spec=pltpu.PrefetchScalarGridSpec(
                num_scalar_prefetch=1,
                grid=(n,),
                in_specs=[
                    pl.BlockSpec((h, 3, HD, shard), lambda s, *_: (0, 0, 0, s)),
                    pl.BlockSpec((shard, width), lambda s, *_: (s, 0)),
                    pl.BlockSpec(weight.shape, whole2),
                    pl.BlockSpec((ROT, shard), lane_at),
                    pl.BlockSpec((ROT, shard), lane_at),
                ]
                + [pl.BlockSpec(v.shape, whole2) for v in base],
                out_specs=[
                    pl.BlockSpec(
                        (slices // 2, 1, sub, width),
                        lambda s, me: (0, lax.bitwise_xor(s, me[0]), 0, 0),
                    )
                ]
                * 2
                + [
                    pl.BlockSpec((3 * joined, width), whole2),
                ],
            ),
            out_shape=[
                jax.ShapeDtypeStruct((slices // 2, n, sub, width), BF16),
                jax.ShapeDtypeStruct((slices // 2, n, sub, width), BF16),
                jax.ShapeDtypeStruct((3 * joined, width), F32),
            ],
            compiler_params=params(),
            cost_estimate=COST,
            name="rows_back",
        )(me, grads, normed, weight, cosine, sine, *base)

    pack_spec = pl.BlockSpec((1, shard, width), lambda p, *_: (p, 0, 0))
    normed_low, normed_cols = pl.pallas_call(
        norm_kernel,
        grid_spec=pltpu.PrefetchScalarGridSpec(
            num_scalar_prefetch=1,
            grid=(packs,),
            in_specs=[
                pack_spec,
                pl.BlockSpec((1, width), whole2),
                pl.BlockSpec((1, width), whole2),
            ],
            out_specs=[pack_spec, pl.BlockSpec((1, shard, cols), lambda p, *_: (p, 0, 0))],
        ),
        out_shape=[
            jax.ShapeDtypeStruct((packs, shard, width), BF16),
            jax.ShapeDtypeStruct((packs, shard, cols), BF16),
        ],
        compiler_params=params(),
        cost_estimate=COST,
        name="norm",
    )(me, tokens, gain, bias)
    send_own = take(normed_cols, own_dest)
    send_shared = take(normed_cols, shared_dest)
    own_x = exchange_x(send_own)

    hidden = (
        jnp.einsum("psd,df->psf", normed_low, up_weight, preferred_element_type=F32) + up_bias
    )
    own_x, hidden, send_own, send_shared = tie(own_x, hidden, send_own, send_shared)

    own_z = exchange_z(send_own, own_x, [2])
    shared_x = exchange_x(send_shared)
    active_low = jax.nn.gelu(hidden, approximate=True).astype(BF16)
    branch_ff = jnp.einsum(
        "psf,fd->psd", active_low, down_weight, preferred_element_type=F32
    ).astype(BF16)
    own_z, shared_x, branch_ff, send_own, own_x, merge_here, down_here, turns, w_own, w_shared = tie(
        own_z,
        shared_x,
        branch_ff,
        send_own,
        own_x,
        merge_weight,
        down_weight,
        turns,
        w_own,
        w_shared,
    )

    own_z += exchange_z(send_own, own_x, range(4, n, 2))
    active_grad = jnp.einsum("psd,fd->psf", cot, down_here, preferred_element_type=F32)
    _, gelu_back = jax.vjp(lambda values: jax.nn.gelu(values, approximate=True), hidden)
    hidden_grad = gelu_back(active_grad)[0].astype(BF16)
    own_z, hidden_grad, send_shared, shared_x = tie(own_z, hidden_grad, send_shared, shared_x)
    rows_own = lax.all_gather(exchanged(send_own, own_x, own_z), "mlp", axis=2, tiled=True)

    shared_z = exchange_z(send_shared, shared_x)
    out_grad = jnp.einsum("hd,psd->phs", merge_here, cot, preferred_element_type=F32).astype(BF16)
    send_grad = take(out_grad.reshape(packs * heads, HD, shard), units_out).reshape(
        n, heads + half, HD, shard
    )
    up_grad = jnp.einsum(
        "psd,psf->df", normed_low, hidden_grad, preferred_element_type=F32
    ).astype(BF16)
    down_grad = jnp.einsum("psd,psf->df", cot, active_low, preferred_element_type=F32).astype(BF16)
    shared_z, send_grad, up_grad, down_grad, send_shared, shared_x, hidden_grad = tie(
        shared_z, send_grad, up_grad, down_grad, send_shared, shared_x, hidden_grad
    )
    rows_shared = lax.all_gather(
        exchanged(send_shared, shared_x, shared_z), "mlp", axis=2, tiled=True
    )

    grad_x = exchange_x(send_grad)
    low_ff = jnp.einsum(
        "psf,df->psd", hidden_grad, up_weight, preferred_element_type=F32
    ).astype(BF16)
    low_ff = jnp.transpose(low_ff.reshape(packs, slices, sub, width), (1, 0, 2, 3)).reshape(
        slices * packs * sub, width
    )
    biases = jnp.sum(hidden_grad.astype(F32), axis=(0, 1)), jnp.sum(cot.astype(F32), axis=(0, 1))
    grad_x, send_grad, low_ff, rows_own, biases = tie(grad_x, send_grad, low_ff, rows_own, biases)
    low_ff = lax.psum_scatter(low_ff, "mlp", scatter_dimension=0, tiled=True).reshape(
        packs, sub, width
    )

    grad_z = exchange_z(send_grad, grad_x)
    normed_own, qkv_own = project(rows_own, w_own, *turns[0])
    out_own, kept_own, log_own = attend(0, qkv_own)
    grad_z, out_own, kept_own, log_own, rows_shared = tie(
        grad_z, out_own, kept_own, log_own, rows_shared
    )
    grads = exchanged(send_grad, grad_x, grad_z)

    def with_row(*parts):
        weight = jnp.concatenate(parts[:2], axis=1)
        row = jnp.concatenate(parts[2:])
        row = jnp.pad(row, (0, weight.shape[1] - row.shape[0])).reshape(1, -1)
        row = jnp.broadcast_to(row, (16, weight.shape[1])).astype(BF16)
        return jnp.concatenate([weight, row], axis=0)

    terms = dict(
        enumerate(
            with_row(*parts)
            for parts in zip(*[cut(v, 0, n, rank) for v in (up_grad, down_grad, *biases)])
        )
    )
    terms_got = cube_send(terms, "seq", n, seq_masks)
    normed_shared, qkv_shared = project(rows_shared, w_shared, *turns[1])
    out_shared, kept_shared, log_shared = attend(1, qkv_shared)
    out_shared, kept_shared, log_shared, grads, terms_got = tie(
        out_shared, kept_shared, log_shared, grads, terms_got
    )
    terms = cube_add(terms, terms_got, seq_masks, BF16)
    terms_got = cube_send(terms, "seq", n, seq_masks[1:])

    send_out = jnp.concatenate([out_own, out_shared], axis=1)
    out_x = exchange_x(send_out)
    back_own = attend_back(0, kept_own, log_own, qkv_own, grads)
    out_x, back_own, terms_got, send_out = tie(out_x, back_own, terms_got, send_out)

    out_z = exchange_z(send_out, out_x)
    low_kept, low_sent, head_own = rows_back(back_own, normed_own, w_own, *turns[0])
    back_shared = attend_back(1, kept_shared, log_shared, qkv_shared, grads)
    out_z, low_kept, low_sent, back_shared, send_out, out_x = tie(
        out_z, low_kept, low_sent, back_shared, send_out, out_x
    )

    others = [(i, i ^ 1) for i in range(slices)]
    low_got, back_shared = tie(lax.ppermute(low_sent, "mlp", others), back_shared)
    low_terms = {
        2 * k: low_kept[k].astype(F32) + low_got[k].astype(F32) for k in range(slices // 2)
    }
    low_own = sum_on(low_terms, "mlp", slices, mlp_masks[1:])
    low_kept, low_sent, head_all = rows_back(back_shared, normed_shared, w_shared, *turns[1], head_own)
    attended = take(
        exchanged(send_out, out_x, out_z).reshape(n * (heads + half), HD, shard), units_in
    ).reshape(packs, joined, shard)
    for step in range(1, len(seq_masks) - 1):
        terms = cube_add(terms, terms_got, seq_masks[step:], BF16)
        terms_got = cube_send(terms, "seq", n, seq_masks[step + 1 :])
    low_own, low_kept, low_sent, attended, terms_got = tie(
        low_own, low_kept, low_sent, attended, terms_got
    )
    terms = cube_add(terms, terms_got, seq_masks[len(seq_masks) - 1 :], F32)[0]

    low_own_x = exchange_x(low_own)
    low_got = lax.ppermute(low_sent, "mlp", others)
    branch, merge_part = pl.pallas_call(
        functools.partial(join_kernel, slices),
        grid=(packs,),
        in_specs=[
            pl.BlockSpec((1, joined, shard), lambda p: (p, 0, 0)),
            pl.BlockSpec((1, shard, width), lambda p: (p, 0, 0)),
            pl.BlockSpec((joined, width), whole2),
            pl.BlockSpec((1, shard, width), lambda p: (p, 0, 0)),
        ],
        out_specs=[
            pl.BlockSpec((slices, 1, shard, cols), lambda p: (0, p, 0, 0)),
            pl.BlockSpec((joined, width), whole2),
        ],
        out_shape=[
            jax.ShapeDtypeStruct((slices, packs, shard, cols), BF16),
            jax.ShapeDtypeStruct((joined, width), F32),
        ],
        compiler_params=params(),
        cost_estimate=COST,
        name="join",
    )(attended, cot, merge_weight, branch_ff)
    low_kept, low_got, low_own, low_own_x, branch, low_ff, head_all = tie(
        low_kept, low_got, low_own, low_own_x, branch, low_ff, head_all
    )
    summed = lax.psum_scatter(branch, "mlp", scatter_dimension=0, tiled=False)

    low_terms = {
        2 * k: low_kept[k].astype(F32) + low_got[k].astype(F32) for k in range(slices // 2)
    }
    low_shared = sum_on(low_terms, "mlp", slices, mlp_masks[1:])
    weights = {
        k: jnp.concatenate(pair, axis=0).astype(BF16)
        for k, pair in enumerate(zip(cut(head_all, 1, n, rank), cut(merge_part, 1, n, rank)))
    }
    low_own_z = exchange_z(low_own, low_own_x)
    weights_got = cube_send(weights, "seq", n, seq_masks)
    low_own_z, low_shared, low_own, low_own_x, weights, weights_got, terms = tie(
        low_own_z, low_shared, low_own, low_own_x, weights, weights_got, terms
    )

    low_shared_x = exchange_x(low_shared)
    weights = cube_add(weights, weights_got, seq_masks, BF16)
    weights_got = cube_send(weights, "seq", n, seq_masks[1:])

    def finish(lows, index, which):
        count = which.shape[0]
        row_spec = pl.BlockSpec((1, sub, width), lambda t, at: (at[count + t], at[0], 0))

        def part(i):
            return pl.BlockSpec(
                (1, sub, width), lambda t, at: (at[(2 + i) * count + t], 0, 0)
            )

        table = [jnp.full((count,), column), which, *index]
        return pl.pallas_call(
            functools.partial(finish_kernel, len(lows)),
            grid_spec=pltpu.PrefetchScalarGridSpec(
                num_scalar_prefetch=1,
                grid=(count,),
                in_specs=[part(i) for i in range(len(lows))]
                + [
                    pl.BlockSpec((1, sub, width), lambda t, at: (at[count + t], 0, 0)),
                    row_spec,
                    row_spec,
                    pl.BlockSpec((1, width), whole2),
                ],
                out_specs=[
                    pl.BlockSpec((1, sub, width), lambda t, *_: (t, 0, 0)),
                    pl.BlockSpec((2, width), whole2),
                ],
            ),
            out_shape=[
                jax.ShapeDtypeStruct((count, sub, width), BF16),
                jax.ShapeDtypeStruct((2, width), F32),
            ],
            compiler_params=params(),
            cost_estimate=COST,
            name="finish",
        )(jnp.concatenate(table), *lows, low_ff, tokens, cot, gain)

    row_own, sums_own = finish(
        [exchanged(low_own, low_own_x, low_own_z)], [devices], own_dest
    )
    low_shared_x, row_own, sums_own, low_shared, weights_got = tie(
        low_shared_x, row_own, sums_own, low_shared, weights_got
    )
    for step in range(1, len(seq_masks)):
        last_step = step == len(seq_masks) - 1
        weights = cube_add(weights, weights_got, seq_masks[step:], F32 if last_step else BF16)
        if not last_step:
            weights_got = cube_send(weights, "seq", n, seq_masks[step + 1 :])
    weights = weights[0]
    low_shared_z = exchange_z(low_shared, low_shared_x)
    pieces = gather_step([row_own[None]], "mlp", slices, mlp_masks[-1])
    result = (
        lax.dynamic_slice_in_dim(tokens, column * cols, cols, 2).astype(F32)
        + summed.astype(F32)
        + lax.dynamic_slice_in_dim(down_bias, column * cols, cols, 0)
    ).astype(BF16)
    low_shared_z, pieces, weights, result = tie(low_shared_z, pieces, weights, result)

    for m in reversed(mlp_masks[:-1]):
        pieces = gather_step(pieces, "mlp", slices, m)
    both = exchanged(low_shared, low_shared_x, low_shared_z)
    even = jnp.bitwise_xor(2 * jnp.arange(pairs, dtype=jnp.int32), rank)
    row_shared, sums = finish([both, both], [even, jnp.bitwise_xor(even, 1)], shared_of)
    last = gather_step([row_shared[None]], "mlp", slices, mlp_masks[-1])
    vectors = small_sum(sums_own + sums, n, slices)
    last, pieces, vectors = tie(last, pieces, vectors)

    for m in reversed(mlp_masks[:-1]):
        last = gather_step(last, "mlp", slices, m)
    pieces += last
    where = [(0, 0)]
    lookup = [0]
    for i, m in enumerate(reversed(mlp_masks)):
        where += [(i + 1, j) for j in range(len(lookup))]
        lookup += [k ^ m for k in lookup]
    per_piece = [where[lookup.index(k)] for k in range(slices)]
    tokens_grad = pl.pallas_call(
        functools.partial(settle_kernel, (n, pairs), slices, sub, per_piece),
        grid_spec=pltpu.PrefetchScalarGridSpec(
            num_scalar_prefetch=1,
            grid=(1,),
            in_specs=[pl.BlockSpec(memory_space=pl.ANY)] * len(pieces),
            out_specs=pl.BlockSpec(memory_space=pl.ANY),
            scratch_shapes=[
                pltpu.VMEM((packs * slices, sub, width), BF16),
                pltpu.SemaphoreType.DMA((packs * slices,)),
                pltpu.SemaphoreType.DMA((packs * slices,)),
            ],
        ),
        out_shape=jax.ShapeDtypeStruct((packs, shard, width), BF16),
        compiler_params=params(),
        name="settle",
    )(jnp.concatenate([own_dest, shared_of, column.reshape(1)]), *pieces)

    part, hidden_here = width // n, up_weight.shape[1]
    return (
        result,
        tokens_grad,
        vectors[0],
        vectors[1],
        jnp.transpose(weights[: 3 * joined].reshape(3, joined, part), (0, 2, 1)),
        weights[3 * joined :],
        terms[:part, :hidden_here],
        terms[part, : hidden_here // n],
        terms[:part, hidden_here:].T,
        terms[part, hidden_here // n : hidden_here // n + part],
    )


def solution(mesh):
    in_specs = (
        P(None, "seq", None),
        P(),
        P(),
        P(),
        P(),
        P(None, None, "mlp"),
        P("mlp", None),
        P(None, "mlp"),
        P("mlp"),
        P("mlp", None),
        P(),
        P(None, "seq", "mlp"),
    )
    out_specs = (
        P(None, "seq", "mlp"),
        P(None, "seq", None),
        P("seq"),
        P("seq"),
        P(None, "seq", "mlp"),
        P("mlp", "seq"),
        P("seq", "mlp"),
        P(("mlp", "seq")),
        P("mlp", "seq"),
        P("seq"),
    )
    n, slices = mesh.shape["seq"], mesh.shape["mlp"]

    def plan(*args):
        packs, pack_len, _ = args[0].shape
        heads = args[6].shape[0] // HD // slices
        pairs = (
            2 * packs == 3 * n
            and n >= 4
            and heads % 4 == 0
            and (pack_len // n) % 128 == 0
            and (pack_len // n) % (16 * slices) == 0
        )
        return jax.shard_map(
            on_device_pairs if pairs else on_device,
            mesh=mesh,
            in_specs=in_specs,
            out_specs=out_specs,
            check_vma=False,
        )(*args)

    return plan
```

```python
import functools
import math

import jax
import jax.numpy as jnp
from jax import lax
from jax.experimental import pallas as pl
from jax.experimental.pallas import tpu as pltpu
from jax.sharding import PartitionSpec as P

HD = 64
ROT = 32
EPS = 1e-05
NEG = -1e30
BF16 = jnp.bfloat16
F32 = jnp.float32
VMEM_LIMIT = 56 * 1024 * 1024
COST = pl.CostEstimate(flops=1 << 20, bytes_accessed=1 << 20, transcendentals=0)


def dot(a, b, dims=((1,), (0,))):
    return lax.dot_general(a, b, (dims, ((), ())), preferred_element_type=F32)


def layout(lengths, counts, pack_len):
    slots = lengths.shape[-1]
    slot_ids = jnp.arange(slots, dtype=jnp.int32)
    used = slot_ids[None, :] < counts[:, None]
    sizes = jnp.where(used, lengths, 0)
    ends = jnp.cumsum(sizes, axis=-1)
    starts = ends - sizes
    filled = ends[:, -1:]
    place = jnp.arange(pack_len, dtype=jnp.int32)[None, :]
    begin = jnp.max(
        jnp.where(used[:, None, :] & (place[:, :, None] >= starts[:, None, :]), starts[:, None, :], 0),
        axis=-1,
    )
    inside = place < filled
    first = jnp.where(inside, begin, place)
    position = jnp.where(inside, place - begin, place - filled)
    cost = jnp.sum(sizes * sizes, axis=-1)
    return first, position, cost


def turn(values, cosine, sine, heads):
    out = []
    parity = lax.broadcasted_iota(jnp.int32, cosine.shape, 0) % 2
    for h in range(heads):
        part = values[h * HD : h * HD + ROT]
        ahead = jnp.concatenate([part[1:], part[:1]], axis=0)
        behind = jnp.concatenate([part[-1:], part[:-1]], axis=0)
        swapped = jnp.where(parity == 0, -ahead, behind)
        out.append(part * cosine + swapped * sine)
        out.append(values[h * HD + ROT : (h + 1) * HD])
    return jnp.concatenate(out, axis=0)


def head_kernel(n, heads, per, me_ref, pack_ref, x_ref, gain_ref, bias_ref, w_ref, cos_ref, sin_ref, *refs):
    normed_ref, copy_ref, outs, scr = refs[0], refs[1], refs[2:-1], refs[-1]
    s_id, g = pl.program_id(0), pl.program_id(1)
    me = me_ref[0]
    width = heads * HD
    copy_ref[0] = x_ref[0]
    x = x_ref[0].astype(F32)
    cent = x - jnp.mean(x, axis=-1, keepdims=True)
    var = jnp.mean(cent * cent, axis=-1, keepdims=True)
    normed = (cent * lax.rsqrt(var + EPS) * gain_ref[...] + bias_ref[...]).astype(BF16)
    normed_ref[0] = normed
    for j in range(3):
        part = dot(w_ref[j * width : (j + 1) * width, :], normed, ((1,), (1,)))
        if j < 2:
            part = turn(part, cos_ref[0], sin_ref[0], heads)
        if j == 0:
            part = part * (1.0 / math.sqrt(HD))
        part = part.astype(BF16)
        for h in range(heads):
            scr[h, j] = part[h * HD : (h + 1) * HD]
    for at, out in enumerate(outs):
        d = lax.bitwise_xor(jnp.int32(at % n), me)

        @pl.when((d // heads == g) & (s_id // per == at // n))
        def _():
            out[0] = scr[d % heads]


def grad_kernel(n, heads, me_ref, c_ref, w_ref, *refs):
    outs, scr = refs[:n], refs[n]
    g = pl.program_id(1)
    me = me_ref[0]
    part = dot(w_ref[...], c_ref[0], ((1,), (1,))).astype(BF16)
    for h in range(heads):
        scr[h] = part[h * HD : (h + 1) * HD]
    for k in range(n):
        d = lax.bitwise_xor(jnp.int32(k), me)

        @pl.when(d // heads == g)
        def _():
            outs[k][0] = scr[d % heads]


def load_parts(n, me, pairs):
    for k in range(n):
        d = lax.bitwise_xor(jnp.int32(k), me)
        for part, t_ref, n_ref in pairs(k):
            if t_ref is not None:
                t_ref[d] = part
            if n_ref is not None:
                n_ref[d] = part.T


def score_of(block, first, i, kn, q_t):
    rows = lax.broadcasted_iota(jnp.int32, (block, block), 0)
    cols = lax.broadcasted_iota(jnp.int32, (block, block), 1)
    ahead = rows - cols

    def scores(j, at):
        s = dot(kn[at], q_t)
        allowed = (rows >= first - j * block) & (ahead <= (i - j) * block)
        return jnp.where(allowed, s, NEG)

    return scores


def attend_kernel(n, block, skip, me_ref, pack_ref, low_ref, first_ref, *refs):
    qkv, outs, keep_ref, logsum_ref = refs[:n], refs[n : 2 * n], refs[2 * n], refs[2 * n + 1]
    qt, vt, kn = refs[2 * n + 2 :]
    s_id = pl.program_id(0) + skip
    me = me_ref[0]
    load_parts(
        n,
        me,
        lambda k: (
            (qkv[k][0, 0, 0], qt, None),
            (qkv[k][0, 0, 1], None, kn),
            (qkv[k][0, 0, 2], vt, None),
        ),
    )

    def outer(i, carry):
        scores = score_of(block, first_ref[0, pl.ds(i, 1), :], i, kn, qt[i])
        j0 = low_ref[s_id, i]

        def forward(t, state):
            top, total, acc = state
            j = j0 + 2 * t
            at = jnp.minimum(j + 1, n - 1)
            s0, s1 = scores(j, j), scores(j + 1, at)
            peak = jnp.max(jnp.maximum(s0, s1), axis=0, keepdims=True)
            new_top = jnp.maximum(top, peak)
            p0, p1 = jnp.exp(s0 - new_top), jnp.exp(s1 - new_top)
            fade = jnp.exp(top - new_top)
            total = total * fade + jnp.sum(p0 + p1, axis=0, keepdims=True)
            acc = acc * fade + dot(vt[j], p0.astype(BF16)) + dot(vt[at], p1.astype(BF16))
            return new_top, total, acc

        top, total, acc = lax.fori_loop(
            0,
            (i - j0) // 2 + 1,
            forward,
            (
                jnp.full((1, block), NEG, F32),
                jnp.zeros((1, block), F32),
                jnp.zeros((HD, block), F32),
            ),
        )
        keep_ref[0, i] = (acc / total).astype(BF16)
        logsum_ref[0, pl.ds(i, 1), :] = top + jnp.log(total)
        return carry

    lax.fori_loop(0, n, outer, 0)
    for k in range(n):
        outs[k][0] = keep_ref[0, lax.bitwise_xor(jnp.int32(k), me)]


def attend_back_kernel(n, block, skip, me_ref, pack_ref, low_ref, first_ref, *refs):
    keep_ref, logsum_ref = refs[:2]
    qkv, grads, outs = refs[2 : n + 2], refs[n + 2 : 2 * n + 2], refs[2 * n + 2 : 3 * n + 2]
    qt, kt, gt, qn, kn, vn, gn, dk, dv, res = refs[3 * n + 2 :]
    s_id = pl.program_id(0) + skip
    me = me_ref[0]
    load_parts(
        n,
        me,
        lambda k: (
            (qkv[k][0, 0, 0], qt, qn),
            (qkv[k][0, 0, 1], kt, kn),
            (qkv[k][0, 0, 2], None, vn),
            (grads[k][0, 0], gt, gn),
        ),
    )
    dk[...] = jnp.zeros_like(dk)
    dv[...] = jnp.zeros_like(dv)

    def outer(i, carry):
        q_t, g_t, q_n, g_n = qt[i], gt[i], qn[i], gn[i]
        scores = score_of(block, first_ref[0, pl.ds(i, 1), :], i, kn, q_t)
        j0 = low_ref[s_id, i]
        inner = jnp.sum(keep_ref[0, i].astype(F32) * g_t.astype(F32), axis=0, keepdims=True)
        logsum = logsum_ref[0, pl.ds(i, 1), :]

        def one(j, at):
            p = jnp.exp(scores(j, at) - logsum)
            ds = (p * (dot(vn[at], g_t) - inner)).astype(BF16)
            return ds, dot(ds, q_n), dot(p.astype(BF16), g_n), dot(kt[at], ds)

        def backward(t, dq):
            j = j0 + 2 * t
            at = jnp.minimum(j + 1, n - 1)
            _, dk0, dv0, dq0 = one(j, j)
            _, dk1, dv1, dq1 = one(j + 1, at)
            dk[j] += dk0
            dv[j] += dv0
            dk[at] += dk1
            dv[at] += dv1
            return dq + dq0 + dq1

        dq = lax.fori_loop(0, (i - j0) // 2 + 1, backward, jnp.zeros((HD, block), F32))
        res[i, 0] = (dq * (1.0 / math.sqrt(HD))).astype(BF16)
        return carry

    lax.fori_loop(0, n, outer, 0)
    for i in range(n):
        res[i, 1] = dk[i].T.astype(BF16)
        res[i, 2] = dv[i].T.astype(BF16)
    for k in range(n):
        outs[k][0] = res[lax.bitwise_xor(jnp.int32(k), me)]


def merge_kernel(n, heads, slices, me_ref, *refs):
    recv = refs[:n]
    c_ref, merge_ref, branch_ref, out_branch, out_weight, scr, acc = refs[n:]
    s_id, g = pl.program_id(0), pl.program_id(1)
    groups = pl.num_programs(1)
    me = me_ref[0]
    width = heads * HD

    @pl.when((s_id == 0) & (g == 0))
    def _():
        acc[...] = jnp.zeros_like(acc)

    for k in range(n):
        d = lax.bitwise_xor(jnp.int32(k), me)

        @pl.when(d // heads == g)
        def _():
            scr[d % heads] = recv[k][0, 0, 0]

    attended = scr[...].reshape(width, c_ref.shape[1])
    acc[...] += dot(attended, c_ref[0])
    branch = dot(attended.T, merge_ref[...]) + branch_ref[0].astype(F32)
    cols = branch.shape[1] // slices
    for m in range(slices):
        out_branch[m, 0] = branch[:, m * cols : (m + 1) * cols].astype(BF16)

    @pl.when((s_id == pl.num_programs(0) - 1) & (g == groups - 1))
    def _():
        out_weight[...] = acc[...].astype(BF16)


def close_kernel(n, heads, me_ref, *refs):
    recv = refs[:n]
    normed_ref, w_ref, cos_ref, sin_ref, low_ref, out_low, out_weight, scr, acc = refs[n:]
    s_id, g = pl.program_id(0), pl.program_id(1)
    groups = pl.num_programs(1)
    me = me_ref[0]
    width = heads * HD
    shard = normed_ref.shape[1]

    @pl.when((s_id == 0) & (g == 0))
    def _():
        acc[...] = jnp.zeros_like(acc)

    for k in range(n):
        d = lax.bitwise_xor(jnp.int32(k), me)

        @pl.when(d // heads == g)
        def _():
            for j in range(3):
                scr[j, d % heads] = recv[k][0, 0, j]

    parts = []
    for j in (0, 1):
        part = scr[j].reshape(width, shard).astype(F32)
        parts.append(turn(part, cos_ref[0], -sin_ref[0], heads).astype(BF16))
    parts.append(scr[2].reshape(width, shard))
    grads = jnp.concatenate(parts, axis=0)
    acc[...] += dot(grads, normed_ref[0])
    low = dot(grads.T, w_ref[...]) + low_ref[0].astype(F32)
    out_low[0] = low.astype(BF16)

    @pl.when((s_id == pl.num_programs(0) - 1) & (g == groups - 1))
    def _():
        out_weight[...] = acc[...]


def place_kernel(block, share, shard, slices, chunks, per_piece, pack_ref, *refs):
    pieces, out, buf, sems, out_sems = refs[:-4], refs[-4], refs[-3], refs[-2], refs[-1]
    me = pack_ref[chunks * slices * share // shard]
    loads, stores = [], []
    arrays = max(ref for ref, _ in per_piece) + 1
    for c in range(chunks):
        for k in range(slices):
            ref, where = per_piece[k]
            for t in range(share // block):
                at = len(loads)
                row = (c * slices + lax.bitwise_xor(jnp.int32(k), me)) * share + t * block
                start = pl.multiple_of(lax.rem(row, shard), block)
                loads.append(
                    pltpu.make_async_copy(
                        pieces[c * arrays + ref].at[where, pl.ds(t * block, block)],
                        buf.at[at],
                        sems.at[at],
                    )
                )
                stores.append(
                    pltpu.make_async_copy(
                        buf.at[at],
                        out.at[pack_ref[row // shard], pl.ds(start, block)],
                        out_sems.at[at],
                    )
                )
    for copy in loads:
        copy.start()
    for load, store in zip(loads, stores):
        load.wait()
        store.start()
    for copy in stores:
        copy.wait()


def small_kernel(n, slices, x_ref, out_ref, first, second, sems, sems2):
    rank, column = lax.axis_index("seq"), lax.axis_index("mlp")
    barrier = pltpu.get_barrier_semaphore()
    peers = [{"seq": lax.bitwise_xor(rank, k)} for k in range(1, n)]
    rows = [{"mlp": lax.bitwise_xor(column, k)} for k in range(1, slices)]
    for peer in peers + rows:
        pl.semaphore_signal(barrier, inc=1, device_id=peer, device_id_type=pl.DeviceIdType.MESH)
    pl.semaphore_wait(barrier, len(peers) + len(rows))

    def exchange(source, target, sems, peers):
        copies = [
            pltpu.make_async_remote_copy(
                src_ref=source(k),
                dst_ref=target.at[k],
                send_sem=sems.at[0, k],
                recv_sem=sems.at[1, k],
                device_id=peer,
                device_id_type=pl.DeviceIdType.MESH,
            )
            for k, peer in enumerate(peers)
        ]
        for copy in copies:
            copy.start()
        for copy in copies:
            copy.wait()

    exchange(lambda k: x_ref.at[lax.bitwise_xor(rank, k + 1)], first, sems, peers)
    total = x_ref[rank]
    for k in range(n - 1):
        total = total + first[k]
    second[slices - 1] = total
    second[slices] = total
    exchange(lambda k: second.at[slices], second, sems2, rows)
    parts = [
        second[jnp.where(column == c, slices - 1, lax.bitwise_xor(column, c) - 1)]
        for c in range(slices)
    ]
    out_ref[...] = functools.reduce(jnp.add, parts)


def small_sum(vectors, n, slices):
    count, width = vectors.shape
    x = jnp.transpose(vectors.reshape(count, n, width // n), (1, 0, 2))
    return pl.pallas_call(
        functools.partial(small_kernel, n, slices),
        out_shape=jax.ShapeDtypeStruct((count, width // n), F32),
        in_specs=[pl.BlockSpec(memory_space=pltpu.VMEM)],
        out_specs=pl.BlockSpec(memory_space=pltpu.VMEM),
        scratch_shapes=[
            pltpu.VMEM((n - 1, count, width // n), F32),
            pltpu.VMEM((slices + 1, count, width // n), F32),
            pltpu.SemaphoreType.DMA((2, n - 1)),
            pltpu.SemaphoreType.DMA((2, slices - 1)),
        ],
        compiler_params=pltpu.CompilerParams(collective_id=0, has_side_effects=True),
        cost_estimate=COST,
        name="small_sum",
    )(x)


def params():
    return pltpu.CompilerParams(vmem_limit_bytes=VMEM_LIMIT)


def tie(*values):
    return lax.optimization_barrier(values)


def send_x(parts):
    n = len(parts)
    sent = jnp.stack([parts[k] for k in range(1, n, 2)])
    return lax.ppermute(sent, "seq", [(i, i ^ 1) for i in range(n)])


def send_z(parts, got, steps=None):
    n = len(parts)
    return [
        lax.ppermute(
            jnp.stack([parts[k], got[k // 2]]), "seq", [(i, i ^ k) for i in range(n)]
        )
        for k in (range(2, n, 2) if steps is None else steps)
    ]


def received(parts, got, gots):
    out = [(parts[0][None], 0), (got, 0)]
    for array in gots:
        out += [(array, 0), (array, 1)]
    return out


def span(masks):
    out = [0]
    for m in masks:
        out += [v ^ m for v in out]
    return out


def cube_send(chunks, axis, n, masks):
    kept = span(masks[1:])
    sent = jnp.stack([chunks[k ^ masks[0]] for k in kept])
    return lax.ppermute(sent, axis, [(i, i ^ masks[0]) for i in range(n)])


def cube_add(chunks, got, masks, kind):
    return {
        k: (chunks[k].astype(F32) + got[at].astype(F32)).astype(kind)
        for at, k in enumerate(span(masks[1:]))
    }


def cube_sum(chunks, axis, masks, kind):
    n = len(chunks)
    chunks = {k: v.astype(kind) for k, v in enumerate(chunks)}
    for step in range(len(masks)):
        got = cube_send(chunks, axis, n, masks[step:])
        chunks = cube_add(chunks, got, masks[step:], F32 if step == len(masks) - 1 else kind)
    return chunks[0]


def gather_step(arrays, axis, n, m):
    sent = jnp.concatenate(arrays, axis=0) if len(arrays) > 1 else arrays[0]
    return arrays + [lax.ppermute(sent, axis, [(i, i ^ m) for i in range(n)])]


def masks_of(n):
    return [1 << b for b in range(n.bit_length() - 1)]


def turned(masks, by):
    by = by % len(masks)
    return masks[by:] + masks[:by]


def cut(array, axis, n, me):
    size = array.shape[axis] // n
    return [
        lax.dynamic_slice_in_dim(array, lax.bitwise_xor(jnp.int32(k), me) * size, size, axis)
        for k in range(n)
    ]


def on_device(
    tokens,
    lengths,
    counts,
    norm_gain,
    norm_bias,
    head_weight,
    merge_weight,
    up_weight,
    up_bias,
    down_weight,
    down_bias,
    cotangent,
):
    packs, shard, width = tokens.shape
    n = lax.axis_size("seq")
    slices = lax.axis_size("mlp")
    pack_len = shard * n
    rank = lax.axis_index("seq")
    column = lax.axis_index("mlp")
    heads = merge_weight.shape[0] // HD
    joined = heads * HD
    groups = n // heads
    slots = -(-packs // groups)
    dealt = groups * slots
    spare = 1 if dealt > packs else 0
    rows = dealt * shard
    chunks = 2 if slots % 2 == 0 else 1
    per = slots // chunks
    seq_masks, mlp_masks = masks_of(n), masks_of(slices)

    first, position, cost = layout(lengths, counts, pack_len)
    ids = jnp.arange(packs, dtype=jnp.int32)
    before = (cost[None, :] > cost[:, None]) | (
        (cost[None, :] == cost[:, None]) & (ids[None, :] < ids[:, None])
    )
    order = jnp.sum(before.astype(jnp.int32), axis=1)
    slot_of = order // groups
    group_of = jnp.where(slot_of % 2 == 0, order % groups, groups - 1 - order % groups)
    at = slot_of * groups + group_of
    hit = at[None, :] == jnp.arange(dealt, dtype=jnp.int32)[:, None]
    pack_at = jnp.where(
        jnp.any(hit, axis=-1), jnp.sum(jnp.where(hit, ids, 0), axis=-1), packs
    ).astype(jnp.int32)
    safe = jnp.minimum(pack_at, packs - 1)
    me = rank.astype(jnp.int32).reshape(1)

    own_cot = jnp.take(cotangent, safe, axis=0, mode="clip")
    if spare:
        own_cot = jnp.where((pack_at < packs)[:, None, None], own_cot, 0)
    cot = lax.all_gather(own_cot, "mlp", axis=2, tiled=True)

    half = ROT // 2
    freq = 10000.0 ** (-(2.0 * jnp.arange(half, dtype=F32)) / ROT)
    own_position = jnp.take(
        lax.dynamic_slice_in_dim(position, rank * shard, shard, 1), safe, axis=0, mode="clip"
    )
    angle = own_position.astype(F32)[:, None, :] * jnp.repeat(freq, 2)[None, :, None]
    cosine, sine = jnp.cos(angle), jnp.sin(angle)

    w_t = jnp.transpose(head_weight, (0, 2, 1)).reshape(3 * joined, width)

    def whole2(s, g, *_):
        return (0, 0)

    def rows_at(skip):
        return pl.BlockSpec((1, shard, width), lambda s, g, *_: ((s + skip) * groups + g, 0, 0))

    def table_at(skip):
        return pl.BlockSpec((1, ROT, shard), lambda s, g, *_: ((s + skip) * groups + g, 0, 0))

    parts = [jax.ShapeDtypeStruct((per, 3, HD, shard), BF16)] * n

    def chunk_at(c):
        return pl.BlockSpec(
            (1, 3, HD, shard), lambda s, g, *_: (jnp.clip(s - c * per, 0, per - 1), 0, 0, 0)
        )

    outs = pl.pallas_call(
        functools.partial(head_kernel, n, heads, per),
        grid_spec=pltpu.PrefetchScalarGridSpec(
            num_scalar_prefetch=2,
            grid=(slots, groups),
            in_specs=[
                pl.BlockSpec((1, shard, width), lambda s, g, a, b: (b[s * groups + g], 0, 0)),
                pl.BlockSpec((1, width), whole2),
                pl.BlockSpec((1, width), whole2),
                pl.BlockSpec((3 * joined, width), whole2),
                table_at(0),
                table_at(0),
            ],
            out_specs=[rows_at(0)] * 2 + [chunk_at(c) for c in range(chunks) for _ in range(n)],
            scratch_shapes=[pltpu.VMEM((heads, 3, HD, shard), BF16)],
        ),
        out_shape=[jax.ShapeDtypeStruct((dealt, shard, width), BF16)] * 2 + parts * chunks,
        compiler_params=params(),
        cost_estimate=COST,
        name="heads",
    )(
        me,
        safe,
        tokens,
        norm_gain.reshape(1, width),
        norm_bias.reshape(1, width),
        w_t,
        cosine,
        sine,
    )
    normed_low, tokens_dealt = outs[0], outs[1]
    qkv = [list(outs[2 + c * n : 2 + (c + 1) * n]) for c in range(chunks)]

    def out_grads(cot, merge_weight):
        return pl.pallas_call(
            functools.partial(grad_kernel, n, heads),
            grid_spec=pltpu.PrefetchScalarGridSpec(
                num_scalar_prefetch=1,
                grid=(slots, groups),
                in_specs=[rows_at(0), pl.BlockSpec((joined, width), whole2)],
                out_specs=[pl.BlockSpec((1, HD, shard), lambda s, g, *_: (s, 0, 0))] * n,
                scratch_shapes=[pltpu.VMEM((heads, HD, shard), BF16)],
            ),
            out_shape=[jax.ShapeDtypeStruct((slots, HD, shard), BF16)] * n,
            compiler_params=params(),
            cost_estimate=COST,
            name="out_grads",
        )(me, cot, merge_weight)

    mine = rank // heads + groups * jnp.arange(slots, dtype=jnp.int32)
    my_packs = jnp.take(safe, mine, mode="clip")
    first = first.reshape(packs, n, shard)
    lows = (jnp.take(first[:, :, 0], my_packs, axis=0, mode="clip") // shard).astype(jnp.int32)
    wide = [pltpu.VMEM((n, HD, shard), BF16)]
    tall = [pltpu.VMEM((n, shard, HD), BF16)]

    def first_at(skip):
        return pl.BlockSpec((1, n, shard), lambda s, a, b, c: (b[s + skip], 0, 0))

    def qkv_at(lead):
        return pl.BlockSpec((1, 1, 3, HD, shard), lambda s, *_: (lead, s, 0, 0, 0))

    def grad_at(lead, skip):
        return pl.BlockSpec((1, 1, HD, shard), lambda s, *_: (lead, s + skip, 0, 0))

    def attend(c, sources):
        return pl.pallas_call(
            functools.partial(attend_kernel, n, shard, c * per),
            grid_spec=pltpu.PrefetchScalarGridSpec(
                num_scalar_prefetch=3,
                grid=(per,),
                in_specs=[first_at(c * per)] + [qkv_at(lead) for _, lead in sources],
                out_specs=[pl.BlockSpec((1, HD, shard), lambda s, *_: (s, 0, 0))] * n
                + [
                    pl.BlockSpec((1, n, HD, shard), lambda s, *_: (s, 0, 0, 0)),
                    pl.BlockSpec((1, n, shard), lambda s, *_: (s, 0, 0)),
                ],
                scratch_shapes=wide * 2 + tall,
            ),
            out_shape=[jax.ShapeDtypeStruct((per, HD, shard), BF16)] * n
            + [
                jax.ShapeDtypeStruct((per, n, HD, shard), BF16),
                jax.ShapeDtypeStruct((per, n, shard), F32),
            ],
            compiler_params=params(),
            cost_estimate=COST,
            name="attend",
        )(me, my_packs, lows, first, *[array for array, _ in sources])

    def attend_back(c, kept, logsum, sources, grads):
        return pl.pallas_call(
            functools.partial(attend_back_kernel, n, shard, c * per),
            grid_spec=pltpu.PrefetchScalarGridSpec(
                num_scalar_prefetch=3,
                grid=(per,),
                in_specs=[
                    first_at(c * per),
                    pl.BlockSpec((1, n, HD, shard), lambda s, *_: (s, 0, 0, 0)),
                    pl.BlockSpec((1, n, shard), lambda s, *_: (s, 0, 0)),
                ]
                + [qkv_at(lead) for _, lead in sources]
                + [grad_at(lead, c * per) for _, lead in grads],
                out_specs=[pl.BlockSpec((1, 3, HD, shard), lambda s, *_: (s, 0, 0, 0))] * n,
                scratch_shapes=wide * 3
                + tall * 4
                + [pltpu.VMEM((n, shard, HD), F32)] * 2
                + [pltpu.VMEM((n, 3, HD, shard), BF16)],
            ),
            out_shape=parts,
            compiler_params=params(),
            cost_estimate=COST,
            name="attend_back",
        )(
            me,
            my_packs,
            lows,
            first,
            kept,
            logsum,
            *[array for array, _ in sources],
            *[array for array, _ in grads],
        )

    def merge(sources, branch_ff):
        return pl.pallas_call(
            functools.partial(merge_kernel, n, heads, slices),
            grid_spec=pltpu.PrefetchScalarGridSpec(
                num_scalar_prefetch=1,
                grid=(slots, groups),
                in_specs=[
                    pl.BlockSpec(
                        (1, 1, 1, HD, shard),
                        lambda s, g, *_, lead=lead: (lead, s // per, s % per, 0, 0),
                    )
                    for _, lead in sources
                ]
                + [rows_at(0), pl.BlockSpec((joined, width), whole2), rows_at(0)],
                out_specs=[
                    pl.BlockSpec(
                        (slices, 1, shard, width // slices),
                        lambda s, g, *_: (0, s * groups + g, 0, 0),
                    ),
                    pl.BlockSpec((joined, width), whole2),
                ],
                scratch_shapes=[
                    pltpu.VMEM((heads, HD, shard), BF16),
                    pltpu.VMEM((joined, width), F32),
                ],
            ),
            out_shape=[
                jax.ShapeDtypeStruct((slices, dealt, shard, width // slices), BF16),
                jax.ShapeDtypeStruct((joined, width), BF16),
            ],
            compiler_params=params(),
            cost_estimate=COST,
            name="merge",
        )(me, *[array for array, _ in sources], cot, merge_weight, branch_ff)

    def close(c, sources):
        skip = c * per
        return pl.pallas_call(
            functools.partial(close_kernel, n, heads),
            grid_spec=pltpu.PrefetchScalarGridSpec(
                num_scalar_prefetch=1,
                grid=(per, groups),
                in_specs=[
                    pl.BlockSpec(
                        (1, 1, 3, HD, shard), lambda s, g, *_, lead=lead: (lead, s, 0, 0, 0)
                    )
                    for _, lead in sources
                ]
                + [
                    rows_at(skip),
                    pl.BlockSpec((3 * joined, width), whole2),
                    table_at(skip),
                    table_at(skip),
                    rows_at(skip),
                ],
                out_specs=[rows_at(0), pl.BlockSpec((3 * joined, width), whole2)],
                scratch_shapes=[
                    pltpu.VMEM((3, heads, HD, shard), BF16),
                    pltpu.VMEM((3 * joined, width), F32),
                ],
            ),
            out_shape=[
                jax.ShapeDtypeStruct((per * groups, shard, width), BF16),
                jax.ShapeDtypeStruct((3 * joined, width), F32),
            ],
            compiler_params=params(),
            cost_estimate=COST,
            name="close",
        )(me, *[array for array, _ in sources], normed_low, w_t, cosine, sine, low_ff)

    got_x = [None] * chunks
    got_z = [None] * chunks
    got_x[0] = send_x(qkv[0])
    hidden = (
        jnp.einsum("psd,df->psf", normed_low, up_weight, preferred_element_type=F32) + up_bias
    )
    active_low = jax.nn.gelu(hidden, approximate=True).astype(BF16)
    branch_ff = jnp.einsum(
        "psf,fd->psd", active_low, down_weight, preferred_element_type=F32
    ).astype(BF16)
    got_x[0], branch_ff, qkv, out_weight, back_weight = tie(
        got_x[0], branch_ff, qkv, merge_weight, down_weight
    )

    got_z[0] = send_z(qkv[0], got_x[0])
    if chunks > 1:
        got_x[1] = send_x(qkv[1])
    sends = out_grads(cot, out_weight)
    active_grad = jnp.einsum("psd,fd->psf", cot, back_weight, preferred_element_type=F32)
    _, gelu_back = jax.vjp(lambda values: jax.nn.gelu(values, approximate=True), hidden)
    hidden_grad = gelu_back(active_grad)[0].astype(BF16)
    got_x, got_z, qkv, sends, hidden_grad = tie(got_x, got_z, qkv, sends, hidden_grad)

    got_dx = send_x(sends)
    sources = [received(qkv[0], got_x[0], got_z[0])]
    if chunks > 1:
        got_z[1] = send_z(qkv[1], got_x[1])
        sources.append(received(qkv[1], got_x[1], got_z[1]))
    ahead = [attend(0, sources[0])]
    up_grad = jnp.einsum(
        "psd,psf->df", normed_low, hidden_grad, preferred_element_type=F32
    ).astype(BF16)
    down_grad = jnp.einsum("psd,psf->df", cot, active_low, preferred_element_type=F32).astype(BF16)
    biases = jnp.sum(hidden_grad.astype(F32), axis=(0, 1)), jnp.sum(cot.astype(F32), axis=(0, 1))
    got_dx, sources_arrays, ahead, sends, hidden_grad, up_grad, down_grad, biases = tie(
        got_dx,
        [[a for a, _ in v] for v in sources],
        ahead,
        sends,
        hidden_grad,
        up_grad,
        down_grad,
        biases,
    )
    def with_row(*parts):
        weight = jnp.concatenate(parts[:2], axis=1)
        row = jnp.concatenate(parts[2:])
        row = jnp.pad(row, (0, weight.shape[1] - row.shape[0])).reshape(1, -1)
        row = jnp.broadcast_to(row, (16, weight.shape[1])).astype(BF16)
        return jnp.concatenate([weight, row], axis=0)

    terms = dict(
        enumerate(
            with_row(*parts)
            for parts in zip(*[cut(v, 0, n, rank) for v in (up_grad, down_grad, *biases)])
        )
    )
    terms_got = cube_send(terms, "seq", n, seq_masks)
    sources = [
        [(a, lead) for a, (_, lead) in zip(arrays, v)] for arrays, v in zip(sources_arrays, sources)
    ]

    got_dz = send_z(sends, got_dx)
    if chunks > 1:
        ahead.append(attend(1, sources[1]))
    low_ff = jnp.einsum(
        "psf,df->psd", hidden_grad, up_weight, preferred_element_type=F32
    ).astype(BF16)
    got_dz, ahead, low_ff = tie(got_dz, ahead, low_ff)
    grads = received(sends, got_dx, got_dz)

    attended = [jnp.stack([outs[k] for outs in ahead]) for k in range(n)]
    got_ax = send_x(attended)
    backs = [attend_back(0, ahead[0][n], ahead[0][n + 1], sources[0], grads)]
    got_ax, terms_got, backs, attended, ahead = tie(got_ax, terms_got, backs, attended, ahead)

    terms = cube_add(terms, terms_got, seq_masks, BF16)
    terms_got = cube_send(terms, "seq", n, seq_masks[1:])
    got_az = send_z(attended, got_ax)
    back_x = [send_x(backs[0])]
    if chunks > 1:
        backs.append(attend_back(1, ahead[1][n], ahead[1][n + 1], sources[1], grads))
    got_az, terms_got, back_x, backs = tie(got_az, terms_got, back_x, backs)

    back_z = [send_z(backs[0], back_x[0])]
    if chunks > 1:
        back_x.append(send_x(backs[1]))
    for step in range(1, len(seq_masks)):
        last_step = step == len(seq_masks) - 1
        terms = cube_add(terms, terms_got, seq_masks[step:], F32 if last_step else BF16)
        if not last_step:
            terms_got = cube_send(terms, "seq", n, seq_masks[step + 1 :])
    terms = terms[0]
    branch, merge_part = merge(received(attended, got_ax, got_az), branch_ff)
    summed = lax.psum_scatter(branch, "mlp", scatter_dimension=0, tiled=False)
    back_x, back_z, backs, merge_part, terms = tie(back_x, back_z, backs, merge_part, terms)

    share = per * groups * shard // slices

    def share_sum(low):
        return cube_sum(
            cut(low.reshape(share * slices, width), 0, slices, column), "mlp", mlp_masks, BF16
        )

    def finish(c, low_sum):
        start = (c * slices + column) * share
        row_in = lax.dynamic_slice_in_dim(
            tokens_dealt.reshape(rows, width), start, share, 0
        ).astype(F32)
        row_cot = lax.dynamic_slice_in_dim(cot.reshape(rows, width), start, share, 0).astype(F32)
        cent = row_in - jnp.mean(row_in, axis=-1, keepdims=True)
        inverse = lax.rsqrt(jnp.mean(cent * cent, axis=-1, keepdims=True) + EPS)
        xhat = cent * inverse
        g = low_sum * norm_gain
        row_grad = (
            row_cot
            + (
                g
                - jnp.mean(g, axis=-1, keepdims=True)
                - xhat * jnp.mean(g * xhat, axis=-1, keepdims=True)
            )
            * inverse
        ).astype(BF16)
        return row_grad, jnp.stack([jnp.sum(low_sum * xhat, axis=0), jnp.sum(low_sum, axis=0)])

    low, head_part = close(0, received(backs[0], back_x[0], back_z[0]))
    head_parts = [head_part]
    if chunks > 1:
        second = send_z(backs[1], back_x[1], [n // 2])
        second, low, head_parts, backs, back_x = tie(second, low, head_parts, backs, back_x)
        others = send_z(backs[1], back_x[1], [k for k in range(2, n, 2) if k != n // 2])
        others.insert(n // 4 - 1, second[0])
        back_z.append(others)
    row_grad, vectors = finish(0, share_sum(low))
    back_z, row_grad, vectors = tie(back_z, row_grad, vectors)

    cols = width // slices
    pieces = gather_step([row_grad[None]], "mlp", slices, mlp_masks[-1])
    result = (
        lax.dynamic_slice_in_dim(tokens, column * cols, cols, 2).astype(F32)
        + jnp.take(summed, at, axis=0, mode="clip").astype(F32)
        + lax.dynamic_slice_in_dim(down_bias, column * cols, cols, 0)
    ).astype(BF16)
    if chunks > 1:
        low, head_part = close(1, received(backs[1], back_x[1], back_z[1]))
        head_parts.append(head_part)
        pieces, low, head_parts, result = tie(pieces, low, head_parts, result)
    weights = functools.reduce(jnp.add, head_parts)
    weights = jnp.concatenate([weights.astype(BF16), merge_part], axis=0)
    weights = dict(enumerate(cut(weights, 1, n, rank)))
    weights_got = cube_send(weights, "seq", n, seq_masks)
    if chunks > 1:
        low_sum = share_sum(low)
        for m in reversed(mlp_masks[:-1]):
            pieces = gather_step(pieces, "mlp", slices, m)
        row_grad, more = finish(1, low_sum)
        vectors = vectors + more
        row_grad, pieces, weights_got, vectors = tie(row_grad, pieces, weights_got, vectors)
        last = gather_step([row_grad[None]], "mlp", slices, mlp_masks[-1])
    else:
        last, pieces = pieces, []
    vectors = small_sum(vectors, n, slices)
    weights = cube_add(weights, weights_got, seq_masks, BF16)
    weights_got = cube_send(weights, "seq", n, seq_masks[1:])
    last, vectors, weights_got = tie(last, vectors, weights_got)
    for m in reversed(mlp_masks[:-1]):
        last = gather_step(last, "mlp", slices, m)
    pieces += last
    where = [(0, 0)]
    lookup = [0]
    for i, m in enumerate(reversed(mlp_masks)):
        where += [(i + 1, j) for j in range(len(lookup))]
        lookup += [k ^ m for k in lookup]
    per_piece = [where[lookup.index(k)] for k in range(slices)]
    block = math.gcd(share, shard)
    tokens_grad = pl.pallas_call(
        functools.partial(
            place_kernel, block, share, shard, slices, chunks, per_piece
        ),
        grid_spec=pltpu.PrefetchScalarGridSpec(
            num_scalar_prefetch=1,
            grid=(1,),
            in_specs=[pl.BlockSpec(memory_space=pl.ANY)] * len(pieces),
            out_specs=pl.BlockSpec(memory_space=pl.ANY),
            scratch_shapes=[
                pltpu.VMEM((rows // block, block, width), BF16),
                pltpu.SemaphoreType.DMA((rows // block,)),
                pltpu.SemaphoreType.DMA((rows // block,)),
            ],
        ),
        out_shape=jax.ShapeDtypeStruct((packs + spare, shard, width), BF16),
        compiler_params=params(),
        name="place",
    )(jnp.concatenate([pack_at, column.astype(jnp.int32).reshape(1)]), *pieces)[:packs]

    for step in range(1, len(seq_masks)):
        weights = cube_add(
            weights, weights_got, seq_masks[step:], F32 if step == len(seq_masks) - 1 else BF16
        )
        if step < len(seq_masks) - 1:
            weights_got = cube_send(weights, "seq", n, seq_masks[step + 1 :])
    weights = weights[0]
    head_grad = jnp.transpose(
        weights[: 3 * joined].reshape(3, joined, width // n), (0, 2, 1)
    )
    merge_grad = weights[3 * joined :]
    part, hidden_here = width // n, up_weight.shape[1]
    up_grad, down_grad = terms[:part, :hidden_here], terms[:part, hidden_here:].T
    up_bias_grad = terms[part, : hidden_here // n]
    down_bias_grad = terms[part, hidden_here // n : hidden_here // n + part]
    return (
        result,
        tokens_grad,
        vectors[0],
        vectors[1],
        head_grad,
        merge_grad,
        up_grad,
        up_bias_grad,
        down_grad,
        down_bias_grad,
    )


def qkv_kernel(heads, me_ref, x_ref, w_ref, cos_ref, sin_ref, normed_ref, out_ref):
    width = heads * HD
    normed = x_ref[0]
    normed_ref[...] = normed
    for j in range(3):
        part = dot(w_ref[j].reshape(width, w_ref.shape[3]), normed, ((1,), (1,)))
        if j < 2:
            part = turn(part, cos_ref[...], sin_ref[...], heads)
        if j == 0:
            part = part * (1.0 / math.sqrt(HD))
        part = part.astype(BF16)
        for h in range(heads):
            out_ref[h, j] = part[h * HD : (h + 1) * HD]


def allowed_of(block, first, i):
    rows = lax.broadcasted_iota(jnp.int32, (block, block), 0)
    cols = lax.broadcasted_iota(jnp.int32, (block, block), 1)
    ahead = rows - cols
    return lambda j: (rows >= first - j * block) & (ahead <= (i - j) * block)


def unit_kernel(n, block, me_ref, low_ref, first_ref, qkv_ref, out_ref, keep_ref, logsum_ref, qt, vt, kn):
    me = me_ref[0]
    pair = range(qkv_ref.shape[0])
    for u in pair:
        for i in range(n):
            at = slice(i * block, (i + 1) * block)
            qt[u, i] = qkv_ref[u, 0, :, at]
            kn[u, i] = qkv_ref[u, 1, :, at].T
            vt[u, i] = qkv_ref[u, 2, :, at]

    def outer(i, carry):
        allowed = allowed_of(block, first_ref[pl.ds(i, 1), :], i)
        j0 = low_ref[i]

        def forward(t, states):
            j = j0 + 2 * t
            at = jnp.minimum(j + 1, n - 1)
            mask0, mask1 = allowed(j), allowed(j + 1)
            out = []
            for u, (top, total, acc) in zip(pair, states):
                q_t = qt[u, i]
                s0 = jnp.where(mask0, dot(kn[u, j], q_t), NEG)
                s1 = jnp.where(mask1, dot(kn[u, at], q_t), NEG)
                peak = jnp.max(jnp.maximum(s0, s1), axis=0, keepdims=True)
                new_top = jnp.maximum(top, peak)
                p0, p1 = jnp.exp(s0 - new_top), jnp.exp(s1 - new_top)
                fade = jnp.exp(top - new_top)
                total = total * fade + jnp.sum(p0 + p1, axis=0, keepdims=True)
                acc = acc * fade + dot(vt[u, j], p0.astype(BF16)) + dot(vt[u, at], p1.astype(BF16))
                out.append((new_top, total, acc))
            return tuple(out)

        states = lax.fori_loop(
            0,
            (i - j0) // 2 + 1,
            forward,
            tuple(
                (
                    jnp.full((1, block), NEG, F32),
                    jnp.zeros((1, block), F32),
                    jnp.zeros((HD, block), F32),
                )
                for _ in pair
            ),
        )
        for u, (top, total, acc) in zip(pair, states):
            keep_ref[u, i] = (acc / total).astype(BF16)
            logsum_ref[u, pl.ds(i, 1), :] = top + jnp.log(total)
        return carry

    lax.fori_loop(0, n, outer, 0)
    for k in range(n):
        for u in pair:
            out_ref[k, u] = keep_ref[u, lax.bitwise_xor(jnp.int32(k), me)]


def unit_back_kernel(
    n, block, by, me_ref, low_ref, first_ref, keep_ref, logsum_ref, qkv_ref, grad_ref, out_ref,
    qt, kt, gt, qn, kn, vn, gn, dk, dv, dqs
):
    me = me_ref[0]
    pair = range(qkv_ref.shape[0])
    for u in pair:
        for i in range(n):
            at = slice(i * block, (i + 1) * block)
            for j, (t_ref, n_ref) in enumerate(((qt, qn), (kt, kn), (None, vn))):
                part = qkv_ref[u, j, :, at]
                if t_ref is not None:
                    t_ref[u, i] = part
                n_ref[u, i] = part.T
        for k in range(n):
            d = lax.bitwise_xor(jnp.int32(k), me)
            part = grad_ref[k, u]
            gt[u, d] = part
            gn[u, d] = part.T
    dk[...] = jnp.zeros_like(dk)
    dv[...] = jnp.zeros_like(dv)

    def outer(i, carry):
        allowed = allowed_of(block, first_ref[pl.ds(i, 1), :], i)
        j0 = low_ref[i]
        inner = [
            jnp.sum(keep_ref[u, i].astype(F32) * gt[u, i].astype(F32), axis=0, keepdims=True)
            for u in pair
        ]
        logsum = [logsum_ref[u, pl.ds(i, 1), :] for u in pair]

        def one(u, mask, at):
            s = jnp.where(mask, dot(kn[u, at], qt[u, i]), NEG)
            p = jnp.exp(s - logsum[u])
            ds = (p * (dot(vn[u, at], gt[u, i]) - inner[u])).astype(BF16)
            return dot(ds, qn[u, i]), dot(p.astype(BF16), gn[u, i]), dot(kt[u, at], ds)

        def backward(t, dqs):
            j = j0 + by * t
            spots = [jnp.minimum(j + b, n - 1) if b else j for b in range(by)]
            masks = [allowed(j + b) for b in range(by)]
            out = []
            for u, dq in zip(pair, dqs):
                terms = [one(u, mask, at) for mask, at in zip(masks, spots)]
                for (dk0, dv0, dq0), at in zip(terms, spots):
                    dk[u, at] += dk0
                    dv[u, at] += dv0
                    dq = dq + dq0
                out.append(dq)
            return tuple(out)

        dq = lax.fori_loop(
            0, (i - j0) // by + 1, backward, tuple(jnp.zeros((HD, block), F32) for _ in pair)
        )
        for u in pair:
            dqs[u, i] = (dq[u] * (1.0 / math.sqrt(HD))).astype(BF16)
        return carry

    lax.fori_loop(0, n, outer, 0)
    for u in pair:
        for i in range(n):
            at = slice(i * block, (i + 1) * block)
            out_ref[u, 0, :, at] = dqs[u, i]
            out_ref[u, 1, :, at] = dk[u, i].T.astype(BF16)
            out_ref[u, 2, :, at] = dv[u, i].T.astype(BF16)


def rows_kernel(heads, slices, me_ref, grad_ref, normed_ref, w_ref, cos_ref, sin_ref, *refs):
    kept_ref, sent_ref, weight_ref = refs[-3:]
    width = heads * HD
    column = me_ref[1]

    @pl.when(pl.program_id(0) == 0)
    def _():
        if len(refs) > 3:
            weight_ref[...] = refs[0][...]
        else:
            weight_ref[...] = jnp.zeros_like(weight_ref)

    parts = []
    for j in range(3):
        part = jnp.concatenate([grad_ref[h, j] for h in range(heads)], axis=0)
        if j < 2:
            part = turn(part.astype(F32), cos_ref[...], -sin_ref[...], heads).astype(BF16)
        parts.append(part)
    grads = jnp.concatenate(parts, axis=0)
    if len(refs) > 3:
        whole = weight_ref.shape[0] // 3
        start = lax.rem(me_ref[0], 2) * width
        for j in range(3):
            rows = pl.ds(pl.multiple_of(j * whole + start, width), width)
            weight_ref[rows, :] += dot(parts[j], normed_ref[...])
    else:
        weight_ref[...] += dot(grads, normed_ref[...])
    low = dot(grads.T, w_ref[...].reshape(3 * width, w_ref.shape[3])).astype(BF16)
    part = low.shape[0] // slices
    for m in range(slices):
        at = lax.bitwise_xor(jnp.int32(m), column)
        for bit, ref in enumerate((kept_ref, sent_ref)):

            @pl.when(at % 2 == bit)
            def _():
                ref[at // 2, 0] = low[m * part : (m + 1) * part]


def norm_kernel(me_ref, x_ref, gain_ref, bias_ref, normed_ref, cols_ref):
    cols = cols_ref.shape[2]
    start = pl.multiple_of(me_ref[1] * cols, cols)
    step = math.gcd(x_ref.shape[1], 32)
    for r in range(0, x_ref.shape[1], step):
        x = x_ref[0, r : r + step].astype(F32)
        cent = x - jnp.mean(x, axis=-1, keepdims=True)
        var = jnp.mean(cent * cent, axis=-1, keepdims=True)
        normed = cent * lax.rsqrt(var + EPS) * gain_ref[...] + bias_ref[...]
        normed_ref[0, r : r + step] = normed.astype(BF16)
    cols_ref[0] = normed_ref[0, :, pl.ds(start, cols)]


def finish_kernel(terms, which_ref, *refs):
    lows = refs[:terms]
    low_ref, x_ref, c_ref, gain_ref, out_ref, sums_ref = refs[terms:]

    @pl.when(pl.program_id(0) == 0)
    def _():
        sums_ref[...] = jnp.zeros_like(sums_ref)

    low = low_ref[0].astype(F32)
    for ref in lows:
        low = low + ref[0].astype(F32)
    x = x_ref[0].astype(F32)
    cent = x - jnp.mean(x, axis=-1, keepdims=True)
    inverse = lax.rsqrt(jnp.mean(cent * cent, axis=-1, keepdims=True) + EPS)
    xhat = cent * inverse
    g = low * gain_ref[...]
    inner = jnp.mean(g * xhat, axis=-1, keepdims=True)
    back = (g - jnp.mean(g, axis=-1, keepdims=True) - xhat * inner) * inverse
    out_ref[0] = (c_ref[0].astype(F32) + back).astype(BF16)
    sums_ref[0:1] += jnp.sum(low * xhat, axis=0, keepdims=True)
    sums_ref[1:2] += jnp.sum(low, axis=0, keepdims=True)


def join_kernel(slices, attended_ref, c_ref, merge_ref, branch_ref, out_branch, out_weight):
    @pl.when(pl.program_id(0) == 0)
    def _():
        out_weight[...] = jnp.zeros_like(out_weight)

    attended = attended_ref[0]
    out_weight[...] += dot(attended, c_ref[0])
    branch = dot(attended.T, merge_ref[...]) + branch_ref[0].astype(F32)
    cols = branch.shape[1] // slices
    for m in range(slices):
        out_branch[m, 0] = branch[:, m * cols : (m + 1) * cols].astype(BF16)


def settle_kernel(counts, slices, sub, per_piece, table_ref, *refs):
    pieces, out, buf, sems, out_sems = refs[:-4], refs[-4], refs[-3], refs[-2], refs[-1]
    column = table_ref[sum(counts)]
    loads, stores = [], []
    arrays = max(ref for ref, _ in per_piece) + 1
    first = 0
    for c, count in enumerate(counts):
        for k in range(slices):
            ref, where = per_piece[k]
            start = pl.multiple_of(lax.bitwise_xor(jnp.int32(k), column) * sub, sub)
            for t in range(count):
                at = len(loads)
                loads.append(
                    pltpu.make_async_copy(
                        pieces[c * arrays + ref].at[where, t], buf.at[at], sems.at[at]
                    )
                )
                stores.append(
                    pltpu.make_async_copy(
                        buf.at[at],
                        out.at[table_ref[first + t], pl.ds(start, sub)],
                        out_sems.at[at],
                    )
                )
        first += count
    for copy in loads:
        copy.start()
    for load, store in zip(loads, stores):
        load.wait()
        store.start()
    for copy in stores:
        copy.wait()


def exchange_x(array):
    n = array.shape[0]
    return lax.ppermute(array[1::2], "seq", [(i, i ^ 1) for i in range(n)])


def exchange_z(array, got, steps=None):
    n = array.shape[0]
    return [
        lax.ppermute(jnp.stack([array[k], got[k // 2]]), "seq", [(i, i ^ k) for i in range(n)])
        for k in (range(2, n, 2) if steps is None else steps)
    ]


def exchanged(array, got, gots):
    return jnp.concatenate([array[:1], got[:1], *gots], axis=0)


def sum_on(terms, axis, n, masks):
    for step in range(len(masks)):
        terms = {k: v.astype(BF16) for k, v in terms.items()}
        got = cube_send(terms, axis, n, masks[step:])
        terms = cube_add(terms, got, masks[step:], F32)
    return terms[0].astype(BF16)


def take(array, index):
    return jnp.take(array, index, axis=0, mode="clip")


def on_device_pairs(
    tokens,
    lengths,
    counts,
    norm_gain,
    norm_bias,
    head_weight,
    merge_weight,
    up_weight,
    up_bias,
    down_weight,
    down_bias,
    cotangent,
):
    packs, shard, width = tokens.shape
    n = lax.axis_size("seq")
    slices = lax.axis_size("mlp")
    pack_len = shard * n
    rank = lax.axis_index("seq").astype(jnp.int32)
    column = lax.axis_index("mlp").astype(jnp.int32)
    heads = merge_weight.shape[0] // HD
    joined = heads * HD
    half = heads // 2
    cols = width // slices
    sub = shard // slices
    seq_masks, mlp_masks = masks_of(n), masks_of(slices)
    pairs = n // 2

    cot = lax.all_gather(cotangent, "mlp", axis=2, tiled=True)

    first, position, cost = layout(lengths, counts, pack_len)
    ids = jnp.arange(packs, dtype=jnp.int32)
    before = (cost[None, :] > cost[:, None]) | (
        (cost[None, :] == cost[:, None]) & (ids[None, :] < ids[:, None])
    )
    order = jnp.sum(before.astype(jnp.int32), axis=1)
    by_order = jnp.sum(
        jnp.where(order[None, :] == ids[:, None], ids[None, :], 0), axis=-1
    ).astype(jnp.int32)
    devices = jnp.arange(n, dtype=jnp.int32)
    shared_of = by_order[:pairs]
    own_of = by_order[pairs + 2 * (pairs - 1 - devices // 2) + devices % 2]
    late = order - pairs
    pair_of = jnp.where(late < 0, order, pairs - 1 - late // 2)
    device_of = 2 * pair_of + jnp.where(late < 0, 0, late % 2)
    dest = jnp.bitwise_xor(rank, devices)
    own_dest, shared_dest = own_of[dest], shared_of[dest // 2]
    me = jnp.stack([rank, column])

    head_ids = jnp.arange(heads, dtype=jnp.int32)
    half_ids = jnp.arange(half, dtype=jnp.int32)
    units_out = jnp.concatenate(
        [
            own_dest[:, None] * heads + head_ids[None, :],
            shared_dest[:, None] * heads + (dest % 2)[:, None] * half + half_ids[None, :],
        ],
        axis=1,
    ).reshape(-1)
    is_shared = (order < pairs)[:, None]
    holder = device_of[:, None] + jnp.where(is_shared, head_ids[None, :] // half, 0)
    units_in = (
        jnp.bitwise_xor(holder, rank) * (heads + half)
        + jnp.where(is_shared, heads + head_ids[None, :] % half, head_ids[None, :])
    ).reshape(-1)

    def tables(pack):
        freq = 10000.0 ** (-(2.0 * jnp.arange(ROT // 2, dtype=F32)) / ROT)
        angle = take(position, pack).astype(F32)[None, :] * jnp.repeat(freq, 2)[:, None]
        return jnp.cos(angle), jnp.sin(angle)

    w_heads = jnp.transpose(head_weight, (0, 2, 1)).reshape(3, heads, HD, width)
    packs_here = (own_of[rank], shared_of[rank // 2])
    turns = [tables(p) for p in packs_here]
    firsts = [take(first, p).reshape(n, shard) for p in packs_here]
    lows = [(f[:, 0] // shard).astype(jnp.int32) for f in firsts]
    gain, bias = norm_gain.reshape(1, width), norm_bias.reshape(1, width)

    def whole2(s, *_):
        return (0, 0)

    def lane_at(s, *_):
        return (0, s)

    def heads_at(h):
        pieces = heads // h
        return pl.BlockSpec(
            (3, h, HD, width), lambda s, me: (0, lax.rem(me[0], jnp.int32(pieces)), 0, 0)
        )

    def project(rows, h, cosine, sine):
        return pl.pallas_call(
            functools.partial(qkv_kernel, h),
            grid_spec=pltpu.PrefetchScalarGridSpec(
                num_scalar_prefetch=1,
                grid=(n,),
                in_specs=[
                    pl.BlockSpec(
                        (1, shard, width), lambda s, me: (lax.bitwise_xor(s, me[0]), 0, 0)
                    ),
                    heads_at(h),
                    pl.BlockSpec((ROT, shard), lane_at),
                    pl.BlockSpec((ROT, shard), lane_at),
                ],
                out_specs=[
                    pl.BlockSpec((shard, width), lambda s, *_: (s, 0)),
                    pl.BlockSpec((h, 3, HD, shard), lambda s, *_: (0, 0, 0, s)),
                ],
            ),
            out_shape=[
                jax.ShapeDtypeStruct((pack_len, width), BF16),
                jax.ShapeDtypeStruct((h, 3, HD, pack_len), BF16),
            ],
            compiler_params=params(),
            cost_estimate=COST,
            name="project",
        )(me, rows, w_heads, cosine, sine)

    def wide(h):
        return [pltpu.VMEM((h, n, HD, shard), BF16)]

    def tall(h, kind=BF16):
        return [pltpu.VMEM((h, n, shard, HD), kind)]

    def keep_spec(h):
        return pl.BlockSpec((h, n, HD, shard), lambda u, *_: (u, 0, 0, 0))

    def log_spec(h):
        return pl.BlockSpec((h, n, shard), lambda u, *_: (u, 0, 0))

    def unit_spec(h):
        return pl.BlockSpec((h, 3, HD, pack_len), lambda u, *_: (u, 0, 0, 0))

    def attend(c, qkv):
        h = qkv.shape[0]
        return pl.pallas_call(
            functools.partial(unit_kernel, n, shard),
            grid_spec=pltpu.PrefetchScalarGridSpec(
                num_scalar_prefetch=2,
                grid=(1,),
                in_specs=[pl.BlockSpec((n, shard), whole2), unit_spec(h)],
                out_specs=[
                    pl.BlockSpec((n, h, HD, shard), lambda u, *_: (0, u, 0, 0)),
                    keep_spec(h),
                    log_spec(h),
                ],
                scratch_shapes=wide(h) * 2 + tall(h),
            ),
            out_shape=[
                jax.ShapeDtypeStruct((n, h, HD, shard), BF16),
                jax.ShapeDtypeStruct((h, n, HD, shard), BF16),
                jax.ShapeDtypeStruct((h, n, shard), F32),
            ],
            compiler_params=params(),
            cost_estimate=COST,
            name="attend",
        )(me, lows[c], firsts[c], qkv)

    def attend_back(c, kept, logsum, qkv, grads):
        h = qkv.shape[0]
        step = h if c == 0 else 2
        skip = c * heads // step
        return pl.pallas_call(
            functools.partial(unit_back_kernel, n, shard, c + 1),
            grid_spec=pltpu.PrefetchScalarGridSpec(
                num_scalar_prefetch=2,
                grid=(h // step,),
                in_specs=[
                    pl.BlockSpec((n, shard), whole2),
                    keep_spec(step),
                    log_spec(step),
                    unit_spec(step),
                    pl.BlockSpec((n, step, HD, shard), lambda u, *_: (0, u + skip, 0, 0)),
                ],
                out_specs=unit_spec(step),
                scratch_shapes=wide(step) * 3 + tall(step) * 4 + tall(step, F32) * 2 + wide(step),
            ),
            out_shape=jax.ShapeDtypeStruct((h, 3, HD, pack_len), BF16),
            compiler_params=params(),
            cost_estimate=COST,
            name="attend_back",
        )(me, lows[c], firsts[c], kept, logsum, qkv, grads)

    def rows_back(grads, normed, cosine, sine, *base):
        h = grads.shape[0]
        return pl.pallas_call(
            functools.partial(rows_kernel, h, slices),
            grid_spec=pltpu.PrefetchScalarGridSpec(
                num_scalar_prefetch=1,
                grid=(n,),
                in_specs=[
                    pl.BlockSpec((h, 3, HD, shard), lambda s, *_: (0, 0, 0, s)),
                    pl.BlockSpec((shard, width), lambda s, *_: (s, 0)),
                    heads_at(h),
                    pl.BlockSpec((ROT, shard), lane_at),
                    pl.BlockSpec((ROT, shard), lane_at),
                ]
                + [pl.BlockSpec(v.shape, whole2) for v in base],
                out_specs=[
                    pl.BlockSpec(
                        (slices // 2, 1, sub, width),
                        lambda s, me: (0, lax.bitwise_xor(s, me[0]), 0, 0),
                    )
                ]
                * 2
                + [
                    pl.BlockSpec((3 * joined, width), whole2),
                ],
            ),
            out_shape=[
                jax.ShapeDtypeStruct((slices // 2, n, sub, width), BF16),
                jax.ShapeDtypeStruct((slices // 2, n, sub, width), BF16),
                jax.ShapeDtypeStruct((3 * joined, width), F32),
            ],
            compiler_params=params(),
            cost_estimate=COST,
            name="rows_back",
        )(me, grads, normed, w_heads, cosine, sine, *base)

    pack_spec = pl.BlockSpec((1, shard, width), lambda p, *_: (p, 0, 0))
    normed_low, normed_cols = pl.pallas_call(
        norm_kernel,
        grid_spec=pltpu.PrefetchScalarGridSpec(
            num_scalar_prefetch=1,
            grid=(packs,),
            in_specs=[
                pack_spec,
                pl.BlockSpec((1, width), whole2),
                pl.BlockSpec((1, width), whole2),
            ],
            out_specs=[pack_spec, pl.BlockSpec((1, shard, cols), lambda p, *_: (p, 0, 0))],
        ),
        out_shape=[
            jax.ShapeDtypeStruct((packs, shard, width), BF16),
            jax.ShapeDtypeStruct((packs, shard, cols), BF16),
        ],
        compiler_params=params(),
        cost_estimate=COST,
        name="norm",
    )(me, tokens, gain, bias)
    send_own = take(normed_cols, own_dest)
    send_shared = take(normed_cols, shared_dest)
    own_x = exchange_x(send_own)

    hidden = (
        jnp.einsum("psd,df->psf", normed_low, up_weight, preferred_element_type=F32) + up_bias
    )
    own_x, hidden, send_own, send_shared = tie(own_x, hidden, send_own, send_shared)

    own_z = exchange_z(send_own, own_x, [2])
    shared_x = exchange_x(send_shared)
    active_low = jax.nn.gelu(hidden, approximate=True).astype(BF16)
    branch_ff = jnp.einsum(
        "psf,fd->psd", active_low, down_weight, preferred_element_type=F32
    ).astype(BF16)
    own_z, shared_x, branch_ff, send_own, own_x, merge_here, down_here, turns, w_heads = tie(
        own_z,
        shared_x,
        branch_ff,
        send_own,
        own_x,
        merge_weight,
        down_weight,
        turns,
        w_heads,
    )

    own_z += exchange_z(send_own, own_x, range(4, n, 2))
    active_grad = jnp.einsum("psd,fd->psf", cot, down_here, preferred_element_type=F32)
    _, gelu_back = jax.vjp(lambda values: jax.nn.gelu(values, approximate=True), hidden)
    hidden_grad = gelu_back(active_grad)[0].astype(BF16)
    biases = jnp.sum(hidden_grad.astype(F32), axis=(0, 1)), jnp.sum(cot.astype(F32), axis=(0, 1))
    own_z, hidden_grad, send_shared, shared_x, biases = tie(
        own_z, hidden_grad, send_shared, shared_x, biases
    )
    rows_own = lax.all_gather(exchanged(send_own, own_x, own_z), "mlp", axis=2, tiled=True)

    shared_z = exchange_z(send_shared, shared_x)
    out_grad = jnp.einsum("hd,psd->phs", merge_here, cot, preferred_element_type=F32).astype(BF16)
    send_grad = take(out_grad.reshape(packs * heads, HD, shard), units_out).reshape(
        n, heads + half, HD, shard
    )
    up_grad = jnp.einsum(
        "psd,psf->df", normed_low, hidden_grad, preferred_element_type=F32
    ).astype(BF16)
    down_grad = jnp.einsum("psd,psf->df", cot, active_low, preferred_element_type=F32).astype(BF16)
    shared_z, send_grad, up_grad, down_grad, send_shared, shared_x, hidden_grad = tie(
        shared_z, send_grad, up_grad, down_grad, send_shared, shared_x, hidden_grad
    )
    rows_shared = lax.all_gather(
        exchanged(send_shared, shared_x, shared_z), "mlp", axis=2, tiled=True
    )

    grad_x = exchange_x(send_grad)
    low_ff = jnp.einsum(
        "psf,df->psd", hidden_grad, up_weight, preferred_element_type=F32
    ).astype(BF16)
    low_ff = jnp.transpose(low_ff.reshape(packs, slices, sub, width), (1, 0, 2, 3)).reshape(
        slices * packs * sub, width
    )
    grad_x, send_grad, low_ff, rows_own, biases = tie(grad_x, send_grad, low_ff, rows_own, biases)
    low_ff = lax.psum_scatter(low_ff, "mlp", scatter_dimension=0, tiled=True).reshape(
        packs, sub, width
    )

    grad_z = exchange_z(send_grad, grad_x)
    normed_own, qkv_own = project(rows_own, heads, *turns[0])
    out_own, kept_own, log_own = attend(0, qkv_own)
    grad_z, out_own, kept_own, log_own, rows_shared = tie(
        grad_z, out_own, kept_own, log_own, rows_shared
    )
    grads = exchanged(send_grad, grad_x, grad_z)

    def with_row(*parts):
        weight = jnp.concatenate(parts[:2], axis=1)
        row = jnp.concatenate(parts[2:])
        row = jnp.pad(row, (0, weight.shape[1] - row.shape[0])).reshape(1, -1)
        row = jnp.broadcast_to(row, (16, weight.shape[1])).astype(BF16)
        return jnp.concatenate([weight, row], axis=0)

    terms = dict(
        enumerate(
            with_row(*parts)
            for parts in zip(*[cut(v, 0, n, rank) for v in (up_grad, down_grad, *biases)])
        )
    )
    terms_got = cube_send(terms, "seq", n, seq_masks)
    normed_shared, qkv_shared = project(rows_shared, half, *turns[1])
    out_shared, kept_shared, log_shared = attend(1, qkv_shared)
    out_shared, kept_shared, log_shared, grads, terms_got = tie(
        out_shared, kept_shared, log_shared, grads, terms_got
    )
    terms = cube_add(terms, terms_got, seq_masks, BF16)
    terms_got = cube_send(terms, "seq", n, seq_masks[1:])

    send_out = jnp.concatenate([out_own, out_shared], axis=1)
    out_x = exchange_x(send_out)
    back_own = attend_back(0, kept_own, log_own, qkv_own, grads)
    out_x, back_own, terms_got, send_out = tie(out_x, back_own, terms_got, send_out)

    out_z = exchange_z(send_out, out_x)
    low_kept, low_sent, head_own = rows_back(back_own, normed_own, *turns[0])
    back_shared = attend_back(1, kept_shared, log_shared, qkv_shared, grads)
    out_z, low_kept, low_sent, back_shared, send_out, out_x = tie(
        out_z, low_kept, low_sent, back_shared, send_out, out_x
    )

    others = [(i, i ^ 1) for i in range(slices)]
    low_got, back_shared = tie(lax.ppermute(low_sent, "mlp", others), back_shared)
    low_terms = {
        2 * k: low_kept[k].astype(F32) + low_got[k].astype(F32) for k in range(slices // 2)
    }
    low_own = sum_on(low_terms, "mlp", slices, mlp_masks[1:])
    low_kept, low_sent, head_all = rows_back(back_shared, normed_shared, *turns[1], head_own)
    attended = take(
        exchanged(send_out, out_x, out_z).reshape(n * (heads + half), HD, shard), units_in
    ).reshape(packs, joined, shard)
    for step in range(1, len(seq_masks) - 1):
        terms = cube_add(terms, terms_got, seq_masks[step:], BF16)
        terms_got = cube_send(terms, "seq", n, seq_masks[step + 1 :])
    low_own, low_kept, low_sent, attended, terms_got = tie(
        low_own, low_kept, low_sent, attended, terms_got
    )
    terms = cube_add(terms, terms_got, seq_masks[len(seq_masks) - 1 :], F32)[0]

    low_own_x = exchange_x(low_own)
    low_got = lax.ppermute(low_sent, "mlp", others)
    branch, merge_part = pl.pallas_call(
        functools.partial(join_kernel, slices),
        grid=(packs,),
        in_specs=[
            pl.BlockSpec((1, joined, shard), lambda p: (p, 0, 0)),
            pl.BlockSpec((1, shard, width), lambda p: (p, 0, 0)),
            pl.BlockSpec((joined, width), whole2),
            pl.BlockSpec((1, shard, width), lambda p: (p, 0, 0)),
        ],
        out_specs=[
            pl.BlockSpec((slices, 1, shard, cols), lambda p: (0, p, 0, 0)),
            pl.BlockSpec((joined, width), whole2),
        ],
        out_shape=[
            jax.ShapeDtypeStruct((slices, packs, shard, cols), BF16),
            jax.ShapeDtypeStruct((joined, width), F32),
        ],
        compiler_params=params(),
        cost_estimate=COST,
        name="join",
    )(attended, cot, merge_weight, branch_ff)
    low_kept, low_got, low_own, low_own_x, branch, low_ff, head_all = tie(
        low_kept, low_got, low_own, low_own_x, branch, low_ff, head_all
    )
    summed = lax.psum_scatter(branch, "mlp", scatter_dimension=0, tiled=False)

    low_terms = {
        2 * k: low_kept[k].astype(F32) + low_got[k].astype(F32) for k in range(slices // 2)
    }
    low_shared = sum_on(low_terms, "mlp", slices, mlp_masks[1:])
    weights = {
        k: jnp.concatenate(pair, axis=0).astype(BF16)
        for k, pair in enumerate(zip(cut(head_all, 1, n, rank), cut(merge_part, 1, n, rank)))
    }
    low_own_z = exchange_z(low_own, low_own_x)
    weights_got = cube_send(weights, "seq", n, seq_masks)
    low_own_z, low_shared, low_own, low_own_x, weights, weights_got, terms = tie(
        low_own_z, low_shared, low_own, low_own_x, weights, weights_got, terms
    )

    low_shared_x = exchange_x(low_shared)
    weights = cube_add(weights, weights_got, seq_masks, BF16)
    weights_got = cube_send(weights, "seq", n, seq_masks[1:])

    def finish(lows, index, which):
        count = which.shape[0]
        row_spec = pl.BlockSpec((1, sub, width), lambda t, at: (at[count + t], at[0], 0))

        def part(i):
            return pl.BlockSpec(
                (1, sub, width), lambda t, at: (at[(2 + i) * count + t], 0, 0)
            )

        table = [jnp.full((count,), column), which, *index]
        return pl.pallas_call(
            functools.partial(finish_kernel, len(lows)),
            grid_spec=pltpu.PrefetchScalarGridSpec(
                num_scalar_prefetch=1,
                grid=(count,),
                in_specs=[part(i) for i in range(len(lows))]
                + [
                    pl.BlockSpec((1, sub, width), lambda t, at: (at[count + t], 0, 0)),
                    row_spec,
                    row_spec,
                    pl.BlockSpec((1, width), whole2),
                ],
                out_specs=[
                    pl.BlockSpec((1, sub, width), lambda t, *_: (t, 0, 0)),
                    pl.BlockSpec((2, width), whole2),
                ],
            ),
            out_shape=[
                jax.ShapeDtypeStruct((count, sub, width), BF16),
                jax.ShapeDtypeStruct((2, width), F32),
            ],
            compiler_params=params(),
            cost_estimate=COST,
            name="finish",
        )(jnp.concatenate(table), *lows, low_ff, tokens, cot, gain)

    row_own, sums_own = finish(
        [exchanged(low_own, low_own_x, low_own_z)], [devices], own_dest
    )
    low_shared_x, row_own, sums_own, low_shared, weights_got = tie(
        low_shared_x, row_own, sums_own, low_shared, weights_got
    )
    for step in range(1, len(seq_masks)):
        last_step = step == len(seq_masks) - 1
        weights = cube_add(weights, weights_got, seq_masks[step:], F32 if last_step else BF16)
        if not last_step:
            weights_got = cube_send(weights, "seq", n, seq_masks[step + 1 :])
    weights = weights[0]
    low_shared_z = exchange_z(low_shared, low_shared_x)
    pieces = gather_step([row_own[None]], "mlp", slices, mlp_masks[-1])
    result = (
        lax.dynamic_slice_in_dim(tokens, column * cols, cols, 2).astype(F32)
        + summed.astype(F32)
        + lax.dynamic_slice_in_dim(down_bias, column * cols, cols, 0)
    ).astype(BF16)
    low_shared_z, pieces, weights, result = tie(low_shared_z, pieces, weights, result)

    for m in reversed(mlp_masks[:-1]):
        pieces = gather_step(pieces, "mlp", slices, m)
    both = exchanged(low_shared, low_shared_x, low_shared_z)
    even = jnp.bitwise_xor(2 * jnp.arange(pairs, dtype=jnp.int32), rank)
    row_shared, sums = finish([both, both], [even, jnp.bitwise_xor(even, 1)], shared_of)
    last = gather_step([row_shared[None]], "mlp", slices, mlp_masks[-1])
    vectors = small_sum(sums_own + sums, n, slices)
    last, pieces, vectors = tie(last, pieces, vectors)

    for m in reversed(mlp_masks[:-1]):
        last = gather_step(last, "mlp", slices, m)
    pieces += last
    where = [(0, 0)]
    lookup = [0]
    for i, m in enumerate(reversed(mlp_masks)):
        where += [(i + 1, j) for j in range(len(lookup))]
        lookup += [k ^ m for k in lookup]
    per_piece = [where[lookup.index(k)] for k in range(slices)]
    tokens_grad = pl.pallas_call(
        functools.partial(settle_kernel, (n, pairs), slices, sub, per_piece),
        grid_spec=pltpu.PrefetchScalarGridSpec(
            num_scalar_prefetch=1,
            grid=(1,),
            in_specs=[pl.BlockSpec(memory_space=pl.ANY)] * len(pieces),
            out_specs=pl.BlockSpec(memory_space=pl.ANY),
            scratch_shapes=[
                pltpu.VMEM((packs * slices, sub, width), BF16),
                pltpu.SemaphoreType.DMA((packs * slices,)),
                pltpu.SemaphoreType.DMA((packs * slices,)),
            ],
        ),
        out_shape=jax.ShapeDtypeStruct((packs, shard, width), BF16),
        compiler_params=params(),
        name="settle",
    )(jnp.concatenate([own_dest, shared_of, column.reshape(1)]), *pieces)

    part, hidden_here = width // n, up_weight.shape[1]
    return (
        result,
        tokens_grad,
        vectors[0],
        vectors[1],
        jnp.transpose(weights[: 3 * joined].reshape(3, joined, part), (0, 2, 1)),
        weights[3 * joined :],
        terms[:part, :hidden_here],
        terms[part, : hidden_here // n],
        terms[:part, hidden_here:].T,
        terms[part, hidden_here // n : hidden_here // n + part],
    )


def solution(mesh):
    in_specs = (
        P(None, "seq", None),
        P(),
        P(),
        P(),
        P(),
        P(None, None, "mlp"),
        P("mlp", None),
        P(None, "mlp"),
        P("mlp"),
        P("mlp", None),
        P(),
        P(None, "seq", "mlp"),
    )
    out_specs = (
        P(None, "seq", "mlp"),
        P(None, "seq", None),
        P("seq"),
        P("seq"),
        P(None, "seq", "mlp"),
        P("mlp", "seq"),
        P("seq", "mlp"),
        P(("mlp", "seq")),
        P("mlp", "seq"),
        P("seq"),
    )
    n, slices = mesh.shape["seq"], mesh.shape["mlp"]

    def plan(*args):
        packs, pack_len, _ = args[0].shape
        heads = args[6].shape[0] // HD // slices
        pairs = (
            2 * packs == 3 * n
            and n >= 4
            and heads % 4 == 0
            and (pack_len // n) % 128 == 0
            and (pack_len // n) % (16 * slices) == 0
        )
        return jax.shard_map(
            on_device_pairs if pairs else on_device,
            mesh=mesh,
            in_specs=in_specs,
            out_specs=out_specs,
            check_vma=False,
        )(*args)

    return plan
```

```python
import functools
import math

import jax
import jax.numpy as jnp
from jax import lax
from jax.experimental import pallas as pl
from jax.experimental.pallas import tpu as pltpu
from jax.sharding import PartitionSpec as P

HD = 64
ROT = 32
EPS = 1e-05
NEG = -1e30
BF16 = jnp.bfloat16
F32 = jnp.float32
VMEM_LIMIT = 56 * 1024 * 1024
COST = pl.CostEstimate(flops=1 << 20, bytes_accessed=1 << 20, transcendentals=0)


def dot(a, b, dims=((1,), (0,))):
    return lax.dot_general(a, b, (dims, ((), ())), preferred_element_type=F32)


def layout(lengths, counts, pack_len):
    slots = lengths.shape[-1]
    slot_ids = jnp.arange(slots, dtype=jnp.int32)
    used = slot_ids[None, :] < counts[:, None]
    sizes = jnp.where(used, lengths, 0)
    ends = jnp.cumsum(sizes, axis=-1)
    starts = ends - sizes
    filled = ends[:, -1:]
    place = jnp.arange(pack_len, dtype=jnp.int32)[None, :]
    begin = jnp.max(
        jnp.where(used[:, None, :] & (place[:, :, None] >= starts[:, None, :]), starts[:, None, :], 0),
        axis=-1,
    )
    inside = place < filled
    first = jnp.where(inside, begin, place)
    position = jnp.where(inside, place - begin, place - filled)
    cost = jnp.sum(sizes * sizes, axis=-1)
    return first, position, cost


def turn(values, cosine, sine, heads):
    out = []
    parity = lax.broadcasted_iota(jnp.int32, cosine.shape, 0) % 2
    for h in range(heads):
        part = values[h * HD : h * HD + ROT]
        ahead = jnp.concatenate([part[1:], part[:1]], axis=0)
        behind = jnp.concatenate([part[-1:], part[:-1]], axis=0)
        swapped = jnp.where(parity == 0, -ahead, behind)
        out.append(part * cosine + swapped * sine)
        out.append(values[h * HD + ROT : (h + 1) * HD])
    return jnp.concatenate(out, axis=0)


def head_kernel(n, heads, per, me_ref, pack_ref, x_ref, gain_ref, bias_ref, w_ref, cos_ref, sin_ref, *refs):
    normed_ref, copy_ref, outs, scr = refs[0], refs[1], refs[2:-1], refs[-1]
    s_id, g = pl.program_id(0), pl.program_id(1)
    me = me_ref[0]
    width = heads * HD
    copy_ref[0] = x_ref[0]
    x = x_ref[0].astype(F32)
    cent = x - jnp.mean(x, axis=-1, keepdims=True)
    var = jnp.mean(cent * cent, axis=-1, keepdims=True)
    normed = (cent * lax.rsqrt(var + EPS) * gain_ref[...] + bias_ref[...]).astype(BF16)
    normed_ref[0] = normed
    for j in range(3):
        part = dot(w_ref[j * width : (j + 1) * width, :], normed, ((1,), (1,)))
        if j < 2:
            part = turn(part, cos_ref[0], sin_ref[0], heads)
        if j == 0:
            part = part * (1.0 / math.sqrt(HD))
        part = part.astype(BF16)
        for h in range(heads):
            scr[h, j] = part[h * HD : (h + 1) * HD]
    for at, out in enumerate(outs):
        d = lax.bitwise_xor(jnp.int32(at % n), me)

        @pl.when((d // heads == g) & (s_id // per == at // n))
        def _():
            out[0] = scr[d % heads]


def grad_kernel(n, heads, me_ref, c_ref, w_ref, *refs):
    outs, scr = refs[:n], refs[n]
    g = pl.program_id(1)
    me = me_ref[0]
    part = dot(w_ref[...], c_ref[0], ((1,), (1,))).astype(BF16)
    for h in range(heads):
        scr[h] = part[h * HD : (h + 1) * HD]
    for k in range(n):
        d = lax.bitwise_xor(jnp.int32(k), me)

        @pl.when(d // heads == g)
        def _():
            outs[k][0] = scr[d % heads]


def load_parts(n, me, pairs):
    for k in range(n):
        d = lax.bitwise_xor(jnp.int32(k), me)
        for part, t_ref, n_ref in pairs(k):
            if t_ref is not None:
                t_ref[d] = part
            if n_ref is not None:
                n_ref[d] = part.T


def score_of(block, first, i, kn, q_t):
    rows = lax.broadcasted_iota(jnp.int32, (block, block), 0)
    cols = lax.broadcasted_iota(jnp.int32, (block, block), 1)
    ahead = rows - cols

    def scores(j, at):
        s = dot(kn[at], q_t)
        allowed = (rows >= first - j * block) & (ahead <= (i - j) * block)
        return jnp.where(allowed, s, NEG)

    return scores


def attend_kernel(n, block, skip, me_ref, pack_ref, low_ref, first_ref, *refs):
    qkv, outs, keep_ref, logsum_ref = refs[:n], refs[n : 2 * n], refs[2 * n], refs[2 * n + 1]
    qt, vt, kn = refs[2 * n + 2 :]
    s_id = pl.program_id(0) + skip
    me = me_ref[0]
    load_parts(
        n,
        me,
        lambda k: (
            (qkv[k][0, 0, 0], qt, None),
            (qkv[k][0, 0, 1], None, kn),
            (qkv[k][0, 0, 2], vt, None),
        ),
    )

    def outer(i, carry):
        scores = score_of(block, first_ref[0, pl.ds(i, 1), :], i, kn, qt[i])
        j0 = low_ref[s_id, i]

        def forward(t, state):
            top, total, acc = state
            j = j0 + 2 * t
            at = jnp.minimum(j + 1, n - 1)
            s0, s1 = scores(j, j), scores(j + 1, at)
            peak = jnp.max(jnp.maximum(s0, s1), axis=0, keepdims=True)
            new_top = jnp.maximum(top, peak)
            p0, p1 = jnp.exp(s0 - new_top), jnp.exp(s1 - new_top)
            fade = jnp.exp(top - new_top)
            total = total * fade + jnp.sum(p0 + p1, axis=0, keepdims=True)
            acc = acc * fade + dot(vt[j], p0.astype(BF16)) + dot(vt[at], p1.astype(BF16))
            return new_top, total, acc

        top, total, acc = lax.fori_loop(
            0,
            (i - j0) // 2 + 1,
            forward,
            (
                jnp.full((1, block), NEG, F32),
                jnp.zeros((1, block), F32),
                jnp.zeros((HD, block), F32),
            ),
        )
        keep_ref[0, i] = (acc / total).astype(BF16)
        logsum_ref[0, pl.ds(i, 1), :] = top + jnp.log(total)
        return carry

    lax.fori_loop(0, n, outer, 0)
    for k in range(n):
        outs[k][0] = keep_ref[0, lax.bitwise_xor(jnp.int32(k), me)]


def attend_back_kernel(n, block, skip, me_ref, pack_ref, low_ref, first_ref, *refs):
    keep_ref, logsum_ref = refs[:2]
    qkv, grads, outs = refs[2 : n + 2], refs[n + 2 : 2 * n + 2], refs[2 * n + 2 : 3 * n + 2]
    qt, kt, gt, qn, kn, vn, gn, dk, dv, res = refs[3 * n + 2 :]
    s_id = pl.program_id(0) + skip
    me = me_ref[0]
    load_parts(
        n,
        me,
        lambda k: (
            (qkv[k][0, 0, 0], qt, qn),
            (qkv[k][0, 0, 1], kt, kn),
            (qkv[k][0, 0, 2], None, vn),
            (grads[k][0, 0], gt, gn),
        ),
    )
    dk[...] = jnp.zeros_like(dk)
    dv[...] = jnp.zeros_like(dv)

    def outer(i, carry):
        q_t, g_t, q_n, g_n = qt[i], gt[i], qn[i], gn[i]
        scores = score_of(block, first_ref[0, pl.ds(i, 1), :], i, kn, q_t)
        j0 = low_ref[s_id, i]
        inner = jnp.sum(keep_ref[0, i].astype(F32) * g_t.astype(F32), axis=0, keepdims=True)
        logsum = logsum_ref[0, pl.ds(i, 1), :]

        def one(j, at):
            p = jnp.exp(scores(j, at) - logsum)
            ds = (p * (dot(vn[at], g_t) - inner)).astype(BF16)
            return ds, dot(ds, q_n), dot(p.astype(BF16), g_n), dot(kt[at], ds)

        def backward(t, dq):
            j = j0 + 2 * t
            at = jnp.minimum(j + 1, n - 1)
            _, dk0, dv0, dq0 = one(j, j)
            _, dk1, dv1, dq1 = one(j + 1, at)
            dk[j] += dk0
            dv[j] += dv0
            dk[at] += dk1
            dv[at] += dv1
            return dq + dq0 + dq1

        dq = lax.fori_loop(0, (i - j0) // 2 + 1, backward, jnp.zeros((HD, block), F32))
        res[i, 0] = (dq * (1.0 / math.sqrt(HD))).astype(BF16)
        return carry

    lax.fori_loop(0, n, outer, 0)
    for i in range(n):
        res[i, 1] = dk[i].T.astype(BF16)
        res[i, 2] = dv[i].T.astype(BF16)
    for k in range(n):
        outs[k][0] = res[lax.bitwise_xor(jnp.int32(k), me)]


def merge_kernel(n, heads, slices, me_ref, *refs):
    recv = refs[:n]
    c_ref, merge_ref, branch_ref, out_branch, out_weight, scr, acc = refs[n:]
    s_id, g = pl.program_id(0), pl.program_id(1)
    groups = pl.num_programs(1)
    me = me_ref[0]
    width = heads * HD

    @pl.when((s_id == 0) & (g == 0))
    def _():
        acc[...] = jnp.zeros_like(acc)

    for k in range(n):
        d = lax.bitwise_xor(jnp.int32(k), me)

        @pl.when(d // heads == g)
        def _():
            scr[d % heads] = recv[k][0, 0, 0]

    attended = scr[...].reshape(width, c_ref.shape[1])
    acc[...] += dot(attended, c_ref[0])
    branch = dot(attended.T, merge_ref[...]) + branch_ref[0].astype(F32)
    cols = branch.shape[1] // slices
    for m in range(slices):
        out_branch[m, 0] = branch[:, m * cols : (m + 1) * cols].astype(BF16)

    @pl.when((s_id == pl.num_programs(0) - 1) & (g == groups - 1))
    def _():
        out_weight[...] = acc[...].astype(BF16)


def close_kernel(n, heads, me_ref, *refs):
    recv = refs[:n]
    normed_ref, w_ref, cos_ref, sin_ref, low_ref, out_low, out_weight, scr, acc = refs[n:]
    s_id, g = pl.program_id(0), pl.program_id(1)
    groups = pl.num_programs(1)
    me = me_ref[0]
    width = heads * HD
    shard = normed_ref.shape[1]

    @pl.when((s_id == 0) & (g == 0))
    def _():
        acc[...] = jnp.zeros_like(acc)

    for k in range(n):
        d = lax.bitwise_xor(jnp.int32(k), me)

        @pl.when(d // heads == g)
        def _():
            for j in range(3):
                scr[j, d % heads] = recv[k][0, 0, j]

    parts = []
    for j in (0, 1):
        part = scr[j].reshape(width, shard).astype(F32)
        parts.append(turn(part, cos_ref[0], -sin_ref[0], heads).astype(BF16))
    parts.append(scr[2].reshape(width, shard))
    grads = jnp.concatenate(parts, axis=0)
    acc[...] += dot(grads, normed_ref[0])
    low = dot(grads.T, w_ref[...]) + low_ref[0].astype(F32)
    out_low[0] = low.astype(BF16)

    @pl.when((s_id == pl.num_programs(0) - 1) & (g == groups - 1))
    def _():
        out_weight[...] = acc[...]


def place_kernel(block, share, shard, slices, chunks, per_piece, pack_ref, *refs):
    pieces, out, buf, sems, out_sems = refs[:-4], refs[-4], refs[-3], refs[-2], refs[-1]
    me = pack_ref[chunks * slices * share // shard]
    loads, stores = [], []
    arrays = max(ref for ref, _ in per_piece) + 1
    for c in range(chunks):
        for k in range(slices):
            ref, where = per_piece[k]
            for t in range(share // block):
                at = len(loads)
                row = (c * slices + lax.bitwise_xor(jnp.int32(k), me)) * share + t * block
                start = pl.multiple_of(lax.rem(row, shard), block)
                loads.append(
                    pltpu.make_async_copy(
                        pieces[c * arrays + ref].at[where, pl.ds(t * block, block)],
                        buf.at[at],
                        sems.at[at],
                    )
                )
                stores.append(
                    pltpu.make_async_copy(
                        buf.at[at],
                        out.at[pack_ref[row // shard], pl.ds(start, block)],
                        out_sems.at[at],
                    )
                )
    for copy in loads:
        copy.start()
    for load, store in zip(loads, stores):
        load.wait()
        store.start()
    for copy in stores:
        copy.wait()


def small_kernel(n, slices, x_ref, out_ref, first, second, sems, sems2):
    rank, column = lax.axis_index("seq"), lax.axis_index("mlp")
    barrier = pltpu.get_barrier_semaphore()
    peers = [{"seq": lax.bitwise_xor(rank, k)} for k in range(1, n)]
    rows = [{"mlp": lax.bitwise_xor(column, k)} for k in range(1, slices)]
    for peer in peers + rows:
        pl.semaphore_signal(barrier, inc=1, device_id=peer, device_id_type=pl.DeviceIdType.MESH)
    pl.semaphore_wait(barrier, len(peers) + len(rows))

    def exchange(source, target, sems, peers):
        copies = [
            pltpu.make_async_remote_copy(
                src_ref=source(k),
                dst_ref=target.at[k],
                send_sem=sems.at[0, k],
                recv_sem=sems.at[1, k],
                device_id=peer,
                device_id_type=pl.DeviceIdType.MESH,
            )
            for k, peer in enumerate(peers)
        ]
        for copy in copies:
            copy.start()
        for copy in copies:
            copy.wait()

    exchange(lambda k: x_ref.at[lax.bitwise_xor(rank, k + 1)], first, sems, peers)
    total = x_ref[rank]
    for k in range(n - 1):
        total = total + first[k]
    second[slices - 1] = total
    second[slices] = total
    exchange(lambda k: second.at[slices], second, sems2, rows)
    parts = [
        second[jnp.where(column == c, slices - 1, lax.bitwise_xor(column, c) - 1)]
        for c in range(slices)
    ]
    out_ref[...] = functools.reduce(jnp.add, parts)


def small_sum(vectors, n, slices):
    count, width = vectors.shape
    x = jnp.transpose(vectors.reshape(count, n, width // n), (1, 0, 2))
    return pl.pallas_call(
        functools.partial(small_kernel, n, slices),
        out_shape=jax.ShapeDtypeStruct((count, width // n), F32),
        in_specs=[pl.BlockSpec(memory_space=pltpu.VMEM)],
        out_specs=pl.BlockSpec(memory_space=pltpu.VMEM),
        scratch_shapes=[
            pltpu.VMEM((n - 1, count, width // n), F32),
            pltpu.VMEM((slices + 1, count, width // n), F32),
            pltpu.SemaphoreType.DMA((2, n - 1)),
            pltpu.SemaphoreType.DMA((2, slices - 1)),
        ],
        compiler_params=pltpu.CompilerParams(collective_id=0, has_side_effects=True),
        cost_estimate=COST,
        name="small_sum",
    )(x)


def params():
    return pltpu.CompilerParams(vmem_limit_bytes=VMEM_LIMIT)


def tie(*values):
    return lax.optimization_barrier(values)


def send_x(parts):
    n = len(parts)
    sent = jnp.stack([parts[k] for k in range(1, n, 2)])
    return lax.ppermute(sent, "seq", [(i, i ^ 1) for i in range(n)])


def send_z(parts, got, steps=None):
    n = len(parts)
    return [
        lax.ppermute(
            jnp.stack([parts[k], got[k // 2]]), "seq", [(i, i ^ k) for i in range(n)]
        )
        for k in (range(2, n, 2) if steps is None else steps)
    ]


def received(parts, got, gots):
    out = [(parts[0][None], 0), (got, 0)]
    for array in gots:
        out += [(array, 0), (array, 1)]
    return out


def span(masks):
    out = [0]
    for m in masks:
        out += [v ^ m for v in out]
    return out


def cube_send(chunks, axis, n, masks):
    kept = span(masks[1:])
    sent = jnp.stack([chunks[k ^ masks[0]] for k in kept])
    return lax.ppermute(sent, axis, [(i, i ^ masks[0]) for i in range(n)])


def cube_add(chunks, got, masks, kind):
    return {
        k: (chunks[k].astype(F32) + got[at].astype(F32)).astype(kind)
        for at, k in enumerate(span(masks[1:]))
    }


def cube_sum(chunks, axis, masks, kind):
    n = len(chunks)
    chunks = {k: v.astype(kind) for k, v in enumerate(chunks)}
    for step in range(len(masks)):
        got = cube_send(chunks, axis, n, masks[step:])
        chunks = cube_add(chunks, got, masks[step:], F32 if step == len(masks) - 1 else kind)
    return chunks[0]


def gather_step(arrays, axis, n, m):
    sent = jnp.concatenate(arrays, axis=0) if len(arrays) > 1 else arrays[0]
    return arrays + [lax.ppermute(sent, axis, [(i, i ^ m) for i in range(n)])]


def masks_of(n):
    return [1 << b for b in range(n.bit_length() - 1)]


def turned(masks, by):
    by = by % len(masks)
    return masks[by:] + masks[:by]


def cut(array, axis, n, me):
    size = array.shape[axis] // n
    return [
        lax.dynamic_slice_in_dim(array, lax.bitwise_xor(jnp.int32(k), me) * size, size, axis)
        for k in range(n)
    ]


def on_device(
    tokens,
    lengths,
    counts,
    norm_gain,
    norm_bias,
    head_weight,
    merge_weight,
    up_weight,
    up_bias,
    down_weight,
    down_bias,
    cotangent,
):
    packs, shard, width = tokens.shape
    n = lax.axis_size("seq")
    slices = lax.axis_size("mlp")
    pack_len = shard * n
    rank = lax.axis_index("seq")
    column = lax.axis_index("mlp")
    heads = merge_weight.shape[0] // HD
    joined = heads * HD
    groups = n // heads
    slots = -(-packs // groups)
    dealt = groups * slots
    spare = 1 if dealt > packs else 0
    rows = dealt * shard
    chunks = 2 if slots % 2 == 0 else 1
    per = slots // chunks
    seq_masks, mlp_masks = masks_of(n), masks_of(slices)

    first, position, cost = layout(lengths, counts, pack_len)
    ids = jnp.arange(packs, dtype=jnp.int32)
    before = (cost[None, :] > cost[:, None]) | (
        (cost[None, :] == cost[:, None]) & (ids[None, :] < ids[:, None])
    )
    order = jnp.sum(before.astype(jnp.int32), axis=1)
    slot_of = order // groups
    group_of = jnp.where(slot_of % 2 == 0, order % groups, groups - 1 - order % groups)
    at = slot_of * groups + group_of
    hit = at[None, :] == jnp.arange(dealt, dtype=jnp.int32)[:, None]
    pack_at = jnp.where(
        jnp.any(hit, axis=-1), jnp.sum(jnp.where(hit, ids, 0), axis=-1), packs
    ).astype(jnp.int32)
    safe = jnp.minimum(pack_at, packs - 1)
    me = rank.astype(jnp.int32).reshape(1)

    own_cot = jnp.take(cotangent, safe, axis=0, mode="clip")
    if spare:
        own_cot = jnp.where((pack_at < packs)[:, None, None], own_cot, 0)
    cot = lax.all_gather(own_cot, "mlp", axis=2, tiled=True)

    half = ROT // 2
    freq = 10000.0 ** (-(2.0 * jnp.arange(half, dtype=F32)) / ROT)
    own_position = jnp.take(
        lax.dynamic_slice_in_dim(position, rank * shard, shard, 1), safe, axis=0, mode="clip"
    )
    angle = own_position.astype(F32)[:, None, :] * jnp.repeat(freq, 2)[None, :, None]
    cosine, sine = jnp.cos(angle), jnp.sin(angle)

    w_t = jnp.transpose(head_weight, (0, 2, 1)).reshape(3 * joined, width)

    def whole2(s, g, *_):
        return (0, 0)

    def rows_at(skip):
        return pl.BlockSpec((1, shard, width), lambda s, g, *_: ((s + skip) * groups + g, 0, 0))

    def table_at(skip):
        return pl.BlockSpec((1, ROT, shard), lambda s, g, *_: ((s + skip) * groups + g, 0, 0))

    parts = [jax.ShapeDtypeStruct((per, 3, HD, shard), BF16)] * n

    def chunk_at(c):
        return pl.BlockSpec(
            (1, 3, HD, shard), lambda s, g, *_: (jnp.clip(s - c * per, 0, per - 1), 0, 0, 0)
        )

    outs = pl.pallas_call(
        functools.partial(head_kernel, n, heads, per),
        grid_spec=pltpu.PrefetchScalarGridSpec(
            num_scalar_prefetch=2,
            grid=(slots, groups),
            in_specs=[
                pl.BlockSpec((1, shard, width), lambda s, g, a, b: (b[s * groups + g], 0, 0)),
                pl.BlockSpec((1, width), whole2),
                pl.BlockSpec((1, width), whole2),
                pl.BlockSpec((3 * joined, width), whole2),
                table_at(0),
                table_at(0),
            ],
            out_specs=[rows_at(0)] * 2 + [chunk_at(c) for c in range(chunks) for _ in range(n)],
            scratch_shapes=[pltpu.VMEM((heads, 3, HD, shard), BF16)],
        ),
        out_shape=[jax.ShapeDtypeStruct((dealt, shard, width), BF16)] * 2 + parts * chunks,
        compiler_params=params(),
        cost_estimate=COST,
        name="heads",
    )(
        me,
        safe,
        tokens,
        norm_gain.reshape(1, width),
        norm_bias.reshape(1, width),
        w_t,
        cosine,
        sine,
    )
    normed_low, tokens_dealt = outs[0], outs[1]
    qkv = [list(outs[2 + c * n : 2 + (c + 1) * n]) for c in range(chunks)]

    def out_grads(cot, merge_weight):
        return pl.pallas_call(
            functools.partial(grad_kernel, n, heads),
            grid_spec=pltpu.PrefetchScalarGridSpec(
                num_scalar_prefetch=1,
                grid=(slots, groups),
                in_specs=[rows_at(0), pl.BlockSpec((joined, width), whole2)],
                out_specs=[pl.BlockSpec((1, HD, shard), lambda s, g, *_: (s, 0, 0))] * n,
                scratch_shapes=[pltpu.VMEM((heads, HD, shard), BF16)],
            ),
            out_shape=[jax.ShapeDtypeStruct((slots, HD, shard), BF16)] * n,
            compiler_params=params(),
            cost_estimate=COST,
            name="out_grads",
        )(me, cot, merge_weight)

    mine = rank // heads + groups * jnp.arange(slots, dtype=jnp.int32)
    my_packs = jnp.take(safe, mine, mode="clip")
    first = first.reshape(packs, n, shard)
    lows = (jnp.take(first[:, :, 0], my_packs, axis=0, mode="clip") // shard).astype(jnp.int32)
    wide = [pltpu.VMEM((n, HD, shard), BF16)]
    tall = [pltpu.VMEM((n, shard, HD), BF16)]

    def first_at(skip):
        return pl.BlockSpec((1, n, shard), lambda s, a, b, c: (b[s + skip], 0, 0))

    def qkv_at(lead):
        return pl.BlockSpec((1, 1, 3, HD, shard), lambda s, *_: (lead, s, 0, 0, 0))

    def grad_at(lead, skip):
        return pl.BlockSpec((1, 1, HD, shard), lambda s, *_: (lead, s + skip, 0, 0))

    def attend(c, sources):
        return pl.pallas_call(
            functools.partial(attend_kernel, n, shard, c * per),
            grid_spec=pltpu.PrefetchScalarGridSpec(
                num_scalar_prefetch=3,
                grid=(per,),
                in_specs=[first_at(c * per)] + [qkv_at(lead) for _, lead in sources],
                out_specs=[pl.BlockSpec((1, HD, shard), lambda s, *_: (s, 0, 0))] * n
                + [
                    pl.BlockSpec((1, n, HD, shard), lambda s, *_: (s, 0, 0, 0)),
                    pl.BlockSpec((1, n, shard), lambda s, *_: (s, 0, 0)),
                ],
                scratch_shapes=wide * 2 + tall,
            ),
            out_shape=[jax.ShapeDtypeStruct((per, HD, shard), BF16)] * n
            + [
                jax.ShapeDtypeStruct((per, n, HD, shard), BF16),
                jax.ShapeDtypeStruct((per, n, shard), F32),
            ],
            compiler_params=params(),
            cost_estimate=COST,
            name="attend",
        )(me, my_packs, lows, first, *[array for array, _ in sources])

    def attend_back(c, kept, logsum, sources, grads):
        return pl.pallas_call(
            functools.partial(attend_back_kernel, n, shard, c * per),
            grid_spec=pltpu.PrefetchScalarGridSpec(
                num_scalar_prefetch=3,
                grid=(per,),
                in_specs=[
                    first_at(c * per),
                    pl.BlockSpec((1, n, HD, shard), lambda s, *_: (s, 0, 0, 0)),
                    pl.BlockSpec((1, n, shard), lambda s, *_: (s, 0, 0)),
                ]
                + [qkv_at(lead) for _, lead in sources]
                + [grad_at(lead, c * per) for _, lead in grads],
                out_specs=[pl.BlockSpec((1, 3, HD, shard), lambda s, *_: (s, 0, 0, 0))] * n,
                scratch_shapes=wide * 3
                + tall * 4
                + [pltpu.VMEM((n, shard, HD), F32)] * 2
                + [pltpu.VMEM((n, 3, HD, shard), BF16)],
            ),
            out_shape=parts,
            compiler_params=params(),
            cost_estimate=COST,
            name="attend_back",
        )(
            me,
            my_packs,
            lows,
            first,
            kept,
            logsum,
            *[array for array, _ in sources],
            *[array for array, _ in grads],
        )

    def merge(sources, branch_ff):
        return pl.pallas_call(
            functools.partial(merge_kernel, n, heads, slices),
            grid_spec=pltpu.PrefetchScalarGridSpec(
                num_scalar_prefetch=1,
                grid=(slots, groups),
                in_specs=[
                    pl.BlockSpec(
                        (1, 1, 1, HD, shard),
                        lambda s, g, *_, lead=lead: (lead, s // per, s % per, 0, 0),
                    )
                    for _, lead in sources
                ]
                + [rows_at(0), pl.BlockSpec((joined, width), whole2), rows_at(0)],
                out_specs=[
                    pl.BlockSpec(
                        (slices, 1, shard, width // slices),
                        lambda s, g, *_: (0, s * groups + g, 0, 0),
                    ),
                    pl.BlockSpec((joined, width), whole2),
                ],
                scratch_shapes=[
                    pltpu.VMEM((heads, HD, shard), BF16),
                    pltpu.VMEM((joined, width), F32),
                ],
            ),
            out_shape=[
                jax.ShapeDtypeStruct((slices, dealt, shard, width // slices), BF16),
                jax.ShapeDtypeStruct((joined, width), BF16),
            ],
            compiler_params=params(),
            cost_estimate=COST,
            name="merge",
        )(me, *[array for array, _ in sources], cot, merge_weight, branch_ff)

    def close(c, sources):
        skip = c * per
        return pl.pallas_call(
            functools.partial(close_kernel, n, heads),
            grid_spec=pltpu.PrefetchScalarGridSpec(
                num_scalar_prefetch=1,
                grid=(per, groups),
                in_specs=[
                    pl.BlockSpec(
                        (1, 1, 3, HD, shard), lambda s, g, *_, lead=lead: (lead, s, 0, 0, 0)
                    )
                    for _, lead in sources
                ]
                + [
                    rows_at(skip),
                    pl.BlockSpec((3 * joined, width), whole2),
                    table_at(skip),
                    table_at(skip),
                    rows_at(skip),
                ],
                out_specs=[rows_at(0), pl.BlockSpec((3 * joined, width), whole2)],
                scratch_shapes=[
                    pltpu.VMEM((3, heads, HD, shard), BF16),
                    pltpu.VMEM((3 * joined, width), F32),
                ],
            ),
            out_shape=[
                jax.ShapeDtypeStruct((per * groups, shard, width), BF16),
                jax.ShapeDtypeStruct((3 * joined, width), F32),
            ],
            compiler_params=params(),
            cost_estimate=COST,
            name="close",
        )(me, *[array for array, _ in sources], normed_low, w_t, cosine, sine, low_ff)

    got_x = [None] * chunks
    got_z = [None] * chunks
    got_x[0] = send_x(qkv[0])
    hidden = (
        jnp.einsum("psd,df->psf", normed_low, up_weight, preferred_element_type=F32) + up_bias
    )
    active_low = jax.nn.gelu(hidden, approximate=True).astype(BF16)
    branch_ff = jnp.einsum(
        "psf,fd->psd", active_low, down_weight, preferred_element_type=F32
    ).astype(BF16)
    got_x[0], branch_ff, qkv, out_weight, back_weight = tie(
        got_x[0], branch_ff, qkv, merge_weight, down_weight
    )

    got_z[0] = send_z(qkv[0], got_x[0])
    if chunks > 1:
        got_x[1] = send_x(qkv[1])
    sends = out_grads(cot, out_weight)
    active_grad = jnp.einsum("psd,fd->psf", cot, back_weight, preferred_element_type=F32)
    _, gelu_back = jax.vjp(lambda values: jax.nn.gelu(values, approximate=True), hidden)
    hidden_grad = gelu_back(active_grad)[0].astype(BF16)
    got_x, got_z, qkv, sends, hidden_grad = tie(got_x, got_z, qkv, sends, hidden_grad)

    got_dx = send_x(sends)
    sources = [received(qkv[0], got_x[0], got_z[0])]
    if chunks > 1:
        got_z[1] = send_z(qkv[1], got_x[1])
        sources.append(received(qkv[1], got_x[1], got_z[1]))
    ahead = [attend(0, sources[0])]
    up_grad = jnp.einsum(
        "psd,psf->df", normed_low, hidden_grad, preferred_element_type=F32
    ).astype(BF16)
    down_grad = jnp.einsum("psd,psf->df", cot, active_low, preferred_element_type=F32).astype(BF16)
    biases = jnp.sum(hidden_grad.astype(F32), axis=(0, 1)), jnp.sum(cot.astype(F32), axis=(0, 1))
    got_dx, sources_arrays, ahead, sends, hidden_grad, up_grad, down_grad, biases = tie(
        got_dx,
        [[a for a, _ in v] for v in sources],
        ahead,
        sends,
        hidden_grad,
        up_grad,
        down_grad,
        biases,
    )
    def with_row(*parts):
        weight = jnp.concatenate(parts[:2], axis=1)
        row = jnp.concatenate(parts[2:])
        row = jnp.pad(row, (0, weight.shape[1] - row.shape[0])).reshape(1, -1)
        row = jnp.broadcast_to(row, (16, weight.shape[1])).astype(BF16)
        return jnp.concatenate([weight, row], axis=0)

    terms = dict(
        enumerate(
            with_row(*parts)
            for parts in zip(*[cut(v, 0, n, rank) for v in (up_grad, down_grad, *biases)])
        )
    )
    terms_got = cube_send(terms, "seq", n, seq_masks)
    sources = [
        [(a, lead) for a, (_, lead) in zip(arrays, v)] for arrays, v in zip(sources_arrays, sources)
    ]

    got_dz = send_z(sends, got_dx)
    if chunks > 1:
        ahead.append(attend(1, sources[1]))
    low_ff = jnp.einsum(
        "psf,df->psd", hidden_grad, up_weight, preferred_element_type=F32
    ).astype(BF16)
    got_dz, ahead, low_ff = tie(got_dz, ahead, low_ff)
    grads = received(sends, got_dx, got_dz)

    attended = [jnp.stack([outs[k] for outs in ahead]) for k in range(n)]
    got_ax = send_x(attended)
    backs = [attend_back(0, ahead[0][n], ahead[0][n + 1], sources[0], grads)]
    got_ax, terms_got, backs, attended, ahead = tie(got_ax, terms_got, backs, attended, ahead)

    terms = cube_add(terms, terms_got, seq_masks, BF16)
    terms_got = cube_send(terms, "seq", n, seq_masks[1:])
    got_az = send_z(attended, got_ax)
    back_x = [send_x(backs[0])]
    if chunks > 1:
        backs.append(attend_back(1, ahead[1][n], ahead[1][n + 1], sources[1], grads))
    got_az, terms_got, back_x, backs = tie(got_az, terms_got, back_x, backs)

    back_z = [send_z(backs[0], back_x[0])]
    if chunks > 1:
        back_x.append(send_x(backs[1]))
    for step in range(1, len(seq_masks)):
        last_step = step == len(seq_masks) - 1
        terms = cube_add(terms, terms_got, seq_masks[step:], F32 if last_step else BF16)
        if not last_step:
            terms_got = cube_send(terms, "seq", n, seq_masks[step + 1 :])
    terms = terms[0]
    branch, merge_part = merge(received(attended, got_ax, got_az), branch_ff)
    summed = lax.psum_scatter(branch, "mlp", scatter_dimension=0, tiled=False)
    back_x, back_z, backs, merge_part, terms = tie(back_x, back_z, backs, merge_part, terms)

    share = per * groups * shard // slices

    def share_sum(low):
        return cube_sum(
            cut(low.reshape(share * slices, width), 0, slices, column), "mlp", mlp_masks, BF16
        )

    def finish(c, low_sum):
        start = (c * slices + column) * share
        row_in = lax.dynamic_slice_in_dim(
            tokens_dealt.reshape(rows, width), start, share, 0
        ).astype(F32)
        row_cot = lax.dynamic_slice_in_dim(cot.reshape(rows, width), start, share, 0).astype(F32)
        cent = row_in - jnp.mean(row_in, axis=-1, keepdims=True)
        inverse = lax.rsqrt(jnp.mean(cent * cent, axis=-1, keepdims=True) + EPS)
        xhat = cent * inverse
        g = low_sum * norm_gain
        row_grad = (
            row_cot
            + (
                g
                - jnp.mean(g, axis=-1, keepdims=True)
                - xhat * jnp.mean(g * xhat, axis=-1, keepdims=True)
            )
            * inverse
        ).astype(BF16)
        return row_grad, jnp.stack([jnp.sum(low_sum * xhat, axis=0), jnp.sum(low_sum, axis=0)])

    low, head_part = close(0, received(backs[0], back_x[0], back_z[0]))
    head_parts = [head_part]
    if chunks > 1:
        second = send_z(backs[1], back_x[1], [n // 2])
        second, low, head_parts, backs, back_x = tie(second, low, head_parts, backs, back_x)
        others = send_z(backs[1], back_x[1], [k for k in range(2, n, 2) if k != n // 2])
        others.insert(n // 4 - 1, second[0])
        back_z.append(others)
    row_grad, vectors = finish(0, share_sum(low))
    back_z, row_grad, vectors = tie(back_z, row_grad, vectors)

    cols = width // slices
    pieces = gather_step([row_grad[None]], "mlp", slices, mlp_masks[-1])
    result = (
        lax.dynamic_slice_in_dim(tokens, column * cols, cols, 2).astype(F32)
        + jnp.take(summed, at, axis=0, mode="clip").astype(F32)
        + lax.dynamic_slice_in_dim(down_bias, column * cols, cols, 0)
    ).astype(BF16)
    if chunks > 1:
        low, head_part = close(1, received(backs[1], back_x[1], back_z[1]))
        head_parts.append(head_part)
        pieces, low, head_parts, result = tie(pieces, low, head_parts, result)
    weights = functools.reduce(jnp.add, head_parts)
    weights = jnp.concatenate([weights.astype(BF16), merge_part], axis=0)
    weights = dict(enumerate(cut(weights, 1, n, rank)))
    weights_got = cube_send(weights, "seq", n, seq_masks)
    if chunks > 1:
        low_sum = share_sum(low)
        for m in reversed(mlp_masks[:-1]):
            pieces = gather_step(pieces, "mlp", slices, m)
        row_grad, more = finish(1, low_sum)
        vectors = vectors + more
        row_grad, pieces, weights_got, vectors = tie(row_grad, pieces, weights_got, vectors)
        last = gather_step([row_grad[None]], "mlp", slices, mlp_masks[-1])
    else:
        last, pieces = pieces, []
    vectors = small_sum(vectors, n, slices)
    weights = cube_add(weights, weights_got, seq_masks, BF16)
    weights_got = cube_send(weights, "seq", n, seq_masks[1:])
    last, vectors, weights_got = tie(last, vectors, weights_got)
    for m in reversed(mlp_masks[:-1]):
        last = gather_step(last, "mlp", slices, m)
    pieces += last
    where = [(0, 0)]
    lookup = [0]
    for i, m in enumerate(reversed(mlp_masks)):
        where += [(i + 1, j) for j in range(len(lookup))]
        lookup += [k ^ m for k in lookup]
    per_piece = [where[lookup.index(k)] for k in range(slices)]
    block = math.gcd(share, shard)
    tokens_grad = pl.pallas_call(
        functools.partial(
            place_kernel, block, share, shard, slices, chunks, per_piece
        ),
        grid_spec=pltpu.PrefetchScalarGridSpec(
            num_scalar_prefetch=1,
            grid=(1,),
            in_specs=[pl.BlockSpec(memory_space=pl.ANY)] * len(pieces),
            out_specs=pl.BlockSpec(memory_space=pl.ANY),
            scratch_shapes=[
                pltpu.VMEM((rows // block, block, width), BF16),
                pltpu.SemaphoreType.DMA((rows // block,)),
                pltpu.SemaphoreType.DMA((rows // block,)),
            ],
        ),
        out_shape=jax.ShapeDtypeStruct((packs + spare, shard, width), BF16),
        compiler_params=params(),
        name="place",
    )(jnp.concatenate([pack_at, column.astype(jnp.int32).reshape(1)]), *pieces)[:packs]

    for step in range(1, len(seq_masks)):
        weights = cube_add(
            weights, weights_got, seq_masks[step:], F32 if step == len(seq_masks) - 1 else BF16
        )
        if step < len(seq_masks) - 1:
            weights_got = cube_send(weights, "seq", n, seq_masks[step + 1 :])
    weights = weights[0]
    head_grad = jnp.transpose(
        weights[: 3 * joined].reshape(3, joined, width // n), (0, 2, 1)
    )
    merge_grad = weights[3 * joined :]
    part, hidden_here = width // n, up_weight.shape[1]
    up_grad, down_grad = terms[:part, :hidden_here], terms[:part, hidden_here:].T
    up_bias_grad = terms[part, : hidden_here // n]
    down_bias_grad = terms[part, hidden_here // n : hidden_here // n + part]
    return (
        result,
        tokens_grad,
        vectors[0],
        vectors[1],
        head_grad,
        merge_grad,
        up_grad,
        up_bias_grad,
        down_grad,
        down_bias_grad,
    )


def qkv_kernel(heads, me_ref, x_ref, w_ref, cos_ref, sin_ref, normed_ref, out_ref):
    width = heads * HD
    normed = x_ref[0]
    normed_ref[...] = normed
    for j in range(3):
        part = dot(w_ref[j].reshape(width, w_ref.shape[3]), normed, ((1,), (1,)))
        if j < 2:
            part = turn(part, cos_ref[...], sin_ref[...], heads)
        if j == 0:
            part = part * (1.0 / math.sqrt(HD))
        part = part.astype(BF16)
        for h in range(heads):
            out_ref[h, j] = part[h * HD : (h + 1) * HD]


def allowed_of(block, first, i):
    rows = lax.broadcasted_iota(jnp.int32, (block, block), 0)
    cols = lax.broadcasted_iota(jnp.int32, (block, block), 1)
    ahead = rows - cols
    return lambda j: (rows >= first - j * block) & (ahead <= (i - j) * block)


def unit_kernel(n, block, me_ref, low_ref, first_ref, qkv_ref, out_ref, keep_ref, logsum_ref, qt, vt, kn):
    me = me_ref[0]
    pair = range(qkv_ref.shape[0])
    for u in pair:
        for i in range(n):
            at = slice(i * block, (i + 1) * block)
            qt[u, i] = qkv_ref[u, 0, :, at]
            kn[u, i] = qkv_ref[u, 1, :, at].T
            vt[u, i] = qkv_ref[u, 2, :, at]

    def outer(i, carry):
        allowed = allowed_of(block, first_ref[pl.ds(i, 1), :], i)
        j0 = low_ref[i]

        def forward(t, states):
            j = j0 + 2 * t
            at = jnp.minimum(j + 1, n - 1)
            mask0, mask1 = allowed(j), allowed(j + 1)
            out = []
            for u, (top, total, acc) in zip(pair, states):
                q_t = qt[u, i]
                s0 = jnp.where(mask0, dot(kn[u, j], q_t), NEG)
                s1 = jnp.where(mask1, dot(kn[u, at], q_t), NEG)
                peak = jnp.max(jnp.maximum(s0, s1), axis=0, keepdims=True)
                new_top = jnp.maximum(top, peak)
                p0, p1 = jnp.exp(s0 - new_top), jnp.exp(s1 - new_top)
                fade = jnp.exp(top - new_top)
                total = total * fade + jnp.sum(p0 + p1, axis=0, keepdims=True)
                acc = acc * fade + dot(vt[u, j], p0.astype(BF16)) + dot(vt[u, at], p1.astype(BF16))
                out.append((new_top, total, acc))
            return tuple(out)

        states = lax.fori_loop(
            0,
            (i - j0) // 2 + 1,
            forward,
            tuple(
                (
                    jnp.full((1, block), NEG, F32),
                    jnp.zeros((1, block), F32),
                    jnp.zeros((HD, block), F32),
                )
                for _ in pair
            ),
        )
        for u, (top, total, acc) in zip(pair, states):
            keep_ref[u, i] = (acc / total).astype(BF16)
            logsum_ref[u, pl.ds(i, 1), :] = top + jnp.log(total)
        return carry

    lax.fori_loop(0, n, outer, 0)
    for k in range(n):
        for u in pair:
            out_ref[k, u] = keep_ref[u, lax.bitwise_xor(jnp.int32(k), me)]


def unit_back_kernel(
    n, block, by, me_ref, low_ref, first_ref, keep_ref, logsum_ref, qkv_ref, *refs
):
    out_ref, qt, kt, gt, qn, kn, vn, gn, dk, dv, dqs = refs[-11:]
    grads = [(refs[0], 0), (refs[1], 0)]
    for ref in refs[2:-11]:
        grads += [(ref, 0), (ref, 1)]
    me = me_ref[0]
    pair = range(qkv_ref.shape[0])
    for u in pair:
        for i in range(n):
            at = slice(i * block, (i + 1) * block)
            for j, (t_ref, n_ref) in enumerate(((qt, qn), (kt, kn), (None, vn))):
                part = qkv_ref[u, j, :, at]
                if t_ref is not None:
                    t_ref[u, i] = part
                n_ref[u, i] = part.T
        for k in range(n):
            d = lax.bitwise_xor(jnp.int32(k), me)
            part = grads[k][0][grads[k][1], u]
            gt[u, d] = part
            gn[u, d] = part.T
    dk[...] = jnp.zeros_like(dk)
    dv[...] = jnp.zeros_like(dv)

    def outer(i, carry):
        allowed = allowed_of(block, first_ref[pl.ds(i, 1), :], i)
        j0 = low_ref[i]
        inner = [
            jnp.sum(keep_ref[u, i].astype(F32) * gt[u, i].astype(F32), axis=0, keepdims=True)
            for u in pair
        ]
        logsum = [logsum_ref[u, pl.ds(i, 1), :] for u in pair]

        def one(u, mask, at):
            s = jnp.where(mask, dot(kn[u, at], qt[u, i]), NEG)
            p = jnp.exp(s - logsum[u])
            ds = (p * (dot(vn[u, at], gt[u, i]) - inner[u])).astype(BF16)
            return dot(ds, qn[u, i]), dot(p.astype(BF16), gn[u, i]), dot(kt[u, at], ds)

        def backward(t, dqs):
            j = j0 + by * t
            spots = [jnp.minimum(j + b, n - 1) if b else j for b in range(by)]
            masks = [allowed(j + b) for b in range(by)]
            out = []
            for u, dq in zip(pair, dqs):
                terms = [one(u, mask, at) for mask, at in zip(masks, spots)]
                for (dk0, dv0, dq0), at in zip(terms, spots):
                    dk[u, at] += dk0
                    dv[u, at] += dv0
                    dq = dq + dq0
                out.append(dq)
            return tuple(out)

        dq = lax.fori_loop(
            0, (i - j0) // by + 1, backward, tuple(jnp.zeros((HD, block), F32) for _ in pair)
        )
        for u in pair:
            dqs[u, i] = (dq[u] * (1.0 / math.sqrt(HD))).astype(BF16)
        return carry

    lax.fori_loop(0, n, outer, 0)
    for u in pair:
        for i in range(n):
            at = slice(i * block, (i + 1) * block)
            out_ref[u, 0, :, at] = dqs[u, i]
            out_ref[u, 1, :, at] = dk[u, i].T.astype(BF16)
            out_ref[u, 2, :, at] = dv[u, i].T.astype(BF16)


def rows_kernel(heads, slices, me_ref, grad_ref, normed_ref, w_ref, cos_ref, sin_ref, *refs):
    kept_ref, sent_ref, weight_ref = refs[-3:]
    width = heads * HD
    column = me_ref[1]

    @pl.when(pl.program_id(0) == 0)
    def _():
        if len(refs) > 3:
            weight_ref[...] = refs[0][...]
        else:
            weight_ref[...] = jnp.zeros_like(weight_ref)

    parts = []
    for j in range(3):
        part = jnp.concatenate([grad_ref[h, j] for h in range(heads)], axis=0)
        if j < 2:
            part = turn(part.astype(F32), cos_ref[...], -sin_ref[...], heads).astype(BF16)
        parts.append(part)
    grads = jnp.concatenate(parts, axis=0)
    if len(refs) > 3:
        whole = weight_ref.shape[0] // 3
        start = lax.rem(me_ref[0], 2) * width
        for j in range(3):
            rows = pl.ds(pl.multiple_of(j * whole + start, width), width)
            weight_ref[rows, :] += dot(parts[j], normed_ref[...])
    else:
        weight_ref[...] += dot(grads, normed_ref[...])
    low = dot(grads.T, w_ref[...].reshape(3 * width, w_ref.shape[3])).astype(BF16)
    part = low.shape[0] // slices
    for m in range(slices):
        at = lax.bitwise_xor(jnp.int32(m), column)
        for bit, ref in enumerate((kept_ref, sent_ref)):

            @pl.when(at % 2 == bit)
            def _():
                ref[at // 2, 0] = low[m * part : (m + 1) * part]


def norm_kernel(me_ref, x_ref, gain_ref, bias_ref, normed_ref, cols_ref):
    cols = cols_ref.shape[2]
    start = pl.multiple_of(me_ref[1] * cols, cols)
    step = math.gcd(x_ref.shape[1], 32)
    for r in range(0, x_ref.shape[1], step):
        x = x_ref[0, r : r + step].astype(F32)
        cent = x - jnp.mean(x, axis=-1, keepdims=True)
        var = jnp.mean(cent * cent, axis=-1, keepdims=True)
        normed = cent * lax.rsqrt(var + EPS) * gain_ref[...] + bias_ref[...]
        normed_ref[0, r : r + step] = normed.astype(BF16)
    cols_ref[0] = normed_ref[0, :, pl.ds(start, cols)]


def finish_kernel(terms, which_ref, *refs):
    lows = refs[:terms]
    low_ref, x_ref, c_ref, gain_ref, out_ref, sums_ref = refs[terms:]

    @pl.when(pl.program_id(0) == 0)
    def _():
        sums_ref[...] = jnp.zeros_like(sums_ref)

    low = low_ref[0].astype(F32)
    for ref in lows:
        low = low + ref[0].astype(F32)
    x = x_ref[0].astype(F32)
    cent = x - jnp.mean(x, axis=-1, keepdims=True)
    inverse = lax.rsqrt(jnp.mean(cent * cent, axis=-1, keepdims=True) + EPS)
    xhat = cent * inverse
    g = low * gain_ref[...]
    inner = jnp.mean(g * xhat, axis=-1, keepdims=True)
    back = (g - jnp.mean(g, axis=-1, keepdims=True) - xhat * inner) * inverse
    out_ref[0] = (c_ref[0].astype(F32) + back).astype(BF16)
    sums_ref[0:1] += jnp.sum(low * xhat, axis=0, keepdims=True)
    sums_ref[1:2] += jnp.sum(low, axis=0, keepdims=True)


def join_kernel(slices, attended_ref, c_ref, merge_ref, branch_ref, out_branch, out_weight):
    @pl.when(pl.program_id(0) == 0)
    def _():
        out_weight[...] = jnp.zeros_like(out_weight)

    attended = attended_ref[0]
    out_weight[...] += dot(attended, c_ref[0])
    branch = dot(attended.T, merge_ref[...]) + branch_ref[0].astype(F32)
    cols = branch.shape[1] // slices
    for m in range(slices):
        out_branch[m, 0] = branch[:, m * cols : (m + 1) * cols].astype(BF16)


def settle_kernel(counts, slices, sub, per_piece, table_ref, *refs):
    pieces, out, buf, sems, out_sems = refs[:-4], refs[-4], refs[-3], refs[-2], refs[-1]
    column = table_ref[sum(counts)]
    loads, stores = [], []
    arrays = max(ref for ref, _ in per_piece) + 1
    first = 0
    for c, count in enumerate(counts):
        for k in range(slices):
            ref, where = per_piece[k]
            start = pl.multiple_of(lax.bitwise_xor(jnp.int32(k), column) * sub, sub)
            for t in range(count):
                at = len(loads)
                loads.append(
                    pltpu.make_async_copy(
                        pieces[c * arrays + ref].at[where, t], buf.at[at], sems.at[at]
                    )
                )
                stores.append(
                    pltpu.make_async_copy(
                        buf.at[at],
                        out.at[table_ref[first + t], pl.ds(start, sub)],
                        out_sems.at[at],
                    )
                )
        first += count
    for copy in loads:
        copy.start()
    for load, store in zip(loads, stores):
        load.wait()
        store.start()
    for copy in stores:
        copy.wait()


def exchange_x(array):
    n = array.shape[0]
    return lax.ppermute(array[1::2], "seq", [(i, i ^ 1) for i in range(n)])


def exchange_z(array, got, steps=None):
    n = array.shape[0]
    return [
        lax.ppermute(jnp.stack([array[k], got[k // 2]]), "seq", [(i, i ^ k) for i in range(n)])
        for k in (range(2, n, 2) if steps is None else steps)
    ]


def exchanged(array, got, gots):
    return jnp.concatenate([array[:1], got[:1], *gots], axis=0)


def sum_on(terms, axis, n, masks):
    for step in range(len(masks)):
        terms = {k: v.astype(BF16) for k, v in terms.items()}
        got = cube_send(terms, axis, n, masks[step:])
        terms = cube_add(terms, got, masks[step:], F32)
    return terms[0].astype(BF16)


def take(array, index):
    return jnp.take(array, index, axis=0, mode="clip")


def on_device_pairs(
    tokens,
    lengths,
    counts,
    norm_gain,
    norm_bias,
    head_weight,
    merge_weight,
    up_weight,
    up_bias,
    down_weight,
    down_bias,
    cotangent,
):
    packs, shard, width = tokens.shape
    n = lax.axis_size("seq")
    slices = lax.axis_size("mlp")
    pack_len = shard * n
    rank = lax.axis_index("seq").astype(jnp.int32)
    column = lax.axis_index("mlp").astype(jnp.int32)
    heads = merge_weight.shape[0] // HD
    joined = heads * HD
    half = heads // 2
    cols = width // slices
    sub = shard // slices
    seq_masks, mlp_masks = masks_of(n), masks_of(slices)
    pairs = n // 2

    cot = lax.all_gather(cotangent, "mlp", axis=2, tiled=True)

    first, position, cost = layout(lengths, counts, pack_len)
    ids = jnp.arange(packs, dtype=jnp.int32)
    before = (cost[None, :] > cost[:, None]) | (
        (cost[None, :] == cost[:, None]) & (ids[None, :] < ids[:, None])
    )
    order = jnp.sum(before.astype(jnp.int32), axis=1)
    by_order = jnp.sum(
        jnp.where(order[None, :] == ids[:, None], ids[None, :], 0), axis=-1
    ).astype(jnp.int32)
    devices = jnp.arange(n, dtype=jnp.int32)
    shared_of = by_order[:pairs]
    own_of = by_order[pairs + 2 * (pairs - 1 - devices // 2) + devices % 2]
    late = order - pairs
    pair_of = jnp.where(late < 0, order, pairs - 1 - late // 2)
    device_of = 2 * pair_of + jnp.where(late < 0, 0, late % 2)
    dest = jnp.bitwise_xor(rank, devices)
    own_dest, shared_dest = own_of[dest], shared_of[dest // 2]
    me = jnp.stack([rank, column])

    head_ids = jnp.arange(heads, dtype=jnp.int32)
    half_ids = jnp.arange(half, dtype=jnp.int32)
    units_out = jnp.concatenate(
        [
            own_dest[:, None] * heads + head_ids[None, :],
            shared_dest[:, None] * heads + (dest % 2)[:, None] * half + half_ids[None, :],
        ],
        axis=1,
    ).reshape(-1)
    is_shared = (order < pairs)[:, None]
    holder = device_of[:, None] + jnp.where(is_shared, head_ids[None, :] // half, 0)
    units_in = (
        jnp.bitwise_xor(holder, rank) * (heads + half)
        + jnp.where(is_shared, heads + head_ids[None, :] % half, head_ids[None, :])
    ).reshape(-1)

    def tables(pack):
        freq = 10000.0 ** (-(2.0 * jnp.arange(ROT // 2, dtype=F32)) / ROT)
        angle = take(position, pack).astype(F32)[None, :] * jnp.repeat(freq, 2)[:, None]
        return jnp.cos(angle), jnp.sin(angle)

    w_heads = jnp.transpose(head_weight, (0, 2, 1)).reshape(3, heads, HD, width)
    packs_here = (own_of[rank], shared_of[rank // 2])
    turns = [tables(p) for p in packs_here]
    firsts = [take(first, p).reshape(n, shard) for p in packs_here]
    lows = [(f[:, 0] // shard).astype(jnp.int32) for f in firsts]
    gain, bias = norm_gain.reshape(1, width), norm_bias.reshape(1, width)

    def whole2(s, *_):
        return (0, 0)

    def lane_at(s, *_):
        return (0, s)

    def heads_at(h):
        pieces = heads // h
        return pl.BlockSpec(
            (3, h, HD, width), lambda s, me: (0, lax.rem(me[0], jnp.int32(pieces)), 0, 0)
        )

    def project(rows, h, cosine, sine):
        return pl.pallas_call(
            functools.partial(qkv_kernel, h),
            grid_spec=pltpu.PrefetchScalarGridSpec(
                num_scalar_prefetch=1,
                grid=(n,),
                in_specs=[
                    pl.BlockSpec(
                        (1, shard, width), lambda s, me: (lax.bitwise_xor(s, me[0]), 0, 0)
                    ),
                    heads_at(h),
                    pl.BlockSpec((ROT, shard), lane_at),
                    pl.BlockSpec((ROT, shard), lane_at),
                ],
                out_specs=[
                    pl.BlockSpec((shard, width), lambda s, *_: (s, 0)),
                    pl.BlockSpec((h, 3, HD, shard), lambda s, *_: (0, 0, 0, s)),
                ],
            ),
            out_shape=[
                jax.ShapeDtypeStruct((pack_len, width), BF16),
                jax.ShapeDtypeStruct((h, 3, HD, pack_len), BF16),
            ],
            compiler_params=params(),
            cost_estimate=COST,
            name="project",
        )(me, rows, w_heads, cosine, sine)

    def wide(h):
        return [pltpu.VMEM((h, n, HD, shard), BF16)]

    def tall(h, kind=BF16):
        return [pltpu.VMEM((h, n, shard, HD), kind)]

    def keep_spec(h):
        return pl.BlockSpec((h, n, HD, shard), lambda u, *_: (u, 0, 0, 0))

    def log_spec(h):
        return pl.BlockSpec((h, n, shard), lambda u, *_: (u, 0, 0))

    def unit_spec(h):
        return pl.BlockSpec((h, 3, HD, pack_len), lambda u, *_: (u, 0, 0, 0))

    def attend(c, qkv):
        h = qkv.shape[0]
        return pl.pallas_call(
            functools.partial(unit_kernel, n, shard),
            grid_spec=pltpu.PrefetchScalarGridSpec(
                num_scalar_prefetch=2,
                grid=(1,),
                in_specs=[pl.BlockSpec((n, shard), whole2), unit_spec(h)],
                out_specs=[
                    pl.BlockSpec((n, h, HD, shard), lambda u, *_: (0, u, 0, 0)),
                    keep_spec(h),
                    log_spec(h),
                ],
                scratch_shapes=wide(h) * 2 + tall(h),
            ),
            out_shape=[
                jax.ShapeDtypeStruct((n, h, HD, shard), BF16),
                jax.ShapeDtypeStruct((h, n, HD, shard), BF16),
                jax.ShapeDtypeStruct((h, n, shard), F32),
            ],
            compiler_params=params(),
            cost_estimate=COST,
            name="attend",
        )(me, lows[c], firsts[c], qkv)

    def attend_back(c, kept, logsum, qkv, grads):
        h = qkv.shape[0]
        step = h if c == 0 else 2
        skip = c * heads // step
        return pl.pallas_call(
            functools.partial(unit_back_kernel, n, shard, c + 1),
            grid_spec=pltpu.PrefetchScalarGridSpec(
                num_scalar_prefetch=2,
                grid=(h // step,),
                in_specs=[
                    pl.BlockSpec((n, shard), whole2),
                    keep_spec(step),
                    log_spec(step),
                    unit_spec(step),
                ]
                + [
                    pl.BlockSpec(
                        (1 if at < 2 else 2, step, HD, shard), lambda u, *_: (0, u + skip, 0, 0)
                    )
                    for at in range(len(grads))
                ],
                out_specs=unit_spec(step),
                scratch_shapes=wide(step) * 3 + tall(step) * 4 + tall(step, F32) * 2 + wide(step),
            ),
            out_shape=jax.ShapeDtypeStruct((h, 3, HD, pack_len), BF16),
            compiler_params=params(),
            cost_estimate=COST,
            name="attend_back",
        )(me, lows[c], firsts[c], kept, logsum, qkv, *grads)

    def rows_back(grads, normed, cosine, sine, *base):
        h = grads.shape[0]
        return pl.pallas_call(
            functools.partial(rows_kernel, h, slices),
            grid_spec=pltpu.PrefetchScalarGridSpec(
                num_scalar_prefetch=1,
                grid=(n,),
                in_specs=[
                    pl.BlockSpec((h, 3, HD, shard), lambda s, *_: (0, 0, 0, s)),
                    pl.BlockSpec((shard, width), lambda s, *_: (s, 0)),
                    heads_at(h),
                    pl.BlockSpec((ROT, shard), lane_at),
                    pl.BlockSpec((ROT, shard), lane_at),
                ]
                + [pl.BlockSpec(v.shape, whole2) for v in base],
                out_specs=[
                    pl.BlockSpec(
                        (slices // 2, 1, sub, width),
                        lambda s, me: (0, lax.bitwise_xor(s, me[0]), 0, 0),
                    )
                ]
                * 2
                + [
                    pl.BlockSpec((3 * joined, width), whole2),
                ],
            ),
            out_shape=[
                jax.ShapeDtypeStruct((slices // 2, n, sub, width), BF16),
                jax.ShapeDtypeStruct((slices // 2, n, sub, width), BF16),
                jax.ShapeDtypeStruct((3 * joined, width), F32),
            ],
            compiler_params=params(),
            cost_estimate=COST,
            name="rows_back",
        )(me, grads, normed, w_heads, cosine, sine, *base)

    pack_spec = pl.BlockSpec((1, shard, width), lambda p, *_: (p, 0, 0))
    normed_low, normed_cols = pl.pallas_call(
        norm_kernel,
        grid_spec=pltpu.PrefetchScalarGridSpec(
            num_scalar_prefetch=1,
            grid=(packs,),
            in_specs=[
                pack_spec,
                pl.BlockSpec((1, width), whole2),
                pl.BlockSpec((1, width), whole2),
            ],
            out_specs=[pack_spec, pl.BlockSpec((1, shard, cols), lambda p, *_: (p, 0, 0))],
        ),
        out_shape=[
            jax.ShapeDtypeStruct((packs, shard, width), BF16),
            jax.ShapeDtypeStruct((packs, shard, cols), BF16),
        ],
        compiler_params=params(),
        cost_estimate=COST,
        name="norm",
    )(me, tokens, gain, bias)
    send_own = take(normed_cols, own_dest)
    send_shared = take(normed_cols, shared_dest)
    own_x = exchange_x(send_own)

    hidden = (
        jnp.einsum("psd,df->psf", normed_low, up_weight, preferred_element_type=F32) + up_bias
    )
    own_x, hidden, send_own, send_shared = tie(own_x, hidden, send_own, send_shared)

    own_z = exchange_z(send_own, own_x, [2])
    shared_x = exchange_x(send_shared)
    active_low = jax.nn.gelu(hidden, approximate=True).astype(BF16)
    branch_ff = jnp.einsum(
        "psf,fd->psd", active_low, down_weight, preferred_element_type=F32
    ).astype(BF16)
    own_z, shared_x, branch_ff, send_own, own_x, merge_here, down_here, turns, w_heads = tie(
        own_z,
        shared_x,
        branch_ff,
        send_own,
        own_x,
        merge_weight,
        down_weight,
        turns,
        w_heads,
    )

    own_z += exchange_z(send_own, own_x, range(4, n, 2))
    active_grad = jnp.einsum("psd,fd->psf", cot, down_here, preferred_element_type=F32)
    _, gelu_back = jax.vjp(lambda values: jax.nn.gelu(values, approximate=True), hidden)
    hidden_grad = gelu_back(active_grad)[0].astype(BF16)
    biases = jnp.sum(hidden_grad.astype(F32), axis=(0, 1)), jnp.sum(cot.astype(F32), axis=(0, 1))
    own_z, hidden_grad, send_shared, shared_x, biases = tie(
        own_z, hidden_grad, send_shared, shared_x, biases
    )
    rows_own = lax.all_gather(exchanged(send_own, own_x, own_z), "mlp", axis=2, tiled=True)

    shared_z = exchange_z(send_shared, shared_x)
    out_grad = jnp.einsum("hd,psd->phs", merge_here, cot, preferred_element_type=F32).astype(BF16)
    send_grad = take(out_grad.reshape(packs * heads, HD, shard), units_out).reshape(
        n, heads + half, HD, shard
    )
    up_grad = jnp.einsum(
        "psd,psf->df", normed_low, hidden_grad, preferred_element_type=F32
    ).astype(BF16)
    down_grad = jnp.einsum("psd,psf->df", cot, active_low, preferred_element_type=F32).astype(BF16)
    shared_z, send_grad, up_grad, down_grad, send_shared, shared_x, hidden_grad = tie(
        shared_z, send_grad, up_grad, down_grad, send_shared, shared_x, hidden_grad
    )
    rows_shared = lax.all_gather(
        exchanged(send_shared, shared_x, shared_z), "mlp", axis=2, tiled=True
    )

    grad_x = exchange_x(send_grad)
    low_ff = jnp.einsum(
        "psf,df->psd", hidden_grad, up_weight, preferred_element_type=F32
    ).astype(BF16)
    low_ff = jnp.transpose(low_ff.reshape(packs, slices, sub, width), (1, 0, 2, 3)).reshape(
        slices * packs * sub, width
    )
    grad_x, send_grad, low_ff, rows_own, biases = tie(grad_x, send_grad, low_ff, rows_own, biases)
    low_ff = lax.psum_scatter(low_ff, "mlp", scatter_dimension=0, tiled=True).reshape(
        packs, sub, width
    )

    grad_z = exchange_z(send_grad, grad_x)
    normed_own, qkv_own = project(rows_own, heads, *turns[0])
    out_own, kept_own, log_own = attend(0, qkv_own)
    grad_z, out_own, kept_own, log_own, rows_shared = tie(
        grad_z, out_own, kept_own, log_own, rows_shared
    )
    grads = [send_grad, grad_x, *grad_z]

    def with_row(*parts):
        weight = jnp.concatenate(parts[:2], axis=1)
        row = jnp.concatenate(parts[2:])
        row = jnp.pad(row, (0, weight.shape[1] - row.shape[0])).reshape(1, -1)
        row = jnp.broadcast_to(row, (16, weight.shape[1])).astype(BF16)
        return jnp.concatenate([weight, row], axis=0)

    terms = dict(
        enumerate(
            with_row(*parts)
            for parts in zip(*[cut(v, 0, n, rank) for v in (up_grad, down_grad, *biases)])
        )
    )
    terms_got = cube_send(terms, "seq", n, seq_masks)
    normed_shared, qkv_shared = project(rows_shared, half, *turns[1])
    out_shared, kept_shared, log_shared = attend(1, qkv_shared)
    out_shared, kept_shared, log_shared, grads, terms_got = tie(
        out_shared, kept_shared, log_shared, grads, terms_got
    )
    terms = cube_add(terms, terms_got, seq_masks, BF16)
    terms_got = cube_send(terms, "seq", n, seq_masks[1:])

    send_out = jnp.concatenate([out_own, out_shared], axis=1)
    out_x = exchange_x(send_out)
    back_own = attend_back(0, kept_own, log_own, qkv_own, grads)
    out_x, back_own, terms_got, send_out = tie(out_x, back_own, terms_got, send_out)

    out_z = exchange_z(send_out, out_x)
    low_kept, low_sent, head_own = rows_back(back_own, normed_own, *turns[0])
    back_shared = attend_back(1, kept_shared, log_shared, qkv_shared, grads)
    out_z, low_kept, low_sent, back_shared, send_out, out_x = tie(
        out_z, low_kept, low_sent, back_shared, send_out, out_x
    )

    others = [(i, i ^ 1) for i in range(slices)]
    low_got, back_shared = tie(lax.ppermute(low_sent, "mlp", others), back_shared)
    low_terms = {
        2 * k: low_kept[k].astype(F32) + low_got[k].astype(F32) for k in range(slices // 2)
    }
    low_own = sum_on(low_terms, "mlp", slices, mlp_masks[1:])
    low_kept, low_sent, head_all = rows_back(back_shared, normed_shared, *turns[1], head_own)
    attended = take(
        exchanged(send_out, out_x, out_z).reshape(n * (heads + half), HD, shard), units_in
    ).reshape(packs, joined, shard)
    for step in range(1, len(seq_masks) - 1):
        terms = cube_add(terms, terms_got, seq_masks[step:], BF16)
        terms_got = cube_send(terms, "seq", n, seq_masks[step + 1 :])
    low_own, low_kept, low_sent, attended, terms_got = tie(
        low_own, low_kept, low_sent, attended, terms_got
    )
    terms = cube_add(terms, terms_got, seq_masks[len(seq_masks) - 1 :], F32)[0]

    low_own_x = exchange_x(low_own)
    low_got = lax.ppermute(low_sent, "mlp", others)
    branch, merge_part = pl.pallas_call(
        functools.partial(join_kernel, slices),
        grid=(packs,),
        in_specs=[
            pl.BlockSpec((1, joined, shard), lambda p: (p, 0, 0)),
            pl.BlockSpec((1, shard, width), lambda p: (p, 0, 0)),
            pl.BlockSpec((joined, width), whole2),
            pl.BlockSpec((1, shard, width), lambda p: (p, 0, 0)),
        ],
        out_specs=[
            pl.BlockSpec((slices, 1, shard, cols), lambda p: (0, p, 0, 0)),
            pl.BlockSpec((joined, width), whole2),
        ],
        out_shape=[
            jax.ShapeDtypeStruct((slices, packs, shard, cols), BF16),
            jax.ShapeDtypeStruct((joined, width), F32),
        ],
        compiler_params=params(),
        cost_estimate=COST,
        name="join",
    )(attended, cot, merge_weight, branch_ff)
    low_kept, low_got, low_own, low_own_x, branch, low_ff, head_all = tie(
        low_kept, low_got, low_own, low_own_x, branch, low_ff, head_all
    )
    summed = lax.psum_scatter(branch, "mlp", scatter_dimension=0, tiled=False)

    low_terms = {
        2 * k: low_kept[k].astype(F32) + low_got[k].astype(F32) for k in range(slices // 2)
    }
    low_shared = sum_on(low_terms, "mlp", slices, mlp_masks[1:])
    weights = {
        k: jnp.concatenate(pair, axis=0).astype(BF16)
        for k, pair in enumerate(zip(cut(head_all, 1, n, rank), cut(merge_part, 1, n, rank)))
    }
    low_own_z = exchange_z(low_own, low_own_x)
    weights_got = cube_send(weights, "seq", n, seq_masks)
    low_own_z, low_shared, low_own, low_own_x, weights, weights_got, terms = tie(
        low_own_z, low_shared, low_own, low_own_x, weights, weights_got, terms
    )

    low_shared_x = exchange_x(low_shared)
    weights = cube_add(weights, weights_got, seq_masks, BF16)
    weights_got = cube_send(weights, "seq", n, seq_masks[1:])

    def finish(lows, index, which):
        count = which.shape[0]
        row_spec = pl.BlockSpec((1, sub, width), lambda t, at: (at[count + t], at[0], 0))

        def part(i):
            return pl.BlockSpec(
                (1, sub, width), lambda t, at: (at[(2 + i) * count + t], 0, 0)
            )

        table = [jnp.full((count,), column), which, *index]
        return pl.pallas_call(
            functools.partial(finish_kernel, len(lows)),
            grid_spec=pltpu.PrefetchScalarGridSpec(
                num_scalar_prefetch=1,
                grid=(count,),
                in_specs=[part(i) for i in range(len(lows))]
                + [
                    pl.BlockSpec((1, sub, width), lambda t, at: (at[count + t], 0, 0)),
                    row_spec,
                    row_spec,
                    pl.BlockSpec((1, width), whole2),
                ],
                out_specs=[
                    pl.BlockSpec((1, sub, width), lambda t, *_: (t, 0, 0)),
                    pl.BlockSpec((2, width), whole2),
                ],
            ),
            out_shape=[
                jax.ShapeDtypeStruct((count, sub, width), BF16),
                jax.ShapeDtypeStruct((2, width), F32),
            ],
            compiler_params=params(),
            cost_estimate=COST,
            name="finish",
        )(jnp.concatenate(table), *lows, low_ff, tokens, cot, gain)

    row_own, sums_own = finish(
        [exchanged(low_own, low_own_x, low_own_z)], [devices], own_dest
    )
    low_shared_x, row_own, sums_own, low_shared, weights_got = tie(
        low_shared_x, row_own, sums_own, low_shared, weights_got
    )
    for step in range(1, len(seq_masks)):
        last_step = step == len(seq_masks) - 1
        weights = cube_add(weights, weights_got, seq_masks[step:], F32 if last_step else BF16)
        if not last_step:
            weights_got = cube_send(weights, "seq", n, seq_masks[step + 1 :])
    weights = weights[0]
    low_shared_z = exchange_z(low_shared, low_shared_x)
    pieces = gather_step([row_own[None]], "mlp", slices, mlp_masks[-1])
    result = (
        lax.dynamic_slice_in_dim(tokens, column * cols, cols, 2).astype(F32)
        + summed.astype(F32)
        + lax.dynamic_slice_in_dim(down_bias, column * cols, cols, 0)
    ).astype(BF16)
    low_shared_z, pieces, weights, result = tie(low_shared_z, pieces, weights, result)

    for m in reversed(mlp_masks[:-1]):
        pieces = gather_step(pieces, "mlp", slices, m)
    both = exchanged(low_shared, low_shared_x, low_shared_z)
    even = jnp.bitwise_xor(2 * jnp.arange(pairs, dtype=jnp.int32), rank)
    row_shared, sums = finish([both, both], [even, jnp.bitwise_xor(even, 1)], shared_of)
    last = gather_step([row_shared[None]], "mlp", slices, mlp_masks[-1])
    vectors = small_sum(sums_own + sums, n, slices)
    last, pieces, vectors = tie(last, pieces, vectors)

    for m in reversed(mlp_masks[:-1]):
        last = gather_step(last, "mlp", slices, m)
    pieces += last
    where = [(0, 0)]
    lookup = [0]
    for i, m in enumerate(reversed(mlp_masks)):
        where += [(i + 1, j) for j in range(len(lookup))]
        lookup += [k ^ m for k in lookup]
    per_piece = [where[lookup.index(k)] for k in range(slices)]
    tokens_grad = pl.pallas_call(
        functools.partial(settle_kernel, (n, pairs), slices, sub, per_piece),
        grid_spec=pltpu.PrefetchScalarGridSpec(
            num_scalar_prefetch=1,
            grid=(1,),
            in_specs=[pl.BlockSpec(memory_space=pl.ANY)] * len(pieces),
            out_specs=pl.BlockSpec(memory_space=pl.ANY),
            scratch_shapes=[
                pltpu.VMEM((packs * slices, sub, width), BF16),
                pltpu.SemaphoreType.DMA((packs * slices,)),
                pltpu.SemaphoreType.DMA((packs * slices,)),
            ],
        ),
        out_shape=jax.ShapeDtypeStruct((packs, shard, width), BF16),
        compiler_params=params(),
        name="settle",
    )(jnp.concatenate([own_dest, shared_of, column.reshape(1)]), *pieces)

    part, hidden_here = width // n, up_weight.shape[1]
    return (
        result,
        tokens_grad,
        vectors[0],
        vectors[1],
        jnp.transpose(weights[: 3 * joined].reshape(3, joined, part), (0, 2, 1)),
        weights[3 * joined :],
        terms[:part, :hidden_here],
        terms[part, : hidden_here // n],
        terms[:part, hidden_here:].T,
        terms[part, hidden_here // n : hidden_here // n + part],
    )


def solution(mesh):
    in_specs = (
        P(None, "seq", None),
        P(),
        P(),
        P(),
        P(),
        P(None, None, "mlp"),
        P("mlp", None),
        P(None, "mlp"),
        P("mlp"),
        P("mlp", None),
        P(),
        P(None, "seq", "mlp"),
    )
    out_specs = (
        P(None, "seq", "mlp"),
        P(None, "seq", None),
        P("seq"),
        P("seq"),
        P(None, "seq", "mlp"),
        P("mlp", "seq"),
        P("seq", "mlp"),
        P(("mlp", "seq")),
        P("mlp", "seq"),
        P("seq"),
    )
    n, slices = mesh.shape["seq"], mesh.shape["mlp"]

    def plan(*args):
        packs, pack_len, _ = args[0].shape
        heads = args[6].shape[0] // HD // slices
        pairs = (
            2 * packs == 3 * n
            and n >= 4
            and heads % 4 == 0
            and (pack_len // n) % 128 == 0
            and (pack_len // n) % (16 * slices) == 0
        )
        return jax.shard_map(
            on_device_pairs if pairs else on_device,
            mesh=mesh,
            in_specs=in_specs,
            out_specs=out_specs,
            check_vma=False,
        )(*args)

    return plan
```
